32 devices in a mesh: section: 2 (over core), expert: 4 (over z), shard: 4 (over y, x).
Axes of the slice: x: 2, y: 2, z: 4, core: 2. Of those that a mesh axis runs over, the one named last changes fastest.
Arguments:
- tokens_in: bfloat16 [2, 2048, 768], P(None, ('expert', 'shard')), may hold values from -6 to 6
- cotangent: bfloat16 [2, 2048, 768], P(None, ('expert', 'shard')), may hold values from -6 to 6
- lengths: int32 [2, 16, 8], P(None, ('expert', 'shard')), may hold values from 0 to 128, as said below
- routes: int32 [2, 2, 2048, 1], P('section', None, ('expert', 'shard')), may hold values from 0 to 15; in each aligned block of 128 rows (0 to 127, 128 to 255, ..., all dimensions but the last counted through in order) at most 12 rows name the same one
- w_query: bfloat16 [2, 768, 768], P('section', 'shard'), may hold values from -0.21875 to 0.21875
- w_key: bfloat16 [2, 768, 768], P('section', 'shard'), may hold values from -0.21875 to 0.21875
- w_value: bfloat16 [2, 768, 768], P('section', 'shard'), may hold values from -0.21875 to 0.21875
- w_output: bfloat16 [2, 768, 768], P('section', 'shard'), may hold values from -1.75 to 1.75
- gain_attn: bfloat16 [2, 768], P('section', 'shard'), may hold values from 0.25 to 1.75
- gain_moe: bfloat16 [2, 768], P('section', 'shard'), may hold values from 0.25 to 1.75
- w_router: bfloat16 [2, 768, 16], P('section', 'shard'), may hold values from -0.14941406 to 0.14941406
- bias_table: bfloat16 [2, 32, 12], P('section', 'shard'), may hold values from -4 to 4
- w_in: bfloat16 [2, 16, 768, 3072], P('section', ('expert', 'shard')), may hold values from -0.21875 to 0.21875
- w_out: bfloat16 [2, 16, 3072, 768], P('section', ('expert', 'shard')), may hold values from -2.65625 to 2.65625
Outputs:
- layer_out: bfloat16 [2, 2, 2048, 768], P('section', None, ('expert', 'shard'))
- input_grad: bfloat16 [2, 2, 2048, 768], P('section', None, ('expert', 'shard'))
- grad_w_query: bfloat16 [2, 768, 768], P('section', 'shard')
- grad_w_key: bfloat16 [2, 768, 768], P('section', 'shard')
- grad_w_value: bfloat16 [2, 768, 768], P('section', 'shard')
- grad_w_output: bfloat16 [2, 768, 768], P('section', 'shard')
- grad_gain_attn: bfloat16 [2, 768], P('section', 'shard')
- grad_gain_moe: bfloat16 [2, 768], P('section', 'shard')
- grad_router: bfloat16 [2, 768, 16], P('section', 'shard')
- grad_table: bfloat16 [2, 32, 12], P('section', 'shard')
- grad_w_in: bfloat16 [2, 16, 768, 3072], P('section', ('expert', 'shard'))
- grad_w_out: bfloat16 [2, 16, 3072, 768], P('section', ('expert', 'shard'))
The draws below stay inside these ranges and needn't reach their ends.
Inputs may be any that keep to these rules, and one draw needn't show every extreme that they name: Each row of 8 lengths sums to 128; zero entries are empty. In every micro-batch some block holds one sequence of all 128 rows. `routes`: within the 128 rows of one block (one device's rows of one micro-batch and layer), no expert is named more than 12 times, a bound that some block reaches.
All inputs are finite; a program needn't handle non-finite values.
Results may differ from the reference program's by a relative error of at most 0.028.
Values may be sent and summed in bfloat16 or wider, within the bound.
No kernel may reach another device: no remote copies, remote signals or barrier semaphores. Data moves between devices by JAX's collectives and lax.ppermute only.
A program may use at most 192 MiB of HBM per device.

```python
import math
import jax
import jax.numpy as jnp
import numpy as np
from jax import lax

D = 768
HEADS = 12
FF = 3072
BUCKETS = 32
MICRO = 2
NSEQ = 8
TOK_DEV = 128
DATA = 16
EXPERTS = 16
TOKENS = 2048
CAP = 12


def draw_lengths(key, part):
    key = jax.random.fold_in(key, 11)
    cut_key, full_key = jax.random.split(key)
    cut_points = jax.random.randint(cut_key, (MICRO, DATA, NSEQ - 1), 0, TOK_DEV + 1)
    cut_points = jnp.sort(cut_points, axis=-1)
    lower_edge = jnp.concatenate([jnp.zeros((MICRO, DATA, 1), jnp.int32), cut_points], axis=-1)
    upper_edge = jnp.concatenate([cut_points, jnp.full((MICRO, DATA, 1), TOK_DEV, jnp.int32)], axis=-1)
    seq_spans = upper_edge - lower_edge
    chosen = jax.random.randint(full_key, (MICRO, 1), 0, DATA)
    whole_row = jnp.zeros((NSEQ,), jnp.int32).at[0].set(TOK_DEV)
    full_device = jnp.arange(DATA, dtype=jnp.int32)[None, :] == chosen
    return jnp.where(full_device[:, :, None], whole_row[None, None, :], seq_spans).astype(jnp.int32)


def level_of(stream_key, extent, cuts, least, top_value):
    loudness = 1.0
    for dim, parts in cuts:
        heights = jax.random.uniform(jax.random.fold_in(jax.random.fold_in(stream_key, 6), dim), (parts,), jnp.float32, least / len(cuts), top_value / len(cuts))
        loudness = loudness * jnp.repeat(jnp.exp(heights), extent[dim] // parts).reshape((-1,) + (1,) * (len(extent) - 1 - dim))
    return loudness


def shared_out(stream_key, own, number, rows, number_of, top, most, slope):
    ranking = jax.random.permutation(stream_key, number_of)
    heavy_load, usual = shares(number_of, rows * top, most, slope, True), shares(number_of, rows * top, most, slope, False)
    places = jnp.arange(number_of)

    def named(tallies, rotation):
        used = int((tallies > 0).sum())
        fixed = max(1, used // 4)
        shifted = fixed + (places - fixed + rotation * (used - fixed)) % max(1, number_of - fixed)
        return jnp.zeros((number_of,), jnp.int32).at[ranking[jnp.where(places < fixed, places, shifted)]].set(jnp.asarray(tallies, jnp.int32))

    tallies = jnp.where(number % 4 == 0, named(heavy_load, number // 4), named(usual, number - number // 4 - 1))
    mixed = jax.random.permutation(jax.random.fold_in(own, 3), number_of)
    source_of, receiver = mixed[0:number_of // 2 * 2:2], mixed[1:number_of // 2 * 2:2]
    margin = jnp.minimum(tallies[source_of] - 1, most - tallies[receiver]) // 2
    margin = jnp.where((source_of == ranking[0]) | (receiver == ranking[0]) | (tallies[receiver] == 0), 0, jnp.maximum(margin, 0))
    shifted = jax.random.randint(jax.random.fold_in(own, 4), (number_of // 2,), 0, 1 << 20) % (margin + 1)
    tallies = tallies.at[source_of].add(-shifted).at[receiver].add(shifted)
    items = jnp.searchsorted(jnp.cumsum(tallies), jnp.arange(rows * top), side="right").astype(jnp.int32)
    listing = items.reshape(top, rows).T
    listing = listing[jax.random.permutation(jax.random.fold_in(own, 1), rows)]
    rotation = jax.random.randint(jax.random.fold_in(own, 2), (rows, 1), 0, top)
    return jnp.take_along_axis(listing, (jnp.arange(top)[None, :] + rotation) % top, axis=1)


def shares(number_of, total, most, slope, full):
    loads = [(1 << 20) // math.isqrt(grade ** slope) + 1 for grade in range(1, number_of + 1)]
    largest = most if full else min(most, max(-(-total // number_of), total * loads[0] // sum(loads)))
    least = 1 if total - largest >= number_of - 1 else 0
    holding, surplus = [largest] + [least] * (number_of - 1), total - largest - least * (number_of - 1)
    while surplus > 0:
        movable = [i for i in range(1, number_of) if holding[i] < largest] or [i for i in range(1, number_of) if holding[i] < most]
        whole, remaining = sum([loads[i] for i in movable]), surplus
        for i in movable:
            addition = min(most - holding[i], max(1, remaining * loads[i] // whole), surplus)
            holding[i] = holding[i] + addition
            surplus = surplus - addition
    return np.array(holding)


def scatter_about(key, shape, scale, most, cuts=(), kind=jnp.bfloat16):
    array = scale * jax.random.normal(key, shape, jnp.float32)
    if cuts:
        array = array * level_of(key, shape, cuts, -0.22, 0.18)
    return jnp.clip(array, -most, most).astype(kind)


def setup_inputs(seed: int = 0) -> dict:
    streams_of = jax.random.split(jax.random.key(seed), 15)
    tokens_in = scatter_about(streams_of[0], (MICRO, TOKENS, D), 1.0, 6.0, ((1, 16),))
    cotangent = scatter_about(streams_of[1], (MICRO, TOKENS, D), 1.0, 6.0, ((1, 16),))
    lengths = draw_lengths(jax.random.fold_in(streams_of[14], 71), 0)
    routes_keys = jax.random.split(jax.random.fold_in(streams_of[3], 1), 2 * MICRO * TOKENS // TOK_DEV)
    routes_turns = jax.random.permutation(jax.random.fold_in(streams_of[3], 3), 2 * MICRO * TOKENS // TOK_DEV)
    routes = jax.vmap(lambda own, number: shared_out(jax.random.fold_in(streams_of[3], 2), own, number, TOK_DEV, EXPERTS, 1, CAP, 1))(routes_keys, routes_turns).reshape((2, MICRO, TOKENS, 1))
    w_query = scatter_about(streams_of[4], (2, D, D), D ** -0.5, 0.21875, ((0, 2), (1, 4)))
    w_key = scatter_about(streams_of[5], (2, D, D), D ** -0.5, 0.21875, ((0, 2), (1, 4)))
    w_value = scatter_about(streams_of[6], (2, D, D), D ** -0.5, 0.21875, ((0, 2), (1, 4)))
    w_output = scatter_about(streams_of[7], (2, D, D), (D // 64) ** -0.5, 1.75, ((0, 2), (1, 4)))
    gain_attn = jnp.clip(1.0 + 0.15 * jax.random.normal(streams_of[8], (2, D), jnp.float32), 0.25, 1.75).astype(jnp.bfloat16)
    gain_moe = jnp.clip(1.0 + 0.15 * jax.random.normal(streams_of[9], (2, D), jnp.float32), 0.25, 1.75).astype(jnp.bfloat16)
    w_router = scatter_about(streams_of[10], (2, D, EXPERTS), 0.025, 0.14941406, ((0, 2), (1, 4)))
    bias_table = scatter_about(streams_of[11], (2, BUCKETS, HEADS), 1.0, 4.0, ((0, 2), (1, 4)))
    w_in = scatter_about(streams_of[12], (2, EXPERTS, D, FF), D ** -0.5, 0.21875, ((0, 2), (1, 16)))
    w_out = scatter_about(streams_of[13], (2, EXPERTS, FF, D), (EXPERTS / (0.65 * FF ** 0.5)), 2.65625, ((0, 2), (1, 16)))
    return dict(tokens_in=tokens_in, cotangent=cotangent, lengths=lengths, routes=routes, w_query=w_query, w_key=w_key, w_value=w_value, w_output=w_output, gain_attn=gain_attn, gain_moe=gain_moe, w_router=w_router, bias_table=bias_table, w_in=w_in, w_out=w_out)


EPSILON = 1e-06
BOUNDS = (8, 12, 16, 23, 32, 46, 64, 91)
MASKED = -1e+30
HIGH = lax.Precision.HIGHEST

@jax.custom_vjp
def low(v):
    return lax.optimization_barrier(v.astype(jnp.bfloat16)).astype(jnp.float32)

@jax.custom_vjp
def low_back(v):
    return v

def low_keep(v):
    return (low(v), None)

def low_pass(kept, grad):
    return (grad,)

def back_keep(v):
    return (v, None)

def back_low(kept, grad):
    return (low(grad),)
low.defvjp(low_keep, low_pass)
low_back.defvjp(back_keep, back_low)

def bucket_index(relative):
    distance = jnp.abs(relative)
    bucket = jnp.zeros_like(relative)
    for lowest in range(1, 8):
        bucket = bucket + (distance >= lowest).astype(jnp.int32)
    for lowest in BOUNDS:
        bucket = bucket + (distance >= lowest).astype(jnp.int32)
    return bucket + 16 * (relative > 0).astype(jnp.int32)

def rms_scale(values, gain_row):
    inverse = lax.rsqrt(lax.optimization_barrier(jnp.mean(values * values, axis=-1, keepdims=True)) + EPSILON)
    return values * inverse * gain_row

def take_rows(source, picks):
    return jnp.take(source, picks, axis=0)

def layer(inputs, params, route_ids, segment, bucket):
    w_query, w_key, w_value, w_output, gain_one, gain_two, w_router, bias_rows, w_in, w_out = params
    block_count, rows_count, model_width = inputs.shape
    head_count = bias_rows.shape[1]
    head_size = model_width // head_count
    score_scale = head_size ** (-0.5)
    experts_count = w_router.shape[1]
    capacity = CAP
    normed_one = low(rms_scale(inputs, gain_one))
    flat_one = normed_one.reshape(-1, model_width)

    def project(weight):
        made = jnp.dot(flat_one, weight, precision=HIGH)
        return low(low_back(made)).reshape(block_count, rows_count, head_count, head_size)
    query_heads = project(w_query)
    key_heads = project(w_key)
    value_heads = project(w_value)
    bias_full = jnp.transpose(bias_rows[bucket], (2, 0, 1))

    def attend(block):
        query_block, key_block, value_block, segment_block = block
        scores = jnp.einsum('qhd,khd->hqk', query_block, key_block, precision=HIGH) * score_scale + bias_full
        scores = low_back(scores)
        visible = segment_block[:, None] == segment_block[None, :]
        scores = jnp.where(visible[None], scores, MASKED)
        probs = low(jax.nn.softmax(scores, axis=-1))
        return jnp.einsum('hqk,khd->qhd', probs, value_block, precision=HIGH)
    attended = lax.map(jax.checkpoint(attend), (query_heads, key_heads, value_heads, segment))
    attended = low(low_back(attended.reshape(block_count, rows_count, model_width)))
    branch = low_back(jnp.dot(attended, w_output, precision=HIGH))
    middle = inputs + branch
    normed_two = low(rms_scale(middle, gain_two))
    logits = low_back(jnp.dot(normed_two, w_router, precision=HIGH))
    router_probs = jax.nn.softmax(logits, axis=-1)
    onehot = (route_ids[..., None] == jnp.arange(experts_count, dtype=jnp.int32)).astype(jnp.int32)
    gate_value = lax.optimization_barrier(jnp.sum(router_probs * onehot.astype(inputs.dtype), axis=-1))
    running = jnp.cumsum(onehot, axis=1)
    position = lax.optimization_barrier(jnp.sum(running * onehot, axis=-1)) - 1
    slot_id = (route_ids * capacity + position).astype(jnp.int32)
    block_ids = jnp.broadcast_to(jnp.arange(block_count, dtype=jnp.int32)[:, None], slot_id.shape)
    token_ids = jnp.broadcast_to(jnp.arange(rows_count, dtype=jnp.int32)[None, :], slot_id.shape)
    slot_token = jnp.zeros((block_count, experts_count * capacity), jnp.int32).at[block_ids, slot_id].set(token_ids)
    filled = jnp.zeros((block_count, experts_count * capacity), inputs.dtype).at[block_ids, slot_id].set(1.0)
    sent = low_back(normed_two)
    buffer = jax.vmap(take_rows)(sent, slot_token) * filled[..., None]
    buffer = buffer.reshape(block_count, experts_count, capacity, model_width)
    buffer = jnp.transpose(buffer, (1, 0, 2, 3)).reshape(experts_count, block_count * capacity, model_width)

    def expert_pass(piece):
        rows_in, weight_in, weight_out = piece
        hidden_pre = low_back(jnp.dot(rows_in, weight_in, precision=HIGH))
        hidden = low(jax.nn.gelu(hidden_pre, approximate=True))
        return low(low_back(jnp.dot(hidden, weight_out, precision=HIGH)))
    produced = lax.map(jax.checkpoint(expert_pass), (buffer, w_in, w_out))
    produced = produced.reshape(experts_count, block_count, capacity, model_width)
    produced = jnp.transpose(produced, (1, 0, 2, 3)).reshape(block_count, experts_count * capacity, model_width)
    token_out = jax.vmap(take_rows)(produced, slot_id)
    return middle + gate_value[..., None] * token_out

def reference(tokens_in, cotangent, lengths, routes, w_query, w_key, w_value, w_output, gain_attn, gain_moe, w_router, bias_table, w_in, w_out):
    micro_count, total_rows, model_width = tokens_in.shape
    block_total = lengths.shape[1]
    rows_count = total_rows // block_total
    places = jnp.arange(rows_count, dtype=jnp.int32)
    bucket = bucket_index(places[None, :] - places[:, None])
    seq_ends = jnp.cumsum(lengths, axis=-1)
    segment = lax.optimization_barrier(jnp.sum((places[None, None, :, None] >= seq_ends[:, :, None, :]).astype(jnp.int32), axis=-1))
    segment = segment.reshape(micro_count * block_total, rows_count)
    route_ids = routes[..., 0].reshape(2, micro_count * block_total, rows_count)

    def params_of(section_id):
        members = (w_query, w_key, w_value, w_output, gain_attn, gain_moe, w_router, bias_table, w_in, w_out)
        return tuple((member[section_id].astype(jnp.float32) for member in members))
    first_in = tokens_in.astype(jnp.float32).reshape(micro_count * block_total, rows_count, model_width)

    def section_zero(inputs, params):
        return low(layer(inputs, params, route_ids[0], segment, bucket))

    def section_one(inputs, params):
        return layer(inputs, params, route_ids[1], segment, bucket)
    out_zero, back_zero = jax.vjp(section_zero, first_in, params_of(0))
    out_one, back_one = jax.vjp(section_one, out_zero, params_of(1))
    top_grad = cotangent.astype(jnp.float32).reshape(micro_count * block_total, rows_count, model_width)
    grad_one_in, grads_one = back_one(top_grad)
    grad_sent = low(grad_one_in)
    grad_zero_in, grads_zero = back_zero(grad_sent)
    full_shape = (micro_count, total_rows, model_width)
    layer_out = jnp.stack([out_zero.reshape(full_shape), out_one.reshape(full_shape)]).astype(jnp.bfloat16)
    input_grad = jnp.stack([grad_zero_in.reshape(full_shape), grad_one_in.reshape(full_shape)]).astype(jnp.bfloat16)
    stacked = [jnp.stack([first, second]).astype(jnp.bfloat16) for first, second in zip(grads_zero, grads_one)]
    return (layer_out, input_grad, stacked[0], stacked[1], stacked[2], stacked[3], stacked[4], stacked[5], stacked[6], stacked[7], stacked[8], stacked[9])
```

```python
import jax
import jax.numpy as jnp
from jax import lax
from jax.sharding import PartitionSpec as P

EPSILON = 1e-06
BOUNDS = (8, 12, 16, 23, 32, 46, 64, 91)
MASKED = -1e30
HIGH = lax.Precision.HIGHEST
F32 = jnp.float32
BF16 = jnp.bfloat16


def bucket_index(relative):
    distance = jnp.abs(relative)
    bucket = jnp.zeros_like(relative)
    for lowest in range(1, 8):
        bucket = bucket + (distance >= lowest).astype(jnp.int32)
    for lowest in BOUNDS:
        bucket = bucket + (distance >= lowest).astype(jnp.int32)
    return bucket + 16 * (relative > 0).astype(jnp.int32)


def rms_scale(values, gain_row):
    inverse = lax.rsqrt(jnp.mean(values * values, axis=-1, keepdims=True) + EPSILON)
    return values * inverse * gain_row


def smooth(values):
    return jax.nn.gelu(values, approximate=True)


def segment_ids(length_row, rows_count):
    seq_ends = jnp.cumsum(length_row)
    places = jnp.arange(rows_count, dtype=jnp.int32)
    return jnp.sum((places[:, None] >= seq_ends[None, :]).astype(jnp.int32), axis=1)


def slot_plan(route_row, experts_count, capacity):
    onehot = (route_row[:, None] == jnp.arange(experts_count, dtype=jnp.int32)[None, :]).astype(
        jnp.int32
    )
    running = jnp.cumsum(onehot, axis=0)
    position = jnp.sum(running * onehot, axis=1) - 1
    slot_id = route_row * capacity + position
    pick = slot_id[:, None] == jnp.arange(experts_count * capacity, dtype=jnp.int32)[None, :]
    return (onehot, pick.astype(BF16))


def cross(value, layer):
    return lax.ppermute(value, "section", [(1 - layer, layer)])


def swap(value):
    return lax.ppermute(value, "section", [(0, 1), (1, 0)])


def within(value, axis, distance, layer):
    size = lax.axis_size(axis)
    pairs = [(layer * size + i, layer * size + (i ^ distance)) for i in range(size)]
    return lax.ppermute(value, ("section", axis), pairs)


def gather_shards(packed, layer):
    me = lax.axis_index("shard")
    half = packed.shape[0] // 2
    top, low = (packed[:half], packed[half:])
    top_x, top_y = (within(top, "shard", 1, layer), within(top, "shard", 2, layer))
    low_x, low_y = (within(low, "shard", 1, layer), within(low, "shard", 2, layer))
    top_d = within(top_x, "shard", 2, layer)
    low_d = within(low_y, "shard", 1, layer)
    pieces = jnp.stack(
        [
            jnp.concatenate(pair)
            for pair in ((top, low), (top_x, low_x), (top_y, low_y), (top_d, low_d))
        ]
    )
    return jnp.stack(
        [lax.dynamic_index_in_dim(pieces, me ^ j, 0, keepdims=False) for j in range(4)]
    )


def reduce_shards(partial, layer):
    me = lax.axis_index("shard")
    low_partial = partial.astype(BF16)
    both = (partial + cross(low_partial, layer).astype(F32)).astype(BF16)
    half = both.shape[1] // 2

    def piece(which, rows):
        return lax.dynamic_index_in_dim(both, me ^ which, 0, keepdims=False)[rows]

    def halve(rows, first, second):
        sent = jnp.stack([piece(first, rows), piece(first ^ second, rows)])
        got = within(sent, "shard", first, layer)
        mine = piece(0, rows).astype(F32) + got[0].astype(F32)
        other = (piece(second, rows).astype(F32) + got[1].astype(F32)).astype(BF16)
        return mine + within(other, "shard", second, layer).astype(F32)

    total = jnp.concatenate([halve(slice(0, half), 1, 2), halve(slice(half, None), 2, 1)])
    count = lax.axis_size("expert")
    place = lax.axis_index("expert")
    distance = count // 2
    while distance:
        rows = total.shape[0] // 2
        upper = (place & distance) > 0
        keep = jnp.where(upper, total[rows:], total[:rows])
        give = jnp.where(upper, total[:rows], total[rows:]).astype(BF16)
        total = keep + within(give, "expert", distance, layer).astype(F32)
        distance //= 2
    total = total.astype(BF16)
    distance = 1
    while distance < count:
        upper = (place & distance) > 0
        got = within(total, "expert", distance, layer)
        total = jnp.where(upper, jnp.concatenate([got, total]), jnp.concatenate([total, got]))
        distance *= 2
    return total


def to_experts(buffer):
    return lax.all_to_all(buffer, ("expert", "shard"), split_axis=0, concat_axis=0, tiled=True)


def attention_forward(inputs32, weights, segment, bias_full):
    w_query, w_key, w_value, w_output, gain_one, gain_two, w_router = weights
    rows_count, model_width = inputs32.shape
    head_count = bias_full.shape[0]
    head_size = model_width // head_count
    normed_one = rms_scale(inputs32, gain_one).astype(BF16)

    def project(weight):
        made = jnp.dot(normed_one, weight, preferred_element_type=F32).astype(BF16)
        return made.reshape(rows_count, head_count, head_size)

    query, key, value = (project(w_query), project(w_key), project(w_value))
    scores = jnp.einsum("qhd,khd->hqk", query, key, preferred_element_type=F32)
    scores = scores * head_size ** (-0.5) + bias_full
    scores = jnp.where((segment[:, None] == segment[None, :])[None], scores, MASKED)
    probs = jax.nn.softmax(scores, axis=-1)
    probs_low = probs.astype(BF16)
    attended = jnp.einsum("hqk,khd->qhd", probs_low, value, preferred_element_type=F32)
    attended = attended.reshape(rows_count, model_width).astype(BF16)
    middle = inputs32 + jnp.dot(attended, w_output, preferred_element_type=F32)
    normed_two = rms_scale(middle, gain_two).astype(BF16)
    logits = jnp.dot(normed_two, w_router, preferred_element_type=F32)
    router_probs = jax.nn.softmax(logits, axis=-1)
    return (normed_one, query, key, value, probs_low, attended, middle, normed_two, router_probs)


def expert_forward(rows, w_in, w_out):
    hidden_pre = jnp.dot(rows, w_in, preferred_element_type=F32)
    hidden = smooth(hidden_pre).astype(BF16)
    produced = jnp.dot(hidden, w_out, preferred_element_type=F32).astype(BF16)
    return (hidden_pre, hidden, produced)


def expert_backward(grad_rows, hidden_pre, w_in, w_out):
    unused, smooth_back = jax.vjp(smooth, hidden_pre)
    grad_hidden = jnp.einsum("cd,fd->cf", grad_rows, w_out, preferred_element_type=F32)
    grad_pre = smooth_back(grad_hidden)[0].astype(BF16)
    grad_slots = jnp.einsum("cf,df->cd", grad_pre, w_in, preferred_element_type=F32).astype(BF16)
    return (grad_pre, grad_slots)


def attention_backward(grad_out, token_out, grad_token, inputs32, kept, weights, onehot, gate, bucket_onehot):
    normed_one, query, key, value, probs_low, attended, middle, normed_two, router_probs = kept
    w_query, w_key, w_value, w_output, gain_one, gain_two, w_router = weights
    rows_count, head_count, head_size = query.shape
    model_width = head_count * head_size
    scale = head_size ** (-0.5)
    grad_gate = jnp.sum(grad_out * token_out, axis=1)
    grad_logits = ((grad_gate * gate)[:, None] * (onehot - router_probs)).astype(BF16)
    grad_router = jnp.einsum("td,te->de", normed_two, grad_logits, preferred_element_type=F32)
    grad_normed_two = grad_token + jnp.einsum(
        "te,de->td", grad_logits, w_router, preferred_element_type=F32
    )
    unused, norm_back = jax.vjp(rms_scale, middle, gain_two)
    grad_from_norm, grad_gain_two = norm_back(grad_normed_two)
    grad_middle = grad_out + grad_from_norm
    grad_branch = grad_middle.astype(BF16)
    grad_w_output = jnp.einsum("td,te->de", attended, grad_branch, preferred_element_type=F32)
    grad_attended = jnp.einsum("te,de->td", grad_branch, w_output, preferred_element_type=F32)
    grad_attended = grad_attended.astype(BF16).reshape(rows_count, head_count, head_size)
    probs = probs_low.astype(F32)
    grad_probs = jnp.einsum("qhd,khd->hqk", grad_attended, value, preferred_element_type=F32)
    row_dot = jnp.sum(grad_probs * probs, axis=-1, keepdims=True)
    grad_scores = (probs * (grad_probs - row_dot)).astype(BF16)
    grad_bias = jnp.einsum(
        "hn,nb->bh", grad_scores.reshape(head_count, -1), bucket_onehot, preferred_element_type=F32
    )

    def flat(made):
        return made.astype(BF16).reshape(rows_count, model_width)

    grad_query = flat(jnp.einsum("hqk,khd->qhd", grad_scores, key, preferred_element_type=F32) * scale)
    grad_keys = flat(jnp.einsum("hqk,qhd->khd", grad_scores, query, preferred_element_type=F32) * scale)
    grad_values = flat(
        jnp.einsum("hqk,qhd->khd", probs_low, grad_attended, preferred_element_type=F32)
    )
    grad_normed_one = 0.0
    weight_grads = []
    for grad, weight in ((grad_query, w_query), (grad_keys, w_key), (grad_values, w_value)):
        weight_grads.append(
            jnp.einsum("td,te->de", normed_one, grad, preferred_element_type=F32)
        )
        grad_normed_one += jnp.einsum("te,de->td", grad, weight, preferred_element_type=F32)
    unused, norm_back_one = jax.vjp(rms_scale, inputs32, gain_one)
    grad_from_first, grad_gain_one = norm_back_one(grad_normed_one)
    grad_in = (grad_middle + grad_from_first).astype(BF16)
    weight_grads += [grad_w_output, grad_gain_one, grad_gain_two, grad_router, grad_bias]
    return (grad_in, weight_grads)


def pad_rows(flat, rows, width):
    flat = flat.reshape(flat.shape[0], -1)
    return jnp.pad(flat, ((0, 0), (0, rows * width - flat.shape[1]))).reshape(-1, rows, width)


def shards(
    tokens_in,
    cotangent,
    lengths,
    routes,
    w_query,
    w_key,
    w_value,
    w_output,
    gain_attn,
    gain_moe,
    w_router,
    bias_table,
    w_in,
    w_out,
):
    micro_count, rows_count, model_width = tokens_in.shape
    section = lax.axis_index("section")
    shard_count = lax.axis_size("shard")
    part = w_query.shape[1]
    experts_count = w_router.shape[2]
    bucket_part, head_count = bias_table.shape[1:]
    capacity = max(2, (3 * rows_count + 2 * experts_count - 1) // (2 * experts_count))
    router_rows = -(-part * experts_count // model_width)
    small_rows = router_rows + 2
    small_rows += -small_rows % 8

    smalls = jnp.concatenate(
        [
            pad_rows(w_router, router_rows, model_width)[0],
            pad_rows(jnp.concatenate([gain_attn, gain_moe], 1), 1, model_width)[0],
            pad_rows(bias_table, small_rows - router_rows - 1, model_width)[0],
        ]
    )
    packed = jnp.concatenate([w_query[0], w_key[0], w_value[0], w_output[0], smalls])

    def unpack(gathered):
        mats = [
            gathered[:, i * part : (i + 1) * part].reshape(shard_count * part, model_width)
            for i in range(4)
        ]
        rest = gathered[:, 4 * part :]
        router = rest[:, :router_rows].reshape(shard_count, -1)[:, : part * experts_count]
        gains = rest[:, router_rows].astype(F32)
        table = rest[:, router_rows + 1 :].reshape(shard_count, -1)[:, : bucket_part * head_count]
        return (
            *mats,
            gains[:, :part].reshape(-1),
            gains[:, part : 2 * part].reshape(-1),
            router.reshape(shard_count * part, experts_count),
        ), table.reshape(shard_count * bucket_part, head_count)

    def both_cores(layer, source):
        own = gather_shards(source, layer)
        other = lax.ppermute(own, "section", [(layer, 1 - layer)])
        return unpack(jnp.where(section == layer, own, other))

    weights0, table0 = both_cores(0, packed)
    other_in, other_out = (swap(w_in[0, 0]), swap(w_out[0, 0]))
    expert_in = [jnp.where(section == l, w_in[0, 0], other_in) for l in range(2)]
    expert_out = [jnp.where(section == l, w_out[0, 0], other_out) for l in range(2)]

    places = jnp.arange(rows_count, dtype=jnp.int32)
    bucket = bucket_index(places[None, :] - places[:, None]).reshape(-1)
    bucket_count = shard_count * bucket_part
    bucket_onehot = (bucket[:, None] == jnp.arange(bucket_count, dtype=jnp.int32)[None, :]).astype(BF16)

    def bias_of(table):
        return jnp.einsum("nb,bh->hn", bucket_onehot, table, preferred_element_type=F32).reshape(
            head_count, rows_count, rows_count
        )

    def mine(stack):
        return lax.dynamic_index_in_dim(stack, section, 0, keepdims=False)

    segment = segment_ids(mine(lengths[:, 0]), rows_count)
    route_table = routes[0, :, :, 0]
    other_route = swap(lax.dynamic_index_in_dim(route_table, 1 - section, 0, keepdims=False))
    own_route = mine(route_table)
    plans = [
        slot_plan(jnp.where(section == l, own_route, other_route), experts_count, capacity)
        for l in range(2)
    ]

    def select(pick, rows):
        return jnp.einsum("ts,td->sd", pick, rows, preferred_element_type=F32).astype(BF16)

    def fetch(pick, slots):
        return jnp.dot(pick, slots, preferred_element_type=F32)

    slots_shape = (experts_count, capacity, model_width)

    inputs0 = mine(tokens_in).astype(F32)
    kept0 = attention_forward(inputs0, weights0, segment, bias_of(table0))
    onehot0, pick0 = plans[0]
    onehot0 = onehot0.astype(F32)
    gate0 = jnp.sum(kept0[8] * onehot0, axis=1)
    packed_late, sent0 = lax.optimization_barrier((packed, select(pick0, kept0[7])))
    arrived0 = to_experts(sent0.reshape(slots_shape)).reshape(-1, model_width)
    weights1, table1 = both_cores(1, packed_late)
    pre0, hidden0, produced0 = expert_forward(arrived0, expert_in[0], expert_out[0])
    back0 = to_experts(produced0.reshape(slots_shape)).reshape(-1, model_width)
    token_out0 = fetch(pick0, back0)
    out0 = (kept0[6] + gate0[:, None] * token_out0).astype(BF16)

    inputs1 = out0.astype(F32)
    kept1 = attention_forward(inputs1, weights1, segment, bias_of(table1))
    onehot1, pick1 = plans[1]
    onehot1 = onehot1.astype(F32)
    gate1 = jnp.sum(kept1[8] * onehot1, axis=1)
    grad1 = mine(cotangent).astype(F32)
    sent1 = jnp.concatenate(
        [
            select(pick1, kept1[7]).reshape(slots_shape),
            select(pick1, (gate1[:, None] * grad1).astype(BF16)).reshape(slots_shape),
        ],
        axis=1,
    )
    arrived1 = to_experts(sent1)
    rows1 = arrived1[:, :capacity].reshape(-1, model_width)
    grad_rows1 = arrived1[:, capacity:].reshape(-1, model_width)
    pre1, hidden1, produced1 = expert_forward(rows1, expert_in[1], expert_out[1])
    grad_pre1, grad_slots1 = expert_backward(grad_rows1, pre1, expert_in[1], expert_out[1])
    back1 = to_experts(
        jnp.concatenate([produced1.reshape(slots_shape), grad_slots1.reshape(slots_shape)], axis=1)
    )
    token_out1 = fetch(pick1, back1[:, :capacity].reshape(-1, model_width))
    grad_token1 = fetch(pick1, back1[:, capacity:].reshape(-1, model_width))
    out1 = (kept1[6] + gate1[:, None] * token_out1).astype(BF16)

    grad_in1, grads1 = attention_backward(
        grad1, token_out1, grad_token1, inputs1, kept1, weights1, onehot1, gate1, bucket_onehot
    )

    grad0 = grad_in1.astype(F32)
    sent2 = select(pick0, (gate0[:, None] * grad0).astype(BF16))
    grad_rows0 = to_experts(sent2.reshape(slots_shape)).reshape(-1, model_width)
    grad_pre0, grad_slots0 = expert_backward(grad_rows0, pre0, expert_in[0], expert_out[0])
    back2 = to_experts(grad_slots0.reshape(slots_shape)).reshape(-1, model_width)
    grad_token0 = fetch(pick0, back2)
    grad_in0, grads0 = attention_backward(
        grad0, token_out0, grad_token0, inputs0, kept0, weights0, onehot0, gate0, bucket_onehot
    )

    count = lax.axis_size("expert")
    total_rows = 4 * part + small_rows
    padding = -total_rows % (16 * count)

    def pack_grads(grads):
        split = [grads[i].reshape(shard_count, part, model_width) for i in range(4)]
        split.append(pad_rows(grads[6].reshape(shard_count, -1), router_rows, model_width))
        gains = [grads[4].reshape(shard_count, part), grads[5].reshape(shard_count, part)]
        split.append(pad_rows(jnp.concatenate(gains, 1), 1, model_width))
        split.append(
            pad_rows(
                grads[7].reshape(shard_count, -1),
                small_rows - router_rows - 1 + padding,
                model_width,
            )
        )
        return jnp.concatenate(split, axis=1)

    total1 = reduce_shards(pack_grads(grads1), 1)
    total0 = reduce_shards(pack_grads(grads0), 0)
    total = jnp.where(section == 0, total0, total1)
    rest = total[4 * part :]
    final_router = rest[:router_rows].reshape(-1)[: part * experts_count]
    final_gains = rest[router_rows]
    final_table = rest[router_rows + 1 :].reshape(-1)[: bucket_part * head_count]

    stuff0 = (arrived0, grad_rows0, hidden0, grad_pre0)
    stuff1 = (rows1, grad_rows1, hidden1, grad_pre1)
    own_stuff, other_stuff = ([], [])
    for first, second in zip(stuff0, stuff1):
        own_stuff.append(jnp.where(section == 0, first, second))
        other_stuff.append(swap(jnp.where(section == 0, second, first)))
    rows, grad_rows, hidden, grad_pre = [
        jnp.concatenate(pair) for pair in zip(own_stuff, other_stuff)
    ]
    grad_w_in = jnp.einsum("cd,cf->df", rows, grad_pre, preferred_element_type=F32).astype(BF16)
    grad_w_out = jnp.einsum("cf,cd->fd", hidden, grad_rows, preferred_element_type=F32).astype(BF16)

    ours = jnp.where(section == 0, jnp.stack([out0, grad_in0]), jnp.stack([out1, grad_in1]))
    theirs = swap(jnp.where(section == 0, jnp.stack([out1, grad_in1]), jnp.stack([out0, grad_in0])))
    ordered = jnp.where(section == 0, jnp.stack([ours, theirs], 1), jnp.stack([theirs, ours], 1))

    return (
        ordered[0][None],
        ordered[1][None],
        total[:part][None],
        total[part : 2 * part][None],
        total[2 * part : 3 * part][None],
        total[3 * part : 4 * part][None],
        final_gains[:part][None],
        final_gains[part : 2 * part][None],
        final_router.reshape(1, part, experts_count),
        final_table.reshape(1, bucket_part, head_count),
        grad_w_in[None, None],
        grad_w_out[None, None],
    )


def solution(mesh):
    both = ("expert", "shard")
    plain = P("section", "shard", None)
    gains = P("section", "shard")
    blocks = P("section", None, both, None)
    experts = P("section", both, None, None)
    tokens = P(None, both, None)
    attention = (plain, plain, plain, plain, gains, gains, plain, plain, experts, experts)
    return jax.shard_map(
        shards,
        mesh=mesh,
        in_specs=(tokens, tokens, tokens, blocks, *attention),
        out_specs=(blocks, blocks, *attention),
        check_vma=False,
    )
```

```python
import functools

import jax
import jax.numpy as jnp
from jax import lax
from jax.experimental import pallas as pl
from jax.experimental.pallas import tpu as pltpu
from jax.sharding import PartitionSpec as P

EPSILON = 1e-06
BOUNDS = (8, 12, 16, 23, 32, 46, 64, 91)
MASKED = -1e30
F32 = jnp.float32
BF16 = jnp.bfloat16
I32 = jnp.int32
GELU_SCALE = 0.7978845608028654
GELU_CUBE = 0.044715
SMEM = pl.BlockSpec(memory_space=pltpu.SMEM)
VMEM = pl.BlockSpec(memory_space=pltpu.VMEM)
ANY = pl.BlockSpec(memory_space=pl.ANY)
LIMIT = pltpu.CompilerParams(vmem_limit_bytes=48 * 1024 * 1024)


def dot_nn(a, b):
    return jnp.dot(a, b, preferred_element_type=F32)


def dot_nt(a, b):
    return lax.dot_general(a, b, (((1,), (1,)), ((), ())), preferred_element_type=F32)


def dot_tn(a, b):
    return lax.dot_general(a, b, (((0,), (0,)), ((), ())), preferred_element_type=F32)


def iota(shape, dimension):
    return lax.broadcasted_iota(I32, shape, dimension)


def call(body, outs, ins, specs, scratch=(), **more):
    return pl.pallas_call(
        body,
        out_shape=outs,
        in_specs=specs,
        scratch_shapes=scratch,
        compiler_params=LIMIT,
        **more,
    )(*ins)


def bucket_of(relative):
    distance = jnp.abs(relative)
    bucket = jnp.zeros_like(relative)
    for lowest in tuple(range(1, 8)) + BOUNDS:
        bucket = bucket + (distance >= lowest).astype(I32)
    return bucket + 16 * (relative > 0).astype(I32)


class Sizes:
    def __init__(self, tokens_in, w_query, w_router, bias_table, w_in, shards):
        self.rows, self.width = tokens_in.shape[1:]
        self.part = w_query.shape[1]
        self.shards = shards
        self.experts = w_router.shape[2]
        self.bucket_part, self.heads = bias_table.shape[1:]
        self.buckets = self.bucket_part * shards
        self.hidden = w_in.shape[3]
        self.chunk = self.hidden // 6
        self.capacity = max(
            2, (3 * self.rows + 2 * self.experts - 1) // (2 * self.experts)
        )
        self.full, rest = divmod(self.capacity, 8)
        self.rest = next((power for power in (0, 1, 2, 4) if power >= rest), None)
        if self.rest is None:
            self.full, self.rest = (self.full + 1, 0)
        self.cuts = 8 // self.rest if self.rest else 0
        self.cut = self.width // self.cuts if self.rest else 0
        self.slot_width = self.full * self.width + self.cut
        self.slot_rows = self.experts * 8
        self.expert_rows = self.slot_rows * self.full + self.experts * self.rest
        self.small = -(-(self.experts + self.heads + 2) // 128) * 128
        self.small_groups = self.width // self.small
        self.small_rows = self.part // self.small_groups
        self.gain_lane = self.experts + self.heads
        self.whole = 4 * self.width + shards * self.small_rows
        self.slab = 6 * self.width + self.small * self.width // self.rows


def slot_picks(z, route):
    onehot = (route == iota((z.rows, z.experts), 1)).astype(F32)
    lower = (iota((z.rows, z.rows), 0) >= iota((z.rows, z.rows), 1)).astype(F32).astype(BF16)
    running = dot_nn(lower, onehot.astype(BF16))
    place = jnp.sum(running * onehot, axis=1, keepdims=True).astype(I32) - 1
    slots = iota((z.rows, z.slot_rows), 1)

    def pick(first, wide, shift):
        inside = (place >= first) & (place < first + wide)
        target = jnp.where(inside, route * 8 + place - first + shift, -1)
        return (slots == target).astype(F32).astype(BF16)

    picks = [pick(8 * i, 8, 0) for i in range(z.full)]
    return picks + [pick(8 * z.full, z.rest, z.rest * i) for i in range(z.cuts)]


def cut_sum(z, picks, values):
    return sum(dot_tn(pick, values[:, i * z.cut : (i + 1) * z.cut]) for i, pick in enumerate(picks))


def put_slots(z, ref, offset, picks, values):
    for i in range(z.full):
        block = dot_tn(picks[i], values)
        ref[:, :, offset : offset + z.width] = block.reshape(z.experts, 8, z.width).astype(BF16)
        offset += z.width
    if z.rest:
        block = cut_sum(z, picks[z.full :], values)
        ref[:, :, offset : offset + z.cut] = block.reshape(z.experts, 8, z.cut).astype(BF16)


def read_slots(z, ref, offset, wide):
    block = ref[:, :, offset : offset + wide].astype(F32)
    return block.reshape(z.slot_rows, wide).astype(BF16)


def get_slots(z, ref, offset, picks):
    total = 0.0
    for i in range(z.full):
        total += dot_nn(picks[i], read_slots(z, ref, offset, z.width))
        offset += z.width
    if z.rest:
        block = read_slots(z, ref, offset, z.cut)
        total += jnp.concatenate([dot_nn(pick, block) for pick in picks[z.full :]], axis=1)
    return total


def extra_picks(z):
    shape = (z.experts * z.rest, z.slot_rows)
    rows, slots = (iota(shape, 0), iota(shape, 1))
    first = (rows // z.rest) * 8 + rows % z.rest
    return [(slots == first + z.rest * i).astype(F32).astype(BF16) for i in range(z.cuts)]


def rows_of_slots(z, ref, offset):
    parts = []
    for i in range(z.full):
        parts.append(read_slots(z, ref, offset, z.width))
        offset += z.width
    if z.rest:
        block = read_slots(z, ref, offset, z.cut)
        pieces = [dot_nn(pick, block) for pick in extra_picks(z)]
        parts.append(jnp.concatenate(pieces, axis=1).astype(BF16))
    return jnp.concatenate(parts, axis=0) if len(parts) > 1 else parts[0]


def slots_of_rows(z, ref, offset, rows):
    for i in range(z.full):
        block = rows[i * z.slot_rows : (i + 1) * z.slot_rows]
        ref[:, :, offset : offset + z.width] = block.reshape(z.experts, 8, z.width).astype(BF16)
        offset += z.width
    if z.rest:
        block = cut_sum(z, extra_picks(z), rows[z.full * z.slot_rows :].astype(BF16))
        ref[:, :, offset : offset + z.cut] = block.reshape(z.experts, 8, z.cut).astype(BF16)


def fetch_weights(z, mine, own, other, mats, packed, sems, order=(4, 0, 1, 2, 3)):
    count = z.shards * z.small_rows

    def copy(source, i):
        if i == 4:
            return pltpu.make_async_copy(source.at[pl.ds(4 * z.width, count)], packed, sems.at[4])
        rows = pl.ds(i * z.width, z.width)
        return pltpu.make_async_copy(source.at[rows], mats.at[i], sems.at[i])

    @pl.when(mine)
    def _():
        for i in order:
            copy(own, i).start()

    @pl.when(jnp.logical_not(mine))
    def _():
        for i in order:
            copy(other, i).start()

    return [functools.partial(lambda i: copy(own, i).wait(), i) for i in range(5)]


def weight_scratch(z):
    return [
        pltpu.VMEM((4, z.width, z.width), BF16),
        pltpu.VMEM((z.shards * z.small_rows, z.width), BF16),
        pltpu.VMEM((z.width, z.small), BF16),
        pltpu.SemaphoreType.DMA((5,)),
    ]


def unpack_small(z, packed, small):
    for j in range(z.shards):
        for g in range(z.small_groups):
            row = j * z.part + g * z.small_rows
            small[row : row + z.small_rows, :] = packed[
                j * z.small_rows : (j + 1) * z.small_rows, g * z.small : (g + 1) * z.small
            ]


def bucket_rows(z):
    rows, buckets = (iota((z.width, z.buckets), 0), iota((z.width, z.buckets), 1))
    held = (buckets // z.bucket_part) * z.part + buckets % z.bucket_part
    return (rows == held).astype(F32).astype(BF16)


def bucket_lanes(z):
    shape = (z.buckets, 2 * z.rows)
    return (bucket_of(iota(shape, 1) - z.rows) == iota(shape, 0)).astype(F32).astype(BF16)


def gain_rows(z, small):
    rows, lanes = (iota((8, z.small), 0), iota((8, z.small), 1))
    pick = ((lanes == z.gain_lane + rows) & (rows < 2)).astype(F32).astype(BF16)
    made = dot_nt(pick, small)
    return (made[0:1], made[1:2])


def unit_rows(values):
    inverse = lax.rsqrt(jnp.mean(values * values, axis=-1, keepdims=True) + EPSILON)
    return (values * inverse, inverse)


def pair_masks(z):
    lanes = iota((z.rows, 128), 1)
    first = (lanes < 64).astype(F32).astype(BF16)
    return (first, (lanes >= 64).astype(F32).astype(BF16))


def double(values, masks):
    return jnp.concatenate([values * masks[0], values * masks[1]], axis=0)


def attend(z, inputs, waits, mats, packed, small, lengths, section, qkv_ref, probs_ref, attended_ref):
    waits[4]()
    unpack_small(z, packed, small)
    small_full = small[...]
    gain_one, gain_two = gain_rows(z, small_full)
    normed_one = (unit_rows(inputs)[0] * gain_one).astype(BF16)
    for i in range(3):
        waits[i]()
        qkv_ref[:, i * z.width : (i + 1) * z.width] = dot_nn(normed_one, mats[i]).astype(BF16)

    table = dot_tn(bucket_rows(z), small_full).astype(BF16)
    bias = dot_tn(table, bucket_lanes(z))[z.experts : z.experts + z.heads]

    rows, lanes = (iota((z.rows, z.rows), 0), iota((z.rows, z.rows), 1))
    segment_q, segment_k = (jnp.zeros_like(rows), jnp.zeros_like(rows))
    end = jnp.int32(0)
    for i in range(lengths.shape[2]):
        end = end + lengths[section, 0, i]
        segment_q += (rows >= end).astype(I32)
        segment_k += (lanes >= end).astype(I32)
    visible = segment_q == segment_k

    masks = pair_masks(z)
    scale = 64 ** (-0.5)
    for p in range(z.heads // 2):
        at = slice(p * 128, (p + 1) * 128)
        query = qkv_ref[:, p * 128 : (p + 1) * 128]
        key = qkv_ref[:, z.width + p * 128 : z.width + (p + 1) * 128]
        value = qkv_ref[:, 2 * z.width + p * 128 : 2 * z.width + (p + 1) * 128]
        scores = dot_nt(query, double(key, masks)) * scale
        halves = []
        for i in range(2):
            spread = jnp.broadcast_to(bias[2 * p + i : 2 * p + i + 1], (z.rows, 2 * z.rows))
            spread = pltpu.roll(spread, z.rows, 1, stride=1, stride_axis=0)[:, : z.rows]
            part = scores[:, i * z.rows : (i + 1) * z.rows] + spread
            part = jnp.where(visible, part, MASKED)
            part = jnp.exp(part - jnp.max(part, axis=-1, keepdims=True))
            halves.append(part / jnp.sum(part, axis=-1, keepdims=True))
        probs = jnp.concatenate(halves, axis=1).astype(BF16)
        probs_ref[p] = probs
        attended_ref[:, at] = dot_nn(probs, double(value, masks)).astype(BF16)

    waits[3]()
    middle = inputs + dot_nn(attended_ref[...], mats[3])
    normed_two = (unit_rows(middle)[0] * gain_two).astype(BF16)
    logits = dot_nn(normed_two, small_full)
    logits = jnp.where(iota((z.rows, z.small), 1) < z.experts, logits, MASKED)
    logits = jnp.exp(logits - jnp.max(logits, axis=-1, keepdims=True))
    router = logits / jnp.sum(logits, axis=-1, keepdims=True)
    return (middle, normed_two, router)


def chosen(z, route):
    return (route == iota((z.rows, z.small), 1)).astype(F32)


def attend_back(
    z, grad_out, token_out, grad_token, inputs, route, waits, mats, packed, small, kept, slab_ref
):
    qkv_ref, probs_ref, attended_ref, middle_ref, router_ref = kept
    waits[4]()
    unpack_small(z, packed, small)
    small_full = small[...]
    gain_one, gain_two = gain_rows(z, small_full)
    onehot = chosen(z, route)
    router = router_ref[...]
    gate = jnp.sum(router * onehot, axis=1, keepdims=True)
    grad_gate = jnp.sum(grad_out * token_out, axis=1, keepdims=True)
    grad_logits = (grad_gate * gate * (onehot - router)).astype(BF16)
    unit_two, inverse_two = unit_rows(middle_ref[...])
    grad_small = dot_tn((unit_two * gain_two).astype(BF16), grad_logits)
    grad_normed = grad_token + dot_nt(grad_logits, small_full)
    gain_two_grad = jnp.sum(grad_normed * unit_two, axis=0, keepdims=True)
    grad_unit = grad_normed * gain_two
    grad_unit -= unit_two * jnp.mean(grad_unit * unit_two, axis=1, keepdims=True)
    grad_middle = grad_out + inverse_two * grad_unit
    grad_branch = grad_middle.astype(BF16)
    slab_ref[:, 4 * z.width : 5 * z.width] = attended_ref[...]
    slab_ref[:, 5 * z.width : 6 * z.width] = grad_branch
    waits[3]()
    grad_attended = dot_nt(grad_branch, mats[3]).astype(BF16)

    masks = pair_masks(z)
    scale = 64 ** (-0.5)
    relative = []
    turn = iota((z.rows, z.rows), 0) + iota((z.rows, z.rows), 1) == z.rows - 1
    turn = turn.astype(F32).astype(BF16)
    for p in range(z.heads // 2):
        at = slice(p * 128, (p + 1) * 128)
        query = qkv_ref[:, p * 128 : (p + 1) * 128]
        keys = double(qkv_ref[:, z.width + p * 128 : z.width + (p + 1) * 128], masks)
        values = double(qkv_ref[:, 2 * z.width + p * 128 : 2 * z.width + (p + 1) * 128], masks)
        grad_heads = grad_attended[:, at]
        probs_low = probs_ref[p]
        probs = probs_low.astype(F32)
        grad_probs = dot_nt(grad_heads, values)
        halves = []
        for i in range(2):
            part = slice(i * z.rows, (i + 1) * z.rows)
            product = grad_probs[:, part] * probs[:, part]
            dots = jnp.sum(product, axis=-1, keepdims=True)
            grads = (product - probs[:, part] * dots).astype(BF16)
            halves.append(grads)
        grad_scores = jnp.concatenate(halves, axis=1)
        turned = dot_nn(turn, grad_scores)
        for i in range(2):
            wide = [turned[:, i * z.rows : (i + 1) * z.rows], jnp.zeros((z.rows, z.rows), F32)]
            wide = pltpu.roll(jnp.concatenate(wide, axis=1), 1, 1, stride=1, stride_axis=0)
            relative.append(jnp.sum(wide, axis=0, keepdims=True))
        start = z.width + p * 128
        slab_ref[:, start : start + 128] = (dot_nn(grad_scores, keys) * scale).astype(BF16)
        made = dot_tn(grad_scores, query) * scale
        mask = masks[0].astype(F32)
        made = made[: z.rows] * mask + made[z.rows :] * (1.0 - mask)
        slab_ref[:, start + z.width : start + z.width + 128] = made.astype(BF16)
        made = dot_tn(probs_low, grad_heads)
        made = made[: z.rows] * mask + made[z.rows :] * (1.0 - mask)
        slab_ref[:, start + 2 * z.width : start + 2 * z.width + 128] = made.astype(BF16)

    unit_one, inverse_one = unit_rows(inputs)
    slab_ref[:, : z.width] = (unit_one * gain_one).astype(BF16)
    grad_normed = 0.0
    for i in range(3):
        waits[i]()
        grad_normed += dot_nt(slab_ref[:, (i + 1) * z.width : (i + 2) * z.width], mats[i])
    gain_one_grad = jnp.sum(grad_normed * unit_one, axis=0, keepdims=True)
    grad_unit = grad_normed * gain_one
    grad_unit -= unit_one * jnp.mean(grad_unit * unit_one, axis=1, keepdims=True)
    grad_in = (grad_middle + inverse_one * grad_unit).astype(BF16)

    relative += [jnp.zeros((1, 2 * z.rows), F32)] * (-z.heads % 8)
    relative = jnp.concatenate(relative, axis=0)
    lanes_of = bucket_lanes(z)
    high = relative.astype(BF16)
    table = dot_nt(lanes_of, high) + dot_nt(lanes_of, (relative - high.astype(F32)).astype(BF16))
    count = relative.shape[0]
    places = iota((count, z.small), 1) == iota((count, z.small), 0) + z.experts
    places = places & (iota((count, z.small), 0) < z.heads)
    table = dot_nn(table.astype(BF16), places.astype(F32).astype(BF16)).astype(BF16)
    grad_small += dot_nn(bucket_rows(z), table)
    gains = jnp.concatenate([gain_one_grad, gain_two_grad, jnp.zeros((6, z.width), F32)], axis=0)
    rows, lanes = (iota((8, z.small), 0), iota((8, z.small), 1))
    pick = ((lanes == z.gain_lane + rows) & (rows < 2)).astype(F32).astype(BF16)
    grad_small += dot_tn(gains.astype(BF16), pick)
    for i in range(z.width // z.rows):
        start = 6 * z.width + i * z.small
        slab_ref[:, start : start + z.small] = grad_small[i * z.rows : (i + 1) * z.rows].astype(BF16)
    return grad_in


def pack_kernel(z, query, key, value, output, small, top, low):
    p = z.part
    top[0:p] = query[0]
    top[p : 2 * p] = key[0]
    low[0:p] = value[0]
    low[p : 2 * p] = output[0]
    for g in range(z.small_groups):
        low[2 * p : 2 * p + z.small_rows, g * z.small : (g + 1) * z.small] = small[
            g * z.small_rows : (g + 1) * z.small_rows
        ]


def assemble_kernel(z, place, *refs):
    pieces, out, sems = (refs[: 2 * z.shards], refs[2 * z.shards], refs[2 * z.shards + 1])
    p = z.part
    copies = []
    for k in range(z.shards):
        shard = place[0] ^ k
        top, low = pieces[2 * k : 2 * k + 2]
        for i, source in enumerate((top, top, low, low)):
            target = pl.ds(pl.multiple_of(i * z.width + shard * p, 16), p)
            copies.append((source.at[pl.ds((i % 2) * p, p)], out.at[target]))
        target = pl.ds(pl.multiple_of(4 * z.width + shard * z.small_rows, 16), z.small_rows)
        copies.append((low.at[pl.ds(2 * p, z.small_rows)], out.at[target]))
    copies = [
        pltpu.make_async_copy(source, target, sems.at[i])
        for i, (source, target) in enumerate(copies)
    ]
    for copy in copies:
        copy.start()
    for copy in copies:
        copy.wait()


def first_kernel(
    z, section, lengths, tokens, own_route, other_route, own, other,
    send, qkv, probs, attended, middle_ref, router_ref,
    mats, packed, small, sems,
):
    core = section[0]
    waits = fetch_weights(z, core == 0, own, other, mats, packed, sems)
    inputs = tokens[core].astype(F32)
    middle, normed_two, router = attend(
        z, inputs, waits, mats, packed, small, lengths, core, qkv, probs, attended
    )
    middle_ref[...] = middle
    router_ref[...] = router
    route = jnp.where(core == 0, own_route[core], other_route[...])
    put_slots(z, send, 0, slot_picks(z, route), normed_two)


def second_kernel(
    z, section, lengths, cotangent, own_route, other_route, own, other, back, middle_zero, router_zero,
    send, out_zero, qkv, probs, attended, middle_ref, router_ref,
    mats, packed, small, sems,
):
    core = section[0]
    waits = fetch_weights(z, core == 1, own, other, mats, packed, sems)
    route = jnp.where(core == 0, own_route[core], other_route[...])
    gate = jnp.sum(router_zero[...] * chosen(z, route), axis=1, keepdims=True)
    token_out = get_slots(z, back, 0, slot_picks(z, route))
    layer_out = (middle_zero[...] + gate * token_out).astype(BF16)
    out_zero[...] = layer_out
    middle, normed_two, router = attend(
        z, layer_out.astype(F32), waits, mats, packed, small, lengths, core, qkv, probs, attended
    )
    middle_ref[...] = middle
    router_ref[...] = router
    route = jnp.where(core == 1, own_route[core], other_route[...])
    picks = slot_picks(z, route)
    put_slots(z, send, 0, picks, normed_two)
    gate = jnp.sum(router * chosen(z, route), axis=1, keepdims=True)
    grad = (gate * cotangent[core].astype(F32)).astype(BF16)
    put_slots(z, send, z.slot_width, picks, grad)


def third_kernel(
    z, section, cotangent, own_route, other_route, own, other, back, inputs, router_zero,
    qkv, probs, attended, middle, router,
    send, out_one, grad_in_ref, slab,
    mats, packed, small, sems,
):
    core = section[0]
    waits = fetch_weights(z, core == 1, own, other, mats, packed, sems, (4, 3, 0, 1, 2))
    route = jnp.where(core == 1, own_route[core], other_route[...])
    picks = slot_picks(z, route)
    token_out = get_slots(z, back, 0, picks)
    grad_token = get_slots(z, back, z.slot_width, picks)
    gate = jnp.sum(router[...] * chosen(z, route), axis=1, keepdims=True)
    out_one[...] = (middle[...] + gate * token_out).astype(BF16)
    grad_in = attend_back(
        z, cotangent[core].astype(F32), token_out, grad_token, inputs[...].astype(F32), route,
        waits, mats, packed, small, (qkv, probs, attended, middle, router), slab,
    )
    grad_in_ref[...] = grad_in
    route = jnp.where(core == 0, own_route[core], other_route[...])
    gate = jnp.sum(router_zero[...] * chosen(z, route), axis=1, keepdims=True)
    grad = (gate * grad_in.astype(F32)).astype(BF16)
    put_slots(z, send, 0, slot_picks(z, route), grad)


def fourth_kernel(
    z, section, grad_out, tokens, own_route, other_route, own, other, back_out, back_grad,
    qkv, probs, attended, middle, router,
    grad_in_ref, slab,
    mats, packed, small, sems,
):
    core = section[0]
    waits = fetch_weights(z, core == 0, own, other, mats, packed, sems, (4, 3, 0, 1, 2))
    route = jnp.where(core == 0, own_route[core], other_route[...])
    picks = slot_picks(z, route)
    token_out = get_slots(z, back_out, 0, picks)
    grad_token = get_slots(z, back_grad, 0, picks)
    grad_in_ref[...] = attend_back(
        z, grad_out[...].astype(F32), token_out, grad_token, tokens[core].astype(F32), route,
        waits, mats, packed, small, (qkv, probs, attended, middle, router), slab,
    )


def fetch_experts(z, mine, own_in, own_out, other_in, other_out, w_in, w_out, sems):
    def copies(source_in, source_out, c):
        at = pl.ds(c * z.chunk, z.chunk)
        return (
            pltpu.make_async_copy(source_in.at[:, at], w_in.at[c], sems.at[2 * c]),
            pltpu.make_async_copy(source_out.at[at], w_out.at[c], sems.at[2 * c + 1]),
        )

    def start(source_in, source_out):
        for c in range(z.hidden // z.chunk):
            for copy in copies(source_in, source_out, c):
                copy.start()

    @pl.when(mine)
    def _():
        start(own_in, own_out)

    @pl.when(jnp.logical_not(mine))
    def _():
        start(other_in, other_out)

    def wait(c):
        for copy in copies(own_in, own_out, c):
            copy.wait()

    return wait


def expert_scratch(z, sums):
    chunks = z.hidden // z.chunk
    return [
        pltpu.VMEM((chunks, z.width, z.chunk), BF16),
        pltpu.VMEM((chunks, z.chunk, z.width), BF16),
        pltpu.SemaphoreType.DMA((2 * chunks,)),
    ] + [pltpu.VMEM((z.expert_rows, z.width), F32)] * sums


def smooth(values):
    square = values * values
    bent = jnp.tanh(GELU_SCALE * values * (1.0 + GELU_CUBE * square))
    return (0.5 * values * (1.0 + bent), square, bent)


def smooth_slope(values, square, bent):
    inner = GELU_SCALE * (1.0 + 3.0 * GELU_CUBE * square)
    return 0.5 * (1.0 + bent) + 0.5 * values * (1.0 - bent * bent) * inner


def expert_forward_kernel(
    z, section, arrived, own_in, own_out, other_in, other_out, result, w_in, w_out, sems, produced
):
    wait = fetch_experts(
        z, section[0] == 0, own_in, own_out, other_in, other_out, w_in, w_out, sems
    )
    rows = rows_of_slots(z, arrived, 0)
    for c in range(z.hidden // z.chunk):
        wait(c)
        hidden = smooth(dot_nn(rows, w_in[c]))[0].astype(BF16)
        made = dot_nn(hidden, w_out[c])
        produced[...] = made if c == 0 else produced[...] + made
    slots_of_rows(z, result, 0, produced[...])


def expert_backward_kernel(
    z, layer, section, arrived, arrived_grad, own_in, own_out, other_in, other_out,
    result, stuff, w_in, w_out, sems, grad_sum, *produced
):
    wait = fetch_experts(
        z, section[0] == layer, own_in, own_out, other_in, other_out, w_in, w_out, sems
    )
    rows = rows_of_slots(z, arrived, 0)
    grads = rows_of_slots(z, arrived_grad, z.slot_width if produced else 0)
    stuff[:, 2 * z.hidden : 2 * z.hidden + z.width] = rows
    stuff[:, 2 * z.hidden + z.width : 2 * z.hidden + 2 * z.width] = grads
    for c in range(z.hidden // z.chunk):
        wait(c)
        before = dot_nn(rows, w_in[c])
        hidden, square, bent = smooth(before)
        hidden = hidden.astype(BF16)
        stuff[:, c * z.chunk : (c + 1) * z.chunk] = hidden
        if produced:
            made = dot_nn(hidden, w_out[c])
            produced[0][...] = made if c == 0 else produced[0][...] + made
        grad_pre = dot_nt(grads, w_out[c]) * smooth_slope(before, square, bent)
        grad_pre = grad_pre.astype(BF16)
        stuff[:, z.hidden + c * z.chunk : z.hidden + (c + 1) * z.chunk] = grad_pre
        made = dot_nt(grad_pre, w_in[c])
        grad_sum[...] = made if c == 0 else grad_sum[...] + made
    if produced:
        slots_of_rows(z, result, 0, produced[0][...])
    slots_of_rows(z, result, z.slot_width if produced else 0, grad_sum[...])


def expert_weights_kernel(
    z, section, own_zero, other_zero, own_one, other_one, grad_in, grad_out, held, turned, sems
):
    step = pl.program_id(0)

    @pl.when(step == 0)
    def _():
        def copies(own, other):
            return [
                pltpu.make_async_copy(
                    source, held.at[pl.ds(i * z.expert_rows, z.expert_rows)], sems.at[i]
                )
                for i, source in enumerate((own, other))
            ]

        @pl.when(section[0] == 0)
        def _():
            for copy in copies(own_zero, other_zero):
                copy.start()

        @pl.when(section[0] != 0)
        def _():
            for copy in copies(own_one, other_one):
                copy.start()

        for copy in copies(own_zero, other_zero):
            copy.wait()
        rows = held[:, 2 * z.hidden : 2 * z.hidden + z.width]
        turned[...] = jnp.transpose(rows.astype(F32)).astype(BF16)

    start = pl.multiple_of(step * z.chunk, z.chunk)
    grad_pre = held[:, pl.ds(z.hidden + start, z.chunk)]
    hidden = held[:, pl.ds(start, z.chunk)]
    grads = held[:, 2 * z.hidden + z.width : 2 * z.hidden + 2 * z.width]
    grad_in[...] = dot_nn(turned[...], grad_pre).astype(BF16)
    grad_out[...] = dot_tn(hidden, grads).astype(BF16)


def attention_weights_kernel(z, layer, section, own, other, out):
    second = section[0] ^ layer

    def both(column):
        at = pl.ds(pl.multiple_of(column * z.width, 128), z.width)
        return jnp.concatenate([own[:, at], other[:, at]], axis=0)

    for i, (left, right) in enumerate(
        ((0, 1 + 2 * second), (4 * second, 2 + 3 * second))
    ):
        made = dot_tn(both(left), both(right))
        for j in range(z.shards):
            out[j, i * z.part : (i + 1) * z.part] = made[j * z.part : (j + 1) * z.part].astype(BF16)
    columns = slice(6 * z.width, z.slab)
    total = own[:, columns].astype(F32) + other[:, columns].astype(F32)
    pieces = [total[:, i * z.small : (i + 1) * z.small] for i in range(z.width // z.rows)]
    total = jnp.concatenate(pieces, axis=0).astype(BF16)
    for j in range(z.shards):
        for g in range(z.small_groups):
            row = j * z.part + g * z.small_rows
            out[j, 2 * z.part :, g * z.small : (g + 1) * z.small] = total[row : row + z.small_rows]


def swap(value):
    return lax.ppermute(value, "section", [(0, 1), (1, 0)])


def cross(value, target):
    return lax.ppermute(value, "section", [(1 - target, target)])


def within(value, distance, layer):
    size = lax.axis_size("shard")
    pairs = [(layer * size + i, layer * size + (i ^ distance)) for i in range(size)]
    return lax.ppermute(value, ("section", "shard"), pairs)


def exchange(buffer, axes=("expert", "shard")):
    return lax.all_to_all(buffer, axes, split_axis=0, concat_axis=0, tiled=True)


def shards(
    tokens_in,
    cotangent,
    lengths,
    routes,
    w_query,
    w_key,
    w_value,
    w_output,
    gain_attn,
    gain_moe,
    w_router,
    bias_table,
    w_in,
    w_out,
):
    z = Sizes(tokens_in, w_query, w_router, bias_table, w_in, lax.axis_size("shard"))
    section = lax.axis_index("section").astype(I32)
    core = section.reshape(1)
    place = lax.axis_index("shard").astype(I32).reshape(1)

    def shape(*dims, kind=BF16):
        return jax.ShapeDtypeStruct(dims, kind)

    table = jnp.pad(bias_table[0], ((0, z.part - z.bucket_part), (0, 0)))
    small = jnp.concatenate([w_router[0], table, gain_attn[0][:, None], gain_moe[0][:, None]], axis=1)
    small = jnp.pad(small, ((0, 0), (0, z.small - small.shape[1])))
    low_rows = 2 * z.part + z.small_rows
    packed = call(
        functools.partial(pack_kernel, z),
        (shape(2 * z.part, z.width), shape(low_rows, z.width)),
        (w_query, w_key, w_value, w_output, small),
        [VMEM] * 5,
    )

    def gather(packed, layer):
        top, low = packed
        top_x, low_y = (within(top, 1, layer), within(low, 2, layer))
        top_y, low_x = (within(top, 2, layer), within(low, 1, layer))
        top_d, low_d = (within(top_x, 2, layer), within(low_y, 1, layer))
        own = call(
            functools.partial(assemble_kernel, z),
            shape(z.whole, z.width),
            (place, top, low, top_x, low_x, top_y, low_y, top_d, low_d),
            [SMEM] + [ANY] * 8,
            [pltpu.SemaphoreType.DMA((5 * z.shards,))],
            out_specs=ANY,
        )
        return (own, cross(own, 1 - layer))

    weights_zero = gather(packed, 0)
    own_route = routes[0]
    other_route = swap(lax.dynamic_index_in_dim(own_route, 1 - section, 0, keepdims=False))
    route_pair = (own_route, other_route)
    experts = (w_in[0, 0], w_out[0, 0], swap(w_in[0, 0]), swap(w_out[0, 0]))

    buffer = shape(z.experts, 8, z.slot_width)
    wide_buffer = shape(z.experts, 8, 2 * z.slot_width)
    kept = (
        shape(z.rows, 3 * z.width),
        shape(z.heads // 2, z.rows, 2 * z.rows),
        shape(z.rows, z.width),
        shape(z.rows, z.width, kind=F32),
        shape(z.rows, z.small, kind=F32),
    )
    scratch = weight_scratch(z)
    rows_shape = shape(z.rows, z.width)
    slab_shape = shape(z.rows, z.slab)

    sent, *kept_zero = call(
        functools.partial(first_kernel, z),
        (buffer, *kept),
        (core, lengths, tokens_in, *route_pair, *weights_zero),
        [SMEM, SMEM, VMEM, VMEM, VMEM, ANY, ANY],
        scratch,
    )
    sent, *packed = lax.optimization_barrier((sent, *packed))
    arrived_zero = exchange(sent)
    weights_one = gather(packed, 1)
    produced = call(
        functools.partial(expert_forward_kernel, z),
        buffer,
        (core, arrived_zero, *experts),
        [SMEM, VMEM, ANY, ANY, ANY, ANY],
        expert_scratch(z, 1),
    )
    back_zero = exchange(produced)

    sent, out_zero, *kept_one = call(
        functools.partial(second_kernel, z),
        (wide_buffer, rows_shape, *kept),
        (core, lengths, cotangent, *route_pair, *weights_one, back_zero, kept_zero[3], kept_zero[4]),
        [SMEM, SMEM, VMEM, VMEM, VMEM, ANY, ANY, VMEM, VMEM, VMEM],
        scratch,
    )
    arrived_one = exchange(sent)
    stuff_shape = shape(z.expert_rows, 2 * z.hidden + 2 * z.width)
    result, stuff_one = call(
        lambda section, arrived, *rest: expert_backward_kernel(
            z, 1, section, arrived, arrived, *rest
        ),
        (wide_buffer, stuff_shape),
        (core, arrived_one, *experts),
        [SMEM, VMEM, ANY, ANY, ANY, ANY],
        expert_scratch(z, 2),
    )
    back_one = exchange(result)

    sent, out_one, grad_in_one, slab_one = call(
        functools.partial(third_kernel, z),
        (buffer, rows_shape, rows_shape, slab_shape),
        (core, cotangent, *route_pair, *weights_one, back_one, out_zero, kept_zero[4], *kept_one),
        [SMEM, VMEM, VMEM, VMEM, ANY, ANY] + [VMEM] * 8,
        scratch,
    )
    arrived_grad = exchange(sent)

    result, stuff_zero = call(
        functools.partial(expert_backward_kernel, z, 0),
        (buffer, stuff_shape),
        (core, arrived_zero, arrived_grad, *experts),
        [SMEM, VMEM, VMEM, ANY, ANY, ANY, ANY],
        expert_scratch(z, 1),
    )
    back_grad = exchange(result)
    grad_in_zero, slab_zero = call(
        functools.partial(fourth_kernel, z),
        (rows_shape, slab_shape),
        (core, grad_in_one, tokens_in, *route_pair, *weights_zero, back_zero, back_grad, *kept_zero),
        [SMEM, VMEM, VMEM, VMEM, VMEM, ANY, ANY] + [VMEM] * 7,
        scratch,
    )

    count = lax.axis_size("expert")

    def reduce(slab, layer):
        partial = call(
            functools.partial(attention_weights_kernel, z, layer),
            shape(z.shards, low_rows, z.width),
            (core, slab, swap(slab)),
            [SMEM, VMEM, VMEM],
        )

        def total(pieces):
            return jnp.sum(pieces.astype(F32), axis=0).astype(BF16)

        summed = total(exchange(partial, "shard")).reshape(count, low_rows // count, z.width)
        summed = total(exchange(summed, "expert"))
        return exchange(jnp.broadcast_to(summed[None], (count, *summed.shape)), "expert").reshape(
            low_rows, z.width
        )

    half_one = reduce(slab_one, 1)
    half_zero = reduce(slab_zero, 0)
    first = jnp.where(section == 0, half_zero, half_one)
    second = swap(jnp.where(section == 0, half_one, half_zero))
    final_small = first[2 * z.part :].reshape(z.small_rows, z.small_groups, z.small)
    final_small = jnp.swapaxes(final_small, 0, 1).reshape(z.part, z.small)

    chunks = z.hidden // z.chunk
    grad_w_in, grad_w_out = call(
        functools.partial(expert_weights_kernel, z),
        (shape(z.width, z.hidden), shape(z.hidden, z.width)),
        (core, stuff_zero, cross(stuff_zero, 0), stuff_one, cross(stuff_one, 1)),
        [SMEM, ANY, ANY, ANY, ANY],
        [
            pltpu.VMEM((2 * z.expert_rows, stuff_shape.shape[1]), BF16),
            pltpu.VMEM((z.width, 2 * z.expert_rows), BF16),
            pltpu.SemaphoreType.DMA((2,)),
        ],
        grid=(chunks,),
        out_specs=(
            pl.BlockSpec((z.width, z.chunk), lambda i: (0, i)),
            pl.BlockSpec((z.chunk, z.width), lambda i: (i, 0)),
        ),
    )

    pair_zero, pair_one = (jnp.stack([out_zero, grad_in_zero]), jnp.stack([out_one, grad_in_one]))
    ours = jnp.where(section == 0, pair_zero, pair_one)
    theirs = swap(jnp.where(section == 0, pair_one, pair_zero))
    ordered = jnp.where(section == 0, jnp.stack([ours, theirs], 1), jnp.stack([theirs, ours], 1))

    return (
        ordered[0][None],
        ordered[1][None],
        first[: z.part][None],
        first[z.part : 2 * z.part][None],
        second[: z.part][None],
        second[z.part : 2 * z.part][None],
        final_small[:, z.gain_lane][None],
        final_small[:, z.gain_lane + 1][None],
        final_small[:, : z.experts][None],
        final_small[: z.bucket_part, z.experts : z.gain_lane][None],
        grad_w_in[None, None],
        grad_w_out[None, None],
    )


def solution(mesh):
    both = ("expert", "shard")
    plain = P("section", "shard", None)
    gains = P("section", "shard")
    blocks = P("section", None, both, None)
    experts = P("section", both, None, None)
    tokens = P(None, both, None)
    attention = (plain, plain, plain, plain, gains, gains, plain, plain, experts, experts)
    return jax.shard_map(
        shards,
        mesh=mesh,
        in_specs=(tokens, tokens, tokens, blocks, *attention),
        out_specs=(blocks, blocks, *attention),
        check_vma=False,
    )
```

```python
import functools

import jax
import jax.numpy as jnp
from jax import lax
from jax.experimental import pallas as pl
from jax.experimental.pallas import tpu as pltpu
from jax.sharding import PartitionSpec as P

EPSILON = 1e-06
BOUNDS = (8, 12, 16, 23, 32, 46, 64, 91)
MASKED = -1e30
F32 = jnp.float32
BF16 = jnp.bfloat16
I32 = jnp.int32
GELU_SCALE = 0.7978845608028654
GELU_CUBE = 0.044715
SMEM = pl.BlockSpec(memory_space=pltpu.SMEM)
VMEM = pl.BlockSpec(memory_space=pltpu.VMEM)
ANY = pl.BlockSpec(memory_space=pl.ANY)
LIMIT = pltpu.CompilerParams(vmem_limit_bytes=48 * 1024 * 1024)


def dot_nn(a, b):
    return jnp.dot(a, b, preferred_element_type=F32)


def dot_nt(a, b):
    return lax.dot_general(a, b, (((1,), (1,)), ((), ())), preferred_element_type=F32)


def dot_tn(a, b):
    return lax.dot_general(a, b, (((0,), (0,)), ((), ())), preferred_element_type=F32)


def iota(shape, dimension):
    return lax.broadcasted_iota(I32, shape, dimension)


def call(body, outs, ins, specs, scratch=(), **more):
    return pl.pallas_call(
        body,
        out_shape=outs,
        in_specs=specs,
        scratch_shapes=scratch,
        compiler_params=LIMIT,
        **more,
    )(*ins)


def bucket_of(relative):
    distance = jnp.abs(relative)
    bucket = jnp.zeros_like(relative)
    for lowest in tuple(range(1, 8)) + BOUNDS:
        bucket = bucket + (distance >= lowest).astype(I32)
    return bucket + 16 * (relative > 0).astype(I32)


class Sizes:
    def __init__(self, tokens_in, w_query, w_router, bias_table, w_in, shards):
        self.rows, self.width = tokens_in.shape[1:]
        self.part = w_query.shape[1]
        self.shards = shards
        self.experts = w_router.shape[2]
        self.bucket_part, self.heads = bias_table.shape[1:]
        self.buckets = self.bucket_part * shards
        self.hidden = w_in.shape[3]
        self.chunk = self.hidden // 6
        self.capacity = max(
            2, (3 * self.rows + 2 * self.experts - 1) // (2 * self.experts)
        )
        self.full, rest = divmod(self.capacity, 8)
        self.rest = next((power for power in (0, 1, 2, 4) if power >= rest), None)
        if self.rest is None:
            self.full, self.rest = (self.full + 1, 0)
        self.cuts = 8 // self.rest if self.rest else 0
        self.cut = self.width // self.cuts if self.rest else 0
        self.slot_width = self.full * self.width + self.cut
        self.slot_rows = self.experts * 8
        self.expert_rows = self.slot_rows * self.full + self.experts * self.rest
        self.small = -(-(self.experts + self.heads + 2) // 128) * 128
        self.small_groups = self.width // self.small
        self.small_rows = self.part // self.small_groups
        self.gain_lane = self.experts + self.heads
        self.piece = 4 * self.part + self.small_rows
        self.cut_row = 2 * self.part
        self.slab = 6 * self.width + self.small * self.width // self.rows


def slot_picks(z, route):
    onehot = (route == iota((z.rows, z.experts), 1)).astype(F32)
    lower = (iota((z.rows, z.rows), 0) >= iota((z.rows, z.rows), 1)).astype(F32).astype(BF16)
    running = dot_nn(lower, onehot.astype(BF16))
    place = jnp.sum(running * onehot, axis=1, keepdims=True).astype(I32) - 1
    slots = iota((z.rows, z.slot_rows), 1)

    def pick(first, wide, shift):
        inside = (place >= first) & (place < first + wide)
        target = jnp.where(inside, route * 8 + place - first + shift, -1)
        return (slots == target).astype(F32).astype(BF16)

    picks = [pick(8 * i, 8, 0) for i in range(z.full)]
    return picks + [pick(8 * z.full, z.rest, z.rest * i) for i in range(z.cuts)]


def cut_sum(z, picks, values):
    return sum(dot_tn(pick, values[:, i * z.cut : (i + 1) * z.cut]) for i, pick in enumerate(picks))


def put_slots(z, ref, offset, picks, values):
    for i in range(z.full):
        block = dot_tn(picks[i], values)
        ref[:, :, offset : offset + z.width] = block.reshape(z.experts, 8, z.width).astype(BF16)
        offset += z.width
    if z.rest:
        block = cut_sum(z, picks[z.full :], values)
        ref[:, :, offset : offset + z.cut] = block.reshape(z.experts, 8, z.cut).astype(BF16)


def read_slots(z, ref, offset, wide):
    block = ref[:, :, offset : offset + wide].astype(F32)
    return block.reshape(z.slot_rows, wide).astype(BF16)


def get_slots(z, ref, offset, picks):
    total = 0.0
    for i in range(z.full):
        total += dot_nn(picks[i], read_slots(z, ref, offset, z.width))
        offset += z.width
    if z.rest:
        block = read_slots(z, ref, offset, z.cut)
        total += jnp.concatenate([dot_nn(pick, block) for pick in picks[z.full :]], axis=1)
    return total


def extra_picks(z):
    shape = (z.experts * z.rest, z.slot_rows)
    rows, slots = (iota(shape, 0), iota(shape, 1))
    first = (rows // z.rest) * 8 + rows % z.rest
    return [(slots == first + z.rest * i).astype(F32).astype(BF16) for i in range(z.cuts)]


def rows_of_slots(z, ref, offset):
    parts = []
    for i in range(z.full):
        parts.append(read_slots(z, ref, offset, z.width))
        offset += z.width
    if z.rest:
        block = read_slots(z, ref, offset, z.cut)
        pieces = [dot_nn(pick, block) for pick in extra_picks(z)]
        parts.append(jnp.concatenate(pieces, axis=1).astype(BF16))
    return jnp.concatenate(parts, axis=0) if len(parts) > 1 else parts[0]


def slots_of_rows(z, ref, offset, rows):
    for i in range(z.full):
        block = rows[i * z.slot_rows : (i + 1) * z.slot_rows]
        ref[:, :, offset : offset + z.width] = block.reshape(z.experts, 8, z.width).astype(BF16)
        offset += z.width
    if z.rest:
        block = cut_sum(z, extra_picks(z), rows[z.full * z.slot_rows :].astype(BF16))
        ref[:, :, offset : offset + z.cut] = block.reshape(z.experts, 8, z.cut).astype(BF16)


def fetch_weights(z, mine, place, own, other, mats, packed, sems, order=(4, 0, 1, 2, 3)):
    def copy(pieces, i, k):
        shard = place ^ k
        count = z.small_rows if i == 4 else z.part
        start = i * z.part
        source = pieces[k]
        if k == 3 and start >= z.cut_row:
            source, start = (pieces[4], start - z.cut_row)
        target = pl.ds(pl.multiple_of(shard * count, 16), count)
        held = packed.at[target] if i == 4 else mats.at[i, target]
        return pltpu.make_async_copy(source.at[pl.ds(start, count)], held, sems.at[i, k])

    def start(pieces):
        for i in order:
            for k in range(z.shards):
                copy(pieces, i, k).start()

    def wait(i):
        for k in range(z.shards):
            copy(own, i, k).wait()

    @pl.when(mine)
    def _():
        start(own)

    @pl.when(jnp.logical_not(mine))
    def _():
        start(other)

    return [functools.partial(wait, i) for i in range(5)]


def weight_scratch(z):
    return [
        pltpu.VMEM((4, z.width, z.width), BF16),
        pltpu.VMEM((z.shards * z.small_rows, z.width), BF16),
        pltpu.VMEM((z.width, z.small), BF16),
        pltpu.SemaphoreType.DMA((5, z.shards)),
    ]


def unpack_small(z, packed, small):
    for j in range(z.shards):
        for g in range(z.small_groups):
            row = j * z.part + g * z.small_rows
            small[row : row + z.small_rows, :] = packed[
                j * z.small_rows : (j + 1) * z.small_rows, g * z.small : (g + 1) * z.small
            ]


def bucket_rows(z):
    rows, buckets = (iota((z.width, z.buckets), 0), iota((z.width, z.buckets), 1))
    held = (buckets // z.bucket_part) * z.part + buckets % z.bucket_part
    return (rows == held).astype(F32).astype(BF16)


def bucket_lanes(z):
    shape = (z.buckets, 2 * z.rows)
    return (bucket_of(iota(shape, 1) - z.rows) == iota(shape, 0)).astype(F32).astype(BF16)


def gain_rows(z, small):
    rows, lanes = (iota((8, z.small), 0), iota((8, z.small), 1))
    pick = ((lanes == z.gain_lane + rows) & (rows < 2)).astype(F32).astype(BF16)
    made = dot_nt(pick, small)
    return (made[0:1], made[1:2])


def unit_rows(values):
    inverse = lax.rsqrt(jnp.mean(values * values, axis=-1, keepdims=True) + EPSILON)
    return (values * inverse, inverse)


def pair_masks(z):
    lanes = iota((z.rows, 128), 1)
    first = (lanes < 64).astype(F32).astype(BF16)
    return (first, (lanes >= 64).astype(F32).astype(BF16))


def double(values, masks):
    return jnp.concatenate([values * masks[0], values * masks[1]], axis=0)


def attend(z, inputs, waits, mats, packed, small, lengths, section, qkv_ref, probs_ref, attended_ref):
    waits[4]()
    unpack_small(z, packed, small)
    small_full = small[...]
    gain_one, gain_two = gain_rows(z, small_full)
    normed_one = (unit_rows(inputs)[0] * gain_one).astype(BF16)
    for i in range(3):
        waits[i]()
        qkv_ref[:, i * z.width : (i + 1) * z.width] = dot_nn(normed_one, mats[i]).astype(BF16)

    table = dot_tn(bucket_rows(z), small_full).astype(BF16)
    bias = dot_tn(table, bucket_lanes(z))[z.experts : z.experts + z.heads]

    rows, lanes = (iota((z.rows, z.rows), 0), iota((z.rows, z.rows), 1))
    segment_q, segment_k = (jnp.zeros_like(rows), jnp.zeros_like(rows))
    end = jnp.int32(0)
    for i in range(lengths.shape[2]):
        end = end + lengths[section, 0, i]
        segment_q += (rows >= end).astype(I32)
        segment_k += (lanes >= end).astype(I32)
    visible = segment_q == segment_k

    masks = pair_masks(z)
    scale = 64 ** (-0.5)
    for p in range(z.heads // 2):
        at = slice(p * 128, (p + 1) * 128)
        query = qkv_ref[:, p * 128 : (p + 1) * 128]
        key = qkv_ref[:, z.width + p * 128 : z.width + (p + 1) * 128]
        value = qkv_ref[:, 2 * z.width + p * 128 : 2 * z.width + (p + 1) * 128]
        scores = dot_nt(query, double(key, masks)) * scale
        halves = []
        for i in range(2):
            spread = jnp.broadcast_to(bias[2 * p + i : 2 * p + i + 1], (z.rows, 2 * z.rows))
            spread = pltpu.roll(spread, z.rows, 1, stride=1, stride_axis=0)[:, : z.rows]
            part = scores[:, i * z.rows : (i + 1) * z.rows] + spread
            part = jnp.where(visible, part, MASKED)
            part = jnp.exp(part - jnp.max(part, axis=-1, keepdims=True))
            halves.append(part / jnp.sum(part, axis=-1, keepdims=True))
        probs = jnp.concatenate(halves, axis=1).astype(BF16)
        probs_ref[p] = probs
        attended_ref[:, at] = dot_nn(probs, double(value, masks)).astype(BF16)

    waits[3]()
    middle = inputs + dot_nn(attended_ref[...], mats[3])
    normed_two = (unit_rows(middle)[0] * gain_two).astype(BF16)
    logits = dot_nn(normed_two, small_full)
    logits = jnp.where(iota((z.rows, z.small), 1) < z.experts, logits, MASKED)
    logits = jnp.exp(logits - jnp.max(logits, axis=-1, keepdims=True))
    router = logits / jnp.sum(logits, axis=-1, keepdims=True)
    return (middle, normed_two, router)


def chosen(z, route):
    return (route == iota((z.rows, z.small), 1)).astype(F32)


def attend_back(
    z, grad_out, token_out, grad_token, inputs, route, waits, mats, packed, small, kept, slab_ref
):
    qkv_ref, probs_ref, attended_ref, middle_ref, router_ref = kept
    waits[4]()
    unpack_small(z, packed, small)
    small_full = small[...]
    gain_one, gain_two = gain_rows(z, small_full)
    onehot = chosen(z, route)
    router = router_ref[...]
    gate = jnp.sum(router * onehot, axis=1, keepdims=True)
    grad_gate = jnp.sum(grad_out * token_out, axis=1, keepdims=True)
    grad_logits = (grad_gate * gate * (onehot - router)).astype(BF16)
    unit_two, inverse_two = unit_rows(middle_ref[...])
    grad_small = dot_tn((unit_two * gain_two).astype(BF16), grad_logits)
    grad_normed = grad_token + dot_nt(grad_logits, small_full)
    gain_two_grad = jnp.sum(grad_normed * unit_two, axis=0, keepdims=True)
    grad_unit = grad_normed * gain_two
    grad_unit -= unit_two * jnp.mean(grad_unit * unit_two, axis=1, keepdims=True)
    grad_middle = grad_out + inverse_two * grad_unit
    grad_branch = grad_middle.astype(BF16)
    slab_ref[:, 4 * z.width : 5 * z.width] = attended_ref[...]
    slab_ref[:, 5 * z.width : 6 * z.width] = grad_branch
    waits[3]()
    grad_attended = dot_nt(grad_branch, mats[3]).astype(BF16)

    masks = pair_masks(z)
    scale = 64 ** (-0.5)
    relative = []
    turn = iota((z.rows, z.rows), 0) + iota((z.rows, z.rows), 1) == z.rows - 1
    turn = turn.astype(F32).astype(BF16)
    for p in range(z.heads // 2):
        at = slice(p * 128, (p + 1) * 128)
        query = qkv_ref[:, p * 128 : (p + 1) * 128]
        keys = double(qkv_ref[:, z.width + p * 128 : z.width + (p + 1) * 128], masks)
        values = double(qkv_ref[:, 2 * z.width + p * 128 : 2 * z.width + (p + 1) * 128], masks)
        grad_heads = grad_attended[:, at]
        probs_low = probs_ref[p]
        probs = probs_low.astype(F32)
        grad_probs = dot_nt(grad_heads, values)
        halves = []
        for i in range(2):
            part = slice(i * z.rows, (i + 1) * z.rows)
            product = grad_probs[:, part] * probs[:, part]
            dots = jnp.sum(product, axis=-1, keepdims=True)
            grads = (product - probs[:, part] * dots).astype(BF16)
            halves.append(grads)
        grad_scores = jnp.concatenate(halves, axis=1)
        turned = dot_nn(turn, grad_scores)
        for i in range(2):
            wide = [turned[:, i * z.rows : (i + 1) * z.rows], jnp.zeros((z.rows, z.rows), F32)]
            wide = pltpu.roll(jnp.concatenate(wide, axis=1), 1, 1, stride=1, stride_axis=0)
            relative.append(jnp.sum(wide, axis=0, keepdims=True))
        start = z.width + p * 128
        slab_ref[:, start : start + 128] = (dot_nn(grad_scores, keys) * scale).astype(BF16)
        made = dot_tn(grad_scores, query) * scale
        mask = masks[0].astype(F32)
        made = made[: z.rows] * mask + made[z.rows :] * (1.0 - mask)
        slab_ref[:, start + z.width : start + z.width + 128] = made.astype(BF16)
        made = dot_tn(probs_low, grad_heads)
        made = made[: z.rows] * mask + made[z.rows :] * (1.0 - mask)
        slab_ref[:, start + 2 * z.width : start + 2 * z.width + 128] = made.astype(BF16)

    unit_one, inverse_one = unit_rows(inputs)
    slab_ref[:, : z.width] = (unit_one * gain_one).astype(BF16)
    grad_normed = 0.0
    for i in range(3):
        waits[i]()
        grad_normed += dot_nt(slab_ref[:, (i + 1) * z.width : (i + 2) * z.width], mats[i])
    gain_one_grad = jnp.sum(grad_normed * unit_one, axis=0, keepdims=True)
    grad_unit = grad_normed * gain_one
    grad_unit -= unit_one * jnp.mean(grad_unit * unit_one, axis=1, keepdims=True)
    grad_in = (grad_middle + inverse_one * grad_unit).astype(BF16)

    relative += [jnp.zeros((1, 2 * z.rows), F32)] * (-z.heads % 8)
    relative = jnp.concatenate(relative, axis=0)
    lanes_of = bucket_lanes(z)
    high = relative.astype(BF16)
    table = dot_nt(lanes_of, high) + dot_nt(lanes_of, (relative - high.astype(F32)).astype(BF16))
    count = relative.shape[0]
    places = iota((count, z.small), 1) == iota((count, z.small), 0) + z.experts
    places = places & (iota((count, z.small), 0) < z.heads)
    table = dot_nn(table.astype(BF16), places.astype(F32).astype(BF16)).astype(BF16)
    grad_small += dot_nn(bucket_rows(z), table)
    gains = jnp.concatenate([gain_one_grad, gain_two_grad, jnp.zeros((6, z.width), F32)], axis=0)
    rows, lanes = (iota((8, z.small), 0), iota((8, z.small), 1))
    pick = ((lanes == z.gain_lane + rows) & (rows < 2)).astype(F32).astype(BF16)
    grad_small += dot_tn(gains.astype(BF16), pick)
    for i in range(z.width // z.rows):
        start = 6 * z.width + i * z.small
        slab_ref[:, start : start + z.small] = grad_small[i * z.rows : (i + 1) * z.rows].astype(BF16)
    return grad_in


def pack_kernel(z, query, key, value, output, router, gain_one, gain_two, table, piece, small, sems):
    copies = [
        pltpu.make_async_copy(source.at[0], piece.at[pl.ds(i * z.part, z.part)], sems.at[i])
        for i, source in enumerate((query, key, value, output))
    ]
    for copy in copies:
        copy.start()
    gains = [gain_one[...].astype(F32), gain_two[...].astype(F32), jnp.zeros((6, z.part), F32)]
    rows, lanes = (iota((8, z.small), 0), iota((8, z.small), 1))
    pick = ((lanes == z.gain_lane + rows) & (rows < 2)).astype(F32).astype(BF16)
    small[...] = dot_tn(jnp.concatenate(gains, axis=0).astype(BF16), pick)
    small[:, : z.experts] = router[0].astype(F32)
    small[: z.bucket_part, z.experts : z.gain_lane] = table[0].astype(F32)
    for g in range(z.small_groups):
        piece[4 * z.part :, g * z.small : (g + 1) * z.small] = small[
            g * z.small_rows : (g + 1) * z.small_rows
        ].astype(BF16)
    for copy in copies:
        copy.wait()


def first_kernel(
    z, section, place, lengths, tokens, own_route, other_route, o0, o1, o2, o3, o4, r0, r1, r2, r3, r4,
    send, qkv, probs, attended, middle_ref, router_ref,
    mats, packed, small, sems,
):
    core = section[0]
    waits = fetch_weights(
        z, core == 0, place[0], (o0, o1, o2, o3, o4), (r0, r1, r2, r3, r4), mats, packed, sems)
    inputs = tokens[core].astype(F32)
    middle, normed_two, router = attend(
        z, inputs, waits, mats, packed, small, lengths, core, qkv, probs, attended
    )
    middle_ref[...] = middle
    router_ref[...] = router
    route = jnp.where(core == 0, own_route[core], other_route[...])
    put_slots(z, send, 0, slot_picks(z, route), normed_two)


def second_kernel(
    z, section, place, lengths, cotangent, own_route, other_route, o0, o1, o2, o3, o4, r0, r1, r2, r3, r4, back, middle_zero, router_zero,
    send, out_zero, qkv, probs, attended, middle_ref, router_ref,
    mats, packed, small, sems,
):
    core = section[0]
    waits = fetch_weights(
        z, core == 1, place[0], (o0, o1, o2, o3, o4), (r0, r1, r2, r3, r4), mats, packed, sems)
    route = jnp.where(core == 0, own_route[core], other_route[...])
    gate = jnp.sum(router_zero[...] * chosen(z, route), axis=1, keepdims=True)
    token_out = get_slots(z, back, 0, slot_picks(z, route))
    layer_out = (middle_zero[...] + gate * token_out).astype(BF16)
    out_zero[...] = layer_out
    middle, normed_two, router = attend(
        z, layer_out.astype(F32), waits, mats, packed, small, lengths, core, qkv, probs, attended
    )
    middle_ref[...] = middle
    router_ref[...] = router
    route = jnp.where(core == 1, own_route[core], other_route[...])
    picks = slot_picks(z, route)
    put_slots(z, send, 0, picks, normed_two)
    gate = jnp.sum(router * chosen(z, route), axis=1, keepdims=True)
    grad = (gate * cotangent[core].astype(F32)).astype(BF16)
    put_slots(z, send, z.slot_width, picks, grad)


def third_kernel(
    z, section, place, cotangent, own_route, other_route, o0, o1, o2, o3, o4, r0, r1, r2, r3, r4, back, inputs, router_zero,
    qkv, probs, attended, middle, router,
    send, pair, slab,
    mats, packed, small, sems,
):
    core = section[0]
    waits = fetch_weights(
        z, core == 1, place[0], (o0, o1, o2, o3, o4), (r0, r1, r2, r3, r4), mats, packed, sems, (4, 3, 0, 1, 2))
    route = jnp.where(core == 1, own_route[core], other_route[...])
    picks = slot_picks(z, route)
    token_out = get_slots(z, back, 0, picks)
    grad_token = get_slots(z, back, z.slot_width, picks)
    gate = jnp.sum(router[...] * chosen(z, route), axis=1, keepdims=True)
    pair[0] = (middle[...] + gate * token_out).astype(BF16)
    grad_in = attend_back(
        z, cotangent[core].astype(F32), token_out, grad_token, inputs[...].astype(F32), route,
        waits, mats, packed, small, (qkv, probs, attended, middle, router), slab,
    )
    pair[1] = grad_in
    route = jnp.where(core == 0, own_route[core], other_route[...])
    gate = jnp.sum(router_zero[...] * chosen(z, route), axis=1, keepdims=True)
    grad = (gate * grad_in.astype(F32)).astype(BF16)
    put_slots(z, send, 0, slot_picks(z, route), grad)


def fourth_kernel(
    z, section, place, out_zero, pair_one, tokens, own_route, other_route, o0, o1, o2, o3, o4, r0, r1, r2, r3, r4, back_out, back_grad,
    qkv, probs, attended, middle, router,
    pair, slab,
    mats, packed, small, sems,
):
    core = section[0]
    waits = fetch_weights(
        z, core == 0, place[0], (o0, o1, o2, o3, o4), (r0, r1, r2, r3, r4), mats, packed, sems, (4, 3, 0, 1, 2))
    route = jnp.where(core == 0, own_route[core], other_route[...])
    picks = slot_picks(z, route)
    token_out = get_slots(z, back_out, 0, picks)
    grad_token = get_slots(z, back_grad, 0, picks)
    pair[0] = out_zero[...]
    pair[1] = attend_back(
        z, pair_one[1].astype(F32), token_out, grad_token, tokens[core].astype(F32), route,
        waits, mats, packed, small, (qkv, probs, attended, middle, router), slab,
    )


def fetch_experts(z, mine, own_in, own_out, other_in, other_out, w_in, w_out, sems):
    def copies(source_in, source_out, c):
        at = pl.ds(c * z.chunk, z.chunk)
        return (
            pltpu.make_async_copy(source_in.at[:, at], w_in.at[c], sems.at[2 * c]),
            pltpu.make_async_copy(source_out.at[at], w_out.at[c], sems.at[2 * c + 1]),
        )

    def start(source_in, source_out):
        for c in range(z.hidden // z.chunk):
            for copy in copies(source_in, source_out, c):
                copy.start()

    @pl.when(mine)
    def _():
        start(own_in, own_out)

    @pl.when(jnp.logical_not(mine))
    def _():
        start(other_in, other_out)

    def wait(c):
        for copy in copies(own_in, own_out, c):
            copy.wait()

    return wait


def expert_scratch(z, sums):
    chunks = z.hidden // z.chunk
    return [
        pltpu.VMEM((chunks, z.width, z.chunk), BF16),
        pltpu.VMEM((chunks, z.chunk, z.width), BF16),
        pltpu.SemaphoreType.DMA((2 * chunks,)),
    ] + [pltpu.VMEM((z.expert_rows, z.width), F32)] * sums


def smooth(values):
    square = values * values
    bent = jnp.tanh(GELU_SCALE * values * (1.0 + GELU_CUBE * square))
    return (0.5 * values * (1.0 + bent), square, bent)


def smooth_slope(values, square, bent):
    inner = GELU_SCALE * (1.0 + 3.0 * GELU_CUBE * square)
    return 0.5 * (1.0 + bent) + 0.5 * values * (1.0 - bent * bent) * inner


def expert_forward_kernel(
    z, section, arrived, own_in, own_out, other_in, other_out, result, w_in, w_out, sems, produced
):
    wait = fetch_experts(
        z, section[0] == 0, own_in, own_out, other_in, other_out, w_in, w_out, sems
    )
    rows = rows_of_slots(z, arrived, 0)
    for c in range(z.hidden // z.chunk):
        wait(c)
        hidden = smooth(dot_nn(rows, w_in[c]))[0].astype(BF16)
        made = dot_nn(hidden, w_out[c])
        produced[...] = made if c == 0 else produced[...] + made
    slots_of_rows(z, result, 0, produced[...])


def expert_backward_kernel(
    z, layer, section, arrived, arrived_grad, own_in, own_out, other_in, other_out,
    result, stuff, w_in, w_out, sems, grad_sum, *produced
):
    wait = fetch_experts(
        z, section[0] == layer, own_in, own_out, other_in, other_out, w_in, w_out, sems
    )
    rows = rows_of_slots(z, arrived, 0)
    grads = rows_of_slots(z, arrived_grad, z.slot_width if produced else 0)
    stuff[:, 2 * z.hidden : 2 * z.hidden + z.width] = rows
    stuff[:, 2 * z.hidden + z.width : 2 * z.hidden + 2 * z.width] = grads
    for c in range(z.hidden // z.chunk):
        wait(c)
        before = dot_nn(rows, w_in[c])
        hidden, square, bent = smooth(before)
        hidden = hidden.astype(BF16)
        stuff[:, c * z.chunk : (c + 1) * z.chunk] = hidden
        if produced:
            made = dot_nn(hidden, w_out[c])
            produced[0][...] = made if c == 0 else produced[0][...] + made
        grad_pre = dot_nt(grads, w_out[c]) * smooth_slope(before, square, bent)
        grad_pre = grad_pre.astype(BF16)
        stuff[:, z.hidden + c * z.chunk : z.hidden + (c + 1) * z.chunk] = grad_pre
        made = dot_nt(grad_pre, w_in[c])
        grad_sum[...] = made if c == 0 else grad_sum[...] + made
    if produced:
        slots_of_rows(z, result, 0, produced[0][...])
    slots_of_rows(z, result, z.slot_width if produced else 0, grad_sum[...])


def expert_weights_kernel(
    z, section, own_zero, other_zero, own_one, other_one, grad_in, grad_out, held, turned, sems
):
    step = pl.program_id(0)

    @pl.when(step == 0)
    def _():
        def copies(own, other):
            return [
                pltpu.make_async_copy(
                    source, held.at[pl.ds(i * z.expert_rows, z.expert_rows)], sems.at[i]
                )
                for i, source in enumerate((own, other))
            ]

        @pl.when(section[0] == 0)
        def _():
            for copy in copies(own_zero, other_zero):
                copy.start()

        @pl.when(section[0] != 0)
        def _():
            for copy in copies(own_one, other_one):
                copy.start()

        for copy in copies(own_zero, other_zero):
            copy.wait()
        rows = held[:, 2 * z.hidden : 2 * z.hidden + z.width]
        turned[...] = jnp.transpose(rows.astype(F32)).astype(BF16)

    start = pl.multiple_of(step * z.chunk, z.chunk)
    grad_pre = held[:, pl.ds(z.hidden + start, z.chunk)]
    hidden = held[:, pl.ds(start, z.chunk)]
    grads = held[:, 2 * z.hidden + z.width : 2 * z.hidden + 2 * z.width]
    grad_in[...] = dot_nn(turned[...], grad_pre).astype(BF16)
    grad_out[...] = dot_tn(hidden, grads).astype(BF16)


def attention_weights_kernel(z, layer, section, own, other, out):
    second = section[0] ^ layer

    def both(column):
        at = pl.ds(pl.multiple_of(column * z.width, 128), z.width)
        return jnp.concatenate([own[:, at], other[:, at]], axis=0)

    for i, (left, right) in enumerate(
        ((0, 1 + 2 * second), (4 * second, 2 + 3 * second))
    ):
        made = dot_tn(both(left), both(right))
        for j in range(z.shards):
            out[j, i * z.part : (i + 1) * z.part] = made[j * z.part : (j + 1) * z.part].astype(BF16)
    columns = slice(6 * z.width, z.slab)
    total = own[:, columns].astype(F32) + other[:, columns].astype(F32)
    pieces = [total[:, i * z.small : (i + 1) * z.small] for i in range(z.width // z.rows)]
    total = jnp.concatenate(pieces, axis=0).astype(BF16)
    for j in range(z.shards):
        for g in range(z.small_groups):
            row = j * z.part + g * z.small_rows
            out[j, 2 * z.part :, g * z.small : (g + 1) * z.small] = total[row : row + z.small_rows]


def sum_kernel(z, pieces, out):
    total = pieces[0].astype(F32)
    for i in range(1, pieces.shape[0]):
        total += pieces[i].astype(F32)
    rows = out.shape[1]
    for i in range(out.shape[0]):
        start = i * rows if total.shape[0] > rows else 0
        out[i] = total[start : start + rows].astype(BF16)


def final_kernel(
    z, section, half_zero, got_zero, half_one, got_one, pair_zero, other_zero, pair_one, other_one,
    layer_out, input_grad, query, key, value, output, gain_one, gain_two, router, table, small,
):
    def finish(first, second, micros):
        query[0] = first[: z.part]
        key[0] = first[z.part : 2 * z.part]
        value[0] = second[: z.part]
        output[0] = second[z.part : 2 * z.part]
        for g in range(z.small_groups):
            small[g * z.small_rows : (g + 1) * z.small_rows] = first[
                2 * z.part :, g * z.small : (g + 1) * z.small
            ].astype(F32)
        for i, pair in enumerate(micros):
            layer_out[0, i] = pair[0]
            input_grad[0, i] = pair[1]

    @pl.when(section[0] == 0)
    def _():
        finish(half_zero, got_zero, (pair_zero, other_zero))

    @pl.when(section[0] != 0)
    def _():
        finish(half_one, got_one, (other_one, pair_one))

    gains = gain_rows(z, small[...].astype(BF16))
    gain_one[...] = gains[0].astype(BF16)
    gain_two[...] = gains[1].astype(BF16)
    router[0] = small[:, : z.experts].astype(BF16)
    table[0] = small[: z.bucket_part, z.experts : z.gain_lane].astype(BF16)


def swap(value):
    return lax.ppermute(value, "section", [(0, 1), (1, 0)])


def cross(value, target):
    return lax.ppermute(value, "section", [(1 - target, target)])


def within(value, distance, layer):
    size = lax.axis_size("shard")
    pairs = [(layer * size + i, layer * size + (i ^ distance)) for i in range(size)]
    return lax.ppermute(value, ("section", "shard"), pairs)


def exchange(buffer, axes=("expert", "shard")):
    return lax.all_to_all(buffer, axes, split_axis=0, concat_axis=0, tiled=True)


def shards(
    tokens_in,
    cotangent,
    lengths,
    routes,
    w_query,
    w_key,
    w_value,
    w_output,
    gain_attn,
    gain_moe,
    w_router,
    bias_table,
    w_in,
    w_out,
):
    z = Sizes(tokens_in, w_query, w_router, bias_table, w_in, lax.axis_size("shard"))
    micro_count = tokens_in.shape[0]
    section = lax.axis_index("section").astype(I32)
    core = section.reshape(1)
    place = lax.axis_index("shard").astype(I32).reshape(1)

    def shape(*dims, kind=BF16):
        return jax.ShapeDtypeStruct(dims, kind)

    own_route = routes[0]
    route_pair = (
        own_route,
        swap(lax.dynamic_index_in_dim(own_route, 1 - section, 0, keepdims=False)),
    )
    piece = call(
        functools.partial(pack_kernel, z),
        shape(z.piece, z.width),
        (w_query, w_key, w_value, w_output, w_router, gain_attn, gain_moe, bias_table),
        [ANY] * 4 + [VMEM] * 4,
        [pltpu.VMEM((z.part, z.small), F32), pltpu.SemaphoreType.DMA((4,))],
    )

    def neighbours(piece, layer):
        held = (piece, within(piece, 1, layer), within(piece, 2, layer))
        return (held, tuple(cross(member, 1 - layer) for member in held))

    def diagonal(held, layer):
        made = (
            within(held[1][: z.cut_row], 2, layer),
            within(held[2][z.cut_row :], 1, layer),
        )
        return (made, tuple(cross(member, 1 - layer) for member in made))

    def handed(layer):
        return tuple(cross(member[0, 0], 1 - layer) for member in (w_in, w_out))

    near, near_other = neighbours(piece, 0)
    far, far_other = diagonal(near, 0)
    weights_zero = (*near, *far, *near_other, *far_other)
    late_piece, unused = lax.optimization_barrier((piece, near_other[1]))
    near, near_other = neighbours(late_piece, 1)

    buffer = shape(z.experts, 8, z.slot_width)
    wide_buffer = shape(z.experts, 8, 2 * z.slot_width)
    kept = (
        shape(z.rows, 3 * z.width),
        shape(z.heads // 2, z.rows, 2 * z.rows),
        shape(z.rows, z.width),
        shape(z.rows, z.width, kind=F32),
        shape(z.rows, z.small, kind=F32),
    )
    scratch = weight_scratch(z)
    rows_shape = shape(z.rows, z.width)
    slab_shape = shape(z.rows, z.slab)

    sent, *kept_zero = call(
        functools.partial(first_kernel, z),
        (buffer, *kept),
        (core, place, lengths, tokens_in, *route_pair, *weights_zero),
        [SMEM, SMEM, SMEM, VMEM, VMEM, VMEM] + [ANY] * 10,
        scratch,
    )
    arrived_zero = exchange(sent)
    (near, arrived_zero) = lax.optimization_barrier((near, arrived_zero))
    far, far_other = diagonal(near, 1)
    weights_one = (*near, *far, *near_other, *far_other)
    given_zero = handed(0)
    given_one = handed(1)
    experts = (w_in[0, 0], w_out[0, 0])
    produced = call(
        functools.partial(expert_forward_kernel, z),
        buffer,
        (core, arrived_zero, *experts, *given_zero),
        [SMEM, VMEM, ANY, ANY, ANY, ANY],
        expert_scratch(z, 1),
    )
    back_zero = exchange(produced)

    sent, out_zero, *kept_one = call(
        functools.partial(second_kernel, z),
        (wide_buffer, rows_shape, *kept),
        (core, place, lengths, cotangent, *route_pair, *weights_one, back_zero, *kept_zero[3:]),
        [SMEM, SMEM, SMEM, VMEM, VMEM, VMEM] + [ANY] * 10 + [VMEM] * 3,
        scratch,
    )
    arrived_one = exchange(sent)
    stuff_shape = shape(z.expert_rows, 2 * z.hidden + 2 * z.width)
    result, stuff_one = call(
        lambda section, arrived, *rest: expert_backward_kernel(
            z, 1, section, arrived, arrived, *rest
        ),
        (wide_buffer, stuff_shape),
        (core, arrived_one, *experts, *given_one),
        [SMEM, VMEM, ANY, ANY, ANY, ANY],
        expert_scratch(z, 2),
    )
    back_one = exchange(result)

    pair_shape = shape(2, z.rows, z.width)
    sent, pair_one, slab_one = call(
        functools.partial(third_kernel, z),
        (buffer, pair_shape, slab_shape),
        (core, place, cotangent, *route_pair, *weights_one, back_one, out_zero, kept_zero[4], *kept_one),
        [SMEM, SMEM, VMEM, VMEM, VMEM] + [ANY] * 10 + [VMEM] * 8,
        scratch,
    )
    arrived_grad = exchange(sent)

    result, stuff_zero = call(
        functools.partial(expert_backward_kernel, z, 0),
        (buffer, stuff_shape),
        (core, arrived_zero, arrived_grad, *experts, *given_zero),
        [SMEM, VMEM, VMEM, ANY, ANY, ANY, ANY],
        expert_scratch(z, 1),
    )
    back_grad = exchange(result)
    pair_zero, slab_zero = call(
        functools.partial(fourth_kernel, z),
        (pair_shape, slab_shape),
        (
            core, place, out_zero, pair_one, tokens_in, *route_pair, *weights_zero,
            back_zero, back_grad, *kept_zero,
        ),
        [SMEM, SMEM, VMEM, VMEM, VMEM, VMEM, VMEM] + [ANY] * 10 + [VMEM] * 7,
        scratch,
    )

    count = lax.axis_size("expert")
    half_rows = 2 * z.part + z.small_rows

    def partial_sums(slab, layer):
        return call(
            functools.partial(attention_weights_kernel, z, layer),
            shape(z.shards, half_rows, z.width),
            (core, slab, swap(slab)),
            [SMEM, VMEM, VMEM],
        )

    def total(pieces):
        part = shape(count, half_rows // count, z.width)
        return call(functools.partial(sum_kernel, z), part, (pieces,), [VMEM])

    sums = partial_sums(slab_one, 1).reshape(z.shards * half_rows, z.width)
    sums = lax.psum_scatter(sums, "shard", scatter_dimension=0, tiled=True)
    half_one = lax.psum(sums, "expert")
    got_one = cross(half_one, 1)
    summed = total(exchange(partial_sums(slab_zero, 0), "shard"))
    summed = total(exchange(summed, "expert"))
    half_zero = exchange(summed, "expert").reshape(half_rows, z.width)
    got_zero = cross(half_zero, 0)

    chunks = z.hidden // z.chunk
    grad_w_in, grad_w_out = call(
        functools.partial(expert_weights_kernel, z),
        (shape(z.width, z.hidden), shape(z.hidden, z.width)),
        (core, stuff_zero, cross(stuff_zero, 0), stuff_one, cross(stuff_one, 1)),
        [SMEM, ANY, ANY, ANY, ANY],
        [
            pltpu.VMEM((2 * z.expert_rows, stuff_shape.shape[1]), BF16),
            pltpu.VMEM((z.width, 2 * z.expert_rows), BF16),
            pltpu.SemaphoreType.DMA((2,)),
        ],
        grid=(chunks,),
        out_specs=(
            pl.BlockSpec((z.width, z.chunk), lambda i: (0, i)),
            pl.BlockSpec((z.chunk, z.width), lambda i: (i, 0)),
        ),
    )

    matrix = shape(1, z.part, z.width)
    finals = call(
        functools.partial(final_kernel, z),
        (
            *[shape(1, micro_count, z.rows, z.width)] * 2,
            *[matrix] * 4,
            *[shape(1, z.part)] * 2,
            shape(1, z.part, z.experts),
            shape(1, z.bucket_part, z.heads),
        ),
        (
            core, half_zero, got_zero, half_one, got_one,
            pair_zero, cross(pair_zero, 0), pair_one, cross(pair_one, 1),
        ),
        [SMEM] + [VMEM] * 8,
        [pltpu.VMEM((z.part, z.small), F32)],
    )
    return (*finals, grad_w_in[None, None], grad_w_out[None, None])


def solution(mesh):
    both = ("expert", "shard")
    plain = P("section", "shard", None)
    gains = P("section", "shard")
    blocks = P("section", None, both, None)
    experts = P("section", both, None, None)
    tokens = P(None, both, None)
    attention = (plain, plain, plain, plain, gains, gains, plain, plain, experts, experts)
    return jax.shard_map(
        shards,
        mesh=mesh,
        in_specs=(tokens, tokens, tokens, blocks, *attention),
        out_specs=(blocks, blocks, *attention),
        check_vma=False,
    )
```

```python
import functools

import jax
import jax.numpy as jnp
from jax import lax
from jax.experimental import pallas as pl
from jax.experimental.pallas import tpu as pltpu
from jax.sharding import PartitionSpec as P

EPSILON = 1e-06
BOUNDS = (8, 12, 16, 23, 32, 46, 64, 91)
MASKED = -1e30
F32 = jnp.float32
BF16 = jnp.bfloat16
I32 = jnp.int32
GELU_SCALE = 0.7978845608028654
GELU_CUBE = 0.044715
SMEM = pl.BlockSpec(memory_space=pltpu.SMEM)
VMEM = pl.BlockSpec(memory_space=pltpu.VMEM)
HBM = pl.BlockSpec(memory_space=pltpu.HBM)
ANY = pl.BlockSpec(memory_space=pl.ANY)


def dot_nn(a, b):
    return jnp.dot(a, b, preferred_element_type=F32)


def dot_nt(a, b):
    return lax.dot_general(a, b, (((1,), (1,)), ((), ())), preferred_element_type=F32)


def dot_tn(a, b):
    return lax.dot_general(a, b, (((0,), (0,)), ((), ())), preferred_element_type=F32)


def iota(shape, dimension):
    return lax.broadcasted_iota(I32, shape, dimension)


def call(body, outs, ins, specs, scratch=(), grant=24, cost=5, **more):
    return pl.pallas_call(
        body,
        out_shape=outs,
        in_specs=specs,
        scratch_shapes=scratch,
        compiler_params=pltpu.CompilerParams(vmem_limit_bytes=grant * 1024 * 1024),
        cost_estimate=pl.CostEstimate(
            flops=int(cost * 5e8), bytes_accessed=int(cost * 3e6), transcendentals=0
        ),
        **more,
    )(*ins)


def bucket_of(relative):
    distance = jnp.abs(relative)
    bucket = jnp.zeros_like(relative)
    for lowest in tuple(range(1, 8)) + BOUNDS:
        bucket = bucket + (distance >= lowest).astype(I32)
    return bucket + 16 * (relative > 0).astype(I32)


class Sizes:
    def __init__(self, tokens_in, w_query, w_router, bias_table, w_in, shards):
        self.rows, self.width = tokens_in.shape[1:]
        self.part = w_query.shape[1]
        self.shards = shards
        self.experts = w_router.shape[2]
        self.bucket_part, self.heads = bias_table.shape[1:]
        self.buckets = self.bucket_part * shards
        self.hidden = w_in.shape[3]
        self.chunk = self.hidden // 6
        self.capacity = max(
            2, (3 * self.rows + 2 * self.experts - 1) // (2 * self.experts)
        )
        self.full, rest = divmod(self.capacity, 8)
        self.rest = next((power for power in (0, 1, 2, 4) if power >= rest), None)
        if self.rest is None:
            self.full, self.rest = (self.full + 1, 0)
        self.cuts = 8 // self.rest if self.rest else 0
        self.cut = self.width // self.cuts if self.rest else 0
        self.slot_width = self.full * self.width + self.cut
        self.slot_rows = self.experts * 8
        self.expert_rows = self.slot_rows * self.full + self.experts * self.rest
        self.small = -(-(self.experts + self.heads + 2) // 128) * 128
        self.small_groups = self.width // self.small
        self.small_rows = self.part // self.small_groups
        self.gain_lane = self.experts + self.heads
        self.piece = 4 * self.part + self.small_rows
        self.slab = 6 * self.width + self.small * self.width // self.rows


def slot_picks(z, route):
    onehot = (route == iota((z.rows, z.experts), 1)).astype(F32)
    lower = (iota((z.rows, z.rows), 0) >= iota((z.rows, z.rows), 1)).astype(F32).astype(BF16)
    running = dot_nn(lower, onehot.astype(BF16))
    place = jnp.sum(running * onehot, axis=1, keepdims=True).astype(I32) - 1
    slots = iota((z.rows, z.slot_rows), 1)

    def pick(first, wide, shift):
        inside = (place >= first) & (place < first + wide)
        target = jnp.where(inside, route * 8 + place - first + shift, -1)
        return (slots == target).astype(F32).astype(BF16)

    picks = [pick(8 * i, 8, 0) for i in range(z.full)]
    return picks + [pick(8 * z.full, z.rest, z.rest * i) for i in range(z.cuts)]


def cut_sum(z, picks, values):
    return sum(dot_tn(pick, values[:, i * z.cut : (i + 1) * z.cut]) for i, pick in enumerate(picks))


def put_slots(z, ref, offset, picks, values):
    for i in range(z.full):
        block = dot_tn(picks[i], values)
        ref[:, :, offset : offset + z.width] = block.reshape(z.experts, 8, z.width).astype(BF16)
        offset += z.width
    if z.rest:
        block = cut_sum(z, picks[z.full :], values)
        ref[:, :, offset : offset + z.cut] = block.reshape(z.experts, 8, z.cut).astype(BF16)


def read_slots(z, ref, offset, wide):
    block = ref[:, :, offset : offset + wide].astype(F32)
    return block.reshape(z.slot_rows, wide).astype(BF16)


def get_slots(z, ref, offset, picks):
    total = 0.0
    for i in range(z.full):
        total += dot_nn(picks[i], read_slots(z, ref, offset, z.width))
        offset += z.width
    if z.rest:
        block = read_slots(z, ref, offset, z.cut)
        total += jnp.concatenate([dot_nn(pick, block) for pick in picks[z.full :]], axis=1)
    return total


def extra_picks(z):
    shape = (z.experts * z.rest, z.slot_rows)
    rows, slots = (iota(shape, 0), iota(shape, 1))
    first = (rows // z.rest) * 8 + rows % z.rest
    return [(slots == first + z.rest * i).astype(F32).astype(BF16) for i in range(z.cuts)]


def rows_of_slots(z, ref, offset):
    parts = []
    for i in range(z.full):
        parts.append(read_slots(z, ref, offset, z.width))
        offset += z.width
    if z.rest:
        block = read_slots(z, ref, offset, z.cut)
        pieces = [dot_nn(pick, block) for pick in extra_picks(z)]
        parts.append(jnp.concatenate(pieces, axis=1).astype(BF16))
    return jnp.concatenate(parts, axis=0) if len(parts) > 1 else parts[0]


def slots_of_rows(z, ref, offset, rows):
    for i in range(z.full):
        block = rows[i * z.slot_rows : (i + 1) * z.slot_rows]
        ref[:, :, offset : offset + z.width] = block.reshape(z.experts, 8, z.width).astype(BF16)
        offset += z.width
    if z.rest:
        block = cut_sum(z, extra_picks(z), rows[z.full * z.slot_rows :].astype(BF16))
        ref[:, :, offset : offset + z.cut] = block.reshape(z.experts, 8, z.cut).astype(BF16)


def fetch_weights(z, mine, place, own, other, mats, packed, sems, order=(4, 0, 1, 2, 3)):
    def copy(pieces, i, k):
        shard = place ^ k
        count = z.small_rows if i == 4 else z.part
        start = i * z.part
        source = pieces[k]
        target = pl.ds(pl.multiple_of(shard * count, 16), count)
        held = packed.at[target] if i == 4 else mats.at[i, target]
        return pltpu.make_async_copy(source.at[pl.ds(start, count)], held, sems.at[i, k])

    def start(pieces):
        for i in order:
            for k in range(z.shards):
                copy(pieces, i, k).start()

    def wait(i):
        for k in range(z.shards):
            copy(own, i, k).wait()

    @pl.when(mine)
    def _():
        start(own)

    @pl.when(jnp.logical_not(mine))
    def _():
        start(other)

    return [functools.partial(wait, i) for i in range(5)]


def weight_scratch(z):
    return [
        pltpu.VMEM((4, z.width, z.width), BF16),
        pltpu.VMEM((z.shards * z.small_rows, z.width), BF16),
        pltpu.VMEM((z.width, z.small), BF16),
        pltpu.SemaphoreType.DMA((5, z.shards)),
    ]


def unpack_small(z, packed, small):
    for j in range(z.shards):
        for g in range(z.small_groups):
            row = j * z.part + g * z.small_rows
            small[row : row + z.small_rows, :] = packed[
                j * z.small_rows : (j + 1) * z.small_rows, g * z.small : (g + 1) * z.small
            ]


def bucket_rows(z):
    rows, buckets = (iota((z.width, z.buckets), 0), iota((z.width, z.buckets), 1))
    held = (buckets // z.bucket_part) * z.part + buckets % z.bucket_part
    return (rows == held).astype(F32).astype(BF16)


def bucket_lanes(z):
    shape = (z.buckets, 2 * z.rows)
    return (bucket_of(iota(shape, 1) - z.rows) == iota(shape, 0)).astype(F32).astype(BF16)


def gain_rows(z, small):
    rows, lanes = (iota((8, z.small), 0), iota((8, z.small), 1))
    pick = ((lanes == z.gain_lane + rows) & (rows < 2)).astype(F32).astype(BF16)
    made = dot_nt(pick, small)
    return (made[0:1], made[1:2])


def unit_rows(values):
    inverse = lax.rsqrt(jnp.mean(values * values, axis=-1, keepdims=True) + EPSILON)
    return (values * inverse, inverse)


def pair_masks(z):
    lanes = iota((z.rows, 128), 1)
    first = (lanes < 64).astype(F32).astype(BF16)
    return (first, (lanes >= 64).astype(F32).astype(BF16))


def double(values, masks):
    return jnp.concatenate([values * masks[0], values * masks[1]], axis=0)


def attend(z, inputs, waits, mats, packed, small, lengths, section, qkv_ref, probs_ref, attended_ref):
    waits[4]()
    unpack_small(z, packed, small)
    small_full = small[...]
    gain_one, gain_two = gain_rows(z, small_full)
    normed_one = (unit_rows(inputs)[0] * gain_one).astype(BF16)
    for i in range(3):
        waits[i]()
        qkv_ref[:, i * z.width : (i + 1) * z.width] = dot_nn(normed_one, mats[i]).astype(BF16)

    table = dot_tn(bucket_rows(z), small_full).astype(BF16)
    bias = dot_tn(table, bucket_lanes(z))[z.experts : z.experts + z.heads]

    rows, lanes = (iota((z.rows, z.rows), 0), iota((z.rows, z.rows), 1))
    segment_q, segment_k = (jnp.zeros_like(rows), jnp.zeros_like(rows))
    end = jnp.int32(0)
    for i in range(lengths.shape[2]):
        end = end + lengths[section, 0, i]
        segment_q += (rows >= end).astype(I32)
        segment_k += (lanes >= end).astype(I32)
    visible = segment_q == segment_k

    masks = pair_masks(z)
    scale = 64 ** (-0.5)
    for p in range(z.heads // 2):
        at = slice(p * 128, (p + 1) * 128)
        query = qkv_ref[:, p * 128 : (p + 1) * 128]
        key = qkv_ref[:, z.width + p * 128 : z.width + (p + 1) * 128]
        value = qkv_ref[:, 2 * z.width + p * 128 : 2 * z.width + (p + 1) * 128]
        scores = dot_nt(query, double(key, masks)) * scale
        halves = []
        for i in range(2):
            spread = jnp.broadcast_to(bias[2 * p + i : 2 * p + i + 1], (z.rows, 2 * z.rows))
            spread = pltpu.roll(spread, z.rows, 1, stride=1, stride_axis=0)[:, : z.rows]
            part = scores[:, i * z.rows : (i + 1) * z.rows] + spread
            part = jnp.where(visible, part, MASKED)
            part = jnp.exp(part - jnp.max(part, axis=-1, keepdims=True))
            halves.append(part / jnp.sum(part, axis=-1, keepdims=True))
        probs = jnp.concatenate(halves, axis=1).astype(BF16)
        probs_ref[p] = probs
        attended_ref[:, at] = dot_nn(probs, double(value, masks)).astype(BF16)

    waits[3]()
    middle = inputs + dot_nn(attended_ref[...], mats[3])
    normed_two = (unit_rows(middle)[0] * gain_two).astype(BF16)
    logits = dot_nn(normed_two, small_full)
    logits = jnp.where(iota((z.rows, z.small), 1) < z.experts, logits, MASKED)
    logits = jnp.exp(logits - jnp.max(logits, axis=-1, keepdims=True))
    router = logits / jnp.sum(logits, axis=-1, keepdims=True)
    return (middle, normed_two, router)


def chosen(z, route):
    return (route == iota((z.rows, z.small), 1)).astype(F32)


def attend_back(
    z, grad_out, token_out, grad_token, inputs, route, waits, mats, packed, small, kept, slab_ref
):
    qkv_ref, probs_ref, attended_ref, middle_ref, router_ref = kept
    waits[4]()
    unpack_small(z, packed, small)
    small_full = small[...]
    gain_one, gain_two = gain_rows(z, small_full)
    onehot = chosen(z, route)
    router = router_ref[...]
    gate = jnp.sum(router * onehot, axis=1, keepdims=True)
    grad_gate = jnp.sum(grad_out * token_out, axis=1, keepdims=True)
    grad_logits = (grad_gate * gate * (onehot - router)).astype(BF16)
    unit_two, inverse_two = unit_rows(middle_ref[...])
    grad_small = dot_tn((unit_two * gain_two).astype(BF16), grad_logits)
    grad_normed = grad_token + dot_nt(grad_logits, small_full)
    gain_two_grad = jnp.sum(grad_normed * unit_two, axis=0, keepdims=True)
    grad_unit = grad_normed * gain_two
    grad_unit -= unit_two * jnp.mean(grad_unit * unit_two, axis=1, keepdims=True)
    grad_middle = grad_out + inverse_two * grad_unit
    grad_branch = grad_middle.astype(BF16)
    slab_ref[:, 4 * z.width : 5 * z.width] = attended_ref[...]
    slab_ref[:, 5 * z.width : 6 * z.width] = grad_branch
    waits[3]()
    grad_attended = dot_nt(grad_branch, mats[3]).astype(BF16)

    masks = pair_masks(z)
    scale = 64 ** (-0.5)
    relative = []
    turn = iota((z.rows, z.rows), 0) + iota((z.rows, z.rows), 1) == z.rows - 1
    turn = turn.astype(F32).astype(BF16)
    for p in range(z.heads // 2):
        at = slice(p * 128, (p + 1) * 128)
        query = qkv_ref[:, p * 128 : (p + 1) * 128]
        keys = double(qkv_ref[:, z.width + p * 128 : z.width + (p + 1) * 128], masks)
        values = double(qkv_ref[:, 2 * z.width + p * 128 : 2 * z.width + (p + 1) * 128], masks)
        grad_heads = grad_attended[:, at]
        probs_low = probs_ref[p]
        probs = probs_low.astype(F32)
        grad_probs = dot_nt(grad_heads, values)
        halves = []
        for i in range(2):
            part = slice(i * z.rows, (i + 1) * z.rows)
            product = grad_probs[:, part] * probs[:, part]
            dots = jnp.sum(product, axis=-1, keepdims=True)
            grads = (product - probs[:, part] * dots).astype(BF16)
            halves.append(grads)
        grad_scores = jnp.concatenate(halves, axis=1)
        turned = dot_nn(turn, grad_scores)
        for i in range(2):
            wide = [turned[:, i * z.rows : (i + 1) * z.rows], jnp.zeros((z.rows, z.rows), F32)]
            wide = pltpu.roll(jnp.concatenate(wide, axis=1), 1, 1, stride=1, stride_axis=0)
            relative.append(jnp.sum(wide, axis=0, keepdims=True))
        start = z.width + p * 128
        slab_ref[:, start : start + 128] = (dot_nn(grad_scores, keys) * scale).astype(BF16)
        made = dot_tn(grad_scores, query) * scale
        mask = masks[0].astype(F32)
        made = made[: z.rows] * mask + made[z.rows :] * (1.0 - mask)
        slab_ref[:, start + z.width : start + z.width + 128] = made.astype(BF16)
        made = dot_tn(probs_low, grad_heads)
        made = made[: z.rows] * mask + made[z.rows :] * (1.0 - mask)
        slab_ref[:, start + 2 * z.width : start + 2 * z.width + 128] = made.astype(BF16)

    unit_one, inverse_one = unit_rows(inputs)
    slab_ref[:, : z.width] = (unit_one * gain_one).astype(BF16)
    grad_normed = 0.0
    for i in range(3):
        waits[i]()
        grad_normed += dot_nt(slab_ref[:, (i + 1) * z.width : (i + 2) * z.width], mats[i])
    gain_one_grad = jnp.sum(grad_normed * unit_one, axis=0, keepdims=True)
    grad_unit = grad_normed * gain_one
    grad_unit -= unit_one * jnp.mean(grad_unit * unit_one, axis=1, keepdims=True)
    grad_in = (grad_middle + inverse_one * grad_unit).astype(BF16)

    relative += [jnp.zeros((1, 2 * z.rows), F32)] * (-z.heads % 8)
    relative = jnp.concatenate(relative, axis=0)
    lanes_of = bucket_lanes(z)
    high = relative.astype(BF16)
    table = dot_nt(lanes_of, high) + dot_nt(lanes_of, (relative - high.astype(F32)).astype(BF16))
    count = relative.shape[0]
    places = iota((count, z.small), 1) == iota((count, z.small), 0) + z.experts
    places = places & (iota((count, z.small), 0) < z.heads)
    table = dot_nn(table.astype(BF16), places.astype(F32).astype(BF16)).astype(BF16)
    grad_small += dot_nn(bucket_rows(z), table)
    gains = jnp.concatenate([gain_one_grad, gain_two_grad, jnp.zeros((6, z.width), F32)], axis=0)
    rows, lanes = (iota((8, z.small), 0), iota((8, z.small), 1))
    pick = ((lanes == z.gain_lane + rows) & (rows < 2)).astype(F32).astype(BF16)
    grad_small += dot_tn(gains.astype(BF16), pick)
    for i in range(z.width // z.rows):
        start = 6 * z.width + i * z.small
        slab_ref[:, start : start + z.small] = grad_small[i * z.rows : (i + 1) * z.rows].astype(BF16)
    return grad_in


def pack_kernel(z, query, key, value, output, router, gain_one, gain_two, table, piece, small, sems):
    copies = [
        pltpu.make_async_copy(source.at[0], piece.at[pl.ds(i * z.part, z.part)], sems.at[i])
        for i, source in enumerate((query, key, value, output))
    ]
    for copy in copies:
        copy.start()
    gains = [gain_one[...].astype(F32), gain_two[...].astype(F32), jnp.zeros((6, z.part), F32)]
    rows, lanes = (iota((8, z.small), 0), iota((8, z.small), 1))
    pick = ((lanes == z.gain_lane + rows) & (rows < 2)).astype(F32).astype(BF16)
    small[...] = dot_tn(jnp.concatenate(gains, axis=0).astype(BF16), pick)
    small[:, : z.experts] = router[0].astype(F32)
    small[: z.bucket_part, z.experts : z.gain_lane] = table[0].astype(F32)
    for g in range(z.small_groups):
        piece[4 * z.part :, g * z.small : (g + 1) * z.small] = small[
            g * z.small_rows : (g + 1) * z.small_rows
        ].astype(BF16)
    for copy in copies:
        copy.wait()


def first_kernel(
    z, section, place, lengths, tokens, own_route, other_route, o0, o1, o2, o3, r0, r1, r2, r3,
    send, qkv, probs, attended, middle_ref, router_ref,
    mats, packed, small, sems,
):
    core = section[0]
    waits = fetch_weights(
        z, core == 0, place[0], (o0, o1, o2, o3), (r0, r1, r2, r3), mats, packed, sems)
    inputs = tokens[core].astype(F32)
    middle, normed_two, router = attend(
        z, inputs, waits, mats, packed, small, lengths, core, qkv, probs, attended
    )
    middle_ref[...] = middle
    router_ref[...] = router
    route = jnp.where(core == 0, own_route[core], other_route[...])
    put_slots(z, send, 0, slot_picks(z, route), normed_two)


def second_kernel(
    z, section, place, lengths, cotangent, own_route, other_route, o0, o1, o2, o3, r0, r1, r2, r3, back, middle_zero, router_zero,
    send, out_zero, qkv, probs, attended, middle_ref, router_ref,
    mats, packed, small, sems,
):
    core = section[0]
    waits = fetch_weights(
        z, core == 1, place[0], (o0, o1, o2, o3), (r0, r1, r2, r3), mats, packed, sems)
    route = jnp.where(core == 0, own_route[core], other_route[...])
    gate = jnp.sum(router_zero[...] * chosen(z, route), axis=1, keepdims=True)
    token_out = get_slots(z, back, 0, slot_picks(z, route))
    layer_out = (middle_zero[...] + gate * token_out).astype(BF16)
    out_zero[...] = layer_out
    middle, normed_two, router = attend(
        z, layer_out.astype(F32), waits, mats, packed, small, lengths, core, qkv, probs, attended
    )
    middle_ref[...] = middle
    router_ref[...] = router
    route = jnp.where(core == 1, own_route[core], other_route[...])
    picks = slot_picks(z, route)
    put_slots(z, send, 0, picks, normed_two)
    gate = jnp.sum(router * chosen(z, route), axis=1, keepdims=True)
    grad = (gate * cotangent[core].astype(F32)).astype(BF16)
    put_slots(z, send, z.slot_width, picks, grad)


def third_kernel(
    z, section, place, cotangent, own_route, other_route, o0, o1, o2, o3, r0, r1, r2, r3, back, inputs, router_zero,
    qkv, probs, attended, middle, router,
    send, pair, slab,
    mats, packed, small, sems,
):
    core = section[0]
    waits = fetch_weights(
        z, core == 1, place[0], (o0, o1, o2, o3), (r0, r1, r2, r3), mats, packed, sems, (4, 3, 0, 1, 2))
    route = jnp.where(core == 1, own_route[core], other_route[...])
    picks = slot_picks(z, route)
    token_out = get_slots(z, back, 0, picks)
    grad_token = get_slots(z, back, z.slot_width, picks)
    gate = jnp.sum(router[...] * chosen(z, route), axis=1, keepdims=True)
    pair[0] = (middle[...] + gate * token_out).astype(BF16)
    grad_in = attend_back(
        z, cotangent[core].astype(F32), token_out, grad_token, inputs[...].astype(F32), route,
        waits, mats, packed, small, (qkv, probs, attended, middle, router), slab,
    )
    pair[1] = grad_in
    route = jnp.where(core == 0, own_route[core], other_route[...])
    gate = jnp.sum(router_zero[...] * chosen(z, route), axis=1, keepdims=True)
    grad = (gate * grad_in.astype(F32)).astype(BF16)
    put_slots(z, send, 0, slot_picks(z, route), grad)


def fourth_kernel(
    z, section, place, out_zero, pair_one, tokens, own_route, other_route, o0, o1, o2, o3, r0, r1, r2, r3, back_out, back_grad,
    qkv, probs, attended, middle, router,
    pair, slab,
    mats, packed, small, sems,
):
    core = section[0]
    waits = fetch_weights(
        z, core == 0, place[0], (o0, o1, o2, o3), (r0, r1, r2, r3), mats, packed, sems, (4, 3, 0, 1, 2))
    route = jnp.where(core == 0, own_route[core], other_route[...])
    picks = slot_picks(z, route)
    token_out = get_slots(z, back_out, 0, picks)
    grad_token = get_slots(z, back_grad, 0, picks)
    pair[0] = out_zero[...]
    pair[1] = attend_back(
        z, pair_one[1].astype(F32), token_out, grad_token, tokens[core].astype(F32), route,
        waits, mats, packed, small, (qkv, probs, attended, middle, router), slab,
    )


def fetch_experts(z, mine, own_in, own_out, other_in, other_out, w_in, w_out, sems):
    def copies(source_in, source_out, c):
        at = pl.ds(c * z.chunk, z.chunk)
        return (
            pltpu.make_async_copy(source_in.at[:, at], w_in.at[c], sems.at[2 * c]),
            pltpu.make_async_copy(source_out.at[at], w_out.at[c], sems.at[2 * c + 1]),
        )

    def start(source_in, source_out):
        for c in range(z.hidden // z.chunk):
            for copy in copies(source_in, source_out, c):
                copy.start()

    @pl.when(mine)
    def _():
        start(own_in, own_out)

    @pl.when(jnp.logical_not(mine))
    def _():
        start(other_in, other_out)

    def wait(c):
        for copy in copies(own_in, own_out, c):
            copy.wait()

    return wait


def expert_scratch(z, sums):
    chunks = z.hidden // z.chunk
    return [
        pltpu.VMEM((chunks, z.width, z.chunk), BF16),
        pltpu.VMEM((chunks, z.chunk, z.width), BF16),
        pltpu.SemaphoreType.DMA((2 * chunks,)),
    ] + [pltpu.VMEM((z.expert_rows, z.width), F32)] * sums


def smooth(values):
    square = values * values
    bent = jnp.tanh(GELU_SCALE * values * (1.0 + GELU_CUBE * square))
    return (0.5 * values * (1.0 + bent), square, bent)


def smooth_slope(values, square, bent):
    inner = GELU_SCALE * (1.0 + 3.0 * GELU_CUBE * square)
    return 0.5 * (1.0 + bent) + 0.5 * values * (1.0 - bent * bent) * inner


def expert_forward_kernel(
    z, section, arrived, own_in, own_out, other_in, other_out, result, w_in, w_out, sems, produced
):
    wait = fetch_experts(
        z, section[0] == 0, own_in, own_out, other_in, other_out, w_in, w_out, sems
    )
    rows = rows_of_slots(z, arrived, 0)
    for c in range(z.hidden // z.chunk):
        wait(c)
        hidden = smooth(dot_nn(rows, w_in[c]))[0].astype(BF16)
        made = dot_nn(hidden, w_out[c])
        produced[...] = made if c == 0 else produced[...] + made
    slots_of_rows(z, result, 0, produced[...])


def expert_backward_kernel(
    z, layer, section, arrived, arrived_grad, own_in, own_out, other_in, other_out,
    result, stuff, w_in, w_out, sems, grad_sum, *produced
):
    wait = fetch_experts(
        z, section[0] == layer, own_in, own_out, other_in, other_out, w_in, w_out, sems
    )
    rows = rows_of_slots(z, arrived, 0)
    grads = rows_of_slots(z, arrived_grad, z.slot_width if produced else 0)
    stuff[:, 2 * z.hidden : 2 * z.hidden + z.width] = rows
    stuff[:, 2 * z.hidden + z.width : 2 * z.hidden + 2 * z.width] = grads
    for c in range(z.hidden // z.chunk):
        wait(c)
        before = dot_nn(rows, w_in[c])
        hidden, square, bent = smooth(before)
        hidden = hidden.astype(BF16)
        stuff[:, c * z.chunk : (c + 1) * z.chunk] = hidden
        if produced:
            made = dot_nn(hidden, w_out[c])
            produced[0][...] = made if c == 0 else produced[0][...] + made
        grad_pre = dot_nt(grads, w_out[c]) * smooth_slope(before, square, bent)
        grad_pre = grad_pre.astype(BF16)
        stuff[:, z.hidden + c * z.chunk : z.hidden + (c + 1) * z.chunk] = grad_pre
        made = dot_nt(grad_pre, w_in[c])
        grad_sum[...] = made if c == 0 else grad_sum[...] + made
    if produced:
        slots_of_rows(z, result, 0, produced[0][...])
    slots_of_rows(z, result, z.slot_width if produced else 0, grad_sum[...])


def expert_weights_kernel(
    z, section, own_zero, other_zero, own_one, other_one, grad_in, grad_out, held, turned, sems
):
    step = pl.program_id(0)

    @pl.when(step == 0)
    def _():
        def copies(own, other):
            return [
                pltpu.make_async_copy(
                    source, held.at[pl.ds(i * z.expert_rows, z.expert_rows)], sems.at[i]
                )
                for i, source in enumerate((own, other))
            ]

        @pl.when(section[0] == 0)
        def _():
            for copy in copies(own_zero, other_zero):
                copy.start()

        @pl.when(section[0] != 0)
        def _():
            for copy in copies(own_one, other_one):
                copy.start()

        for copy in copies(own_zero, other_zero):
            copy.wait()
        rows = held[:, 2 * z.hidden : 2 * z.hidden + z.width]
        turned[...] = jnp.transpose(rows.astype(F32)).astype(BF16)

    start = pl.multiple_of(step * z.chunk, z.chunk)
    grad_pre = held[:, pl.ds(z.hidden + start, z.chunk)]
    hidden = held[:, pl.ds(start, z.chunk)]
    grads = held[:, 2 * z.hidden + z.width : 2 * z.hidden + 2 * z.width]
    grad_in[...] = dot_nn(turned[...], grad_pre).astype(BF16)
    grad_out[...] = dot_tn(hidden, grads).astype(BF16)


def attention_weights_kernel(z, layer, section, place, own, other, *refs):
    outs, made = (refs[: z.shards], refs[z.shards])
    second = section[0] ^ layer

    def both(column):
        at = pl.ds(pl.multiple_of(column * z.width, 128), z.width)
        return jnp.concatenate([own[:, at], other[:, at]], axis=0)

    for i, (left, right) in enumerate(
        ((0, 1 + 2 * second), (4 * second, 2 + 3 * second))
    ):
        made[...] = dot_tn(both(left), both(right))
        for k in range(z.shards):
            start = pl.multiple_of((place[0] ^ k) * z.part, 16)
            outs[k][i * z.part : (i + 1) * z.part] = made[pl.ds(start, z.part)].astype(BF16)
    for i in range(z.width // z.rows):
        columns = slice(6 * z.width + i * z.small, 6 * z.width + (i + 1) * z.small)
        total = own[:, columns].astype(F32) + other[:, columns].astype(F32)
        made[i * z.rows : (i + 1) * z.rows, : z.small] = total
    for k in range(z.shards):
        for g in range(z.small_groups):
            start = pl.multiple_of((place[0] ^ k) * z.part + g * z.small_rows, 16)
            outs[k][2 * z.part :, g * z.small : (g + 1) * z.small] = made[
                pl.ds(start, z.small_rows), : z.small
            ].astype(BF16)


def pieces_sum_kernel(z, *refs):
    out = refs[-1]
    rows = out.shape[1] // 2
    for layer in range(2):
        pieces = refs[layer * z.shards : (layer + 1) * z.shards]
        total = sum(piece[...].astype(F32) for piece in pieces)
        for i in range(out.shape[0]):
            out[i, layer * rows : (layer + 1) * rows] = total[i * rows : (i + 1) * rows].astype(BF16)


def spread_sum_kernel(pieces, out):
    total = sum(pieces[i].astype(F32) for i in range(pieces.shape[0])).astype(BF16)
    for i in range(out.shape[0]):
        out[i] = total


def final_kernel(
    z, section, own, other, pair_zero, other_zero, pair_one, other_one,
    layer_out, input_grad, query, key, value, output, gain_one, gain_two, router, table, held, small,
):
    rows = own.shape[1] // 2

    def finish(layer, micros):
        for source, targets in ((own, (query, key)), (other, (value, output))):
            for i in range(own.shape[0]):
                part = source[i, layer * rows : (layer + 1) * rows]
                held[i * rows : (i + 1) * rows] = part.astype(F32)
            for i, target in enumerate(targets):
                target[0] = held[i * z.part : (i + 1) * z.part].astype(BF16)
            if source is own:
                for g in range(z.small_groups):
                    small[g * z.small_rows : (g + 1) * z.small_rows] = held[
                        2 * z.part :, g * z.small : (g + 1) * z.small
                    ]
        for i, pair in enumerate(micros):
            layer_out[0, i] = pair[0]
            input_grad[0, i] = pair[1]

    @pl.when(section[0] == 0)
    def _():
        finish(0, (pair_zero, other_zero))

    @pl.when(section[0] != 0)
    def _():
        finish(1, (other_one, pair_one))

    gains = gain_rows(z, small[...].astype(BF16))
    gain_one[...] = gains[0].astype(BF16)
    gain_two[...] = gains[1].astype(BF16)
    router[0] = small[:, : z.experts].astype(BF16)
    table[0] = small[: z.bucket_part, z.experts : z.gain_lane].astype(BF16)


def swap(value):
    return lax.ppermute(value, "section", [(0, 1), (1, 0)])


def cross(value, target):
    return lax.ppermute(value, "section", [(1 - target, target)])


def within(value, distance, layer):
    size = lax.axis_size("shard")
    pairs = [(layer * size + i, layer * size + (i ^ distance)) for i in range(size)]
    return lax.ppermute(value, ("section", "shard"), pairs)


def exchange(buffer, axes=("expert", "shard")):
    return lax.all_to_all(buffer, axes, split_axis=0, concat_axis=0, tiled=True)


def shards(
    tokens_in,
    cotangent,
    lengths,
    routes,
    w_query,
    w_key,
    w_value,
    w_output,
    gain_attn,
    gain_moe,
    w_router,
    bias_table,
    w_in,
    w_out,
):
    z = Sizes(tokens_in, w_query, w_router, bias_table, w_in, lax.axis_size("shard"))
    micro_count = tokens_in.shape[0]
    section = lax.axis_index("section").astype(I32)
    core = section.reshape(1)
    place = lax.axis_index("shard").astype(I32).reshape(1)

    def shape(*dims, kind=BF16):
        return jax.ShapeDtypeStruct(dims, kind)

    own_route = routes[0]
    sent_route = lax.dynamic_index_in_dim(own_route, 1 - section, 0, keepdims=False)
    piece = call(
        functools.partial(pack_kernel, z),
        shape(z.piece, z.width),
        (w_query, w_key, w_value, w_output, w_router, gain_attn, gain_moe, bias_table),
        [HBM] * 4 + [VMEM] * 4,
        [pltpu.VMEM((z.part, z.small), F32), pltpu.SemaphoreType.DMA((4,))],
        grant=8,
        cost=2,
    )

    def spread(piece, layer):
        return (piece, *[within(piece, distance, layer) for distance in range(1, z.shards)])

    def hand(pieces, layer):
        first = cross(pieces[0], 1 - layer)
        return (first, *[cross(after(member, first), 1 - layer) for member in pieces[1:]])

    def after(values, *first):
        values, unused = lax.optimization_barrier((values, first))
        return values

    piece, sent_route = lax.optimization_barrier((piece, sent_route))
    route_pair = (own_route, swap(sent_route))
    pieces = spread(piece, 0)
    given = hand(pieces, 0)
    weights_zero = (*pieces, *given)
    pieces_one = spread(after(piece, given[1]), 1)
    experts = (w_in[0, 0], w_out[0, 0])
    given_zero = tuple(cross(member, 1) for member in after(experts, given))

    buffer = shape(z.experts, 8, z.slot_width)
    wide_buffer = shape(z.experts, 8, 2 * z.slot_width)
    kept = (
        shape(z.rows, 3 * z.width),
        shape(z.heads // 2, z.rows, 2 * z.rows),
        shape(z.rows, z.width),
        shape(z.rows, z.width, kind=F32),
        shape(z.rows, z.small, kind=F32),
    )
    scratch = weight_scratch(z)
    rows_shape = shape(z.rows, z.width)
    slab_shape = shape(z.rows, z.slab)

    sent, *kept_zero = call(
        functools.partial(first_kernel, z),
        (buffer, *kept),
        (core, place, lengths, tokens_in, *route_pair, *weights_zero),
        [SMEM, SMEM, SMEM, VMEM, VMEM, VMEM] + [ANY] * 8,
        scratch,
        cost=6,
    )
    arrived_zero = exchange(sent)
    produced = call(
        functools.partial(expert_forward_kernel, z),
        buffer,
        (core, arrived_zero, *experts, *given_zero),
        [SMEM, VMEM, HBM, HBM, HBM, HBM],
        expert_scratch(z, 1),
        cost=6,
    )
    back_zero = exchange(produced)
    weights_one = (*pieces_one, *hand(after(pieces_one, produced), 1))
    given_one = tuple(cross(member, 0) for member in after(experts, produced))

    sent, out_zero, *kept_one = call(
        functools.partial(second_kernel, z),
        (wide_buffer, rows_shape, *kept),
        (core, place, lengths, cotangent, *route_pair, *weights_one, back_zero, *kept_zero[3:]),
        [SMEM, SMEM, SMEM, VMEM, VMEM, VMEM] + [ANY] * 8 + [VMEM] * 3,
        scratch,
        cost=7,
    )
    arrived_one = exchange(sent)
    stuff_shape = shape(z.expert_rows, 2 * z.hidden + 2 * z.width)
    result, stuff_one = call(
        lambda section, arrived, *rest: expert_backward_kernel(
            z, 1, section, arrived, arrived, *rest
        ),
        (wide_buffer, stuff_shape),
        (core, arrived_one, *experts, *given_one),
        [SMEM, VMEM, HBM, HBM, HBM, HBM],
        expert_scratch(z, 2),
        grant=28,
        cost=10,
    )
    back_one = exchange(result)

    pair_shape = shape(2, z.rows, z.width)
    sent, pair_one, slab_one = call(
        functools.partial(third_kernel, z),
        (buffer, pair_shape, slab_shape),
        (core, place, cotangent, *route_pair, *weights_one, back_one, out_zero, kept_zero[4], *kept_one),
        [SMEM, SMEM, VMEM, VMEM, VMEM] + [ANY] * 8 + [VMEM] * 8,
        scratch,
        cost=8,
    )
    arrived_grad = exchange(sent)

    count = lax.axis_size("expert")
    half_rows = 2 * z.part + z.small_rows

    def partial_sums(slab, layer):
        return call(
            functools.partial(attention_weights_kernel, z, layer),
            (shape(half_rows, z.width),) * z.shards,
            (core, place, slab, swap(slab)),
            [SMEM, SMEM, VMEM, VMEM],
            [pltpu.VMEM((z.width, z.width), F32)],
            cost=4,
        )

    def send_pieces(pieces):
        size = lax.axis_size("shard")
        got = [pieces[0]]
        for distance in range(1, z.shards):
            pairs = [(i, i ^ distance) for i in range(size)]
            got.append(lax.ppermute(pieces[distance], "shard", pairs))
        return tuple(got)

    sums_one = partial_sums(slab_one, 1)
    arrived_grad, *sums_one = lax.optimization_barrier((arrived_grad, *sums_one))
    got_one = send_pieces(sums_one)

    result, stuff_zero = call(
        functools.partial(expert_backward_kernel, z, 0),
        (buffer, stuff_shape),
        (core, arrived_zero, arrived_grad, *experts, *given_zero),
        [SMEM, VMEM, VMEM, HBM, HBM, HBM, HBM],
        expert_scratch(z, 1),
        grant=28,
        cost=8,
    )
    back_grad = after(exchange(result), got_one)
    pair_zero, slab_zero = call(
        functools.partial(fourth_kernel, z),
        (pair_shape, slab_shape),
        (
            core, place, out_zero, pair_one, tokens_in, *route_pair, *weights_zero,
            back_zero, back_grad, *kept_zero,
        ),
        [SMEM, SMEM, VMEM, VMEM, VMEM, VMEM, VMEM] + [ANY] * 8 + [VMEM] * 7,
        scratch,
        cost=8,
    )

    got_zero = send_pieces(partial_sums(slab_zero, 0))
    part = shape(count, 2 * half_rows // count, z.width)
    summed = call(
        functools.partial(pieces_sum_kernel, z), part, (*got_zero, *got_one), [VMEM] * 8, cost=2
    )
    summed = call(spread_sum_kernel, part, (exchange(summed, "expert"),), [VMEM], cost=1)
    summed = exchange(summed, "expert")
    summed_other = swap(summed)

    chunks = z.hidden // z.chunk
    grad_w_in, grad_w_out = call(
        functools.partial(expert_weights_kernel, z),
        (shape(z.width, z.hidden), shape(z.hidden, z.width)),
        (core, stuff_zero, cross(stuff_zero, 0), stuff_one, cross(stuff_one, 1)),
        [SMEM, HBM, HBM, HBM, HBM],
        [
            pltpu.VMEM((2 * z.expert_rows, stuff_shape.shape[1]), BF16),
            pltpu.VMEM((z.width, 2 * z.expert_rows), BF16),
            pltpu.SemaphoreType.DMA((2,)),
        ],
        grant=28,
        cost=9,
        grid=(chunks,),
        out_specs=(
            pl.BlockSpec((z.width, z.chunk), lambda i: (0, i)),
            pl.BlockSpec((z.chunk, z.width), lambda i: (i, 0)),
        ),
    )

    matrix = shape(1, z.part, z.width)
    finals = call(
        functools.partial(final_kernel, z),
        (
            *[shape(1, micro_count, z.rows, z.width)] * 2,
            *[matrix] * 4,
            *[shape(1, z.part)] * 2,
            shape(1, z.part, z.experts),
            shape(1, z.bucket_part, z.heads),
        ),
        (
            core, summed, summed_other,
            pair_zero, cross(pair_zero, 0), pair_one, cross(pair_one, 1),
        ),
        [SMEM] + [VMEM] * 6,
        [pltpu.VMEM((half_rows, z.width), F32), pltpu.VMEM((z.part, z.small), F32)],
        cost=3,
    )
    return (*finals, grad_w_in[None, None], grad_w_out[None, None])


def solution(mesh):
    both = ("expert", "shard")
    plain = P("section", "shard", None)
    gains = P("section", "shard")
    blocks = P("section", None, both, None)
    experts = P("section", both, None, None)
    tokens = P(None, both, None)
    attention = (plain, plain, plain, plain, gains, gains, plain, plain, experts, experts)
    return jax.shard_map(
        shards,
        mesh=mesh,
        in_specs=(tokens, tokens, tokens, blocks, *attention),
        out_specs=(blocks, blocks, *attention),
        check_vma=False,
    )
```

```python
import functools

import jax
import jax.numpy as jnp
from jax import lax
from jax.experimental import pallas as pl
from jax.experimental.pallas import tpu as pltpu
from jax.sharding import PartitionSpec as P

EPSILON = 1e-06
BOUNDS = (8, 12, 16, 23, 32, 46, 64, 91)
MASKED = -1e30
F32 = jnp.float32
BF16 = jnp.bfloat16
I32 = jnp.int32
GELU_SCALE = 0.7978845608028654
GELU_CUBE = 0.044715
SMEM = pl.BlockSpec(memory_space=pltpu.SMEM)
VMEM = pl.BlockSpec(memory_space=pltpu.VMEM)
LOOSE = pl.BlockSpec(memory_space=pltpu.VMEM)
HBM = pl.BlockSpec(memory_space=pltpu.HBM)
ANY = pl.BlockSpec(memory_space=pl.ANY)


def dot_nn(a, b):
    return jnp.dot(a, b, preferred_element_type=F32)


def dot_nt(a, b):
    return lax.dot_general(a, b, (((1,), (1,)), ((), ())), preferred_element_type=F32)


def dot_tn(a, b):
    return lax.dot_general(a, b, (((0,), (0,)), ((), ())), preferred_element_type=F32)


def iota(shape, dimension):
    return lax.broadcasted_iota(I32, shape, dimension)


def call(body, outs, ins, specs, scratch=(), grant=24, cost=5, **more):
    ins = [
        value if spec is SMEM or spec is LOOSE else pltpu.with_memory_space_constraint(value, pltpu.HBM)
        for value, spec in zip(ins, specs)
    ]
    single = not isinstance(outs, tuple)
    outs = tuple(pltpu.HBM(out.shape, out.dtype) for out in ((outs,) if single else outs))
    more.setdefault("out_specs", (VMEM,) * len(outs))
    made = pl.pallas_call(
        body,
        out_shape=outs,
        in_specs=specs,
        scratch_shapes=scratch,
        compiler_params=pltpu.CompilerParams(vmem_limit_bytes=grant * 1024 * 1024),
        cost_estimate=pl.CostEstimate(
            flops=int(cost * 5e8), bytes_accessed=int(cost * 3e6), transcendentals=0
        ),
        **more,
    )(*ins)
    return made[0] if single else made


def bucket_of(relative):
    distance = jnp.abs(relative)
    bucket = jnp.zeros_like(relative)
    for lowest in tuple(range(1, 8)) + BOUNDS:
        bucket = bucket + (distance >= lowest).astype(I32)
    return bucket + 16 * (relative > 0).astype(I32)


class Sizes:
    def __init__(self, tokens_in, w_query, w_router, bias_table, w_in, shards):
        self.rows, self.width = tokens_in.shape[1:]
        self.part = w_query.shape[1]
        self.shards = shards
        self.experts = w_router.shape[2]
        self.bucket_part, self.heads = bias_table.shape[1:]
        self.buckets = self.bucket_part * shards
        self.hidden = w_in.shape[3]
        self.chunk = self.hidden // 6
        self.capacity = max(
            2, (3 * self.rows + 2 * self.experts - 1) // (2 * self.experts)
        )
        self.full, rest = divmod(self.capacity, 8)
        self.rest = next((power for power in (0, 1, 2, 4) if power >= rest), None)
        if self.rest is None:
            self.full, self.rest = (self.full + 1, 0)
        self.cuts = 8 // self.rest if self.rest else 0
        self.cut = self.width // self.cuts if self.rest else 0
        self.slot_width = self.full * self.width + self.cut
        self.slot_rows = self.experts * 8
        self.expert_rows = self.slot_rows * self.full + self.experts * self.rest
        self.small = -(-(self.experts + self.heads + 2) // 128) * 128
        self.small_groups = self.width // self.small
        self.small_rows = self.part // self.small_groups
        self.gain_lane = self.experts + self.heads
        self.piece = 4 * self.part + self.small_rows
        self.half_rows = 2 * self.part + self.small_rows
        self.slab = 6 * self.width + self.small * self.width // self.rows


def slot_picks(z, route):
    onehot = (route == iota((z.rows, z.experts), 1)).astype(F32)
    lower = (iota((z.rows, z.rows), 0) >= iota((z.rows, z.rows), 1)).astype(F32).astype(BF16)
    running = dot_nn(lower, onehot.astype(BF16))
    place = jnp.sum(running * onehot, axis=1, keepdims=True).astype(I32) - 1
    slots = iota((z.rows, z.slot_rows), 1)

    def pick(first, wide, shift):
        inside = (place >= first) & (place < first + wide)
        target = jnp.where(inside, route * 8 + place - first + shift, -1)
        return (slots == target).astype(F32).astype(BF16)

    picks = [pick(8 * i, 8, 0) for i in range(z.full)]
    return picks + [pick(8 * z.full, z.rest, z.rest * i) for i in range(z.cuts)]


def cut_sum(z, picks, values):
    return sum(dot_tn(pick, values[:, i * z.cut : (i + 1) * z.cut]) for i, pick in enumerate(picks))


def put_slots(z, ref, offset, picks, values):
    for i in range(z.full):
        block = dot_tn(picks[i], values)
        ref[:, :, offset : offset + z.width] = block.reshape(z.experts, 8, z.width).astype(BF16)
        offset += z.width
    if z.rest:
        block = cut_sum(z, picks[z.full :], values)
        ref[:, :, offset : offset + z.cut] = block.reshape(z.experts, 8, z.cut).astype(BF16)


def read_slots(z, ref, offset, wide):
    block = ref[:, :, offset : offset + wide].astype(F32)
    return block.reshape(z.slot_rows, wide).astype(BF16)


def get_slots(z, ref, offset, picks):
    total = 0.0
    for i in range(z.full):
        total += dot_nn(picks[i], read_slots(z, ref, offset, z.width))
        offset += z.width
    if z.rest:
        block = read_slots(z, ref, offset, z.cut)
        total += jnp.concatenate([dot_nn(pick, block) for pick in picks[z.full :]], axis=1)
    return total


def extra_picks(z):
    shape = (z.experts * z.rest, z.slot_rows)
    rows, slots = (iota(shape, 0), iota(shape, 1))
    first = (rows // z.rest) * 8 + rows % z.rest
    return [(slots == first + z.rest * i).astype(F32).astype(BF16) for i in range(z.cuts)]


def rows_of_slots(z, ref, offset):
    parts = []
    for i in range(z.full):
        parts.append(read_slots(z, ref, offset, z.width))
        offset += z.width
    if z.rest:
        block = read_slots(z, ref, offset, z.cut)
        pieces = [dot_nn(pick, block) for pick in extra_picks(z)]
        parts.append(jnp.concatenate(pieces, axis=1).astype(BF16))
    return jnp.concatenate(parts, axis=0) if len(parts) > 1 else parts[0]


def slots_of_rows(z, ref, offset, rows):
    for i in range(z.full):
        block = rows[i * z.slot_rows : (i + 1) * z.slot_rows]
        ref[:, :, offset : offset + z.width] = block.reshape(z.experts, 8, z.width).astype(BF16)
        offset += z.width
    if z.rest:
        block = cut_sum(z, extra_picks(z), rows[z.full * z.slot_rows :].astype(BF16))
        ref[:, :, offset : offset + z.cut] = block.reshape(z.experts, 8, z.cut).astype(BF16)


def fetch_weights(z, mine, place, own, other, mats, packed, sems, order=(4, 0, 1, 2, 3)):
    def copy(pieces, i, k):
        shard = place ^ k
        count = z.small_rows if i == 4 else z.part
        start = i * z.part
        source = pieces[k]
        target = pl.ds(pl.multiple_of(shard * count, 16), count)
        held = packed.at[target] if i == 4 else mats.at[i, target]
        return pltpu.make_async_copy(source.at[pl.ds(start, count)], held, sems.at[i, k])

    def start(pieces):
        for i in order:
            for k in range(z.shards):
                copy(pieces, i, k).start()

    def wait(i):
        for k in range(z.shards):
            copy(own, i, k).wait()

    @pl.when(mine)
    def _():
        start(own)

    @pl.when(jnp.logical_not(mine))
    def _():
        start(other)

    return [functools.partial(wait, i) for i in range(5)]


def fetch_halves(z, core, own, other, mats, packed, sems, order=(4, 0, 1, 2, 3)):
    def copy(source, i, k):
        count = z.small_rows if i == 4 else z.part
        start = k * z.half_rows + (i if i < 2 else i - 2) * z.part
        target = pl.ds(k * count, count)
        held = packed.at[target] if i == 4 else mats.at[i, target]
        return pltpu.make_async_copy(source.at[pl.ds(start, count)], held, sems.at[i, k])

    def start(first, second):
        for i in order:
            for k in range(z.shards):
                copy(first if i < 2 else second, i, k).start()

    def wait(i):
        for k in range(z.shards):
            copy(own, i, k).wait()

    @pl.when(core == 0)
    def _():
        start(own, other)

    @pl.when(core != 0)
    def _():
        start(other, own)

    return [functools.partial(wait, i) for i in range(5)]


def weight_scratch(z):
    return [
        pltpu.VMEM((4, z.width, z.width), BF16),
        pltpu.VMEM((z.shards * z.small_rows, z.width), BF16),
        pltpu.VMEM((z.width, z.small), BF16),
        pltpu.SemaphoreType.DMA((5, z.shards)),
    ]


def unpack_small(z, packed, small):
    for j in range(z.shards):
        for g in range(z.small_groups):
            row = j * z.part + g * z.small_rows
            small[row : row + z.small_rows, :] = packed[
                j * z.small_rows : (j + 1) * z.small_rows, g * z.small : (g + 1) * z.small
            ]


def bucket_rows(z):
    rows, buckets = (iota((z.width, z.buckets), 0), iota((z.width, z.buckets), 1))
    held = (buckets // z.bucket_part) * z.part + buckets % z.bucket_part
    return (rows == held).astype(F32).astype(BF16)


def bucket_lanes(z):
    shape = (z.buckets, 2 * z.rows)
    return (bucket_of(iota(shape, 1) - z.rows) == iota(shape, 0)).astype(F32).astype(BF16)


def gain_rows(z, small):
    rows, lanes = (iota((8, z.small), 0), iota((8, z.small), 1))
    pick = ((lanes == z.gain_lane + rows) & (rows < 2)).astype(F32).astype(BF16)
    made = dot_nt(pick, small)
    return (made[0:1], made[1:2])


def unit_rows(values):
    inverse = lax.rsqrt(jnp.mean(values * values, axis=-1, keepdims=True) + EPSILON)
    return (values * inverse, inverse)


def pair_masks(z):
    lanes = iota((z.rows, 128), 1)
    first = (lanes < 64).astype(F32).astype(BF16)
    return (first, (lanes >= 64).astype(F32).astype(BF16))


def double(values, masks):
    return jnp.concatenate([values * masks[0], values * masks[1]], axis=0)


def attend(z, inputs, waits, mats, packed, small, lengths, section, qkv_ref, probs_ref, attended_ref):
    waits[4]()
    unpack_small(z, packed, small)
    small_full = small[...]
    gain_one, gain_two = gain_rows(z, small_full)
    normed_one = (unit_rows(inputs)[0] * gain_one).astype(BF16)
    for i in range(3):
        waits[i]()
        qkv_ref[:, i * z.width : (i + 1) * z.width] = dot_nn(normed_one, mats[i]).astype(BF16)

    table = dot_tn(bucket_rows(z), small_full).astype(BF16)
    bias = dot_tn(table, bucket_lanes(z))[z.experts : z.experts + z.heads]

    rows, lanes = (iota((z.rows, z.rows), 0), iota((z.rows, z.rows), 1))
    segment_q, segment_k = (jnp.zeros_like(rows), jnp.zeros_like(rows))
    end = jnp.int32(0)
    for i in range(lengths.shape[2]):
        end = end + lengths[section, 0, i]
        segment_q += (rows >= end).astype(I32)
        segment_k += (lanes >= end).astype(I32)
    visible = segment_q == segment_k

    masks = pair_masks(z)
    scale = 64 ** (-0.5)
    for p in range(z.heads // 2):
        at = slice(p * 128, (p + 1) * 128)
        query = qkv_ref[:, p * 128 : (p + 1) * 128]
        key = qkv_ref[:, z.width + p * 128 : z.width + (p + 1) * 128]
        value = qkv_ref[:, 2 * z.width + p * 128 : 2 * z.width + (p + 1) * 128]
        scores = dot_nt(query, double(key, masks)) * scale
        halves = []
        for i in range(2):
            spread = jnp.broadcast_to(bias[2 * p + i : 2 * p + i + 1], (z.rows, 2 * z.rows))
            spread = pltpu.roll(spread, z.rows, 1, stride=1, stride_axis=0)[:, : z.rows]
            part = scores[:, i * z.rows : (i + 1) * z.rows] + spread
            part = jnp.where(visible, part, MASKED)
            part = jnp.exp(part - jnp.max(part, axis=-1, keepdims=True))
            halves.append(part / jnp.sum(part, axis=-1, keepdims=True))
        probs = jnp.concatenate(halves, axis=1).astype(BF16)
        probs_ref[p] = probs
        attended_ref[:, at] = dot_nn(probs, double(value, masks)).astype(BF16)

    waits[3]()
    middle = inputs + dot_nn(attended_ref[...], mats[3])
    normed_two = (unit_rows(middle)[0] * gain_two).astype(BF16)
    logits = dot_nn(normed_two, small_full)
    logits = jnp.where(iota((z.rows, z.small), 1) < z.experts, logits, MASKED)
    logits = jnp.exp(logits - jnp.max(logits, axis=-1, keepdims=True))
    router = logits / jnp.sum(logits, axis=-1, keepdims=True)
    return (middle, normed_two, router)


def chosen(z, route):
    return (route == iota((z.rows, z.small), 1)).astype(F32)


def attend_back(
    z, grad_out, token_out, grad_token, inputs, route, waits, mats, packed, small, kept, slab_ref
):
    qkv_ref, probs_ref, attended_ref, middle_ref, router_ref = kept
    waits[4]()
    unpack_small(z, packed, small)
    small_full = small[...]
    gain_one, gain_two = gain_rows(z, small_full)
    onehot = chosen(z, route)
    router = router_ref[...]
    gate = jnp.sum(router * onehot, axis=1, keepdims=True)
    grad_gate = jnp.sum(grad_out * token_out, axis=1, keepdims=True)
    grad_logits = (grad_gate * gate * (onehot - router)).astype(BF16)
    unit_two, inverse_two = unit_rows(middle_ref[...])
    grad_small = dot_tn((unit_two * gain_two).astype(BF16), grad_logits)
    grad_normed = grad_token + dot_nt(grad_logits, small_full)
    gain_two_grad = jnp.sum(grad_normed * unit_two, axis=0, keepdims=True)
    grad_unit = grad_normed * gain_two
    grad_unit -= unit_two * jnp.mean(grad_unit * unit_two, axis=1, keepdims=True)
    grad_middle = grad_out + inverse_two * grad_unit
    grad_branch = grad_middle.astype(BF16)
    slab_ref[:, 4 * z.width : 5 * z.width] = attended_ref[...]
    slab_ref[:, 5 * z.width : 6 * z.width] = grad_branch
    waits[3]()
    grad_attended = dot_nt(grad_branch, mats[3]).astype(BF16)

    masks = pair_masks(z)
    scale = 64 ** (-0.5)
    relative = []
    turn = iota((z.rows, z.rows), 0) + iota((z.rows, z.rows), 1) == z.rows - 1
    turn = turn.astype(F32).astype(BF16)
    for p in range(z.heads // 2):
        at = slice(p * 128, (p + 1) * 128)
        query = qkv_ref[:, p * 128 : (p + 1) * 128]
        keys = double(qkv_ref[:, z.width + p * 128 : z.width + (p + 1) * 128], masks)
        values = double(qkv_ref[:, 2 * z.width + p * 128 : 2 * z.width + (p + 1) * 128], masks)
        grad_heads = grad_attended[:, at]
        probs_low = probs_ref[p]
        probs = probs_low.astype(F32)
        grad_probs = dot_nt(grad_heads, values)
        halves = []
        for i in range(2):
            part = slice(i * z.rows, (i + 1) * z.rows)
            product = grad_probs[:, part] * probs[:, part]
            dots = jnp.sum(product, axis=-1, keepdims=True)
            grads = (product - probs[:, part] * dots).astype(BF16)
            halves.append(grads)
        grad_scores = jnp.concatenate(halves, axis=1)
        turned = dot_nn(turn, grad_scores)
        for i in range(2):
            wide = [turned[:, i * z.rows : (i + 1) * z.rows], jnp.zeros((z.rows, z.rows), F32)]
            wide = pltpu.roll(jnp.concatenate(wide, axis=1), 1, 1, stride=1, stride_axis=0)
            relative.append(jnp.sum(wide, axis=0, keepdims=True))
        start = z.width + p * 128
        slab_ref[:, start : start + 128] = (dot_nn(grad_scores, keys) * scale).astype(BF16)
        made = dot_tn(grad_scores, query) * scale
        mask = masks[0].astype(F32)
        made = made[: z.rows] * mask + made[z.rows :] * (1.0 - mask)
        slab_ref[:, start + z.width : start + z.width + 128] = made.astype(BF16)
        made = dot_tn(probs_low, grad_heads)
        made = made[: z.rows] * mask + made[z.rows :] * (1.0 - mask)
        slab_ref[:, start + 2 * z.width : start + 2 * z.width + 128] = made.astype(BF16)

    unit_one, inverse_one = unit_rows(inputs)
    slab_ref[:, : z.width] = (unit_one * gain_one).astype(BF16)
    grad_normed = 0.0
    for i in range(3):
        waits[i]()
        grad_normed += dot_nt(slab_ref[:, (i + 1) * z.width : (i + 2) * z.width], mats[i])
    gain_one_grad = jnp.sum(grad_normed * unit_one, axis=0, keepdims=True)
    grad_unit = grad_normed * gain_one
    grad_unit -= unit_one * jnp.mean(grad_unit * unit_one, axis=1, keepdims=True)
    grad_in = (grad_middle + inverse_one * grad_unit).astype(BF16)

    relative += [jnp.zeros((1, 2 * z.rows), F32)] * (-z.heads % 8)
    relative = jnp.concatenate(relative, axis=0)
    lanes_of = bucket_lanes(z)
    high = relative.astype(BF16)
    table = dot_nt(lanes_of, high) + dot_nt(lanes_of, (relative - high.astype(F32)).astype(BF16))
    count = relative.shape[0]
    places = iota((count, z.small), 1) == iota((count, z.small), 0) + z.experts
    places = places & (iota((count, z.small), 0) < z.heads)
    table = dot_nn(table.astype(BF16), places.astype(F32).astype(BF16)).astype(BF16)
    grad_small += dot_nn(bucket_rows(z), table)
    gains = jnp.concatenate([gain_one_grad, gain_two_grad, jnp.zeros((6, z.width), F32)], axis=0)
    rows, lanes = (iota((8, z.small), 0), iota((8, z.small), 1))
    pick = ((lanes == z.gain_lane + rows) & (rows < 2)).astype(F32).astype(BF16)
    grad_small += dot_tn(gains.astype(BF16), pick)
    for i in range(z.width // z.rows):
        start = 6 * z.width + i * z.small
        slab_ref[:, start : start + z.small] = grad_small[i * z.rows : (i + 1) * z.rows].astype(BF16)
    return grad_in


def pack_kernel(z, query, key, value, output, router, gain_one, gain_two, table, piece, small, sems):
    copies = [
        pltpu.make_async_copy(source.at[0], piece.at[pl.ds(i * z.part, z.part)], sems.at[i])
        for i, source in enumerate((query, key, value, output))
    ]
    for copy in copies:
        copy.start()
    gains = [gain_one[...].astype(F32), gain_two[...].astype(F32), jnp.zeros((6, z.part), F32)]
    rows, lanes = (iota((8, z.small), 0), iota((8, z.small), 1))
    pick = ((lanes == z.gain_lane + rows) & (rows < 2)).astype(F32).astype(BF16)
    small[...] = dot_tn(jnp.concatenate(gains, axis=0).astype(BF16), pick)
    small[:, : z.experts] = router[0].astype(F32)
    small[: z.bucket_part, z.experts : z.gain_lane] = table[0].astype(F32)
    for g in range(z.small_groups):
        piece[4 * z.part :, g * z.small : (g + 1) * z.small] = small[
            g * z.small_rows : (g + 1) * z.small_rows
        ].astype(BF16)
    for copy in copies:
        copy.wait()


def first_kernel(
    z, section, place, lengths, tokens, own_route, other_route, o0, o1, o2, o3, r0, r1, r2, r3,
    send, qkv, probs, attended, middle_ref, router_ref,
    mats, packed, small, sems,
):
    core = section[0]
    waits = fetch_weights(
        z, core == 0, place[0], (o0, o1, o2, o3), (r0, r1, r2, r3), mats, packed, sems)
    inputs = tokens[core].astype(F32)
    middle, normed_two, router = attend(
        z, inputs, waits, mats, packed, small, lengths, core, qkv, probs, attended
    )
    middle_ref[...] = middle
    router_ref[...] = router
    route = jnp.where(core == 0, own_route[core], other_route[...])
    put_slots(z, send, 0, slot_picks(z, route), normed_two)


def second_kernel(
    z, section, lengths, cotangent, own_route, other_route, own, other, back, middle_zero, router_zero,
    send, out_zero, qkv, probs, attended, middle_ref, router_ref,
    mats, packed, small, sems,
):
    core = section[0]
    waits = fetch_halves(
        z, core, own, other, mats, packed, sems)
    route = jnp.where(core == 0, own_route[core], other_route[...])
    gate = jnp.sum(router_zero[...] * chosen(z, route), axis=1, keepdims=True)
    token_out = get_slots(z, back, 0, slot_picks(z, route))
    layer_out = (middle_zero[...] + gate * token_out).astype(BF16)
    out_zero[...] = layer_out
    middle, normed_two, router = attend(
        z, layer_out.astype(F32), waits, mats, packed, small, lengths, core, qkv, probs, attended
    )
    middle_ref[...] = middle
    router_ref[...] = router
    route = jnp.where(core == 1, own_route[core], other_route[...])
    picks = slot_picks(z, route)
    put_slots(z, send, 0, picks, normed_two)
    gate = jnp.sum(router * chosen(z, route), axis=1, keepdims=True)
    grad = (gate * cotangent[core].astype(F32)).astype(BF16)
    put_slots(z, send, z.slot_width, picks, grad)


def third_kernel(
    z, section, cotangent, own_route, other_route, own, other, back, inputs, router_zero,
    qkv, probs, attended, middle, router,
    send, pair, slab,
    mats, packed, small, sems,
):
    core = section[0]
    waits = fetch_halves(
        z, core, own, other, mats, packed, sems, (4, 3, 0, 1, 2))
    route = jnp.where(core == 1, own_route[core], other_route[...])
    picks = slot_picks(z, route)
    token_out = get_slots(z, back, 0, picks)
    grad_token = get_slots(z, back, z.slot_width, picks)
    gate = jnp.sum(router[...] * chosen(z, route), axis=1, keepdims=True)
    pair[0] = (middle[...] + gate * token_out).astype(BF16)
    grad_in = attend_back(
        z, cotangent[core].astype(F32), token_out, grad_token, inputs[...].astype(F32), route,
        waits, mats, packed, small, (qkv, probs, attended, middle, router), slab,
    )
    pair[1] = grad_in
    route = jnp.where(core == 0, own_route[core], other_route[...])
    gate = jnp.sum(router_zero[...] * chosen(z, route), axis=1, keepdims=True)
    grad = (gate * grad_in.astype(F32)).astype(BF16)
    put_slots(z, send, 0, slot_picks(z, route), grad)


def fourth_kernel(
    z, section, place, out_zero, pair_one, tokens, own_route, other_route, o0, o1, o2, o3, r0, r1, r2, r3, back_out, back_grad,
    qkv, probs, attended, middle, router,
    pair, slab,
    mats, packed, small, sems,
):
    core = section[0]
    waits = fetch_weights(
        z, core == 0, place[0], (o0, o1, o2, o3), (r0, r1, r2, r3), mats, packed, sems, (4, 3, 0, 1, 2))
    route = jnp.where(core == 0, own_route[core], other_route[...])
    picks = slot_picks(z, route)
    token_out = get_slots(z, back_out, 0, picks)
    grad_token = get_slots(z, back_grad, 0, picks)
    pair[0] = out_zero[...]
    pair[1] = attend_back(
        z, pair_one[1].astype(F32), token_out, grad_token, tokens[core].astype(F32), route,
        waits, mats, packed, small, (qkv, probs, attended, middle, router), slab,
    )


def fetch_experts(z, mine, own_in, own_out, other_in, other_out, w_in, w_out, sems):
    def copies(source_in, source_out, c):
        at = pl.ds(c * z.chunk, z.chunk)
        return (
            pltpu.make_async_copy(source_in.at[:, at], w_in.at[c], sems.at[2 * c]),
            pltpu.make_async_copy(source_out.at[at], w_out.at[c], sems.at[2 * c + 1]),
        )

    def start(source_in, source_out):
        for c in range(z.hidden // z.chunk):
            for copy in copies(source_in, source_out, c):
                copy.start()

    @pl.when(mine)
    def _():
        start(own_in, own_out)

    @pl.when(jnp.logical_not(mine))
    def _():
        start(other_in, other_out)

    def wait(c):
        for copy in copies(own_in, own_out, c):
            copy.wait()

    return wait


def expert_scratch(z, sums):
    chunks = z.hidden // z.chunk
    return [
        pltpu.VMEM((chunks, z.width, z.chunk), BF16),
        pltpu.VMEM((chunks, z.chunk, z.width), BF16),
        pltpu.SemaphoreType.DMA((2 * chunks,)),
    ] + [pltpu.VMEM((z.expert_rows, z.width), F32)] * sums


def smooth(values):
    square = values * values
    bent = jnp.tanh(GELU_SCALE * values * (1.0 + GELU_CUBE * square))
    return (0.5 * values * (1.0 + bent), square, bent)


def smooth_slope(values, square, bent):
    inner = GELU_SCALE * (1.0 + 3.0 * GELU_CUBE * square)
    return 0.5 * (1.0 + bent) + 0.5 * values * (1.0 - bent * bent) * inner


def expert_forward_kernel(
    z, section, arrived, own_in, own_out, other_in, other_out, result, w_in, w_out, sems, produced
):
    wait = fetch_experts(
        z, section[0] == 0, own_in, own_out, other_in, other_out, w_in, w_out, sems
    )
    rows = rows_of_slots(z, arrived, 0)
    for c in range(z.hidden // z.chunk):
        wait(c)
        hidden = smooth(dot_nn(rows, w_in[c]))[0].astype(BF16)
        made = dot_nn(hidden, w_out[c])
        produced[...] = made if c == 0 else produced[...] + made
    slots_of_rows(z, result, 0, produced[...])


def expert_backward_kernel(
    z, layer, section, arrived, arrived_grad, own_in, own_out, other_in, other_out,
    result, stuff, w_in, w_out, sems, grad_sum, *produced
):
    wait = fetch_experts(
        z, section[0] == layer, own_in, own_out, other_in, other_out, w_in, w_out, sems
    )
    rows = rows_of_slots(z, arrived, 0)
    grads = rows_of_slots(z, arrived_grad, z.slot_width if produced else 0)
    stuff[:, 2 * z.hidden : 2 * z.hidden + z.width] = rows
    stuff[:, 2 * z.hidden + z.width : 2 * z.hidden + 2 * z.width] = grads
    for c in range(z.hidden // z.chunk):
        wait(c)
        before = dot_nn(rows, w_in[c])
        hidden, square, bent = smooth(before)
        hidden = hidden.astype(BF16)
        stuff[:, c * z.chunk : (c + 1) * z.chunk] = hidden
        if produced:
            made = dot_nn(hidden, w_out[c])
            produced[0][...] = made if c == 0 else produced[0][...] + made
        grad_pre = dot_nt(grads, w_out[c]) * smooth_slope(before, square, bent)
        grad_pre = grad_pre.astype(BF16)
        stuff[:, z.hidden + c * z.chunk : z.hidden + (c + 1) * z.chunk] = grad_pre
        made = dot_nt(grad_pre, w_in[c])
        grad_sum[...] = made if c == 0 else grad_sum[...] + made
    if produced:
        slots_of_rows(z, result, 0, produced[0][...])
    slots_of_rows(z, result, z.slot_width if produced else 0, grad_sum[...])


def expert_weights_kernel(
    z, section, own_zero, other_zero, own_one, other_one, grad_in, grad_out, held, turned, sems
):
    step = pl.program_id(0)

    @pl.when(step == 0)
    def _():
        def copies(own, other):
            return [
                pltpu.make_async_copy(
                    source, held.at[pl.ds(i * z.expert_rows, z.expert_rows)], sems.at[i]
                )
                for i, source in enumerate((own, other))
            ]

        @pl.when(section[0] == 0)
        def _():
            for copy in copies(own_zero, other_zero):
                copy.start()

        @pl.when(section[0] != 0)
        def _():
            for copy in copies(own_one, other_one):
                copy.start()

        for copy in copies(own_zero, other_zero):
            copy.wait()
        rows = held[:, 2 * z.hidden : 2 * z.hidden + z.width]
        turned[...] = jnp.transpose(rows.astype(F32)).astype(BF16)

    start = pl.multiple_of(step * z.chunk, z.chunk)
    grad_pre = held[:, pl.ds(z.hidden + start, z.chunk)]
    hidden = held[:, pl.ds(start, z.chunk)]
    grads = held[:, 2 * z.hidden + z.width : 2 * z.hidden + 2 * z.width]
    grad_in[...] = dot_nn(turned[...], grad_pre).astype(BF16)
    grad_out[...] = dot_tn(hidden, grads).astype(BF16)


def attention_weights_kernel(z, layer, section, place, own, other, *refs):
    outs, made = (refs[: z.shards], refs[z.shards])
    second = section[0] ^ layer

    def both(column):
        at = pl.ds(pl.multiple_of(column * z.width, 128), z.width)
        return jnp.concatenate([own[:, at], other[:, at]], axis=0)

    for i, (left, right) in enumerate(
        ((0, 1 + 2 * second), (4 * second, 2 + 3 * second))
    ):
        made[...] = dot_tn(both(left), both(right))
        for k in range(z.shards):
            start = pl.multiple_of((place[0] ^ k) * z.part, 16)
            outs[k][i * z.part : (i + 1) * z.part] = made[pl.ds(start, z.part)].astype(BF16)
    for i in range(z.width // z.rows):
        columns = slice(6 * z.width + i * z.small, 6 * z.width + (i + 1) * z.small)
        total = own[:, columns].astype(F32) + other[:, columns].astype(F32)
        made[i * z.rows : (i + 1) * z.rows, : z.small] = total
    for k in range(z.shards):
        for g in range(z.small_groups):
            start = pl.multiple_of((place[0] ^ k) * z.part + g * z.small_rows, 16)
            outs[k][2 * z.part :, g * z.small : (g + 1) * z.small] = made[
                pl.ds(start, z.small_rows), : z.small
            ].astype(BF16)


def pieces_sum_kernel(*refs):
    out = refs[-1]
    rows = out.shape[1]
    total = sum(piece[...].astype(F32) for piece in refs[:-1])
    for i in range(out.shape[0]):
        out[i] = total[i * rows : (i + 1) * rows].astype(BF16)


def spread_sum_kernel(pieces, out):
    total = sum(pieces[i].astype(F32) for i in range(pieces.shape[0])).astype(BF16)
    for i in range(out.shape[0]):
        out[i] = total


def final_kernel(
    z, section, own_zero, got_zero, own_one, got_one, pair_zero, other_zero, pair_one, other_one,
    layer_out, input_grad, query, key, value, output, gain_one, gain_two, router, table, held, small,
):
    rows = own_zero.shape[1]

    def finish(own, other, micros):
        for source, targets in ((own, (query, key)), (other, (value, output))):
            for i in range(own.shape[0]):
                held[i * rows : (i + 1) * rows] = source[i].astype(F32)
            for i, target in enumerate(targets):
                target[0] = held[i * z.part : (i + 1) * z.part].astype(BF16)
            if source is own:
                for g in range(z.small_groups):
                    small[g * z.small_rows : (g + 1) * z.small_rows] = held[
                        2 * z.part :, g * z.small : (g + 1) * z.small
                    ]
        for i, pair in enumerate(micros):
            layer_out[0, i] = pair[0]
            input_grad[0, i] = pair[1]

    @pl.when(section[0] == 0)
    def _():
        finish(own_zero, got_zero, (pair_zero, other_zero))

    @pl.when(section[0] != 0)
    def _():
        finish(own_one, got_one, (other_one, pair_one))

    gains = gain_rows(z, small[...].astype(BF16))
    gain_one[...] = gains[0].astype(BF16)
    gain_two[...] = gains[1].astype(BF16)
    router[0] = small[:, : z.experts].astype(BF16)
    table[0] = small[: z.bucket_part, z.experts : z.gain_lane].astype(BF16)


def swap(value):
    return lax.ppermute(value, "section", [(0, 1), (1, 0)])


def cross(value, target):
    return lax.ppermute(value, "section", [(1 - target, target)])


def within(value, distance, layer):
    size = lax.axis_size("shard")
    pairs = [(layer * size + i, layer * size + (i ^ distance)) for i in range(size)]
    return lax.ppermute(value, ("section", "shard"), pairs)


def exchange(buffer, axes=("expert", "shard")):
    return lax.all_to_all(buffer, axes, split_axis=0, concat_axis=0, tiled=True)


def shards(
    tokens_in,
    cotangent,
    lengths,
    routes,
    w_query,
    w_key,
    w_value,
    w_output,
    gain_attn,
    gain_moe,
    w_router,
    bias_table,
    w_in,
    w_out,
):
    z = Sizes(tokens_in, w_query, w_router, bias_table, w_in, lax.axis_size("shard"))
    micro_count = tokens_in.shape[0]
    section = lax.axis_index("section").astype(I32)
    core = section.reshape(1)
    place = lax.axis_index("shard").astype(I32).reshape(1)

    def shape(*dims, kind=BF16):
        return jax.ShapeDtypeStruct(dims, kind)

    own_route = routes[0]
    sent_route = lax.dynamic_index_in_dim(own_route, 1 - section, 0, keepdims=False)
    piece = call(
        functools.partial(pack_kernel, z),
        shape(z.piece, z.width),
        (w_query, w_key, w_value, w_output, w_router, gain_attn, gain_moe, bias_table),
        [HBM] * 4 + [VMEM] * 4,
        [pltpu.VMEM((z.part, z.small), F32), pltpu.SemaphoreType.DMA((4,))],
        grant=8,
        cost=2,
    )

    def spread(piece, layer):
        return (piece, *[within(piece, distance, layer) for distance in range(1, z.shards)])

    def after(values, *first):
        values, unused = lax.optimization_barrier((values, first))
        return values

    half = cross(piece[: z.half_rows], 0)
    half = jnp.where(section == 0, half, piece[z.piece - z.half_rows :])
    half_one = lax.all_gather(half, "shard", axis=0, tiled=True)

    piece, sent_route = lax.optimization_barrier((piece, sent_route))
    route_pair = (own_route, swap(sent_route))
    pieces = spread(piece, 0)
    given = [cross(piece, 1)]
    given += [cross(after(member, given[0], route_pair[1], half), 1) for member in pieces[1:]]
    weights_zero = (*pieces, *given)
    experts = (w_in[0, 0], w_out[0, 0])
    given_zero = tuple(cross(member, 1) for member in after(experts, given))

    buffer = shape(z.experts, 8, z.slot_width)
    wide_buffer = shape(z.experts, 8, 2 * z.slot_width)
    kept = (
        shape(z.rows, 3 * z.width),
        shape(z.heads // 2, z.rows, 2 * z.rows),
        shape(z.rows, z.width),
        shape(z.rows, z.width, kind=F32),
        shape(z.rows, z.small, kind=F32),
    )
    scratch = weight_scratch(z)
    rows_shape = shape(z.rows, z.width)
    slab_shape = shape(z.rows, z.slab)

    sent, *kept_zero = call(
        functools.partial(first_kernel, z),
        (buffer, *kept),
        (core, place, lengths, tokens_in, *route_pair, *weights_zero),
        [SMEM, SMEM, SMEM, VMEM, VMEM, VMEM] + [ANY] * 8,
        scratch,
        cost=6,
    )
    arrived_zero = exchange(sent)
    produced = call(
        functools.partial(expert_forward_kernel, z),
        buffer,
        (core, arrived_zero, *experts, *given_zero),
        [SMEM, VMEM, HBM, HBM, HBM, HBM],
        expert_scratch(z, 1),
        cost=6,
    )
    back_zero = exchange(produced)
    weights_one = (half_one, swap(after(half_one, produced)))
    given_one = tuple(cross(member, 0) for member in after(experts, back_zero))

    sent, out_zero, *kept_one = call(
        functools.partial(second_kernel, z),
        (wide_buffer, rows_shape, *kept),
        (core, lengths, cotangent, *route_pair, *weights_one, back_zero, *kept_zero[3:]),
        [SMEM, SMEM, VMEM, VMEM, VMEM] + [ANY] * 2 + [VMEM] * 3,
        scratch,
        cost=7,
    )
    arrived_one = exchange(sent)
    stuff_shape = shape(z.expert_rows, 2 * z.hidden + 2 * z.width)
    result, stuff_one = call(
        lambda section, arrived, *rest: expert_backward_kernel(
            z, 1, section, arrived, arrived, *rest
        ),
        (wide_buffer, stuff_shape),
        (core, arrived_one, *experts, *given_one),
        [SMEM, VMEM, HBM, HBM, HBM, HBM],
        expert_scratch(z, 2),
        grant=28,
        cost=10,
    )
    back_one = exchange(result)

    pair_shape = shape(2, z.rows, z.width)
    sent, pair_one, slab_one = call(
        functools.partial(third_kernel, z),
        (buffer, pair_shape, slab_shape),
        (core, cotangent, *route_pair, *weights_one, back_one, out_zero, kept_zero[4], *kept_one),
        [SMEM, VMEM, VMEM, VMEM] + [ANY] * 2 + [VMEM] * 8,
        scratch,
        cost=8,
    )
    arrived_grad = exchange(sent)

    count = lax.axis_size("expert")

    def partial_sums(slab, layer):
        return call(
            functools.partial(attention_weights_kernel, z, layer),
            (shape(z.half_rows, z.width),) * z.shards,
            (core, place, slab, swap(slab)),
            [SMEM, SMEM, VMEM, LOOSE],
            [pltpu.VMEM((z.width, z.width), F32)],
            cost=4,
        )

    def send_pieces(pieces):
        size = lax.axis_size("shard")
        got = [pieces[0]]
        for distance in range(1, z.shards):
            pairs = [(i, i ^ distance) for i in range(size)]
            got.append(lax.ppermute(pieces[distance], "shard", pairs))
        return tuple(got)

    sums_one = partial_sums(slab_one, 1)
    arrived_grad, *sums_one = lax.optimization_barrier((arrived_grad, *sums_one))
    got_one = send_pieces(sums_one)

    result, stuff_zero = call(
        functools.partial(expert_backward_kernel, z, 0),
        (buffer, stuff_shape),
        (core, arrived_zero, arrived_grad, *experts, *given_zero),
        [SMEM, VMEM, VMEM, HBM, HBM, HBM, HBM],
        expert_scratch(z, 1),
        grant=28,
        cost=8,
    )
    back_grad = after(exchange(result), got_one)
    pair_zero, slab_zero = call(
        functools.partial(fourth_kernel, z),
        (pair_shape, slab_shape),
        (
            core, place, out_zero, pair_one, tokens_in, *route_pair, *weights_zero,
            back_zero, back_grad, *kept_zero,
        ),
        [SMEM, SMEM, VMEM, VMEM, VMEM, VMEM, VMEM] + [ANY] * 8 + [VMEM] * 7,
        scratch,
        cost=8,
    )

    sums_zero = partial_sums(slab_zero, 0)
    got_zero = send_pieces(sums_zero)

    chunks = z.hidden // z.chunk
    grad_w_in, grad_w_out = call(
        functools.partial(expert_weights_kernel, z),
        (shape(z.width, z.hidden), shape(z.hidden, z.width)),
        (
            core, stuff_zero, cross(after(stuff_zero, sums_zero), 0),
            stuff_one, cross(after(stuff_one, sums_zero), 1),
        ),
        [SMEM, HBM, HBM, HBM, HBM],
        [
            pltpu.VMEM((2 * z.expert_rows, stuff_shape.shape[1]), BF16),
            pltpu.VMEM((z.width, 2 * z.expert_rows), BF16),
            pltpu.SemaphoreType.DMA((2,)),
        ],
        grant=28,
        cost=9,
        grid=(chunks,),
        out_specs=(
            pl.BlockSpec((z.width, z.chunk), lambda i: (0, i)),
            pl.BlockSpec((z.chunk, z.width), lambda i: (i, 0)),
        ),
    )

    part = shape(count, z.half_rows // count, z.width)

    def over_blocks(pieces):
        summed = call(pieces_sum_kernel, part, pieces, [LOOSE] * z.shards, cost=2)
        summed = call(spread_sum_kernel, part, (exchange(summed, "expert"),), [VMEM], cost=1)
        return exchange(summed, "expert")

    whole_one = over_blocks(after(got_one, sums_zero))
    whole_zero = over_blocks(after(got_zero, whole_one, grad_w_in))

    matrix = shape(1, z.part, z.width)
    finals = call(
        functools.partial(final_kernel, z),
        (
            *[shape(1, micro_count, z.rows, z.width)] * 2,
            *[matrix] * 4,
            *[shape(1, z.part)] * 2,
            shape(1, z.part, z.experts),
            shape(1, z.bucket_part, z.heads),
        ),
        (
            core, whole_zero, swap(whole_zero), whole_one, swap(whole_one),
            pair_zero, cross(pair_zero, 0), pair_one, cross(pair_one, 1),
        ),
        [SMEM] + [LOOSE] * 8,
        [pltpu.VMEM((z.half_rows, z.width), F32), pltpu.VMEM((z.part, z.small), F32)],
        cost=3,
    )
    return (*finals, grad_w_in[None, None], grad_w_out[None, None])


def solution(mesh):
    both = ("expert", "shard")
    plain = P("section", "shard", None)
    gains = P("section", "shard")
    blocks = P("section", None, both, None)
    experts = P("section", both, None, None)
    tokens = P(None, both, None)
    attention = (plain, plain, plain, plain, gains, gains, plain, plain, experts, experts)
    return jax.shard_map(
        shards,
        mesh=mesh,
        in_specs=(tokens, tokens, tokens, blocks, *attention),
        out_specs=(blocks, blocks, *attention),
        check_vma=False,
    )
```

```python
import functools

import jax
import jax.numpy as jnp
from jax import lax
from jax.experimental import pallas as pl
from jax.experimental.pallas import tpu as pltpu
from jax.sharding import PartitionSpec as P

EPSILON = 1e-06
BOUNDS = (8, 12, 16, 23, 32, 46, 64, 91)
MASKED = -1e30
F32 = jnp.float32
BF16 = jnp.bfloat16
I32 = jnp.int32
GELU_SCALE = 0.7978845608028654
GELU_CUBE = 0.044715
SMEM = pl.BlockSpec(memory_space=pltpu.SMEM)
VMEM = pl.BlockSpec(memory_space=pltpu.VMEM)
LOOSE = pl.BlockSpec(memory_space=pltpu.VMEM)
HBM = pl.BlockSpec(memory_space=pltpu.HBM)
ANY = pl.BlockSpec(memory_space=pl.ANY)


def dot_nn(a, b):
    return jnp.dot(a, b, preferred_element_type=F32)


def dot_nt(a, b):
    return lax.dot_general(a, b, (((1,), (1,)), ((), ())), preferred_element_type=F32)


def dot_tn(a, b):
    return lax.dot_general(a, b, (((0,), (0,)), ((), ())), preferred_element_type=F32)


def iota(shape, dimension):
    return lax.broadcasted_iota(I32, shape, dimension)


def call(body, outs, ins, specs, scratch=(), grant=24, cost=5, **more):
    ins = [
        value if spec is SMEM or spec is LOOSE else pltpu.with_memory_space_constraint(value, pltpu.HBM)
        for value, spec in zip(ins, specs)
    ]
    single = not isinstance(outs, tuple)
    outs = tuple(pltpu.HBM(out.shape, out.dtype) for out in ((outs,) if single else outs))
    more.setdefault("out_specs", (VMEM,) * len(outs))
    made = pl.pallas_call(
        body,
        out_shape=outs,
        in_specs=specs,
        scratch_shapes=scratch,
        compiler_params=pltpu.CompilerParams(vmem_limit_bytes=grant * 1024 * 1024),
        cost_estimate=pl.CostEstimate(
            flops=int(cost * 1e8), bytes_accessed=int(cost * 4e5), transcendentals=0
        ),
        **more,
    )(*ins)
    return made[0] if single else made


def bucket_of(relative):
    distance = jnp.abs(relative)
    bucket = jnp.zeros_like(relative)
    for lowest in tuple(range(1, 8)) + BOUNDS:
        bucket = bucket + (distance >= lowest).astype(I32)
    return bucket + 16 * (relative > 0).astype(I32)


class Sizes:
    def __init__(self, tokens_in, w_query, w_router, bias_table, w_in, shards):
        self.rows, self.width = tokens_in.shape[1:]
        self.part = w_query.shape[1]
        self.shards = shards
        self.experts = w_router.shape[2]
        self.bucket_part, self.heads = bias_table.shape[1:]
        self.buckets = self.bucket_part * shards
        self.hidden = w_in.shape[3]
        self.chunk = self.hidden // 6
        self.capacity = max(
            2, (3 * self.rows + 2 * self.experts - 1) // (2 * self.experts)
        )
        self.full, rest = divmod(self.capacity, 8)
        self.rest = next((power for power in (0, 1, 2, 4) if power >= rest), None)
        if self.rest is None:
            self.full, self.rest = (self.full + 1, 0)
        self.cuts = 8 // self.rest if self.rest else 0
        self.cut = self.width // self.cuts if self.rest else 0
        self.slot_width = self.full * self.width + self.cut
        self.slot_rows = self.experts * 8
        self.expert_rows = self.slot_rows * self.full + self.experts * self.rest
        self.small = -(-(self.experts + self.heads + 2) // 128) * 128
        self.small_groups = self.width // self.small
        self.small_rows = self.part // self.small_groups
        self.gain_lane = self.experts + self.heads
        self.piece = 4 * self.part + self.small_rows
        self.half_rows = 2 * self.part + self.small_rows
        self.slab = 6 * self.width + self.small * self.width // self.rows


def slot_picks(z, route):
    onehot = (route == iota((z.rows, z.experts), 1)).astype(F32)
    lower = (iota((z.rows, z.rows), 0) >= iota((z.rows, z.rows), 1)).astype(F32).astype(BF16)
    running = dot_nn(lower, onehot.astype(BF16))
    place = jnp.sum(running * onehot, axis=1, keepdims=True).astype(I32) - 1
    slots = iota((z.rows, z.slot_rows), 1)

    def pick(first, wide, shift):
        inside = (place >= first) & (place < first + wide)
        target = jnp.where(inside, route * 8 + place - first + shift, -1)
        return (slots == target).astype(F32).astype(BF16)

    picks = [pick(8 * i, 8, 0) for i in range(z.full)]
    return picks + [pick(8 * z.full, z.rest, z.rest * i) for i in range(z.cuts)]


def cut_sum(z, picks, values):
    return sum(dot_tn(pick, values[:, i * z.cut : (i + 1) * z.cut]) for i, pick in enumerate(picks))


def put_slots(z, ref, offset, picks, values):
    for i in range(z.full):
        block = dot_tn(picks[i], values)
        ref[:, :, offset : offset + z.width] = block.reshape(z.experts, 8, z.width).astype(BF16)
        offset += z.width
    if z.rest:
        block = cut_sum(z, picks[z.full :], values)
        ref[:, :, offset : offset + z.cut] = block.reshape(z.experts, 8, z.cut).astype(BF16)


def read_slots(z, ref, offset, wide):
    block = ref[:, :, offset : offset + wide].astype(F32)
    return block.reshape(z.slot_rows, wide).astype(BF16)


def get_slots(z, ref, offset, picks):
    total = 0.0
    for i in range(z.full):
        total += dot_nn(picks[i], read_slots(z, ref, offset, z.width))
        offset += z.width
    if z.rest:
        block = read_slots(z, ref, offset, z.cut)
        total += jnp.concatenate([dot_nn(pick, block) for pick in picks[z.full :]], axis=1)
    return total


def extra_picks(z):
    shape = (z.experts * z.rest, z.slot_rows)
    rows, slots = (iota(shape, 0), iota(shape, 1))
    first = (rows // z.rest) * 8 + rows % z.rest
    return [(slots == first + z.rest * i).astype(F32).astype(BF16) for i in range(z.cuts)]


def rows_of_slots(z, ref, offset):
    parts = []
    for i in range(z.full):
        parts.append(read_slots(z, ref, offset, z.width))
        offset += z.width
    if z.rest:
        block = read_slots(z, ref, offset, z.cut)
        pieces = [dot_nn(pick, block) for pick in extra_picks(z)]
        parts.append(jnp.concatenate(pieces, axis=1).astype(BF16))
    return jnp.concatenate(parts, axis=0) if len(parts) > 1 else parts[0]


def slots_of_rows(z, ref, offset, rows):
    for i in range(z.full):
        block = rows[i * z.slot_rows : (i + 1) * z.slot_rows]
        ref[:, :, offset : offset + z.width] = block.reshape(z.experts, 8, z.width).astype(BF16)
        offset += z.width
    if z.rest:
        block = cut_sum(z, extra_picks(z), rows[z.full * z.slot_rows :].astype(BF16))
        ref[:, :, offset : offset + z.cut] = block.reshape(z.experts, 8, z.cut).astype(BF16)


def fetch_weights(z, mine, place, own, other, mats, packed, sems, order=(4, 0, 1, 2, 3)):
    def copy(pieces, i, k):
        shard = place ^ k
        count = z.small_rows if i == 4 else z.part
        start = i * z.part
        source = pieces[k]
        target = pl.ds(pl.multiple_of(shard * count, 16), count)
        held = packed.at[target] if i == 4 else mats.at[i, target]
        return pltpu.make_async_copy(source.at[pl.ds(start, count)], held, sems.at[i, k])

    def start(pieces):
        for i in order:
            for k in range(z.shards):
                copy(pieces, i, k).start()

    def wait(i):
        for k in range(z.shards):
            copy(own, i, k).wait()

    @pl.when(mine)
    def _():
        start(own)

    @pl.when(jnp.logical_not(mine))
    def _():
        start(other)

    return [functools.partial(wait, i) for i in range(5)]


def fetch_halves(z, core, own, other, mats, packed, sems, order=(4, 0, 1, 2, 3)):
    def copy(source, i, k):
        count = z.small_rows if i == 4 else z.part
        start = k * z.half_rows + (i if i < 2 else i - 2) * z.part
        target = pl.ds(k * count, count)
        held = packed.at[target] if i == 4 else mats.at[i, target]
        return pltpu.make_async_copy(source.at[pl.ds(start, count)], held, sems.at[i, k])

    def start(first, second):
        for i in order:
            for k in range(z.shards):
                copy(first if i < 2 else second, i, k).start()

    def wait(i):
        for k in range(z.shards):
            copy(own, i, k).wait()

    @pl.when(core == 0)
    def _():
        start(own, other)

    @pl.when(core != 0)
    def _():
        start(other, own)

    return [functools.partial(wait, i) for i in range(5)]


def weight_scratch(z):
    return [
        pltpu.VMEM((4, z.width, z.width), BF16),
        pltpu.VMEM((z.shards * z.small_rows, z.width), BF16),
        pltpu.VMEM((z.width, z.small), BF16),
        pltpu.SemaphoreType.DMA((5, z.shards)),
    ]


def unpack_small(z, packed, small):
    for j in range(z.shards):
        for g in range(z.small_groups):
            row = j * z.part + g * z.small_rows
            small[row : row + z.small_rows, :] = packed[
                j * z.small_rows : (j + 1) * z.small_rows, g * z.small : (g + 1) * z.small
            ]


def bucket_rows(z):
    rows, buckets = (iota((z.width, z.buckets), 0), iota((z.width, z.buckets), 1))
    held = (buckets // z.bucket_part) * z.part + buckets % z.bucket_part
    return (rows == held).astype(F32).astype(BF16)


def bucket_lanes(z):
    shape = (z.buckets, 2 * z.rows)
    return (bucket_of(iota(shape, 1) - z.rows) == iota(shape, 0)).astype(F32).astype(BF16)


def identity(size):
    return (iota((size, size), 0) == iota((size, size), 1)).astype(F32).astype(BF16)


def gain_rows(z, small):
    rows, lanes = (iota((8, z.small), 0), iota((8, z.small), 1))
    pick = ((lanes == z.gain_lane + rows) & (rows < 2)).astype(F32).astype(BF16)
    made = dot_nt(pick, small)
    return (made[0:1], made[1:2])


def unit_rows(values):
    inverse = lax.rsqrt(jnp.mean(values * values, axis=-1, keepdims=True) + EPSILON)
    return (values * inverse, inverse)


def pair_masks(z):
    lanes = iota((z.rows, 128), 1)
    first = (lanes < 64).astype(F32).astype(BF16)
    return (first, (lanes >= 64).astype(F32).astype(BF16))


def double(values, masks):
    return jnp.concatenate([values * masks[0], values * masks[1]], axis=0)


def attend(z, inputs, waits, mats, packed, small, lengths, section, qkv_ref, probs_ref, attended_ref):
    waits[4]()
    unpack_small(z, packed, small)
    small_full = small[...]
    gain_one, gain_two = gain_rows(z, small_full)
    normed_one = (unit_rows(inputs)[0] * gain_one).astype(BF16)
    for i in range(3):
        waits[i]()
        qkv_ref[:, i * z.width : (i + 1) * z.width] = dot_nn(normed_one, mats[i]).astype(BF16)

    table = dot_tn(bucket_rows(z), small_full).astype(BF16)
    bias = dot_tn(table, bucket_lanes(z))[z.experts : z.experts + z.heads]

    rows, lanes = (iota((z.rows, z.rows), 0), iota((z.rows, z.rows), 1))
    segment_q, segment_k = (jnp.zeros_like(rows), jnp.zeros_like(rows))
    end = jnp.int32(0)
    for i in range(lengths.shape[2]):
        end = end + lengths[section, 0, i]
        segment_q += (rows >= end).astype(I32)
        segment_k += (lanes >= end).astype(I32)
    visible = segment_q == segment_k

    masks = pair_masks(z)
    scale = 64 ** (-0.5)
    for p in range(z.heads // 2):
        at = slice(p * 128, (p + 1) * 128)
        query = qkv_ref[:, p * 128 : (p + 1) * 128]
        key = qkv_ref[:, z.width + p * 128 : z.width + (p + 1) * 128]
        value = qkv_ref[:, 2 * z.width + p * 128 : 2 * z.width + (p + 1) * 128]
        scores = dot_nt(query, double(key, masks)) * scale
        halves = []
        for i in range(2):
            spread = jnp.broadcast_to(bias[2 * p + i : 2 * p + i + 1], (z.rows, 2 * z.rows))
            spread = pltpu.roll(spread, z.rows, 1, stride=1, stride_axis=0)[:, : z.rows]
            part = scores[:, i * z.rows : (i + 1) * z.rows] + spread
            part = jnp.where(visible, part, MASKED)
            part = jnp.exp(part - jnp.max(part, axis=-1, keepdims=True))
            halves.append(part / jnp.sum(part, axis=-1, keepdims=True))
        probs = jnp.concatenate(halves, axis=1).astype(BF16)
        probs_ref[p] = probs
        attended_ref[:, at] = dot_nn(probs, double(value, masks)).astype(BF16)

    waits[3]()
    middle = inputs + dot_nn(attended_ref[...], mats[3])
    normed_two = (unit_rows(middle)[0] * gain_two).astype(BF16)
    logits = dot_nn(normed_two, small_full)
    logits = jnp.where(iota((z.rows, z.small), 1) < z.experts, logits, MASKED)
    logits = jnp.exp(logits - jnp.max(logits, axis=-1, keepdims=True))
    router = logits / jnp.sum(logits, axis=-1, keepdims=True)
    return (middle, normed_two, router)


def chosen(z, route):
    return (route == iota((z.rows, z.small), 1)).astype(F32)


def attend_back(
    z, grad_out, token_out, grad_token, inputs, route, waits, mats, packed, small, kept, slab_ref
):
    qkv_ref, probs_ref, attended_ref, middle_ref, router_ref = kept
    waits[4]()
    unpack_small(z, packed, small)
    small_full = small[...]
    gain_one, gain_two = gain_rows(z, small_full)
    onehot = chosen(z, route)
    router = router_ref[...]
    gate = jnp.sum(router * onehot, axis=1, keepdims=True)
    grad_gate = jnp.sum(grad_out * token_out, axis=1, keepdims=True)
    grad_logits = (grad_gate * gate * (onehot - router)).astype(BF16)
    unit_two, inverse_two = unit_rows(middle_ref[...])
    grad_small = dot_tn((unit_two * gain_two).astype(BF16), grad_logits)
    grad_normed = grad_token + dot_nt(grad_logits, small_full)
    gain_two_grad = jnp.sum(grad_normed * unit_two, axis=0, keepdims=True)
    grad_unit = grad_normed * gain_two
    grad_unit -= unit_two * jnp.mean(grad_unit * unit_two, axis=1, keepdims=True)
    grad_middle = grad_out + inverse_two * grad_unit
    grad_branch = grad_middle.astype(BF16)
    slab_ref[:, 4 * z.width : 5 * z.width] = attended_ref[...]
    slab_ref[:, 5 * z.width : 6 * z.width] = grad_branch
    waits[3]()
    grad_attended = dot_nt(grad_branch, mats[3]).astype(BF16)

    masks = pair_masks(z)
    scale = 64 ** (-0.5)
    relative = []
    turn = iota((z.rows, z.rows), 0) + iota((z.rows, z.rows), 1) == z.rows - 1
    turn = turn.astype(F32).astype(BF16)
    for p in range(z.heads // 2):
        at = slice(p * 128, (p + 1) * 128)
        query = qkv_ref[:, p * 128 : (p + 1) * 128]
        keys = double(qkv_ref[:, z.width + p * 128 : z.width + (p + 1) * 128], masks)
        values = double(qkv_ref[:, 2 * z.width + p * 128 : 2 * z.width + (p + 1) * 128], masks)
        grad_heads = grad_attended[:, at]
        probs_low = probs_ref[p]
        probs = probs_low.astype(F32)
        grad_probs = dot_nt(grad_heads, values)
        halves = []
        for i in range(2):
            part = slice(i * z.rows, (i + 1) * z.rows)
            product = grad_probs[:, part] * probs[:, part]
            dots = jnp.sum(product, axis=-1, keepdims=True)
            grads = (product - probs[:, part] * dots).astype(BF16)
            halves.append(grads)
        grad_scores = jnp.concatenate(halves, axis=1)
        turned = dot_nn(turn, grad_scores)
        for i in range(2):
            wide = [turned[:, i * z.rows : (i + 1) * z.rows], jnp.zeros((z.rows, z.rows), F32)]
            wide = pltpu.roll(jnp.concatenate(wide, axis=1), 1, 1, stride=1, stride_axis=0)
            relative.append(jnp.sum(wide, axis=0, keepdims=True))
        start = z.width + p * 128
        slab_ref[:, start : start + 128] = (dot_nn(grad_scores, keys) * scale).astype(BF16)
        made = dot_tn(grad_scores, query) * scale
        mask = masks[0].astype(F32)
        made = made[: z.rows] * mask + made[z.rows :] * (1.0 - mask)
        slab_ref[:, start + z.width : start + z.width + 128] = made.astype(BF16)
        made = dot_tn(probs_low, grad_heads)
        made = made[: z.rows] * mask + made[z.rows :] * (1.0 - mask)
        slab_ref[:, start + 2 * z.width : start + 2 * z.width + 128] = made.astype(BF16)

    unit_one, inverse_one = unit_rows(inputs)
    slab_ref[:, : z.width] = (unit_one * gain_one).astype(BF16)
    grad_normed = 0.0
    for i in range(3):
        waits[i]()
        grad_normed += dot_nt(slab_ref[:, (i + 1) * z.width : (i + 2) * z.width], mats[i])
    gain_one_grad = jnp.sum(grad_normed * unit_one, axis=0, keepdims=True)
    grad_unit = grad_normed * gain_one
    grad_unit -= unit_one * jnp.mean(grad_unit * unit_one, axis=1, keepdims=True)
    grad_in = (grad_middle + inverse_one * grad_unit).astype(BF16)

    relative += [jnp.zeros((1, 2 * z.rows), F32)] * (-z.heads % 8)
    relative = jnp.concatenate(relative, axis=0)
    lanes_of = bucket_lanes(z)
    high = relative.astype(BF16)
    table = dot_nt(lanes_of, high) + dot_nt(lanes_of, (relative - high.astype(F32)).astype(BF16))
    count = relative.shape[0]
    places = iota((count, z.small), 1) == iota((count, z.small), 0) + z.experts
    places = places & (iota((count, z.small), 0) < z.heads)
    table = dot_nn(table.astype(BF16), places.astype(F32).astype(BF16)).astype(BF16)
    grad_small += dot_nn(bucket_rows(z), table)
    gains = jnp.concatenate([gain_one_grad, gain_two_grad, jnp.zeros((6, z.width), F32)], axis=0)
    rows, lanes = (iota((8, z.small), 0), iota((8, z.small), 1))
    pick = ((lanes == z.gain_lane + rows) & (rows < 2)).astype(F32).astype(BF16)
    grad_small += dot_tn(gains.astype(BF16), pick)
    for i in range(z.width // z.rows):
        start = 6 * z.width + i * z.small
        slab_ref[:, start : start + z.small] = grad_small[i * z.rows : (i + 1) * z.rows].astype(BF16)
    return grad_in


def pack_kernel(z, query, key, value, output, router, gain_one, gain_two, table, piece, small, sems):
    copies = [
        pltpu.make_async_copy(source.at[0], piece.at[pl.ds(i * z.part, z.part)], sems.at[i])
        for i, source in enumerate((query, key, value, output))
    ]
    for copy in copies:
        copy.start()
    gains = [gain_one[...].astype(F32), gain_two[...].astype(F32), jnp.zeros((6, z.part), F32)]
    rows, lanes = (iota((8, z.small), 0), iota((8, z.small), 1))
    pick = ((lanes == z.gain_lane + rows) & (rows < 2)).astype(F32).astype(BF16)
    small[...] = dot_tn(jnp.concatenate(gains, axis=0).astype(BF16), pick)
    small[:, : z.experts] = dot_tn(router[0], identity(z.experts))
    small[: z.bucket_part, z.experts : z.gain_lane] = table[0].astype(F32)
    for g in range(z.small_groups):
        piece[4 * z.part :, g * z.small : (g + 1) * z.small] = small[
            g * z.small_rows : (g + 1) * z.small_rows
        ].astype(BF16)
    for copy in copies:
        copy.wait()


def first_kernel(
    z, section, place, lengths, tokens, own_route, other_route, o0, o1, o2, o3, r0, r1, r2, r3,
    send, qkv, probs, attended, middle_ref, router_ref,
    mats, packed, small, sems,
):
    core = section[0]
    waits = fetch_weights(
        z, core == 0, place[0], (o0, o1, o2, o3), (r0, r1, r2, r3), mats, packed, sems)
    inputs = tokens[core].astype(F32)
    middle, normed_two, router = attend(
        z, inputs, waits, mats, packed, small, lengths, core, qkv, probs, attended
    )
    middle_ref[...] = middle
    router_ref[...] = router
    route = jnp.where(core == 0, own_route[core], other_route[...])
    put_slots(z, send, 0, slot_picks(z, route), normed_two)


def second_kernel(
    z, section, lengths, cotangent, own_route, other_route, own, other, back, middle_zero, router_zero,
    send, out_zero, qkv, probs, attended, middle_ref, router_ref,
    mats, packed, small, sems,
):
    core = section[0]
    waits = fetch_halves(
        z, core, own, other, mats, packed, sems)
    route = jnp.where(core == 0, own_route[core], other_route[...])
    gate = jnp.sum(router_zero[...] * chosen(z, route), axis=1, keepdims=True)
    token_out = get_slots(z, back, 0, slot_picks(z, route))
    layer_out = (middle_zero[...] + gate * token_out).astype(BF16)
    out_zero[...] = layer_out
    middle, normed_two, router = attend(
        z, layer_out.astype(F32), waits, mats, packed, small, lengths, core, qkv, probs, attended
    )
    middle_ref[...] = middle
    router_ref[...] = router
    route = jnp.where(core == 1, own_route[core], other_route[...])
    picks = slot_picks(z, route)
    put_slots(z, send, 0, picks, normed_two)
    gate = jnp.sum(router * chosen(z, route), axis=1, keepdims=True)
    grad = (gate * cotangent[core].astype(F32)).astype(BF16)
    put_slots(z, send, z.slot_width, picks, grad)


def third_kernel(
    z, section, cotangent, own_route, other_route, own, other, back, inputs, router_zero,
    qkv, probs, attended, middle, router,
    send, pair, slab,
    mats, packed, small, sems,
):
    core = section[0]
    waits = fetch_halves(
        z, core, own, other, mats, packed, sems, (4, 3, 0, 1, 2))
    route = jnp.where(core == 1, own_route[core], other_route[...])
    picks = slot_picks(z, route)
    token_out = get_slots(z, back, 0, picks)
    grad_token = get_slots(z, back, z.slot_width, picks)
    gate = jnp.sum(router[...] * chosen(z, route), axis=1, keepdims=True)
    pair[0] = (middle[...] + gate * token_out).astype(BF16)
    grad_in = attend_back(
        z, cotangent[core].astype(F32), token_out, grad_token, inputs[...].astype(F32), route,
        waits, mats, packed, small, (qkv, probs, attended, middle, router), slab,
    )
    pair[1] = grad_in
    route = jnp.where(core == 0, own_route[core], other_route[...])
    gate = jnp.sum(router_zero[...] * chosen(z, route), axis=1, keepdims=True)
    grad = (gate * grad_in.astype(F32)).astype(BF16)
    put_slots(z, send, 0, slot_picks(z, route), grad)


def fourth_kernel(
    z, section, place, out_zero, pair_one, tokens, own_route, other_route, o0, o1, o2, o3, r0, r1, r2, r3, back_out, back_grad,
    qkv, probs, attended, middle, router,
    pair, slab,
    mats, packed, small, sems,
):
    core = section[0]
    waits = fetch_weights(
        z, core == 0, place[0], (o0, o1, o2, o3), (r0, r1, r2, r3), mats, packed, sems, (4, 3, 0, 1, 2))
    route = jnp.where(core == 0, own_route[core], other_route[...])
    picks = slot_picks(z, route)
    token_out = get_slots(z, back_out, 0, picks)
    grad_token = get_slots(z, back_grad, 0, picks)
    pair[0] = out_zero[...]
    pair[1] = attend_back(
        z, pair_one[1].astype(F32), token_out, grad_token, tokens[core].astype(F32), route,
        waits, mats, packed, small, (qkv, probs, attended, middle, router), slab,
    )


def fetch_experts(z, mine, own_in, own_out, other_in, other_out, w_in, w_out, sems):
    def copies(source_in, source_out, c):
        at = pl.ds(c * z.chunk, z.chunk)
        return (
            pltpu.make_async_copy(source_in.at[:, at], w_in.at[c], sems.at[2 * c]),
            pltpu.make_async_copy(source_out.at[at], w_out.at[c], sems.at[2 * c + 1]),
        )

    def start(source_in, source_out):
        for c in range(z.hidden // z.chunk):
            for copy in copies(source_in, source_out, c):
                copy.start()

    @pl.when(mine)
    def _():
        start(own_in, own_out)

    @pl.when(jnp.logical_not(mine))
    def _():
        start(other_in, other_out)

    def wait(c):
        for copy in copies(own_in, own_out, c):
            copy.wait()

    return wait


def expert_scratch(z, sums):
    chunks = z.hidden // z.chunk
    return [
        pltpu.VMEM((chunks, z.width, z.chunk), BF16),
        pltpu.VMEM((chunks, z.chunk, z.width), BF16),
        pltpu.SemaphoreType.DMA((2 * chunks,)),
    ] + [pltpu.VMEM((z.expert_rows, z.width), F32)] * sums


def smooth(values):
    square = values * values
    bent = jnp.tanh(GELU_SCALE * values * (1.0 + GELU_CUBE * square))
    return (0.5 * values * (1.0 + bent), square, bent)


def smooth_slope(values, square, bent):
    inner = GELU_SCALE * (1.0 + 3.0 * GELU_CUBE * square)
    return 0.5 * (1.0 + bent) + 0.5 * values * (1.0 - bent * bent) * inner


def expert_forward_kernel(
    z, section, arrived, own_in, own_out, other_in, other_out, result, w_in, w_out, sems, produced
):
    wait = fetch_experts(
        z, section[0] == 0, own_in, own_out, other_in, other_out, w_in, w_out, sems
    )
    rows = rows_of_slots(z, arrived, 0)
    for c in range(z.hidden // z.chunk):
        wait(c)
        hidden = smooth(dot_nn(rows, w_in[c]))[0].astype(BF16)
        made = dot_nn(hidden, w_out[c])
        produced[...] = made if c == 0 else produced[...] + made
    slots_of_rows(z, result, 0, produced[...])


def expert_backward_kernel(
    z, layer, section, arrived, arrived_grad, own_in, own_out, other_in, other_out,
    result, stuff, w_in, w_out, sems, grad_sum, *produced
):
    wait = fetch_experts(
        z, section[0] == layer, own_in, own_out, other_in, other_out, w_in, w_out, sems
    )
    rows = rows_of_slots(z, arrived, 0)
    grads = rows_of_slots(z, arrived_grad, z.slot_width if produced else 0)
    stuff[:, 2 * z.hidden : 2 * z.hidden + z.width] = rows
    stuff[:, 2 * z.hidden + z.width : 2 * z.hidden + 2 * z.width] = grads
    for c in range(z.hidden // z.chunk):
        wait(c)
        before = dot_nn(rows, w_in[c])
        hidden, square, bent = smooth(before)
        hidden = hidden.astype(BF16)
        stuff[:, c * z.chunk : (c + 1) * z.chunk] = hidden
        if produced:
            made = dot_nn(hidden, w_out[c])
            produced[0][...] = made if c == 0 else produced[0][...] + made
        grad_pre = dot_nt(grads, w_out[c]) * smooth_slope(before, square, bent)
        grad_pre = grad_pre.astype(BF16)
        stuff[:, z.hidden + c * z.chunk : z.hidden + (c + 1) * z.chunk] = grad_pre
        made = dot_nt(grad_pre, w_in[c])
        grad_sum[...] = made if c == 0 else grad_sum[...] + made
    if produced:
        slots_of_rows(z, result, 0, produced[0][...])
    slots_of_rows(z, result, z.slot_width if produced else 0, grad_sum[...])


def expert_weights_kernel(
    z, section, own_zero, other_zero, own_one, other_one, grad_in, grad_out, held, turned, sems
):
    step = pl.program_id(0)

    @pl.when(step == 0)
    def _():
        def copies(own, other):
            return [
                pltpu.make_async_copy(
                    source, held.at[pl.ds(i * z.expert_rows, z.expert_rows)], sems.at[i]
                )
                for i, source in enumerate((own, other))
            ]

        @pl.when(section[0] == 0)
        def _():
            for copy in copies(own_zero, other_zero):
                copy.start()

        @pl.when(section[0] != 0)
        def _():
            for copy in copies(own_one, other_one):
                copy.start()

        for copy in copies(own_zero, other_zero):
            copy.wait()
        rows = held[:, 2 * z.hidden : 2 * z.hidden + z.width]
        turned[...] = jnp.transpose(rows.astype(F32)).astype(BF16)

    start = pl.multiple_of(step * z.chunk, z.chunk)
    grad_pre = held[:, pl.ds(z.hidden + start, z.chunk)]
    hidden = held[:, pl.ds(start, z.chunk)]
    grads = held[:, 2 * z.hidden + z.width : 2 * z.hidden + 2 * z.width]
    grad_in[...] = dot_nn(turned[...], grad_pre).astype(BF16)
    grad_out[...] = dot_tn(hidden, grads).astype(BF16)


def attention_weights_kernel(z, layer, section, place, own, other, *refs):
    outs, made = (refs[: z.shards], refs[z.shards])
    second = section[0] ^ layer

    def both(column):
        at = pl.ds(pl.multiple_of(column * z.width, 128), z.width)
        return jnp.concatenate([own[:, at], other[:, at]], axis=0)

    for i, (left, right) in enumerate(
        ((0, 1 + 2 * second), (4 * second, 2 + 3 * second))
    ):
        made[...] = dot_tn(both(left), both(right))
        for k in range(z.shards):
            start = pl.multiple_of((place[0] ^ k) * z.part, 16)
            outs[k][i * z.part : (i + 1) * z.part] = made[pl.ds(start, z.part)].astype(BF16)
    for i in range(z.width // z.rows):
        columns = slice(6 * z.width + i * z.small, 6 * z.width + (i + 1) * z.small)
        total = own[:, columns].astype(F32) + other[:, columns].astype(F32)
        made[i * z.rows : (i + 1) * z.rows, : z.small] = total
    for k in range(z.shards):
        for g in range(z.small_groups):
            start = pl.multiple_of((place[0] ^ k) * z.part + g * z.small_rows, 16)
            outs[k][2 * z.part :, g * z.small : (g + 1) * z.small] = made[
                pl.ds(start, z.small_rows), : z.small
            ].astype(BF16)


def pieces_sum_kernel(*refs):
    out = refs[-1]
    rows = out.shape[1]
    total = sum(piece[...].astype(F32) for piece in refs[:-1])
    for i in range(out.shape[0]):
        out[i] = total[i * rows : (i + 1) * rows].astype(BF16)


def spread_sum_kernel(pieces, out):
    total = sum(pieces[i].astype(F32) for i in range(pieces.shape[0])).astype(BF16)
    for i in range(out.shape[0]):
        out[i] = total


def final_kernel(
    z, section, own_zero, got_zero, own_one, got_one, pair_zero, other_zero, pair_one, other_one,
    layer_out, input_grad, query, key, value, output, gain_one, gain_two, router, table, held, small,
):
    rows = own_zero.shape[1]

    def finish(own, other, micros):
        for source, targets in ((own, (query, key)), (other, (value, output))):
            for i in range(own.shape[0]):
                held[i * rows : (i + 1) * rows] = source[i].astype(F32)
            for i, target in enumerate(targets):
                target[0] = held[i * z.part : (i + 1) * z.part].astype(BF16)
            if source is own:
                for g in range(z.small_groups):
                    small[g * z.small_rows : (g + 1) * z.small_rows] = held[
                        2 * z.part :, g * z.small : (g + 1) * z.small
                    ]
        for i, pair in enumerate(micros):
            layer_out[0, i] = pair[0]
            input_grad[0, i] = pair[1]

    @pl.when(section[0] == 0)
    def _():
        finish(own_zero, got_zero, (pair_zero, other_zero))

    @pl.when(section[0] != 0)
    def _():
        finish(own_one, got_one, (other_one, pair_one))

    gains = gain_rows(z, small[...].astype(BF16))
    gain_one[...] = gains[0].astype(BF16)
    gain_two[...] = gains[1].astype(BF16)
    router[0] = dot_nt(identity(z.experts), small[:, : z.experts].astype(BF16)).astype(BF16)
    table[0] = small[: z.bucket_part, z.experts : z.gain_lane].astype(BF16)


def swap(value):
    return lax.ppermute(value, "section", [(0, 1), (1, 0)])


def cross(value, target):
    return lax.ppermute(value, "section", [(1 - target, target)])


def within(value, distance, layer):
    size = lax.axis_size("shard")
    pairs = [(layer * size + i, layer * size + (i ^ distance)) for i in range(size)]
    return lax.ppermute(value, ("section", "shard"), pairs)


def exchange(buffer, axes=("expert", "shard")):
    return lax.all_to_all(buffer, axes, split_axis=0, concat_axis=0, tiled=True)


def shards(
    tokens_in,
    cotangent,
    lengths,
    routes,
    w_query,
    w_key,
    w_value,
    w_output,
    gain_attn,
    gain_moe,
    w_router,
    bias_table,
    w_in,
    w_out,
):
    z = Sizes(tokens_in, w_query, w_router, bias_table, w_in, lax.axis_size("shard"))
    micro_count = tokens_in.shape[0]
    section = lax.axis_index("section").astype(I32)
    core = section.reshape(1)
    place = lax.axis_index("shard").astype(I32).reshape(1)

    def shape(*dims, kind=BF16):
        return jax.ShapeDtypeStruct(dims, kind)

    own_route = routes[0]
    sent_route = lax.dynamic_index_in_dim(own_route, 1 - section, 0, keepdims=False)
    piece = call(
        functools.partial(pack_kernel, z),
        shape(z.piece, z.width),
        (
            w_query, w_key, w_value, w_output, jnp.swapaxes(w_router, 1, 2), gain_attn, gain_moe,
            bias_table,
        ),
        [HBM] * 4 + [VMEM] * 4,
        [pltpu.VMEM((z.part, z.small), F32), pltpu.SemaphoreType.DMA((4,))],
        grant=8,
        cost=2,
    )

    def spread(piece, layer):
        return (piece, *[within(piece, distance, layer) for distance in range(1, z.shards)])

    def after(values, *first):
        values, unused = lax.optimization_barrier((values, first))
        return values

    half = cross(piece[: z.half_rows], 0)
    half = jnp.where(section == 0, half, piece[z.piece - z.half_rows :])
    half_one = lax.all_gather(half, "shard", axis=0, tiled=True)

    piece, sent_route = lax.optimization_barrier((piece, sent_route))
    route_pair = (own_route, swap(sent_route))
    pieces = spread(piece, 0)
    experts = (w_in[0, 0], w_out[0, 0])
    given = [cross(piece, 1)]
    early = (given[0], route_pair[1], half)
    given += [cross(after(member, early), 1) for member in pieces[1:]]
    given_zero = tuple(cross(member, 1) for member in after(experts, given))
    weights_zero = (*pieces, *given)

    buffer = shape(z.experts, 8, z.slot_width)
    wide_buffer = shape(z.experts, 8, 2 * z.slot_width)
    kept = (
        shape(z.rows, 3 * z.width),
        shape(z.heads // 2, z.rows, 2 * z.rows),
        shape(z.rows, z.width),
        shape(z.rows, z.width, kind=F32),
        shape(z.rows, z.small, kind=F32),
    )
    scratch = weight_scratch(z)
    rows_shape = shape(z.rows, z.width)
    slab_shape = shape(z.rows, z.slab)

    sent, *kept_zero = call(
        functools.partial(first_kernel, z),
        (buffer, *kept),
        (core, place, lengths, tokens_in, *route_pair, *weights_zero),
        [SMEM, SMEM, SMEM, VMEM, VMEM, VMEM] + [ANY] * 8,
        scratch,
        cost=6,
    )
    arrived_zero = exchange(sent)
    produced = call(
        functools.partial(expert_forward_kernel, z),
        buffer,
        (core, arrived_zero, *experts, *given_zero),
        [SMEM, VMEM, HBM, HBM, HBM, HBM],
        expert_scratch(z, 1),
        cost=6,
    )
    back_zero = exchange(produced)
    weights_one = (half_one, swap(after(half_one, produced)))
    given_one = tuple(cross(member, 0) for member in after(experts, back_zero))

    sent, out_zero, *kept_one = call(
        functools.partial(second_kernel, z),
        (wide_buffer, rows_shape, *kept),
        (core, lengths, cotangent, *route_pair, *weights_one, back_zero, *kept_zero[3:]),
        [SMEM, SMEM, VMEM, VMEM, VMEM] + [ANY] * 2 + [VMEM] * 3,
        scratch,
        cost=7,
    )
    arrived_one = exchange(sent)
    stuff_shape = shape(z.expert_rows, 2 * z.hidden + 2 * z.width)
    result, stuff_one = call(
        lambda section, arrived, *rest: expert_backward_kernel(
            z, 1, section, arrived, arrived, *rest
        ),
        (wide_buffer, stuff_shape),
        (core, arrived_one, *experts, *given_one),
        [SMEM, VMEM, HBM, HBM, HBM, HBM],
        expert_scratch(z, 2),
        grant=28,
        cost=10,
    )
    back_one = exchange(result)

    pair_shape = shape(2, z.rows, z.width)
    sent, pair_one, slab_one = call(
        functools.partial(third_kernel, z),
        (buffer, pair_shape, slab_shape),
        (core, cotangent, *route_pair, *weights_one, back_one, out_zero, kept_zero[4], *kept_one),
        [SMEM, VMEM, VMEM, VMEM] + [ANY] * 2 + [VMEM] * 8,
        scratch,
        cost=8,
    )
    arrived_grad = exchange(sent)

    count = lax.axis_size("expert")

    def partial_sums(slab, layer):
        return call(
            functools.partial(attention_weights_kernel, z, layer),
            (shape(z.half_rows, z.width),) * z.shards,
            (core, place, slab, swap(slab)),
            [SMEM, SMEM, VMEM, LOOSE],
            [pltpu.VMEM((z.width, z.width), F32)],
            cost=4,
        )

    def send_pieces(pieces):
        size = lax.axis_size("shard")
        got = [pieces[0]]
        for distance in range(1, z.shards):
            pairs = [(i, i ^ distance) for i in range(size)]
            got.append(lax.ppermute(pieces[distance], "shard", pairs))
        return tuple(got)

    part = shape(count, z.half_rows // count, z.width)

    def pieces_sum(pieces):
        return call(pieces_sum_kernel, part, pieces, [LOOSE] * z.shards, cost=2)

    def spread_sum(pieces):
        return call(spread_sum_kernel, part, (pieces,), [VMEM], cost=1)

    sums_one = partial_sums(slab_one, 1)
    other_stuff_one = cross(stuff_one, 1)
    arrived_grad, *sums_one = lax.optimization_barrier((arrived_grad, *sums_one))
    arrived_grad = after(arrived_grad, other_stuff_one)
    got_one = send_pieces(sums_one)

    result, stuff_zero = call(
        functools.partial(expert_backward_kernel, z, 0),
        (buffer, stuff_shape),
        (core, arrived_zero, arrived_grad, *experts, *given_zero),
        [SMEM, VMEM, VMEM, HBM, HBM, HBM, HBM],
        expert_scratch(z, 1),
        grant=28,
        cost=8,
    )
    back_grad = after(exchange(result), got_one)
    whole_one = pieces_sum(after(got_one, back_grad)).reshape(z.half_rows, z.width)
    whole_one = lax.psum(whole_one, "expert").reshape(part.shape)
    pair_zero, slab_zero = call(
        functools.partial(fourth_kernel, z),
        (pair_shape, slab_shape),
        (
            core, place, out_zero, pair_one, tokens_in, *route_pair, *weights_zero,
            back_zero, back_grad, *kept_zero,
        ),
        [SMEM, SMEM, VMEM, VMEM, VMEM, VMEM, VMEM] + [ANY] * 8 + [VMEM] * 7,
        scratch,
        cost=8,
    )

    sums_zero = partial_sums(slab_zero, 0)
    got_zero = send_pieces(sums_zero)
    other_stuff_zero = cross(after(stuff_zero, sums_zero), 0)
    other_pairs = (cross(pair_zero, 0), cross(pair_one, 1))

    chunks = z.hidden // z.chunk
    grad_w_in, grad_w_out = call(
        functools.partial(expert_weights_kernel, z),
        (shape(z.width, z.hidden), shape(z.hidden, z.width)),
        (
            core, after(stuff_zero, sums_zero), other_stuff_zero, stuff_one, other_stuff_one,
        ),
        [SMEM, HBM, HBM, HBM, HBM],
        [
            pltpu.VMEM((2 * z.expert_rows, stuff_shape.shape[1]), BF16),
            pltpu.VMEM((z.width, 2 * z.expert_rows), BF16),
            pltpu.SemaphoreType.DMA((2,)),
        ],
        grant=28,
        cost=9,
        grid=(chunks,),
        out_specs=(
            pl.BlockSpec((z.width, z.chunk), lambda i: (0, i)),
            pl.BlockSpec((z.chunk, z.width), lambda i: (i, 0)),
        ),
    )

    got_zero = after(got_zero, whole_one, grad_w_in, other_pairs)
    scattered_zero = exchange(pieces_sum(got_zero), "expert")
    whole_zero = exchange(spread_sum(scattered_zero), "expert")

    matrix = shape(1, z.part, z.width)
    finals = call(
        functools.partial(final_kernel, z),
        (
            *[shape(1, micro_count, z.rows, z.width)] * 2,
            *[matrix] * 4,
            *[shape(1, z.part)] * 2,
            shape(1, z.experts, z.part),
            shape(1, z.bucket_part, z.heads),
        ),
        (
            core, whole_zero, swap(whole_zero), whole_one, swap(whole_one),
            pair_zero, other_pairs[0], pair_one, other_pairs[1],
        ),
        [SMEM] + [LOOSE] * 8,
        [pltpu.VMEM((z.half_rows, z.width), F32), pltpu.VMEM((z.part, z.small), F32)],
        cost=3,
    )
    finals = (*finals[:8], jnp.swapaxes(finals[8], 1, 2), finals[9])
    return (*finals, grad_w_in[None, None], grad_w_out[None, None])


def solution(mesh):
    both = ("expert", "shard")
    plain = P("section", "shard", None)
    gains = P("section", "shard")
    blocks = P("section", None, both, None)
    experts = P("section", both, None, None)
    tokens = P(None, both, None)
    attention = (plain, plain, plain, plain, gains, gains, plain, plain, experts, experts)
    return jax.shard_map(
        shards,
        mesh=mesh,
        in_specs=(tokens, tokens, tokens, blocks, *attention),
        out_specs=(blocks, blocks, *attention),
        check_vma=False,
    )
```

```python
import functools

import jax
import jax.numpy as jnp
from jax import lax
from jax.experimental import pallas as pl
from jax.experimental.pallas import tpu as pltpu
from jax.sharding import PartitionSpec as P

EPSILON = 1e-06
BOUNDS = (8, 12, 16, 23, 32, 46, 64, 91)
MASKED = -1e30
F32 = jnp.float32
BF16 = jnp.bfloat16
I32 = jnp.int32
GELU_SCALE = 0.7978845608028654
GELU_CUBE = 0.044715
SMEM = pl.BlockSpec(memory_space=pltpu.SMEM)
VMEM = pl.BlockSpec(memory_space=pltpu.VMEM)
LOOSE = pl.BlockSpec(memory_space=pltpu.VMEM)
HBM = pl.BlockSpec(memory_space=pltpu.HBM)
ANY = pl.BlockSpec(memory_space=pl.ANY)


def dot_nn(a, b):
    return jnp.dot(a, b, preferred_element_type=F32)


def dot_nt(a, b):
    return lax.dot_general(a, b, (((1,), (1,)), ((), ())), preferred_element_type=F32)


def dot_tn(a, b):
    return lax.dot_general(a, b, (((0,), (0,)), ((), ())), preferred_element_type=F32)


def iota(shape, dimension):
    return lax.broadcasted_iota(I32, shape, dimension)


def call(body, outs, ins, specs, scratch=(), grant=24, cost=5, loose=(), **more):
    ins = [
        value if spec is SMEM or spec is LOOSE else pltpu.with_memory_space_constraint(value, pltpu.HBM)
        for value, spec in zip(ins, specs)
    ]
    single = not isinstance(outs, tuple)
    outs = (outs,) if single else outs
    outs = tuple(
        out if i in loose else pltpu.HBM(out.shape, out.dtype) for i, out in enumerate(outs)
    )
    more.setdefault("out_specs", (VMEM,) * len(outs))
    made = pl.pallas_call(
        body,
        out_shape=outs,
        in_specs=specs,
        scratch_shapes=scratch,
        compiler_params=pltpu.CompilerParams(vmem_limit_bytes=grant * 1024 * 1024),
        cost_estimate=pl.CostEstimate(
            flops=int(cost * 1e8), bytes_accessed=int(cost * 4e5), transcendentals=0
        ),
        **more,
    )(*ins)
    return made[0] if single else made


def bucket_of(relative):
    distance = jnp.abs(relative)
    bucket = jnp.zeros_like(relative)
    for lowest in tuple(range(1, 8)) + BOUNDS:
        bucket = bucket + (distance >= lowest).astype(I32)
    return bucket + 16 * (relative > 0).astype(I32)


class Sizes:
    def __init__(self, tokens_in, w_query, w_router, bias_table, w_in, shards):
        self.rows, self.width = tokens_in.shape[1:]
        self.part = w_query.shape[1]
        self.shards = shards
        self.experts = w_router.shape[2]
        self.bucket_part, self.heads = bias_table.shape[1:]
        self.buckets = self.bucket_part * shards
        self.hidden = w_in.shape[3]
        self.chunk = self.hidden // 6
        self.capacity = max(
            2, (3 * self.rows + 2 * self.experts - 1) // (2 * self.experts)
        )
        self.full, rest = divmod(self.capacity, 8)
        self.rest = next((power for power in (0, 1, 2, 4) if power >= rest), None)
        if self.rest is None:
            self.full, self.rest = (self.full + 1, 0)
        self.cuts = 8 // self.rest if self.rest else 0
        self.cut = self.width // self.cuts if self.rest else 0
        self.slot_width = self.full * self.width + self.cut
        self.slot_rows = self.experts * 8
        self.expert_rows = self.slot_rows * self.full + self.experts * self.rest
        self.small = -(-(self.experts + self.heads + 2) // 128) * 128
        self.small_groups = self.width // self.small
        self.small_rows = self.part // self.small_groups
        self.gain_lane = self.experts + self.heads
        self.piece = 4 * self.part + self.small_rows
        self.half_rows = 2 * self.part + self.small_rows
        self.slab = 6 * self.width + self.small * self.width // self.rows


def slot_picks(z, route):
    onehot = (route == iota((z.rows, z.experts), 1)).astype(F32)
    lower = (iota((z.rows, z.rows), 0) >= iota((z.rows, z.rows), 1)).astype(F32).astype(BF16)
    running = dot_nn(lower, onehot.astype(BF16))
    place = jnp.sum(running * onehot, axis=1, keepdims=True).astype(I32) - 1
    slots = iota((z.rows, z.slot_rows), 1)

    def pick(first, wide, shift):
        inside = (place >= first) & (place < first + wide)
        target = jnp.where(inside, route * 8 + place - first + shift, -1)
        return (slots == target).astype(F32).astype(BF16)

    picks = [pick(8 * i, 8, 0) for i in range(z.full)]
    return picks + [pick(8 * z.full, z.rest, z.rest * i) for i in range(z.cuts)]


def cut_sum(z, picks, values):
    return sum(dot_tn(pick, values[:, i * z.cut : (i + 1) * z.cut]) for i, pick in enumerate(picks))


def put_slots(z, ref, offset, picks, values):
    for i in range(z.full):
        block = dot_tn(picks[i], values)
        ref[:, :, offset : offset + z.width] = block.reshape(z.experts, 8, z.width).astype(BF16)
        offset += z.width
    if z.rest:
        block = cut_sum(z, picks[z.full :], values)
        ref[:, :, offset : offset + z.cut] = block.reshape(z.experts, 8, z.cut).astype(BF16)


def read_slots(z, ref, offset, wide):
    block = ref[:, :, offset : offset + wide].astype(F32)
    return block.reshape(z.slot_rows, wide).astype(BF16)


def get_slots(z, ref, offset, picks):
    total = 0.0
    for i in range(z.full):
        total += dot_nn(picks[i], read_slots(z, ref, offset, z.width))
        offset += z.width
    if z.rest:
        block = read_slots(z, ref, offset, z.cut)
        total += jnp.concatenate([dot_nn(pick, block) for pick in picks[z.full :]], axis=1)
    return total


def extra_picks(z):
    shape = (z.experts * z.rest, z.slot_rows)
    rows, slots = (iota(shape, 0), iota(shape, 1))
    first = (rows // z.rest) * 8 + rows % z.rest
    return [(slots == first + z.rest * i).astype(F32).astype(BF16) for i in range(z.cuts)]


def rows_of_slots(z, ref, offset):
    parts = []
    for i in range(z.full):
        parts.append(read_slots(z, ref, offset, z.width))
        offset += z.width
    if z.rest:
        block = read_slots(z, ref, offset, z.cut)
        pieces = [dot_nn(pick, block) for pick in extra_picks(z)]
        parts.append(jnp.concatenate(pieces, axis=1).astype(BF16))
    return jnp.concatenate(parts, axis=0) if len(parts) > 1 else parts[0]


def slots_of_rows(z, ref, offset, rows):
    for i in range(z.full):
        block = rows[i * z.slot_rows : (i + 1) * z.slot_rows]
        ref[:, :, offset : offset + z.width] = block.reshape(z.experts, 8, z.width).astype(BF16)
        offset += z.width
    if z.rest:
        block = cut_sum(z, extra_picks(z), rows[z.full * z.slot_rows :].astype(BF16))
        ref[:, :, offset : offset + z.cut] = block.reshape(z.experts, 8, z.cut).astype(BF16)


def fetch_weights(z, mine, place, own, other, mats, packed, sems, order=(4, 0, 1, 2, 3)):
    def copy(pieces, i, k):
        shard = place ^ k
        count = z.small_rows if i == 4 else z.part
        start = i * z.part
        source = pieces[k]
        target = pl.ds(pl.multiple_of(shard * count, 16), count)
        held = packed.at[target] if i == 4 else mats.at[i, target]
        return pltpu.make_async_copy(source.at[pl.ds(start, count)], held, sems.at[i, k])

    def start(pieces):
        for i in order:
            for k in range(z.shards):
                copy(pieces, i, k).start()

    def wait(i):
        for k in range(z.shards):
            copy(own, i, k).wait()

    @pl.when(mine)
    def _():
        start(own)

    @pl.when(jnp.logical_not(mine))
    def _():
        start(other)

    return [functools.partial(wait, i) for i in range(5)]


def fetch_halves(z, core, own, other, mats, packed, sems, order=(4, 0, 1, 2, 3)):
    def copy(source, i, k):
        count = z.small_rows if i == 4 else z.part
        start = k * z.half_rows + (i if i < 2 else i - 2) * z.part
        target = pl.ds(k * count, count)
        held = packed.at[target] if i == 4 else mats.at[i, target]
        return pltpu.make_async_copy(source.at[pl.ds(start, count)], held, sems.at[i, k])

    def start(first, second):
        for i in order:
            for k in range(z.shards):
                copy(first if i < 2 else second, i, k).start()

    def wait(i):
        for k in range(z.shards):
            copy(own, i, k).wait()

    @pl.when(core == 0)
    def _():
        start(own, other)

    @pl.when(core != 0)
    def _():
        start(other, own)

    return [functools.partial(wait, i) for i in range(5)]


def weight_scratch(z):
    return [
        pltpu.VMEM((4, z.width, z.width), BF16),
        pltpu.VMEM((z.shards * z.small_rows, z.width), BF16),
        pltpu.VMEM((z.width, z.small), BF16),
        pltpu.SemaphoreType.DMA((5, z.shards)),
    ]


def unpack_small(z, packed, small):
    for j in range(z.shards):
        for g in range(z.small_groups):
            row = j * z.part + g * z.small_rows
            small[row : row + z.small_rows, :] = packed[
                j * z.small_rows : (j + 1) * z.small_rows, g * z.small : (g + 1) * z.small
            ]


def bucket_rows(z):
    rows, buckets = (iota((z.width, z.buckets), 0), iota((z.width, z.buckets), 1))
    held = (buckets // z.bucket_part) * z.part + buckets % z.bucket_part
    return (rows == held).astype(F32).astype(BF16)


def bucket_lanes(z):
    shape = (z.buckets, 2 * z.rows)
    return (bucket_of(iota(shape, 1) - z.rows) == iota(shape, 0)).astype(F32).astype(BF16)


def identity(size):
    return (iota((size, size), 0) == iota((size, size), 1)).astype(F32).astype(BF16)


def gain_rows(z, small):
    rows, lanes = (iota((8, z.small), 0), iota((8, z.small), 1))
    pick = ((lanes == z.gain_lane + rows) & (rows < 2)).astype(F32).astype(BF16)
    made = dot_nt(pick, small)
    return (made[0:1], made[1:2])


def unit_rows(values):
    inverse = lax.rsqrt(jnp.mean(values * values, axis=-1, keepdims=True) + EPSILON)
    return (values * inverse, inverse)


def pair_masks(z):
    lanes = iota((z.rows, 128), 1)
    first = (lanes < 64).astype(F32).astype(BF16)
    return (first, (lanes >= 64).astype(F32).astype(BF16))


def double(values, masks):
    return jnp.concatenate([values * masks[0], values * masks[1]], axis=0)


def attend(z, inputs, waits, mats, packed, small, lengths, section, qkv_ref, probs_ref, attended_ref):
    waits[4]()
    unpack_small(z, packed, small)
    small_full = small[...]
    gain_one, gain_two = gain_rows(z, small_full)
    normed_one = (unit_rows(inputs)[0] * gain_one).astype(BF16)
    for i in range(3):
        waits[i]()
        qkv_ref[:, i * z.width : (i + 1) * z.width] = dot_nn(normed_one, mats[i]).astype(BF16)

    table = dot_tn(bucket_rows(z), small_full).astype(BF16)
    bias = dot_tn(table, bucket_lanes(z))[z.experts : z.experts + z.heads]

    rows, lanes = (iota((z.rows, z.rows), 0), iota((z.rows, z.rows), 1))
    segment_q, segment_k = (jnp.zeros_like(rows), jnp.zeros_like(rows))
    end = jnp.int32(0)
    for i in range(lengths.shape[2]):
        end = end + lengths[section, 0, i]
        segment_q += (rows >= end).astype(I32)
        segment_k += (lanes >= end).astype(I32)
    visible = segment_q == segment_k

    masks = pair_masks(z)
    scale = 64 ** (-0.5)
    for p in range(z.heads // 2):
        at = slice(p * 128, (p + 1) * 128)
        query = qkv_ref[:, p * 128 : (p + 1) * 128]
        key = qkv_ref[:, z.width + p * 128 : z.width + (p + 1) * 128]
        value = qkv_ref[:, 2 * z.width + p * 128 : 2 * z.width + (p + 1) * 128]
        scores = dot_nt(query, double(key, masks)) * scale
        halves = []
        for i in range(2):
            spread = jnp.broadcast_to(bias[2 * p + i : 2 * p + i + 1], (z.rows, 2 * z.rows))
            spread = pltpu.roll(spread, z.rows, 1, stride=1, stride_axis=0)[:, : z.rows]
            part = scores[:, i * z.rows : (i + 1) * z.rows] + spread
            part = jnp.where(visible, part, MASKED)
            part = jnp.exp(part - jnp.max(part, axis=-1, keepdims=True))
            halves.append(part / jnp.sum(part, axis=-1, keepdims=True))
        probs = jnp.concatenate(halves, axis=1).astype(BF16)
        probs_ref[p] = probs
        attended_ref[:, at] = dot_nn(probs, double(value, masks)).astype(BF16)

    waits[3]()
    middle = inputs + dot_nn(attended_ref[...], mats[3])
    normed_two = (unit_rows(middle)[0] * gain_two).astype(BF16)
    logits = dot_nn(normed_two, small_full)
    logits = jnp.where(iota((z.rows, z.small), 1) < z.experts, logits, MASKED)
    logits = jnp.exp(logits - jnp.max(logits, axis=-1, keepdims=True))
    router = logits / jnp.sum(logits, axis=-1, keepdims=True)
    return (middle, normed_two, router)


def chosen(z, route):
    return (route == iota((z.rows, z.small), 1)).astype(F32)


def attend_back(
    z, grad_out, token_out, grad_token, inputs, route, waits, mats, packed, small, kept, slab_ref
):
    qkv_ref, probs_ref, attended_ref, middle_ref, router_ref = kept
    waits[4]()
    unpack_small(z, packed, small)
    small_full = small[...]
    gain_one, gain_two = gain_rows(z, small_full)
    onehot = chosen(z, route)
    router = router_ref[...]
    gate = jnp.sum(router * onehot, axis=1, keepdims=True)
    grad_gate = jnp.sum(grad_out * token_out, axis=1, keepdims=True)
    grad_logits = (grad_gate * gate * (onehot - router)).astype(BF16)
    unit_two, inverse_two = unit_rows(middle_ref[...])
    grad_small = dot_tn((unit_two * gain_two).astype(BF16), grad_logits)
    grad_normed = grad_token + dot_nt(grad_logits, small_full)
    gain_two_grad = jnp.sum(grad_normed * unit_two, axis=0, keepdims=True)
    grad_unit = grad_normed * gain_two
    grad_unit -= unit_two * jnp.mean(grad_unit * unit_two, axis=1, keepdims=True)
    grad_middle = grad_out + inverse_two * grad_unit
    grad_branch = grad_middle.astype(BF16)
    slab_ref[:, 4 * z.width : 5 * z.width] = attended_ref[...]
    slab_ref[:, 5 * z.width : 6 * z.width] = grad_branch
    waits[3]()
    grad_attended = dot_nt(grad_branch, mats[3]).astype(BF16)

    masks = pair_masks(z)
    scale = 64 ** (-0.5)
    relative = []
    turn = iota((z.rows, z.rows), 0) + iota((z.rows, z.rows), 1) == z.rows - 1
    turn = turn.astype(F32).astype(BF16)
    for p in range(z.heads // 2):
        at = slice(p * 128, (p + 1) * 128)
        query = qkv_ref[:, p * 128 : (p + 1) * 128]
        keys = double(qkv_ref[:, z.width + p * 128 : z.width + (p + 1) * 128], masks)
        values = double(qkv_ref[:, 2 * z.width + p * 128 : 2 * z.width + (p + 1) * 128], masks)
        grad_heads = grad_attended[:, at]
        probs_low = probs_ref[p]
        probs = probs_low.astype(F32)
        grad_probs = dot_nt(grad_heads, values)
        halves = []
        for i in range(2):
            part = slice(i * z.rows, (i + 1) * z.rows)
            product = grad_probs[:, part] * probs[:, part]
            dots = jnp.sum(product, axis=-1, keepdims=True)
            grads = (product - probs[:, part] * dots).astype(BF16)
            halves.append(grads)
        grad_scores = jnp.concatenate(halves, axis=1)
        turned = dot_nn(turn, grad_scores)
        for i in range(2):
            wide = [turned[:, i * z.rows : (i + 1) * z.rows], jnp.zeros((z.rows, z.rows), F32)]
            wide = pltpu.roll(jnp.concatenate(wide, axis=1), 1, 1, stride=1, stride_axis=0)
            relative.append(jnp.sum(wide, axis=0, keepdims=True))
        start = z.width + p * 128
        slab_ref[:, start : start + 128] = (dot_nn(grad_scores, keys) * scale).astype(BF16)
        made = dot_tn(grad_scores, query) * scale
        mask = masks[0].astype(F32)
        made = made[: z.rows] * mask + made[z.rows :] * (1.0 - mask)
        slab_ref[:, start + z.width : start + z.width + 128] = made.astype(BF16)
        made = dot_tn(probs_low, grad_heads)
        made = made[: z.rows] * mask + made[z.rows :] * (1.0 - mask)
        slab_ref[:, start + 2 * z.width : start + 2 * z.width + 128] = made.astype(BF16)

    unit_one, inverse_one = unit_rows(inputs)
    slab_ref[:, : z.width] = (unit_one * gain_one).astype(BF16)
    grad_normed = 0.0
    for i in range(3):
        waits[i]()
        grad_normed += dot_nt(slab_ref[:, (i + 1) * z.width : (i + 2) * z.width], mats[i])
    gain_one_grad = jnp.sum(grad_normed * unit_one, axis=0, keepdims=True)
    grad_unit = grad_normed * gain_one
    grad_unit -= unit_one * jnp.mean(grad_unit * unit_one, axis=1, keepdims=True)
    grad_in = (grad_middle + inverse_one * grad_unit).astype(BF16)

    relative += [jnp.zeros((1, 2 * z.rows), F32)] * (-z.heads % 8)
    relative = jnp.concatenate(relative, axis=0)
    lanes_of = bucket_lanes(z)
    high = relative.astype(BF16)
    table = dot_nt(lanes_of, high) + dot_nt(lanes_of, (relative - high.astype(F32)).astype(BF16))
    count = relative.shape[0]
    places = iota((count, z.small), 1) == iota((count, z.small), 0) + z.experts
    places = places & (iota((count, z.small), 0) < z.heads)
    table = dot_nn(table.astype(BF16), places.astype(F32).astype(BF16)).astype(BF16)
    grad_small += dot_nn(bucket_rows(z), table)
    gains = jnp.concatenate([gain_one_grad, gain_two_grad, jnp.zeros((6, z.width), F32)], axis=0)
    rows, lanes = (iota((8, z.small), 0), iota((8, z.small), 1))
    pick = ((lanes == z.gain_lane + rows) & (rows < 2)).astype(F32).astype(BF16)
    grad_small += dot_tn(gains.astype(BF16), pick)
    for i in range(z.width // z.rows):
        start = 6 * z.width + i * z.small
        slab_ref[:, start : start + z.small] = grad_small[i * z.rows : (i + 1) * z.rows].astype(BF16)
    return grad_in


def pack_kernel(z, query, key, value, output, router, gain_one, gain_two, table, piece, small, sems):
    copies = [
        pltpu.make_async_copy(source.at[0], piece.at[pl.ds(i * z.part, z.part)], sems.at[i])
        for i, source in enumerate((query, key, value, output))
    ]
    for copy in copies:
        copy.start()
    gains = [gain_one[...].astype(F32), gain_two[...].astype(F32), jnp.zeros((6, z.part), F32)]
    rows, lanes = (iota((8, z.small), 0), iota((8, z.small), 1))
    pick = ((lanes == z.gain_lane + rows) & (rows < 2)).astype(F32).astype(BF16)
    small[...] = dot_tn(jnp.concatenate(gains, axis=0).astype(BF16), pick)
    small[:, : z.experts] = dot_tn(router[0], identity(z.experts))
    small[: z.bucket_part, z.experts : z.gain_lane] = table[0].astype(F32)
    for g in range(z.small_groups):
        piece[4 * z.part :, g * z.small : (g + 1) * z.small] = small[
            g * z.small_rows : (g + 1) * z.small_rows
        ].astype(BF16)
    for copy in copies:
        copy.wait()


def first_kernel(
    z, section, place, lengths, tokens, own_route, other_route, o0, o1, o2, o3, r0, r1, r2, r3,
    send, qkv, probs, attended, middle_ref, router_ref,
    mats, packed, small, sems,
):
    core = section[0]
    waits = fetch_weights(
        z, core == 0, place[0], (o0, o1, o2, o3), (r0, r1, r2, r3), mats, packed, sems)
    inputs = tokens[core].astype(F32)
    middle, normed_two, router = attend(
        z, inputs, waits, mats, packed, small, lengths, core, qkv, probs, attended
    )
    middle_ref[...] = middle
    router_ref[...] = router
    route = jnp.where(core == 0, own_route[core], other_route[...])
    put_slots(z, send, 0, slot_picks(z, route), normed_two)


def second_kernel(
    z, section, lengths, cotangent, own_route, other_route, own, other, back, middle_zero, router_zero,
    send, out_zero, qkv, probs, attended, middle_ref, router_ref,
    mats, packed, small, sems,
):
    core = section[0]
    waits = fetch_halves(
        z, core, own, other, mats, packed, sems)
    route = jnp.where(core == 0, own_route[core], other_route[...])
    gate = jnp.sum(router_zero[...] * chosen(z, route), axis=1, keepdims=True)
    token_out = get_slots(z, back, 0, slot_picks(z, route))
    layer_out = (middle_zero[...] + gate * token_out).astype(BF16)
    out_zero[...] = layer_out
    middle, normed_two, router = attend(
        z, layer_out.astype(F32), waits, mats, packed, small, lengths, core, qkv, probs, attended
    )
    middle_ref[...] = middle
    router_ref[...] = router
    route = jnp.where(core == 1, own_route[core], other_route[...])
    picks = slot_picks(z, route)
    put_slots(z, send, 0, picks, normed_two)
    gate = jnp.sum(router * chosen(z, route), axis=1, keepdims=True)
    grad = (gate * cotangent[core].astype(F32)).astype(BF16)
    put_slots(z, send, z.slot_width, picks, grad)


def third_kernel(
    z, section, cotangent, own_route, other_route, own, other, back, inputs, router_zero,
    qkv, probs, attended, middle, router,
    send, pair, slab,
    mats, packed, small, sems,
):
    core = section[0]
    waits = fetch_halves(
        z, core, own, other, mats, packed, sems, (4, 3, 0, 1, 2))
    route = jnp.where(core == 1, own_route[core], other_route[...])
    picks = slot_picks(z, route)
    token_out = get_slots(z, back, 0, picks)
    grad_token = get_slots(z, back, z.slot_width, picks)
    gate = jnp.sum(router[...] * chosen(z, route), axis=1, keepdims=True)
    pair[0] = (middle[...] + gate * token_out).astype(BF16)
    grad_in = attend_back(
        z, cotangent[core].astype(F32), token_out, grad_token, inputs[...].astype(F32), route,
        waits, mats, packed, small, (qkv, probs, attended, middle, router), slab,
    )
    pair[1] = grad_in
    route = jnp.where(core == 0, own_route[core], other_route[...])
    gate = jnp.sum(router_zero[...] * chosen(z, route), axis=1, keepdims=True)
    grad = (gate * grad_in.astype(F32)).astype(BF16)
    put_slots(z, send, 0, slot_picks(z, route), grad)


def fourth_kernel(
    z, section, place, out_zero, pair_one, tokens, own_route, other_route, o0, o1, o2, o3, r0, r1, r2, r3, back_out, back_grad,
    qkv, probs, attended, middle, router,
    pair, slab,
    mats, packed, small, sems,
):
    core = section[0]
    waits = fetch_weights(
        z, core == 0, place[0], (o0, o1, o2, o3), (r0, r1, r2, r3), mats, packed, sems, (4, 3, 0, 1, 2))
    route = jnp.where(core == 0, own_route[core], other_route[...])
    picks = slot_picks(z, route)
    token_out = get_slots(z, back_out, 0, picks)
    grad_token = get_slots(z, back_grad, 0, picks)
    pair[0] = out_zero[...]
    pair[1] = attend_back(
        z, pair_one[1].astype(F32), token_out, grad_token, tokens[core].astype(F32), route,
        waits, mats, packed, small, (qkv, probs, attended, middle, router), slab,
    )


def fetch_experts(z, mine, own_in, own_out, other_in, other_out, w_in, w_out, sems):
    def copies(source_in, source_out, c):
        at = pl.ds(c * z.chunk, z.chunk)
        return (
            pltpu.make_async_copy(source_in.at[:, at], w_in.at[c], sems.at[2 * c]),
            pltpu.make_async_copy(source_out.at[at], w_out.at[c], sems.at[2 * c + 1]),
        )

    def start(source_in, source_out):
        for c in range(z.hidden // z.chunk):
            for copy in copies(source_in, source_out, c):
                copy.start()

    @pl.when(mine)
    def _():
        start(own_in, own_out)

    @pl.when(jnp.logical_not(mine))
    def _():
        start(other_in, other_out)

    def wait(c):
        for copy in copies(own_in, own_out, c):
            copy.wait()

    return wait


def expert_scratch(z, sums):
    chunks = z.hidden // z.chunk
    return [
        pltpu.VMEM((chunks, z.width, z.chunk), BF16),
        pltpu.VMEM((chunks, z.chunk, z.width), BF16),
        pltpu.SemaphoreType.DMA((2 * chunks,)),
    ] + [pltpu.VMEM((z.expert_rows, z.width), F32)] * sums


def smooth(values):
    square = values * values
    bent = jnp.tanh(GELU_SCALE * values * (1.0 + GELU_CUBE * square))
    return (0.5 * values * (1.0 + bent), square, bent)


def smooth_slope(values, square, bent):
    inner = GELU_SCALE * (1.0 + 3.0 * GELU_CUBE * square)
    return 0.5 * (1.0 + bent) + 0.5 * values * (1.0 - bent * bent) * inner


def expert_forward_kernel(
    z, section, arrived, own_in, own_out, other_in, other_out, result, w_in, w_out, sems, produced
):
    wait = fetch_experts(
        z, section[0] == 0, own_in, own_out, other_in, other_out, w_in, w_out, sems
    )
    rows = rows_of_slots(z, arrived, 0)
    for c in range(z.hidden // z.chunk):
        wait(c)
        hidden = smooth(dot_nn(rows, w_in[c]))[0].astype(BF16)
        made = dot_nn(hidden, w_out[c])
        produced[...] = made if c == 0 else produced[...] + made
    slots_of_rows(z, result, 0, produced[...])


def expert_backward_kernel(
    z, layer, section, arrived, arrived_grad, own_in, own_out, other_in, other_out,
    result, stuff, w_in, w_out, sems, grad_sum, *produced
):
    wait = fetch_experts(
        z, section[0] == layer, own_in, own_out, other_in, other_out, w_in, w_out, sems
    )
    rows = rows_of_slots(z, arrived, 0)
    grads = rows_of_slots(z, arrived_grad, z.slot_width if produced else 0)
    stuff[:, 2 * z.hidden : 2 * z.hidden + z.width] = rows
    stuff[:, 2 * z.hidden + z.width : 2 * z.hidden + 2 * z.width] = grads
    for c in range(z.hidden // z.chunk):
        wait(c)
        before = dot_nn(rows, w_in[c])
        hidden, square, bent = smooth(before)
        hidden = hidden.astype(BF16)
        stuff[:, c * z.chunk : (c + 1) * z.chunk] = hidden
        if produced:
            made = dot_nn(hidden, w_out[c])
            produced[0][...] = made if c == 0 else produced[0][...] + made
        grad_pre = dot_nt(grads, w_out[c]) * smooth_slope(before, square, bent)
        grad_pre = grad_pre.astype(BF16)
        stuff[:, z.hidden + c * z.chunk : z.hidden + (c + 1) * z.chunk] = grad_pre
        made = dot_nt(grad_pre, w_in[c])
        grad_sum[...] = made if c == 0 else grad_sum[...] + made
    if produced:
        slots_of_rows(z, result, 0, produced[0][...])
    slots_of_rows(z, result, z.slot_width if produced else 0, grad_sum[...])


def expert_weights_kernel(
    z, section, own_zero, other_zero, own_one, other_one, grad_in, grad_out, held, turned, sems
):
    step = pl.program_id(0)

    @pl.when(step == 0)
    def _():
        def copies(own, other):
            return [
                pltpu.make_async_copy(
                    source, held.at[pl.ds(i * z.expert_rows, z.expert_rows)], sems.at[i]
                )
                for i, source in enumerate((own, other))
            ]

        @pl.when(section[0] == 0)
        def _():
            for copy in copies(own_zero, other_zero):
                copy.start()

        @pl.when(section[0] != 0)
        def _():
            for copy in copies(own_one, other_one):
                copy.start()

        for copy in copies(own_zero, other_zero):
            copy.wait()
        rows = held[:, 2 * z.hidden : 2 * z.hidden + z.width]
        turned[...] = jnp.transpose(rows.astype(F32)).astype(BF16)

    start = pl.multiple_of(step * z.chunk, z.chunk)
    grad_pre = held[:, pl.ds(z.hidden + start, z.chunk)]
    hidden = held[:, pl.ds(start, z.chunk)]
    grads = held[:, 2 * z.hidden + z.width : 2 * z.hidden + 2 * z.width]
    grad_in[...] = dot_nn(turned[...], grad_pre).astype(BF16)
    grad_out[...] = dot_tn(hidden, grads).astype(BF16)


def attention_weights_kernel(z, layer, section, place, own, other, *refs):
    outs, made = (refs[: z.shards], refs[z.shards])
    second = section[0] ^ layer

    def both(column):
        at = pl.ds(pl.multiple_of(column * z.width, 128), z.width)
        return jnp.concatenate([own[:, at], other[:, at]], axis=0)

    for i, (left, right) in enumerate(
        ((0, 1 + 2 * second), (4 * second, 2 + 3 * second))
    ):
        made[...] = dot_tn(both(left), both(right))
        for k in range(z.shards):
            start = pl.multiple_of((place[0] ^ k) * z.part, 16)
            outs[k][i * z.part : (i + 1) * z.part] = made[pl.ds(start, z.part)].astype(BF16)
    for i in range(z.width // z.rows):
        columns = slice(6 * z.width + i * z.small, 6 * z.width + (i + 1) * z.small)
        total = own[:, columns].astype(F32) + other[:, columns].astype(F32)
        made[i * z.rows : (i + 1) * z.rows, : z.small] = total
    for k in range(z.shards):
        for g in range(z.small_groups):
            start = pl.multiple_of((place[0] ^ k) * z.part + g * z.small_rows, 16)
            outs[k][2 * z.part :, g * z.small : (g + 1) * z.small] = made[
                pl.ds(start, z.small_rows), : z.small
            ].astype(BF16)


def pieces_sum_kernel(*refs):
    out = refs[-1]
    rows = out.shape[1]
    total = sum(piece[...].astype(F32) for piece in refs[:-1])
    for i in range(out.shape[0]):
        out[i] = total[i * rows : (i + 1) * rows].astype(BF16)


def parted_sum_kernel(*refs):
    first, out = refs[-2:]
    rows = out.shape[1]
    total = sum(piece[...].astype(F32) for piece in refs[:-2])
    first[...] = total[: first.shape[0]].astype(BF16)
    for i in range(out.shape[0]):
        start = first.shape[0] + i * rows
        out[i] = total[start : start + rows].astype(BF16)


def spread_sum_kernel(pieces, out):
    total = sum(pieces[i].astype(F32) for i in range(pieces.shape[0])).astype(BF16)
    for i in range(out.shape[0]):
        out[i] = total


def final_kernel(
    z, section, own_first, got_first, own_zero, got_zero, own_one, got_one, pair_zero, other_zero, pair_one, other_one,
    layer_out, input_grad, query, key, value, output, gain_one, gain_two, router, table, held, small,
):
    def parts_of(first, parts):
        rest = [parts.at[i] for i in range(parts.shape[0])]
        return rest if first is None else [first, *rest]

    def finish(own, other, micros):
        for parts, targets in ((own, (query, key)), (other, (value, output))):
            start = 0
            for part in parts:
                rows = part.shape[0]
                held[start : start + rows] = part[...].astype(F32)
                start += rows
            for i, target in enumerate(targets):
                target[0] = held[i * z.part : (i + 1) * z.part].astype(BF16)
            if parts is own:
                for g in range(z.small_groups):
                    small[g * z.small_rows : (g + 1) * z.small_rows] = held[
                        2 * z.part :, g * z.small : (g + 1) * z.small
                    ]
        for i, pair in enumerate(micros):
            layer_out[0, i] = pair[0]
            input_grad[0, i] = pair[1]

    @pl.when(section[0] == 0)
    def _():
        finish(parts_of(own_first, own_zero), parts_of(got_first, got_zero), (pair_zero, other_zero))

    @pl.when(section[0] != 0)
    def _():
        finish(parts_of(None, own_one), parts_of(None, got_one), (other_one, pair_one))

    gains = gain_rows(z, small[...].astype(BF16))
    gain_one[...] = gains[0].astype(BF16)
    gain_two[...] = gains[1].astype(BF16)
    router[0] = dot_nt(identity(z.experts), small[:, : z.experts].astype(BF16)).astype(BF16)
    table[0] = small[: z.bucket_part, z.experts : z.gain_lane].astype(BF16)


def swap(value):
    return lax.ppermute(value, "section", [(0, 1), (1, 0)])


def cross(value, target):
    return lax.ppermute(value, "section", [(1 - target, target)])


def within(value, distance, layer):
    size = lax.axis_size("shard")
    pairs = [(layer * size + i, layer * size + (i ^ distance)) for i in range(size)]
    return lax.ppermute(value, ("section", "shard"), pairs)


def exchange(buffer, axes=("expert", "shard")):
    return lax.all_to_all(buffer, axes, split_axis=0, concat_axis=0, tiled=True)


def shards(
    tokens_in,
    cotangent,
    lengths,
    routes,
    w_query,
    w_key,
    w_value,
    w_output,
    gain_attn,
    gain_moe,
    w_router,
    bias_table,
    w_in,
    w_out,
):
    z = Sizes(tokens_in, w_query, w_router, bias_table, w_in, lax.axis_size("shard"))
    micro_count = tokens_in.shape[0]
    section = lax.axis_index("section").astype(I32)
    core = section.reshape(1)
    place = lax.axis_index("shard").astype(I32).reshape(1)

    def shape(*dims, kind=BF16):
        return jax.ShapeDtypeStruct(dims, kind)

    own_route = routes[0]
    sent_route = lax.dynamic_index_in_dim(own_route, 1 - section, 0, keepdims=False)
    piece = call(
        functools.partial(pack_kernel, z),
        shape(z.piece, z.width),
        (
            w_query, w_key, w_value, w_output, jnp.swapaxes(w_router, 1, 2), gain_attn, gain_moe,
            bias_table,
        ),
        [HBM] * 4 + [VMEM] * 4,
        [pltpu.VMEM((z.part, z.small), F32), pltpu.SemaphoreType.DMA((4,))],
        grant=8,
        cost=2,
    )

    def spread(piece, layer):
        return (piece, *[within(piece, distance, layer) for distance in range(1, z.shards)])

    def after(values, *first):
        values, unused = lax.optimization_barrier((values, first))
        return values

    half = cross(piece[: z.half_rows], 0)
    half = jnp.where(section == 0, half, piece[z.piece - z.half_rows :])
    half_one = lax.all_gather(half, "shard", axis=0, tiled=True)

    piece, sent_route = lax.optimization_barrier((piece, sent_route))
    route_pair = (own_route, swap(sent_route))
    pieces = spread(piece, 0)
    experts = (w_in[0, 0], w_out[0, 0])
    given = [cross(piece, 1)]
    early = (given[0], route_pair[1], half)
    given += [cross(after(member, early), 1) for member in pieces[1:]]
    given_zero = tuple(cross(member, 1) for member in after(experts, given))
    weights_zero = (*pieces, *given)

    buffer = shape(z.experts, 8, z.slot_width)
    wide_buffer = shape(z.experts, 8, 2 * z.slot_width)
    kept = (
        shape(z.rows, 3 * z.width),
        shape(z.heads // 2, z.rows, 2 * z.rows),
        shape(z.rows, z.width),
        shape(z.rows, z.width, kind=F32),
        shape(z.rows, z.small, kind=F32),
    )
    scratch = weight_scratch(z)
    rows_shape = shape(z.rows, z.width)
    slab_shape = shape(z.rows, z.slab)

    sent, *kept_zero = call(
        functools.partial(first_kernel, z),
        (buffer, *kept),
        (core, place, lengths, tokens_in, *route_pair, *weights_zero),
        [SMEM, SMEM, SMEM, VMEM, VMEM, VMEM] + [ANY] * 8,
        scratch,
        cost=6,
        loose=(0,),
    )
    arrived_zero = exchange(sent)
    produced = call(
        functools.partial(expert_forward_kernel, z),
        buffer,
        (core, arrived_zero, *experts, *given_zero),
        [SMEM, LOOSE, HBM, HBM, HBM, HBM],
        expert_scratch(z, 1),
        cost=6,
        loose=(0,),
    )
    back_zero = exchange(produced)
    weights_one = (half_one, swap(after(half_one, produced)))
    given_one = tuple(cross(member, 0) for member in after(experts, produced))

    sent, out_zero, *kept_one = call(
        functools.partial(second_kernel, z),
        (wide_buffer, rows_shape, *kept),
        (core, lengths, cotangent, *route_pair, *weights_one, back_zero, *kept_zero[3:]),
        [SMEM, SMEM, VMEM, VMEM, VMEM] + [ANY] * 2 + [LOOSE] + [VMEM] * 2,
        scratch,
        cost=7,
        loose=(0,),
    )
    arrived_one = exchange(sent)
    stuff_shape = shape(z.expert_rows, 2 * z.hidden + 2 * z.width)
    result, stuff_one = call(
        lambda section, arrived, *rest: expert_backward_kernel(
            z, 1, section, arrived, arrived, *rest
        ),
        (wide_buffer, stuff_shape),
        (core, arrived_one, *experts, *given_one),
        [SMEM, LOOSE, HBM, HBM, HBM, HBM],
        expert_scratch(z, 2),
        grant=28,
        cost=10,
        loose=(0,),
    )
    back_one = exchange(result)

    pair_shape = shape(2, z.rows, z.width)
    sent, pair_one, slab_one = call(
        functools.partial(third_kernel, z),
        (buffer, pair_shape, slab_shape),
        (core, cotangent, *route_pair, *weights_one, back_one, out_zero, kept_zero[4], *kept_one),
        [SMEM, VMEM, VMEM, VMEM] + [ANY] * 2 + [LOOSE] + [VMEM] * 7,
        scratch,
        cost=8,
        loose=(0,),
    )
    arrived_grad = exchange(sent)

    count = lax.axis_size("expert")

    def partial_sums(slab, layer):
        return call(
            functools.partial(attention_weights_kernel, z, layer),
            (shape(z.half_rows, z.width),) * z.shards,
            (core, place, slab, swap(slab)),
            [SMEM, SMEM, VMEM, LOOSE],
            [pltpu.VMEM((z.width, z.width), F32)],
            cost=4,
        )

    def send_pieces(pieces):
        size = lax.axis_size("shard")
        got = [pieces[0]]
        for distance in range(1, z.shards):
            pairs = [(i, i ^ distance) for i in range(size)]
            got.append(lax.ppermute(pieces[distance], "shard", pairs))
        return tuple(got)

    part = shape(count, z.half_rows // count, z.width)

    def pieces_sum(pieces):
        return call(pieces_sum_kernel, part, pieces, [LOOSE] * z.shards, cost=2)

    sums_one = partial_sums(slab_one, 1)
    other_stuff_one = cross(stuff_one, 1)
    arrived_grad, *sums_one = lax.optimization_barrier((arrived_grad, *sums_one))
    arrived_grad = after(arrived_grad, other_stuff_one)
    got_one = send_pieces(sums_one)

    result, stuff_zero = call(
        functools.partial(expert_backward_kernel, z, 0),
        (buffer, stuff_shape),
        (core, arrived_zero, arrived_grad, *experts, *given_zero),
        [SMEM, VMEM, LOOSE, HBM, HBM, HBM, HBM],
        expert_scratch(z, 1),
        grant=28,
        cost=8,
        loose=(0,),
    )
    back_grad = after(exchange(result), got_one)
    whole_one = pieces_sum(after(got_one, back_grad)).reshape(z.half_rows, z.width)
    whole_one = lax.psum(whole_one, "expert").reshape(part.shape)
    pair_zero, slab_zero = call(
        functools.partial(fourth_kernel, z),
        (pair_shape, slab_shape),
        (
            core, place, out_zero, pair_one, tokens_in, *route_pair, *weights_zero,
            back_zero, back_grad, *kept_zero,
        ),
        [SMEM, SMEM, VMEM, VMEM, VMEM, VMEM, VMEM] + [ANY] * 8 + [VMEM] * 7,
        scratch,
        cost=8,
    )

    sums_zero = partial_sums(slab_zero, 0)
    got_zero = send_pieces(sums_zero)
    other_stuff_zero = cross(after(stuff_zero, sums_zero), 0)
    other_pairs = (cross(pair_zero, 0), cross(pair_one, 1))

    chunks = z.hidden // z.chunk
    grad_w_in, grad_w_out = call(
        functools.partial(expert_weights_kernel, z),
        (shape(z.width, z.hidden), shape(z.hidden, z.width)),
        (
            core, after(stuff_zero, sums_zero), other_stuff_zero, stuff_one, other_stuff_one,
        ),
        [SMEM, HBM, HBM, HBM, HBM],
        [
            pltpu.VMEM((2 * z.expert_rows, stuff_shape.shape[1]), BF16),
            pltpu.VMEM((z.width, 2 * z.expert_rows), BF16),
            pltpu.SemaphoreType.DMA((2,)),
        ],
        grant=28,
        cost=9,
        grid=(chunks,),
        out_specs=(
            pl.BlockSpec((z.width, z.chunk), lambda i: (0, i)),
            pl.BlockSpec((z.chunk, z.width), lambda i: (i, 0)),
        ),
    )

    got_zero = after(got_zero, whole_one, grad_w_in, other_pairs)
    less = shape(count, (z.half_rows - z.part) // count, z.width)
    first_zero, rest_zero = call(
        parted_sum_kernel, (shape(z.part, z.width), less), got_zero, [LOOSE] * z.shards, cost=2
    )
    first_zero = lax.psum(first_zero, "expert")
    rest_zero = call(
        spread_sum_kernel, less, (exchange(rest_zero, "expert"),), [LOOSE], cost=1, loose=(0,)
    )
    rest_zero = exchange(rest_zero, "expert")

    matrix = shape(1, z.part, z.width)
    finals = call(
        functools.partial(final_kernel, z),
        (
            *[shape(1, micro_count, z.rows, z.width)] * 2,
            *[matrix] * 4,
            *[shape(1, z.part)] * 2,
            shape(1, z.experts, z.part),
            shape(1, z.bucket_part, z.heads),
        ),
        (
            core, first_zero, swap(first_zero), rest_zero, swap(rest_zero), whole_one, swap(whole_one),
            pair_zero, other_pairs[0], pair_one, other_pairs[1],
        ),
        [SMEM] + [LOOSE] * 10,
        [pltpu.VMEM((z.half_rows, z.width), F32), pltpu.VMEM((z.part, z.small), F32)],
        cost=3,
    )
    finals = (*finals[:8], jnp.swapaxes(finals[8], 1, 2), finals[9])
    return (*finals, grad_w_in[None, None], grad_w_out[None, None])


def solution(mesh):
    both = ("expert", "shard")
    plain = P("section", "shard", None)
    gains = P("section", "shard")
    blocks = P("section", None, both, None)
    experts = P("section", both, None, None)
    tokens = P(None, both, None)
    attention = (plain, plain, plain, plain, gains, gains, plain, plain, experts, experts)
    return jax.shard_map(
        shards,
        mesh=mesh,
        in_specs=(tokens, tokens, tokens, blocks, *attention),
        out_specs=(blocks, blocks, *attention),
        check_vma=False,
    )
```

```python
import functools

import jax
import jax.numpy as jnp
from jax import lax
from jax.experimental import pallas as pl
from jax.experimental.pallas import tpu as pltpu
from jax.sharding import PartitionSpec as P

EPSILON = 1e-06
BOUNDS = (8, 12, 16, 23, 32, 46, 64, 91)
MASKED = -1e30
F32 = jnp.float32
BF16 = jnp.bfloat16
I32 = jnp.int32
GELU_SCALE = 0.7978845608028654
GELU_CUBE = 0.044715
SMEM = pl.BlockSpec(memory_space=pltpu.SMEM)
VMEM = pl.BlockSpec(memory_space=pltpu.VMEM)
LOOSE = pl.BlockSpec(memory_space=pltpu.VMEM)
HBM = pl.BlockSpec(memory_space=pltpu.HBM)
ANY = pl.BlockSpec(memory_space=pl.ANY)


def dot_nn(a, b):
    return jnp.dot(a, b, preferred_element_type=F32)


def dot_nt(a, b):
    return lax.dot_general(a, b, (((1,), (1,)), ((), ())), preferred_element_type=F32)


def dot_tn(a, b):
    return lax.dot_general(a, b, (((0,), (0,)), ((), ())), preferred_element_type=F32)


def iota(shape, dimension):
    return lax.broadcasted_iota(I32, shape, dimension)


def call(body, outs, ins, specs, scratch=(), grant=24, cost=5, loose=(), **more):
    ins = [
        value if spec is SMEM or spec is LOOSE else pltpu.with_memory_space_constraint(value, pltpu.HBM)
        for value, spec in zip(ins, specs)
    ]
    single = not isinstance(outs, tuple)
    outs = (outs,) if single else outs
    outs = tuple(
        out if i in loose else pltpu.HBM(out.shape, out.dtype) for i, out in enumerate(outs)
    )
    more.setdefault("out_specs", (VMEM,) * len(outs))
    made = pl.pallas_call(
        body,
        out_shape=outs,
        in_specs=specs,
        scratch_shapes=scratch,
        compiler_params=pltpu.CompilerParams(vmem_limit_bytes=grant * 1024 * 1024),
        cost_estimate=pl.CostEstimate(
            flops=int(cost * 1e8), bytes_accessed=int(cost * 4e5), transcendentals=0
        ),
        **more,
    )(*ins)
    return made[0] if single else made


def bucket_of(relative):
    distance = jnp.abs(relative)
    bucket = jnp.zeros_like(relative)
    for lowest in tuple(range(1, 8)) + BOUNDS:
        bucket = bucket + (distance >= lowest).astype(I32)
    return bucket + 16 * (relative > 0).astype(I32)


class Sizes:
    def __init__(self, tokens_in, w_query, w_router, bias_table, w_in, shards):
        self.rows, self.width = tokens_in.shape[1:]
        self.part = w_query.shape[1]
        self.shards = shards
        self.experts = w_router.shape[2]
        self.bucket_part, self.heads = bias_table.shape[1:]
        self.buckets = self.bucket_part * shards
        self.hidden = w_in.shape[3]
        self.chunk = self.hidden // 6
        self.capacity = max(
            2, (3 * self.rows + 2 * self.experts - 1) // (2 * self.experts)
        )
        self.full, rest = divmod(self.capacity, 8)
        self.rest = next((power for power in (0, 1, 2, 4) if power >= rest), None)
        if self.rest is None:
            self.full, self.rest = (self.full + 1, 0)
        self.cuts = 8 // self.rest if self.rest else 0
        self.cut = self.width // self.cuts if self.rest else 0
        self.slot_width = self.full * self.width + self.cut
        self.slot_rows = self.experts * 8
        self.expert_rows = self.slot_rows * self.full + self.experts * self.rest
        self.small = -(-(self.experts + self.heads + 2) // 128) * 128
        self.small_groups = self.width // self.small
        self.small_rows = self.part // self.small_groups
        self.gain_lane = self.experts + self.heads
        self.piece = 4 * self.part + self.small_rows
        self.half_rows = 2 * self.part + self.small_rows
        self.slab = 6 * self.width + self.small * self.width // self.rows


def slot_picks(z, route):
    onehot = (route == iota((z.rows, z.experts), 1)).astype(F32)
    lower = (iota((z.rows, z.rows), 0) >= iota((z.rows, z.rows), 1)).astype(F32).astype(BF16)
    running = dot_nn(lower, onehot.astype(BF16))
    place = jnp.sum(running * onehot, axis=1, keepdims=True).astype(I32) - 1
    slots = iota((z.rows, z.slot_rows), 1)

    def pick(first, wide, shift):
        inside = (place >= first) & (place < first + wide)
        target = jnp.where(inside, route * 8 + place - first + shift, -1)
        return (slots == target).astype(F32).astype(BF16)

    picks = [pick(8 * i, 8, 0) for i in range(z.full)]
    return picks + [pick(8 * z.full, z.rest, z.rest * i) for i in range(z.cuts)]


def cut_sum(z, picks, values):
    return sum(dot_tn(pick, values[:, i * z.cut : (i + 1) * z.cut]) for i, pick in enumerate(picks))


def put_slots(z, ref, offset, picks, values):
    for i in range(z.full):
        block = dot_tn(picks[i], values)
        ref[:, :, offset : offset + z.width] = block.reshape(z.experts, 8, z.width).astype(BF16)
        offset += z.width
    if z.rest:
        block = cut_sum(z, picks[z.full :], values)
        ref[:, :, offset : offset + z.cut] = block.reshape(z.experts, 8, z.cut).astype(BF16)


def read_slots(z, ref, offset, wide):
    block = ref[:, :, offset : offset + wide].astype(F32)
    return block.reshape(z.slot_rows, wide).astype(BF16)


def get_slots(z, ref, offset, picks):
    total = 0.0
    for i in range(z.full):
        total += dot_nn(picks[i], read_slots(z, ref, offset, z.width))
        offset += z.width
    if z.rest:
        block = read_slots(z, ref, offset, z.cut)
        total += jnp.concatenate([dot_nn(pick, block) for pick in picks[z.full :]], axis=1)
    return total


def extra_picks(z):
    shape = (z.experts * z.rest, z.slot_rows)
    rows, slots = (iota(shape, 0), iota(shape, 1))
    first = (rows // z.rest) * 8 + rows % z.rest
    return [(slots == first + z.rest * i).astype(F32).astype(BF16) for i in range(z.cuts)]


def rows_of_slots(z, ref, offset):
    parts = []
    for i in range(z.full):
        parts.append(read_slots(z, ref, offset, z.width))
        offset += z.width
    if z.rest:
        block = read_slots(z, ref, offset, z.cut)
        pieces = [dot_nn(pick, block) for pick in extra_picks(z)]
        parts.append(jnp.concatenate(pieces, axis=1).astype(BF16))
    return jnp.concatenate(parts, axis=0) if len(parts) > 1 else parts[0]


def slots_of_rows(z, ref, offset, rows):
    for i in range(z.full):
        block = rows[i * z.slot_rows : (i + 1) * z.slot_rows]
        ref[:, :, offset : offset + z.width] = block.reshape(z.experts, 8, z.width).astype(BF16)
        offset += z.width
    if z.rest:
        block = cut_sum(z, extra_picks(z), rows[z.full * z.slot_rows :].astype(BF16))
        ref[:, :, offset : offset + z.cut] = block.reshape(z.experts, 8, z.cut).astype(BF16)


def fetch_weights(z, mine, place, own, other, mats, packed, sems, order=(4, 0, 1, 2, 3)):
    def copy(pieces, i, k):
        shard = place ^ k
        count = z.small_rows if i == 4 else z.part
        start = i * z.part
        source = pieces[k]
        target = pl.ds(pl.multiple_of(shard * count, 16), count)
        held = packed.at[target] if i == 4 else mats.at[i, target]
        return pltpu.make_async_copy(source.at[pl.ds(start, count)], held, sems.at[i, k])

    def start(pieces):
        for i in order:
            for k in range(z.shards):
                copy(pieces, i, k).start()

    def wait(i):
        for k in range(z.shards):
            copy(own, i, k).wait()

    @pl.when(mine)
    def _():
        start(own)

    @pl.when(jnp.logical_not(mine))
    def _():
        start(other)

    return [functools.partial(wait, i) for i in range(5)]


def fetch_halves(z, core, own, other, mats, packed, sems, order=(4, 0, 1, 2, 3)):
    def copy(source, i, k):
        count = z.small_rows if i == 4 else z.part
        start = k * z.half_rows + (i if i < 2 else i - 2) * z.part
        target = pl.ds(k * count, count)
        held = packed.at[target] if i == 4 else mats.at[i, target]
        return pltpu.make_async_copy(source.at[pl.ds(start, count)], held, sems.at[i, k])

    def start(first, second):
        for i in order:
            for k in range(z.shards):
                copy(first if i < 2 else second, i, k).start()

    def wait(i):
        for k in range(z.shards):
            copy(own, i, k).wait()

    @pl.when(core == 0)
    def _():
        start(own, other)

    @pl.when(core != 0)
    def _():
        start(other, own)

    return [functools.partial(wait, i) for i in range(5)]


def weight_scratch(z):
    return [
        pltpu.VMEM((4, z.width, z.width), BF16),
        pltpu.VMEM((z.shards * z.small_rows, z.width), BF16),
        pltpu.VMEM((z.width, z.small), BF16),
        pltpu.SemaphoreType.DMA((5, z.shards)),
    ]


def unpack_small(z, packed, small):
    for j in range(z.shards):
        for g in range(z.small_groups):
            row = j * z.part + g * z.small_rows
            small[row : row + z.small_rows, :] = packed[
                j * z.small_rows : (j + 1) * z.small_rows, g * z.small : (g + 1) * z.small
            ]


def bucket_rows(z):
    rows, buckets = (iota((z.width, z.buckets), 0), iota((z.width, z.buckets), 1))
    held = (buckets // z.bucket_part) * z.part + buckets % z.bucket_part
    return (rows == held).astype(F32).astype(BF16)


def bucket_lanes(z):
    shape = (z.buckets, 2 * z.rows)
    return (bucket_of(iota(shape, 1) - z.rows) == iota(shape, 0)).astype(F32).astype(BF16)


def identity(size):
    return (iota((size, size), 0) == iota((size, size), 1)).astype(F32).astype(BF16)


def gain_rows(z, small):
    rows, lanes = (iota((8, z.small), 0), iota((8, z.small), 1))
    pick = ((lanes == z.gain_lane + rows) & (rows < 2)).astype(F32).astype(BF16)
    made = dot_nt(pick, small)
    return (made[0:1], made[1:2])


def unit_rows(values):
    inverse = lax.rsqrt(jnp.mean(values * values, axis=-1, keepdims=True) + EPSILON)
    return (values * inverse, inverse)


def pair_masks(z):
    lanes = iota((z.rows, 128), 1)
    first = (lanes < 64).astype(F32).astype(BF16)
    return (first, (lanes >= 64).astype(F32).astype(BF16))


def double(values, masks):
    return jnp.concatenate([values * masks[0], values * masks[1]], axis=0)


def attend(z, inputs, waits, mats, packed, small, lengths, section, qkv_ref, probs_ref, attended_ref):
    waits[4]()
    unpack_small(z, packed, small)
    small_full = small[...]
    gain_one, gain_two = gain_rows(z, small_full)
    normed_one = (unit_rows(inputs)[0] * gain_one).astype(BF16)
    for i in range(3):
        waits[i]()
        qkv_ref[:, i * z.width : (i + 1) * z.width] = dot_nn(normed_one, mats[i]).astype(BF16)

    table = dot_tn(bucket_rows(z), small_full).astype(BF16)
    bias = dot_tn(table, bucket_lanes(z))[z.experts : z.experts + z.heads]

    rows, lanes = (iota((z.rows, z.rows), 0), iota((z.rows, z.rows), 1))
    segment_q, segment_k = (jnp.zeros_like(rows), jnp.zeros_like(rows))
    end = jnp.int32(0)
    for i in range(lengths.shape[2]):
        end = end + lengths[section, 0, i]
        segment_q += (rows >= end).astype(I32)
        segment_k += (lanes >= end).astype(I32)
    visible = segment_q == segment_k

    masks = pair_masks(z)
    scale = 64 ** (-0.5)
    for p in range(z.heads // 2):
        at = slice(p * 128, (p + 1) * 128)
        query = qkv_ref[:, p * 128 : (p + 1) * 128]
        key = qkv_ref[:, z.width + p * 128 : z.width + (p + 1) * 128]
        value = qkv_ref[:, 2 * z.width + p * 128 : 2 * z.width + (p + 1) * 128]
        scores = dot_nt(query, double(key, masks)) * scale
        halves = []
        for i in range(2):
            spread = jnp.broadcast_to(bias[2 * p + i : 2 * p + i + 1], (z.rows, 2 * z.rows))
            spread = pltpu.roll(spread, z.rows, 1, stride=1, stride_axis=0)[:, : z.rows]
            part = scores[:, i * z.rows : (i + 1) * z.rows] + spread
            part = jnp.where(visible, part, MASKED)
            part = jnp.exp(part - jnp.max(part, axis=-1, keepdims=True))
            halves.append(part / jnp.sum(part, axis=-1, keepdims=True))
        probs = jnp.concatenate(halves, axis=1).astype(BF16)
        probs_ref[p] = probs
        attended_ref[:, at] = dot_nn(probs, double(value, masks)).astype(BF16)

    waits[3]()
    middle = inputs + dot_nn(attended_ref[...], mats[3])
    normed_two = (unit_rows(middle)[0] * gain_two).astype(BF16)
    logits = dot_nn(normed_two, small_full)
    logits = jnp.where(iota((z.rows, z.small), 1) < z.experts, logits, MASKED)
    logits = jnp.exp(logits - jnp.max(logits, axis=-1, keepdims=True))
    router = logits / jnp.sum(logits, axis=-1, keepdims=True)
    return (middle, normed_two, router)


def chosen(z, route):
    return (route == iota((z.rows, z.small), 1)).astype(F32)


def attend_back(
    z, grad_out, token_out, grad_token, inputs, route, waits, mats, packed, small, kept, slab_out,
    slab_ref, slab_sems,
):
    def send(i, first, last):
        columns = pl.ds(first, last - first)
        copy = pltpu.make_async_copy(
            slab_ref.at[:, columns], slab_out.at[:, columns], slab_sems.at[i]
        )
        copy.start()
        return copy

    qkv_ref, probs_ref, attended_ref, middle_ref, router_ref = kept
    waits[4]()
    unpack_small(z, packed, small)
    small_full = small[...]
    gain_one, gain_two = gain_rows(z, small_full)
    onehot = chosen(z, route)
    router = router_ref[...]
    gate = jnp.sum(router * onehot, axis=1, keepdims=True)
    grad_gate = jnp.sum(grad_out * token_out, axis=1, keepdims=True)
    grad_logits = (grad_gate * gate * (onehot - router)).astype(BF16)
    unit_two, inverse_two = unit_rows(middle_ref[...])
    grad_small = dot_tn((unit_two * gain_two).astype(BF16), grad_logits)
    grad_normed = grad_token + dot_nt(grad_logits, small_full)
    gain_two_grad = jnp.sum(grad_normed * unit_two, axis=0, keepdims=True)
    grad_unit = grad_normed * gain_two
    grad_unit -= unit_two * jnp.mean(grad_unit * unit_two, axis=1, keepdims=True)
    grad_middle = grad_out + inverse_two * grad_unit
    grad_branch = grad_middle.astype(BF16)
    slab_ref[:, 4 * z.width : 5 * z.width] = attended_ref[...]
    slab_ref[:, 5 * z.width : 6 * z.width] = grad_branch
    sent = [send(0, 4 * z.width, 6 * z.width)]
    waits[3]()
    grad_attended = dot_nt(grad_branch, mats[3]).astype(BF16)

    masks = pair_masks(z)
    scale = 64 ** (-0.5)
    relative = []
    turn = iota((z.rows, z.rows), 0) + iota((z.rows, z.rows), 1) == z.rows - 1
    turn = turn.astype(F32).astype(BF16)
    for p in range(z.heads // 2):
        at = slice(p * 128, (p + 1) * 128)
        query = qkv_ref[:, p * 128 : (p + 1) * 128]
        keys = double(qkv_ref[:, z.width + p * 128 : z.width + (p + 1) * 128], masks)
        values = double(qkv_ref[:, 2 * z.width + p * 128 : 2 * z.width + (p + 1) * 128], masks)
        grad_heads = grad_attended[:, at]
        probs_low = probs_ref[p]
        probs = probs_low.astype(F32)
        grad_probs = dot_nt(grad_heads, values)
        halves = []
        for i in range(2):
            part = slice(i * z.rows, (i + 1) * z.rows)
            product = grad_probs[:, part] * probs[:, part]
            dots = jnp.sum(product, axis=-1, keepdims=True)
            grads = (product - probs[:, part] * dots).astype(BF16)
            halves.append(grads)
        grad_scores = jnp.concatenate(halves, axis=1)
        turned = dot_nn(turn, grad_scores)
        for i in range(2):
            wide = [turned[:, i * z.rows : (i + 1) * z.rows], jnp.zeros((z.rows, z.rows), F32)]
            wide = pltpu.roll(jnp.concatenate(wide, axis=1), 1, 1, stride=1, stride_axis=0)
            relative.append(jnp.sum(wide, axis=0, keepdims=True))
        start = z.width + p * 128
        slab_ref[:, start : start + 128] = (dot_nn(grad_scores, keys) * scale).astype(BF16)
        made = dot_tn(grad_scores, query) * scale
        mask = masks[0].astype(F32)
        made = made[: z.rows] * mask + made[z.rows :] * (1.0 - mask)
        slab_ref[:, start + z.width : start + z.width + 128] = made.astype(BF16)
        made = dot_tn(probs_low, grad_heads)
        made = made[: z.rows] * mask + made[z.rows :] * (1.0 - mask)
        slab_ref[:, start + 2 * z.width : start + 2 * z.width + 128] = made.astype(BF16)

    unit_one, inverse_one = unit_rows(inputs)
    slab_ref[:, : z.width] = (unit_one * gain_one).astype(BF16)
    sent.append(send(1, 0, 4 * z.width))
    grad_normed = 0.0
    for i in range(3):
        waits[i]()
        grad_normed += dot_nt(slab_ref[:, (i + 1) * z.width : (i + 2) * z.width], mats[i])
    gain_one_grad = jnp.sum(grad_normed * unit_one, axis=0, keepdims=True)
    grad_unit = grad_normed * gain_one
    grad_unit -= unit_one * jnp.mean(grad_unit * unit_one, axis=1, keepdims=True)
    grad_in = (grad_middle + inverse_one * grad_unit).astype(BF16)

    relative += [jnp.zeros((1, 2 * z.rows), F32)] * (-z.heads % 8)
    relative = jnp.concatenate(relative, axis=0)
    lanes_of = bucket_lanes(z)
    high = relative.astype(BF16)
    table = dot_nt(lanes_of, high) + dot_nt(lanes_of, (relative - high.astype(F32)).astype(BF16))
    count = relative.shape[0]
    places = iota((count, z.small), 1) == iota((count, z.small), 0) + z.experts
    places = places & (iota((count, z.small), 0) < z.heads)
    table = dot_nn(table.astype(BF16), places.astype(F32).astype(BF16)).astype(BF16)
    grad_small += dot_nn(bucket_rows(z), table)
    gains = jnp.concatenate([gain_one_grad, gain_two_grad, jnp.zeros((6, z.width), F32)], axis=0)
    rows, lanes = (iota((8, z.small), 0), iota((8, z.small), 1))
    pick = ((lanes == z.gain_lane + rows) & (rows < 2)).astype(F32).astype(BF16)
    grad_small += dot_tn(gains.astype(BF16), pick)
    for i in range(z.width // z.rows):
        start = 6 * z.width + i * z.small
        slab_ref[:, start : start + z.small] = grad_small[i * z.rows : (i + 1) * z.rows].astype(BF16)
    sent.append(send(2, 6 * z.width, z.slab))
    return (grad_in, sent)


def pack_kernel(z, query, key, value, output, router, gain_one, gain_two, table, piece, small, sems):
    copies = [
        pltpu.make_async_copy(source.at[0], piece.at[pl.ds(i * z.part, z.part)], sems.at[i])
        for i, source in enumerate((query, key, value, output))
    ]
    for copy in copies:
        copy.start()
    gains = [gain_one[...].astype(F32), gain_two[...].astype(F32), jnp.zeros((6, z.part), F32)]
    rows, lanes = (iota((8, z.small), 0), iota((8, z.small), 1))
    pick = ((lanes == z.gain_lane + rows) & (rows < 2)).astype(F32).astype(BF16)
    small[...] = dot_tn(jnp.concatenate(gains, axis=0).astype(BF16), pick)
    small[:, : z.experts] = dot_tn(router[0], identity(z.experts))
    small[: z.bucket_part, z.experts : z.gain_lane] = table[0].astype(F32)
    for g in range(z.small_groups):
        piece[4 * z.part :, g * z.small : (g + 1) * z.small] = small[
            g * z.small_rows : (g + 1) * z.small_rows
        ].astype(BF16)
    for copy in copies:
        copy.wait()


def first_kernel(
    z, section, place, lengths, tokens, own_route, other_route, o0, o1, o2, o3, r0, r1, r2, r3,
    send, qkv, probs, attended, middle_ref, router_ref,
    mats, packed, small, sems,
):
    core = section[0]
    waits = fetch_weights(
        z, core == 0, place[0], (o0, o1, o2, o3), (r0, r1, r2, r3), mats, packed, sems)
    inputs = tokens[core].astype(F32)
    middle, normed_two, router = attend(
        z, inputs, waits, mats, packed, small, lengths, core, qkv, probs, attended
    )
    middle_ref[...] = middle
    router_ref[...] = router
    route = jnp.where(core == 0, own_route[core], other_route[...])
    put_slots(z, send, 0, slot_picks(z, route), normed_two)


def second_kernel(
    z, section, lengths, cotangent, own_route, other_route, own, other, back, middle_zero, router_zero,
    send, out_zero, qkv, probs, attended, middle_ref, router_ref,
    mats, packed, small, sems,
):
    core = section[0]
    waits = fetch_halves(
        z, core, own, other, mats, packed, sems)
    route = jnp.where(core == 0, own_route[core], other_route[...])
    gate = jnp.sum(router_zero[...] * chosen(z, route), axis=1, keepdims=True)
    token_out = get_slots(z, back, 0, slot_picks(z, route))
    layer_out = (middle_zero[...] + gate * token_out).astype(BF16)
    out_zero[...] = layer_out
    middle, normed_two, router = attend(
        z, layer_out.astype(F32), waits, mats, packed, small, lengths, core, qkv, probs, attended
    )
    middle_ref[...] = middle
    router_ref[...] = router
    route = jnp.where(core == 1, own_route[core], other_route[...])
    picks = slot_picks(z, route)
    put_slots(z, send, 0, picks, normed_two)
    gate = jnp.sum(router * chosen(z, route), axis=1, keepdims=True)
    grad = (gate * cotangent[core].astype(F32)).astype(BF16)
    put_slots(z, send, z.slot_width, picks, grad)


def third_kernel(
    z, section, cotangent, own_route, other_route, own, other, back, inputs, router_zero,
    qkv, probs, attended, middle, router,
    send, pair, slab,
    mats, packed, small, sems, held, held_sems,
):
    core = section[0]
    waits = fetch_halves(
        z, core, own, other, mats, packed, sems, (4, 3, 0, 1, 2))
    route = jnp.where(core == 1, own_route[core], other_route[...])
    picks = slot_picks(z, route)
    token_out = get_slots(z, back, 0, picks)
    grad_token = get_slots(z, back, z.slot_width, picks)
    gate = jnp.sum(router[...] * chosen(z, route), axis=1, keepdims=True)
    pair[0] = (middle[...] + gate * token_out).astype(BF16)
    grad_in, copies = attend_back(
        z, cotangent[core].astype(F32), token_out, grad_token, inputs[...].astype(F32), route,
        waits, mats, packed, small, (qkv, probs, attended, middle, router), slab, held, held_sems,
    )
    pair[1] = grad_in
    route = jnp.where(core == 0, own_route[core], other_route[...])
    gate = jnp.sum(router_zero[...] * chosen(z, route), axis=1, keepdims=True)
    grad = (gate * grad_in.astype(F32)).astype(BF16)
    put_slots(z, send, 0, slot_picks(z, route), grad)
    for copy in copies:
        copy.wait()


def fourth_kernel(
    z, section, place, out_zero, pair_one, tokens, own_route, other_route, o0, o1, o2, o3, r0, r1, r2, r3, back_out, back_grad,
    qkv, probs, attended, middle, router,
    pair, slab,
    mats, packed, small, sems, held, held_sems,
):
    core = section[0]
    waits = fetch_weights(
        z, core == 0, place[0], (o0, o1, o2, o3), (r0, r1, r2, r3), mats, packed, sems, (4, 3, 0, 1, 2))
    route = jnp.where(core == 0, own_route[core], other_route[...])
    picks = slot_picks(z, route)
    token_out = get_slots(z, back_out, 0, picks)
    grad_token = get_slots(z, back_grad, 0, picks)
    pair[0] = out_zero[...]
    pair[1], copies = attend_back(
        z, pair_one[1].astype(F32), token_out, grad_token, tokens[core].astype(F32), route,
        waits, mats, packed, small, (qkv, probs, attended, middle, router), slab, held, held_sems,
    )
    for copy in copies:
        copy.wait()


def fetch_experts(z, mine, own_in, own_out, other_in, other_out, w_in, w_out, sems):
    def copies(source_in, source_out, c):
        at = pl.ds(c * z.chunk, z.chunk)
        return (
            pltpu.make_async_copy(source_in.at[:, at], w_in.at[c], sems.at[2 * c]),
            pltpu.make_async_copy(source_out.at[at], w_out.at[c], sems.at[2 * c + 1]),
        )

    def start(source_in, source_out):
        for c in range(z.hidden // z.chunk):
            for copy in copies(source_in, source_out, c):
                copy.start()

    @pl.when(mine)
    def _():
        start(own_in, own_out)

    @pl.when(jnp.logical_not(mine))
    def _():
        start(other_in, other_out)

    def wait(c):
        for copy in copies(own_in, own_out, c):
            copy.wait()

    return wait


def expert_scratch(z, sums, stuff=None):
    chunks = z.hidden // z.chunk
    kept = [] if stuff is None else [
        pltpu.VMEM(stuff.shape, stuff.dtype), pltpu.SemaphoreType.DMA((2 * chunks + 1,)),
    ]
    return [
        pltpu.VMEM((chunks, z.width, z.chunk), BF16),
        pltpu.VMEM((chunks, z.chunk, z.width), BF16),
        pltpu.SemaphoreType.DMA((2 * chunks,)),
        *kept,
    ] + [pltpu.VMEM((z.expert_rows, z.width), F32)] * sums


def smooth(values):
    square = values * values
    bent = jnp.tanh(GELU_SCALE * values * (1.0 + GELU_CUBE * square))
    return (0.5 * values * (1.0 + bent), square, bent)


def smooth_slope(values, square, bent):
    inner = GELU_SCALE * (1.0 + 3.0 * GELU_CUBE * square)
    return 0.5 * (1.0 + bent) + 0.5 * values * (1.0 - bent * bent) * inner


def expert_forward_kernel(
    z, section, arrived, own_in, own_out, other_in, other_out, result, w_in, w_out, sems, produced
):
    wait = fetch_experts(
        z, section[0] == 0, own_in, own_out, other_in, other_out, w_in, w_out, sems
    )
    rows = rows_of_slots(z, arrived, 0)
    for c in range(z.hidden // z.chunk):
        wait(c)
        hidden = smooth(dot_nn(rows, w_in[c]))[0].astype(BF16)
        made = dot_nn(hidden, w_out[c])
        produced[...] = made if c == 0 else produced[...] + made
    slots_of_rows(z, result, 0, produced[...])


def expert_backward_kernel(
    z, layer, section, arrived, arrived_grad, own_in, own_out, other_in, other_out,
    result, stuff_out, w_in, w_out, sems, stuff, out_sems, grad_sum, *produced
):
    sent = []

    def send(first, wide):
        columns = pl.ds(first, wide)
        copy = pltpu.make_async_copy(
            stuff.at[:, columns], stuff_out.at[:, columns], out_sems.at[len(sent)]
        )
        copy.start()
        sent.append(copy)

    wait = fetch_experts(
        z, section[0] == layer, own_in, own_out, other_in, other_out, w_in, w_out, sems
    )
    rows = rows_of_slots(z, arrived, 0)
    grads = rows_of_slots(z, arrived_grad, z.slot_width if produced else 0)
    stuff[:, 2 * z.hidden : 2 * z.hidden + z.width] = rows
    stuff[:, 2 * z.hidden + z.width : 2 * z.hidden + 2 * z.width] = grads
    send(2 * z.hidden, 2 * z.width)
    for c in range(z.hidden // z.chunk):
        wait(c)
        before = dot_nn(rows, w_in[c])
        hidden, square, bent = smooth(before)
        hidden = hidden.astype(BF16)
        stuff[:, c * z.chunk : (c + 1) * z.chunk] = hidden
        if produced:
            made = dot_nn(hidden, w_out[c])
            produced[0][...] = made if c == 0 else produced[0][...] + made
        grad_pre = dot_nt(grads, w_out[c]) * smooth_slope(before, square, bent)
        grad_pre = grad_pre.astype(BF16)
        stuff[:, z.hidden + c * z.chunk : z.hidden + (c + 1) * z.chunk] = grad_pre
        send(c * z.chunk, z.chunk)
        send(z.hidden + c * z.chunk, z.chunk)
        made = dot_nt(grad_pre, w_in[c])
        grad_sum[...] = made if c == 0 else grad_sum[...] + made
    if produced:
        slots_of_rows(z, result, 0, produced[0][...])
    slots_of_rows(z, result, z.slot_width if produced else 0, grad_sum[...])
    for copy in sent:
        copy.wait()


def expert_weights_kernel(
    z, section, own_zero, other_zero, own_one, other_one, grad_in, grad_out, held, turned, sems
):
    step = pl.program_id(0)

    @pl.when(step == 0)
    def _():
        def copies(own, other):
            return [
                pltpu.make_async_copy(
                    source, held.at[pl.ds(i * z.expert_rows, z.expert_rows)], sems.at[i]
                )
                for i, source in enumerate((own, other))
            ]

        @pl.when(section[0] == 0)
        def _():
            for copy in copies(own_zero, other_zero):
                copy.start()

        @pl.when(section[0] != 0)
        def _():
            for copy in copies(own_one, other_one):
                copy.start()

        for copy in copies(own_zero, other_zero):
            copy.wait()
        rows = held[:, 2 * z.hidden : 2 * z.hidden + z.width]
        turned[...] = jnp.transpose(rows.astype(F32)).astype(BF16)

    start = pl.multiple_of(step * z.chunk, z.chunk)
    grad_pre = held[:, pl.ds(z.hidden + start, z.chunk)]
    hidden = held[:, pl.ds(start, z.chunk)]
    grads = held[:, 2 * z.hidden + z.width : 2 * z.hidden + 2 * z.width]
    grad_in[...] = dot_nn(turned[...], grad_pre).astype(BF16)
    grad_out[...] = dot_tn(hidden, grads).astype(BF16)


def attention_weights_kernel(z, layer, section, place, own, other, *refs):
    outs, made = (refs[: z.shards], refs[z.shards])
    second = section[0] ^ layer

    def both(column):
        at = pl.ds(pl.multiple_of(column * z.width, 128), z.width)
        return jnp.concatenate([own[:, at], other[:, at]], axis=0)

    for i, (left, right) in enumerate(
        ((0, 1 + 2 * second), (4 * second, 2 + 3 * second))
    ):
        made[...] = dot_tn(both(left), both(right))
        for k in range(z.shards):
            start = pl.multiple_of((place[0] ^ k) * z.part, 16)
            outs[k][i * z.part : (i + 1) * z.part] = made[pl.ds(start, z.part)].astype(BF16)
    for i in range(z.width // z.rows):
        columns = slice(6 * z.width + i * z.small, 6 * z.width + (i + 1) * z.small)
        total = own[:, columns].astype(F32) + other[:, columns].astype(F32)
        made[i * z.rows : (i + 1) * z.rows, : z.small] = total
    for k in range(z.shards):
        for g in range(z.small_groups):
            start = pl.multiple_of((place[0] ^ k) * z.part + g * z.small_rows, 16)
            outs[k][2 * z.part :, g * z.small : (g + 1) * z.small] = made[
                pl.ds(start, z.small_rows), : z.small
            ].astype(BF16)


def pieces_sum_kernel(*refs):
    out = refs[-1]
    rows = out.shape[1]
    total = sum(piece[...].astype(F32) for piece in refs[:-1])
    for i in range(out.shape[0]):
        out[i] = total[i * rows : (i + 1) * rows].astype(BF16)


def spread_sum_kernel(pieces, out):
    total = sum(pieces[i].astype(F32) for i in range(pieces.shape[0])).astype(BF16)
    for i in range(out.shape[0]):
        out[i] = total


def final_kernel(
    z, section, own_zero, got_zero, own_one, got_one, pair_zero, other_zero, pair_one, other_one,
    layer_out, input_grad, query, key, value, output, gain_one, gain_two, router, table, held, small,
):
    rows = own_zero.shape[1]

    def finish(own, other, micros):
        for source, targets in ((own, (query, key)), (other, (value, output))):
            for i in range(source.shape[0]):
                held[i * rows : (i + 1) * rows] = source[i].astype(F32)
            for i, target in enumerate(targets):
                target[0] = held[i * z.part : (i + 1) * z.part].astype(BF16)
            if source is own:
                for g in range(z.small_groups):
                    small[g * z.small_rows : (g + 1) * z.small_rows] = held[
                        2 * z.part :, g * z.small : (g + 1) * z.small
                    ]
        for i, pair in enumerate(micros):
            layer_out[0, i] = pair[0]
            input_grad[0, i] = pair[1]

    @pl.when(section[0] == 0)
    def _():
        finish(own_zero, got_zero, (pair_zero, other_zero))

    @pl.when(section[0] != 0)
    def _():
        finish(own_one, got_one, (other_one, pair_one))

    gains = gain_rows(z, small[...].astype(BF16))
    gain_one[...] = gains[0].astype(BF16)
    gain_two[...] = gains[1].astype(BF16)
    router[0] = dot_nt(identity(z.experts), small[:, : z.experts].astype(BF16)).astype(BF16)
    table[0] = small[: z.bucket_part, z.experts : z.gain_lane].astype(BF16)


def swap(value):
    return lax.ppermute(value, "section", [(0, 1), (1, 0)])


def cross(value, target):
    return lax.ppermute(value, "section", [(1 - target, target)])


def within(value, distance, layer):
    size = lax.axis_size("shard")
    pairs = [(layer * size + i, layer * size + (i ^ distance)) for i in range(size)]
    return lax.ppermute(value, ("section", "shard"), pairs)


def exchange(buffer, axes=("expert", "shard")):
    return lax.all_to_all(buffer, axes, split_axis=0, concat_axis=0, tiled=True)


def shards(
    tokens_in,
    cotangent,
    lengths,
    routes,
    w_query,
    w_key,
    w_value,
    w_output,
    gain_attn,
    gain_moe,
    w_router,
    bias_table,
    w_in,
    w_out,
):
    z = Sizes(tokens_in, w_query, w_router, bias_table, w_in, lax.axis_size("shard"))
    micro_count = tokens_in.shape[0]
    section = lax.axis_index("section").astype(I32)
    core = section.reshape(1)
    place = lax.axis_index("shard").astype(I32).reshape(1)

    def shape(*dims, kind=BF16):
        return jax.ShapeDtypeStruct(dims, kind)

    own_route = routes[0]
    sent_route = lax.dynamic_index_in_dim(own_route, 1 - section, 0, keepdims=False)
    piece = call(
        functools.partial(pack_kernel, z),
        shape(z.piece, z.width),
        (
            w_query, w_key, w_value, w_output, jnp.swapaxes(w_router, 1, 2), gain_attn, gain_moe,
            bias_table,
        ),
        [HBM] * 4 + [VMEM] * 4,
        [pltpu.VMEM((z.part, z.small), F32), pltpu.SemaphoreType.DMA((4,))],
        grant=8,
        cost=2,
    )

    def spread(piece, layer):
        return (piece, *[within(piece, distance, layer) for distance in range(1, z.shards)])

    def after(values, *first):
        values, unused = lax.optimization_barrier((values, first))
        return values

    half = cross(piece[: z.half_rows], 0)
    half = jnp.where(section == 0, half, piece[z.piece - z.half_rows :])
    half_one = lax.all_gather(half, "shard", axis=0, tiled=True)

    piece, sent_route = lax.optimization_barrier((piece, sent_route))
    route_pair = (own_route, swap(sent_route))
    pieces = spread(piece, 0)
    experts = (w_in[0, 0], w_out[0, 0])
    given = [cross(piece, 1)]
    early = (given[0], route_pair[1], half)
    given += [cross(after(member, early), 1) for member in pieces[1:]]
    given_zero = tuple(cross(member, 1) for member in after(experts, given))
    weights_zero = (*pieces, *given)

    buffer = shape(z.experts, 8, z.slot_width)
    wide_buffer = shape(z.experts, 8, 2 * z.slot_width)
    kept = (
        shape(z.rows, 3 * z.width),
        shape(z.heads // 2, z.rows, 2 * z.rows),
        shape(z.rows, z.width),
        shape(z.rows, z.width, kind=F32),
        shape(z.rows, z.small, kind=F32),
    )
    scratch = weight_scratch(z)
    rows_shape = shape(z.rows, z.width)
    slab_shape = shape(z.rows, z.slab)
    back_scratch = [
        *scratch,
        pltpu.VMEM(slab_shape.shape, slab_shape.dtype),
        pltpu.SemaphoreType.DMA((3,)),
    ]

    sent, *kept_zero = call(
        functools.partial(first_kernel, z),
        (buffer, *kept),
        (core, place, lengths, tokens_in, *route_pair, *weights_zero),
        [SMEM, SMEM, SMEM, VMEM, VMEM, VMEM] + [ANY] * 8,
        scratch,
        cost=6,
        loose=(0,),
    )
    arrived_zero = exchange(sent)
    produced = call(
        functools.partial(expert_forward_kernel, z),
        buffer,
        (core, arrived_zero, *experts, *given_zero),
        [SMEM, LOOSE, HBM, HBM, HBM, HBM],
        expert_scratch(z, 1),
        cost=6,
        loose=(0,),
    )
    back_zero = exchange(produced)
    weights_one = (half_one, swap(after(half_one, produced)))
    given_one = tuple(cross(member, 0) for member in after(experts, produced))

    sent, out_zero, *kept_one = call(
        functools.partial(second_kernel, z),
        (wide_buffer, rows_shape, *kept),
        (core, lengths, cotangent, *route_pair, *weights_one, back_zero, *kept_zero[3:]),
        [SMEM, SMEM, VMEM, VMEM, VMEM] + [ANY] * 2 + [LOOSE] + [VMEM] * 2,
        scratch,
        cost=7,
        loose=(0,),
    )
    arrived_one = exchange(sent)
    stuff_shape = shape(z.expert_rows, 2 * z.hidden + 2 * z.width)
    result, stuff_one = call(
        lambda section, arrived, *rest: expert_backward_kernel(
            z, 1, section, arrived, arrived, *rest
        ),
        (wide_buffer, stuff_shape),
        (core, arrived_one, *experts, *given_one),
        [SMEM, LOOSE, HBM, HBM, HBM, HBM],
        expert_scratch(z, 2, stuff_shape),
        grant=28,
        cost=10,
        out_specs=(VMEM, HBM),
        loose=(0,),
    )
    back_one = exchange(result)

    pair_shape = shape(2, z.rows, z.width)
    sent, pair_one, slab_one = call(
        functools.partial(third_kernel, z),
        (buffer, pair_shape, slab_shape),
        (core, cotangent, *route_pair, *weights_one, back_one, out_zero, kept_zero[4], *kept_one),
        [SMEM, VMEM, VMEM, VMEM] + [ANY] * 2 + [LOOSE] + [VMEM] * 7,
        back_scratch,
        cost=8,
        loose=(0,),
        out_specs=(VMEM, VMEM, HBM),
    )
    arrived_grad = exchange(sent)

    count = lax.axis_size("expert")

    def partial_sums(slab, layer):
        return call(
            functools.partial(attention_weights_kernel, z, layer),
            (shape(z.half_rows, z.width),) * z.shards,
            (core, place, slab, swap(slab)),
            [SMEM, SMEM, VMEM, LOOSE],
            [pltpu.VMEM((z.width, z.width), F32)],
            cost=4,
        )

    def send_pieces(pieces):
        size = lax.axis_size("shard")
        got = [pieces[0]]
        for distance in range(1, z.shards):
            pairs = [(i, i ^ distance) for i in range(size)]
            got.append(lax.ppermute(pieces[distance], "shard", pairs))
        return tuple(got)

    part = shape(count, z.half_rows // count, z.width)

    def pieces_sum(pieces, loose=()):
        return call(pieces_sum_kernel, part, pieces, [LOOSE] * z.shards, cost=2, loose=loose)

    sums_one = partial_sums(slab_one, 1)
    other_stuff_one = cross(stuff_one, 1)
    arrived_grad, *sums_one = lax.optimization_barrier((arrived_grad, *sums_one))
    arrived_grad = after(arrived_grad, other_stuff_one)
    got_one = send_pieces(sums_one)

    result, stuff_zero = call(
        functools.partial(expert_backward_kernel, z, 0),
        (buffer, stuff_shape),
        (core, arrived_zero, arrived_grad, *experts, *given_zero),
        [SMEM, VMEM, LOOSE, HBM, HBM, HBM, HBM],
        expert_scratch(z, 1, stuff_shape),
        grant=28,
        cost=8,
        out_specs=(VMEM, HBM),
        loose=(0,),
    )
    back_grad = after(exchange(result), got_one)
    whole_one = pieces_sum(after(got_one, back_grad)).reshape(z.half_rows, z.width)
    whole_one = lax.psum(whole_one, "expert").reshape(part.shape)
    pair_zero, slab_zero = call(
        functools.partial(fourth_kernel, z),
        (pair_shape, slab_shape),
        (
            core, place, out_zero, pair_one, tokens_in, *route_pair, *weights_zero,
            back_zero, back_grad, *kept_zero,
        ),
        [SMEM, SMEM, VMEM, VMEM, VMEM, VMEM, VMEM] + [ANY] * 8 + [VMEM] * 7,
        back_scratch,
        cost=8,
        out_specs=(VMEM, HBM),
    )

    sums_zero = partial_sums(slab_zero, 0)
    got_zero = send_pieces(sums_zero)
    other_stuff_zero = cross(after(stuff_zero, sums_zero), 0)
    other_pairs = (cross(pair_zero, 0), cross(pair_one, 1))

    chunks = z.hidden // z.chunk
    grad_w_in, grad_w_out = call(
        functools.partial(expert_weights_kernel, z),
        (shape(z.width, z.hidden), shape(z.hidden, z.width)),
        (
            core, after(stuff_zero, sums_zero), other_stuff_zero, stuff_one, other_stuff_one,
        ),
        [SMEM, HBM, HBM, HBM, HBM],
        [
            pltpu.VMEM((2 * z.expert_rows, stuff_shape.shape[1]), BF16),
            pltpu.VMEM((z.width, 2 * z.expert_rows), BF16),
            pltpu.SemaphoreType.DMA((2,)),
        ],
        grant=28,
        cost=9,
        grid=(chunks,),
        out_specs=(
            pl.BlockSpec((z.width, z.chunk), lambda i: (0, i)),
            pl.BlockSpec((z.chunk, z.width), lambda i: (i, 0)),
        ),
    )

    got_zero = after(got_zero, whole_one, grad_w_in, other_pairs)
    summed_zero = call(
        spread_sum_kernel, part, (exchange(pieces_sum(got_zero, (0,)), "expert"),), [LOOSE],
        cost=1, loose=(0,),
    )
    whole_zero = exchange(summed_zero, "expert")

    matrix = shape(1, z.part, z.width)
    finals = call(
        functools.partial(final_kernel, z),
        (
            *[shape(1, micro_count, z.rows, z.width)] * 2,
            *[matrix] * 4,
            *[shape(1, z.part)] * 2,
            shape(1, z.experts, z.part),
            shape(1, z.bucket_part, z.heads),
        ),
        (
            core, whole_zero, swap(whole_zero), whole_one, swap(whole_one),
            pair_zero, other_pairs[0], pair_one, other_pairs[1],
        ),
        [SMEM] + [LOOSE] * 8,
        [pltpu.VMEM((z.half_rows, z.width), F32), pltpu.VMEM((z.part, z.small), F32)],
        cost=3,
    )
    finals = (*finals[:8], jnp.swapaxes(finals[8], 1, 2), finals[9])
    return (*finals, grad_w_in[None, None], grad_w_out[None, None])


def solution(mesh):
    both = ("expert", "shard")
    plain = P("section", "shard", None)
    gains = P("section", "shard")
    blocks = P("section", None, both, None)
    experts = P("section", both, None, None)
    tokens = P(None, both, None)
    attention = (plain, plain, plain, plain, gains, gains, plain, plain, experts, experts)
    return jax.shard_map(
        shards,
        mesh=mesh,
        in_specs=(tokens, tokens, tokens, blocks, *attention),
        out_specs=(blocks, blocks, *attention),
        check_vma=False,
    )
```

```python
import functools

import jax
import jax.numpy as jnp
from jax import lax
from jax.experimental import pallas as pl
from jax.experimental.pallas import tpu as pltpu
from jax.sharding import PartitionSpec as P

EPSILON = 1e-06
BOUNDS = (8, 12, 16, 23, 32, 46, 64, 91)
MASKED = -1e30
F32 = jnp.float32
BF16 = jnp.bfloat16
I32 = jnp.int32
GELU_SCALE = 0.7978845608028654
GELU_CUBE = 0.044715
SMEM = pl.BlockSpec(memory_space=pltpu.SMEM)
VMEM = pl.BlockSpec(memory_space=pltpu.VMEM)
LOOSE = pl.BlockSpec(memory_space=pltpu.VMEM)
HBM = pl.BlockSpec(memory_space=pltpu.HBM)
ANY = pl.BlockSpec(memory_space=pl.ANY)


def dot_nn(a, b):
    return jnp.dot(a, b, preferred_element_type=F32)


def dot_nt(a, b):
    return lax.dot_general(a, b, (((1,), (1,)), ((), ())), preferred_element_type=F32)


def dot_tn(a, b):
    return lax.dot_general(a, b, (((0,), (0,)), ((), ())), preferred_element_type=F32)


def iota(shape, dimension):
    return lax.broadcasted_iota(I32, shape, dimension)


def call(body, outs, ins, specs, scratch=(), grant=24, cost=5, loose=(), **more):
    ins = [
        value if spec is SMEM or spec is LOOSE else pltpu.with_memory_space_constraint(value, pltpu.HBM)
        for value, spec in zip(ins, specs)
    ]
    single = not isinstance(outs, tuple)
    outs = (outs,) if single else outs
    outs = tuple(
        out if i in loose else pltpu.HBM(out.shape, out.dtype) for i, out in enumerate(outs)
    )
    more.setdefault("out_specs", (VMEM,) * len(outs))
    made = pl.pallas_call(
        body,
        out_shape=outs,
        in_specs=specs,
        scratch_shapes=scratch,
        compiler_params=pltpu.CompilerParams(vmem_limit_bytes=grant * 1024 * 1024),
        cost_estimate=pl.CostEstimate(
            flops=int(cost * 1e8), bytes_accessed=int(cost * 4e5), transcendentals=0
        ),
        **more,
    )(*ins)
    return made[0] if single else made


def bucket_of(relative):
    distance = jnp.abs(relative)
    bucket = jnp.zeros_like(relative)
    for lowest in tuple(range(1, 8)) + BOUNDS:
        bucket = bucket + (distance >= lowest).astype(I32)
    return bucket + 16 * (relative > 0).astype(I32)


class Sizes:
    def __init__(self, tokens_in, w_query, w_router, bias_table, w_in, shards):
        self.rows, self.width = tokens_in.shape[1:]
        self.part = w_query.shape[1]
        self.shards = shards
        self.experts = w_router.shape[2]
        self.bucket_part, self.heads = bias_table.shape[1:]
        self.buckets = self.bucket_part * shards
        self.hidden = w_in.shape[3]
        self.chunk = self.hidden // 6
        self.capacity = max(
            2, (3 * self.rows + 2 * self.experts - 1) // (2 * self.experts)
        )
        self.full, rest = divmod(self.capacity, 8)
        self.rest = next((power for power in (0, 1, 2, 4) if power >= rest), None)
        if self.rest is None:
            self.full, self.rest = (self.full + 1, 0)
        self.cuts = 8 // self.rest if self.rest else 0
        self.cut = self.width // self.cuts if self.rest else 0
        self.slot_width = self.full * self.width + self.cut
        self.slot_rows = self.experts * 8
        self.expert_rows = self.slot_rows * self.full + self.experts * self.rest
        self.small = -(-(self.experts + self.heads + 2) // 128) * 128
        self.small_groups = self.width // self.small
        self.small_rows = self.part // self.small_groups
        self.gain_lane = self.experts + self.heads
        self.piece = 4 * self.part + self.small_rows
        self.half_rows = 2 * self.part + self.small_rows
        self.slab = 6 * self.width + self.small * self.width // self.rows


def slot_picks(z, route):
    onehot = (route == iota((z.rows, z.experts), 1)).astype(F32)
    lower = (iota((z.rows, z.rows), 0) >= iota((z.rows, z.rows), 1)).astype(F32).astype(BF16)
    running = dot_nn(lower, onehot.astype(BF16))
    place = jnp.sum(running * onehot, axis=1, keepdims=True).astype(I32) - 1
    slots = iota((z.rows, z.slot_rows), 1)

    def pick(first, wide, shift):
        inside = (place >= first) & (place < first + wide)
        target = jnp.where(inside, route * 8 + place - first + shift, -1)
        return (slots == target).astype(F32).astype(BF16)

    picks = [pick(8 * i, 8, 0) for i in range(z.full)]
    return picks + [pick(8 * z.full, z.rest, z.rest * i) for i in range(z.cuts)]


def cut_sum(z, picks, values):
    return sum(dot_tn(pick, values[:, i * z.cut : (i + 1) * z.cut]) for i, pick in enumerate(picks))


def put_slots(z, ref, offset, picks, values):
    for i in range(z.full):
        block = dot_tn(picks[i], values)
        ref[:, :, offset : offset + z.width] = block.reshape(z.experts, 8, z.width).astype(BF16)
        offset += z.width
    if z.rest:
        block = cut_sum(z, picks[z.full :], values)
        ref[:, :, offset : offset + z.cut] = block.reshape(z.experts, 8, z.cut).astype(BF16)


def read_slots(z, ref, offset, wide):
    block = ref[:, :, offset : offset + wide].astype(F32)
    return block.reshape(z.slot_rows, wide).astype(BF16)


def get_slots(z, ref, offset, picks):
    total = 0.0
    for i in range(z.full):
        total += dot_nn(picks[i], read_slots(z, ref, offset, z.width))
        offset += z.width
    if z.rest:
        block = read_slots(z, ref, offset, z.cut)
        total += jnp.concatenate([dot_nn(pick, block) for pick in picks[z.full :]], axis=1)
    return total


def extra_picks(z):
    shape = (z.experts * z.rest, z.slot_rows)
    rows, slots = (iota(shape, 0), iota(shape, 1))
    first = (rows // z.rest) * 8 + rows % z.rest
    return [(slots == first + z.rest * i).astype(F32).astype(BF16) for i in range(z.cuts)]


def rows_of_slots(z, ref, offset):
    parts = []
    for i in range(z.full):
        parts.append(read_slots(z, ref, offset, z.width))
        offset += z.width
    if z.rest:
        block = read_slots(z, ref, offset, z.cut)
        pieces = [dot_nn(pick, block) for pick in extra_picks(z)]
        parts.append(jnp.concatenate(pieces, axis=1).astype(BF16))
    return jnp.concatenate(parts, axis=0) if len(parts) > 1 else parts[0]


def slots_of_rows(z, ref, offset, rows):
    for i in range(z.full):
        block = rows[i * z.slot_rows : (i + 1) * z.slot_rows]
        ref[:, :, offset : offset + z.width] = block.reshape(z.experts, 8, z.width).astype(BF16)
        offset += z.width
    if z.rest:
        block = cut_sum(z, extra_picks(z), rows[z.full * z.slot_rows :].astype(BF16))
        ref[:, :, offset : offset + z.cut] = block.reshape(z.experts, 8, z.cut).astype(BF16)


def fetch_weights(z, mine, place, own, other, mats, packed, sems, order=(4, 0, 1, 2, 3)):
    def copy(pieces, i, k):
        shard = place ^ k
        count = z.small_rows if i == 4 else z.part
        start = i * z.part
        source = pieces[k]
        target = pl.ds(pl.multiple_of(shard * count, 16), count)
        held = packed.at[target] if i == 4 else mats.at[i, target]
        return pltpu.make_async_copy(source.at[pl.ds(start, count)], held, sems.at[i, k])

    def start(pieces):
        for i in order:
            for k in range(z.shards):
                copy(pieces, i, k).start()

    def wait(i):
        for k in range(z.shards):
            copy(own, i, k).wait()

    @pl.when(mine)
    def _():
        start(own)

    @pl.when(jnp.logical_not(mine))
    def _():
        start(other)

    return [functools.partial(wait, i) for i in range(5)]


def fetch_halves(z, core, own, other, mats, packed, sems, order=(4, 0, 1, 2, 3)):
    def copy(source, i, k):
        count = z.small_rows if i == 4 else z.part
        start = k * z.half_rows + (i if i < 2 else i - 2) * z.part
        target = pl.ds(k * count, count)
        held = packed.at[target] if i == 4 else mats.at[i, target]
        return pltpu.make_async_copy(source.at[pl.ds(start, count)], held, sems.at[i, k])

    def start(first, second):
        for i in order:
            for k in range(z.shards):
                copy(first if i < 2 else second, i, k).start()

    def wait(i):
        for k in range(z.shards):
            copy(own, i, k).wait()

    @pl.when(core == 0)
    def _():
        start(own, other)

    @pl.when(core != 0)
    def _():
        start(other, own)

    return [functools.partial(wait, i) for i in range(5)]


def weight_scratch(z):
    return [
        pltpu.VMEM((4, z.width, z.width), BF16),
        pltpu.VMEM((z.shards * z.small_rows, z.width), BF16),
        pltpu.VMEM((z.width, z.small), BF16),
        pltpu.SemaphoreType.DMA((5, z.shards)),
    ]


def unpack_small(z, packed, small):
    for j in range(z.shards):
        for g in range(z.small_groups):
            row = j * z.part + g * z.small_rows
            small[row : row + z.small_rows, :] = packed[
                j * z.small_rows : (j + 1) * z.small_rows, g * z.small : (g + 1) * z.small
            ]


def bucket_rows(z):
    rows, buckets = (iota((z.width, z.buckets), 0), iota((z.width, z.buckets), 1))
    held = (buckets // z.bucket_part) * z.part + buckets % z.bucket_part
    return (rows == held).astype(F32).astype(BF16)


def bucket_lanes(z):
    shape = (z.buckets, 2 * z.rows)
    return (bucket_of(iota(shape, 1) - z.rows) == iota(shape, 0)).astype(F32).astype(BF16)


def identity(size):
    return (iota((size, size), 0) == iota((size, size), 1)).astype(F32).astype(BF16)


def gain_rows(z, small):
    rows, lanes = (iota((8, z.small), 0), iota((8, z.small), 1))
    pick = ((lanes == z.gain_lane + rows) & (rows < 2)).astype(F32).astype(BF16)
    made = dot_nt(pick, small)
    return (made[0:1], made[1:2])


def unit_rows(values):
    inverse = lax.rsqrt(jnp.mean(values * values, axis=-1, keepdims=True) + EPSILON)
    return (values * inverse, inverse)


def pair_masks(z):
    lanes = iota((z.rows, 128), 1)
    first = (lanes < 64).astype(F32).astype(BF16)
    return (first, (lanes >= 64).astype(F32).astype(BF16))


def double(values, masks):
    return jnp.concatenate([values * masks[0], values * masks[1]], axis=0)


def attend(z, inputs, waits, mats, packed, small, lengths, section, qkv_ref, probs_ref, attended_ref):
    waits[4]()
    unpack_small(z, packed, small)
    small_full = small[...]
    gain_one, gain_two = gain_rows(z, small_full)
    normed_one = (unit_rows(inputs)[0] * gain_one).astype(BF16)
    for i in range(3):
        waits[i]()
        qkv_ref[:, i * z.width : (i + 1) * z.width] = dot_nn(normed_one, mats[i]).astype(BF16)

    table = dot_tn(bucket_rows(z), small_full).astype(BF16)
    bias = dot_tn(table, bucket_lanes(z))[z.experts : z.experts + z.heads]

    rows, lanes = (iota((z.rows, z.rows), 0), iota((z.rows, z.rows), 1))
    segment_q, segment_k = (jnp.zeros_like(rows), jnp.zeros_like(rows))
    end = jnp.int32(0)
    for i in range(lengths.shape[2]):
        end = end + lengths[section, 0, i]
        segment_q += (rows >= end).astype(I32)
        segment_k += (lanes >= end).astype(I32)
    visible = segment_q == segment_k

    masks = pair_masks(z)
    scale = 64 ** (-0.5)
    for p in range(z.heads // 2):
        at = slice(p * 128, (p + 1) * 128)
        query = qkv_ref[:, p * 128 : (p + 1) * 128]
        key = qkv_ref[:, z.width + p * 128 : z.width + (p + 1) * 128]
        value = qkv_ref[:, 2 * z.width + p * 128 : 2 * z.width + (p + 1) * 128]
        scores = dot_nt(query, double(key, masks)) * scale
        halves = []
        for i in range(2):
            spread = jnp.broadcast_to(bias[2 * p + i : 2 * p + i + 1], (z.rows, 2 * z.rows))
            spread = pltpu.roll(spread, z.rows, 1, stride=1, stride_axis=0)[:, : z.rows]
            part = scores[:, i * z.rows : (i + 1) * z.rows] + spread
            part = jnp.where(visible, part, MASKED)
            part = jnp.exp(part - jnp.max(part, axis=-1, keepdims=True))
            halves.append(part / jnp.sum(part, axis=-1, keepdims=True))
        probs = jnp.concatenate(halves, axis=1).astype(BF16)
        probs_ref[p] = probs
        attended_ref[:, at] = dot_nn(probs, double(value, masks)).astype(BF16)

    waits[3]()
    middle = inputs + dot_nn(attended_ref[...], mats[3])
    normed_two = (unit_rows(middle)[0] * gain_two).astype(BF16)
    logits = dot_nn(normed_two, small_full)
    logits = jnp.where(iota((z.rows, z.small), 1) < z.experts, logits, MASKED)
    logits = jnp.exp(logits - jnp.max(logits, axis=-1, keepdims=True))
    router = logits / jnp.sum(logits, axis=-1, keepdims=True)
    return (middle, normed_two, router)


def fetch_kept(sources, targets, sems):
    copies = [
        pltpu.make_async_copy(source, target, sems.at[i])
        for i, (source, target) in enumerate(zip(sources, targets))
    ]
    for i in (3, 2, 0, 1):
        copies[i].start()
    return lambda i: copies[i].wait()


def chosen(z, route):
    return (route == iota((z.rows, z.small), 1)).astype(F32)


def attend_back(
    z, grad_out, token_out, grad_token, inputs, route, waits, mats, packed, small, kept, slab_out,
    slab_ref, slab_sems,
):
    def send(i, first, last):
        columns = pl.ds(first, last - first)
        copy = pltpu.make_async_copy(
            slab_ref.at[:, columns], slab_out.at[:, columns], slab_sems.at[i]
        )
        copy.start()
        return copy

    (qkv_ref, probs_ref, attended_ref, middle_ref), router_ref, arrive = kept
    waits[4]()
    unpack_small(z, packed, small)
    small_full = small[...]
    gain_one, gain_two = gain_rows(z, small_full)
    onehot = chosen(z, route)
    router = router_ref[...]
    gate = jnp.sum(router * onehot, axis=1, keepdims=True)
    grad_gate = jnp.sum(grad_out * token_out, axis=1, keepdims=True)
    grad_logits = (grad_gate * gate * (onehot - router)).astype(BF16)
    unit_two, inverse_two = unit_rows(middle_ref[...])
    grad_small = dot_tn((unit_two * gain_two).astype(BF16), grad_logits)
    grad_normed = grad_token + dot_nt(grad_logits, small_full)
    gain_two_grad = jnp.sum(grad_normed * unit_two, axis=0, keepdims=True)
    grad_unit = grad_normed * gain_two
    grad_unit -= unit_two * jnp.mean(grad_unit * unit_two, axis=1, keepdims=True)
    grad_middle = grad_out + inverse_two * grad_unit
    grad_branch = grad_middle.astype(BF16)
    arrive(2)
    slab_ref[:, 4 * z.width : 5 * z.width] = attended_ref[...]
    slab_ref[:, 5 * z.width : 6 * z.width] = grad_branch
    sent = [send(0, 4 * z.width, 6 * z.width)]
    waits[3]()
    grad_attended = dot_nt(grad_branch, mats[3]).astype(BF16)

    masks = pair_masks(z)
    scale = 64 ** (-0.5)
    arrive(0)
    arrive(1)
    relative = []
    turn = iota((z.rows, z.rows), 0) + iota((z.rows, z.rows), 1) == z.rows - 1
    turn = turn.astype(F32).astype(BF16)
    for p in range(z.heads // 2):
        at = slice(p * 128, (p + 1) * 128)
        query = qkv_ref[:, p * 128 : (p + 1) * 128]
        keys = double(qkv_ref[:, z.width + p * 128 : z.width + (p + 1) * 128], masks)
        values = double(qkv_ref[:, 2 * z.width + p * 128 : 2 * z.width + (p + 1) * 128], masks)
        grad_heads = grad_attended[:, at]
        probs_low = probs_ref[p]
        probs = probs_low.astype(F32)
        grad_probs = dot_nt(grad_heads, values)
        halves = []
        for i in range(2):
            part = slice(i * z.rows, (i + 1) * z.rows)
            product = grad_probs[:, part] * probs[:, part]
            dots = jnp.sum(product, axis=-1, keepdims=True)
            grads = (product - probs[:, part] * dots).astype(BF16)
            halves.append(grads)
        grad_scores = jnp.concatenate(halves, axis=1)
        turned = dot_nn(turn, grad_scores)
        for i in range(2):
            wide = [turned[:, i * z.rows : (i + 1) * z.rows], jnp.zeros((z.rows, z.rows), F32)]
            wide = pltpu.roll(jnp.concatenate(wide, axis=1), 1, 1, stride=1, stride_axis=0)
            relative.append(jnp.sum(wide, axis=0, keepdims=True))
        start = z.width + p * 128
        slab_ref[:, start : start + 128] = (dot_nn(grad_scores, keys) * scale).astype(BF16)
        made = dot_tn(grad_scores, query) * scale
        mask = masks[0].astype(F32)
        made = made[: z.rows] * mask + made[z.rows :] * (1.0 - mask)
        slab_ref[:, start + z.width : start + z.width + 128] = made.astype(BF16)
        made = dot_tn(probs_low, grad_heads)
        made = made[: z.rows] * mask + made[z.rows :] * (1.0 - mask)
        slab_ref[:, start + 2 * z.width : start + 2 * z.width + 128] = made.astype(BF16)

    unit_one, inverse_one = unit_rows(inputs)
    slab_ref[:, : z.width] = (unit_one * gain_one).astype(BF16)
    sent.append(send(1, 0, 4 * z.width))
    grad_normed = 0.0
    for i in range(3):
        waits[i]()
        grad_normed += dot_nt(slab_ref[:, (i + 1) * z.width : (i + 2) * z.width], mats[i])
    gain_one_grad = jnp.sum(grad_normed * unit_one, axis=0, keepdims=True)
    grad_unit = grad_normed * gain_one
    grad_unit -= unit_one * jnp.mean(grad_unit * unit_one, axis=1, keepdims=True)
    grad_in = (grad_middle + inverse_one * grad_unit).astype(BF16)

    relative += [jnp.zeros((1, 2 * z.rows), F32)] * (-z.heads % 8)
    relative = jnp.concatenate(relative, axis=0)
    lanes_of = bucket_lanes(z)
    high = relative.astype(BF16)
    table = dot_nt(lanes_of, high) + dot_nt(lanes_of, (relative - high.astype(F32)).astype(BF16))
    count = relative.shape[0]
    places = iota((count, z.small), 1) == iota((count, z.small), 0) + z.experts
    places = places & (iota((count, z.small), 0) < z.heads)
    table = dot_nn(table.astype(BF16), places.astype(F32).astype(BF16)).astype(BF16)
    grad_small += dot_nn(bucket_rows(z), table)
    gains = jnp.concatenate([gain_one_grad, gain_two_grad, jnp.zeros((6, z.width), F32)], axis=0)
    rows, lanes = (iota((8, z.small), 0), iota((8, z.small), 1))
    pick = ((lanes == z.gain_lane + rows) & (rows < 2)).astype(F32).astype(BF16)
    grad_small += dot_tn(gains.astype(BF16), pick)
    for i in range(z.width // z.rows):
        start = 6 * z.width + i * z.small
        slab_ref[:, start : start + z.small] = grad_small[i * z.rows : (i + 1) * z.rows].astype(BF16)
    sent.append(send(2, 6 * z.width, z.slab))
    return (grad_in, sent)


def pack_kernel(z, query, key, value, output, router, gain_one, gain_two, table, piece, small, sems):
    copies = [
        pltpu.make_async_copy(source.at[0], piece.at[pl.ds(i * z.part, z.part)], sems.at[i])
        for i, source in enumerate((query, key, value, output))
    ]
    for copy in copies:
        copy.start()
    gains = [gain_one[...].astype(F32), gain_two[...].astype(F32), jnp.zeros((6, z.part), F32)]
    rows, lanes = (iota((8, z.small), 0), iota((8, z.small), 1))
    pick = ((lanes == z.gain_lane + rows) & (rows < 2)).astype(F32).astype(BF16)
    small[...] = dot_tn(jnp.concatenate(gains, axis=0).astype(BF16), pick)
    small[:, : z.experts] = dot_tn(router[0], identity(z.experts))
    small[: z.bucket_part, z.experts : z.gain_lane] = table[0].astype(F32)
    for g in range(z.small_groups):
        piece[4 * z.part :, g * z.small : (g + 1) * z.small] = small[
            g * z.small_rows : (g + 1) * z.small_rows
        ].astype(BF16)
    for copy in copies:
        copy.wait()


def first_kernel(
    z, section, place, lengths, tokens, own_route, other_route, o0, o1, o2, o3, r0, r1, r2, r3,
    send, qkv, probs, attended, middle_ref, router_ref,
    mats, packed, small, sems,
):
    core = section[0]
    waits = fetch_weights(
        z, core == 0, place[0], (o0, o1, o2, o3), (r0, r1, r2, r3), mats, packed, sems)
    inputs = tokens[core].astype(F32)
    middle, normed_two, router = attend(
        z, inputs, waits, mats, packed, small, lengths, core, qkv, probs, attended
    )
    middle_ref[...] = middle
    router_ref[...] = router
    route = jnp.where(core == 0, own_route[core], other_route[...])
    put_slots(z, send, 0, slot_picks(z, route), normed_two)


def second_kernel(
    z, section, lengths, cotangent, own_route, other_route, own, other, back, middle_zero, router_zero,
    send, out_zero, qkv, probs, attended, middle_ref, router_ref,
    mats, packed, small, sems,
):
    core = section[0]
    waits = fetch_halves(
        z, core, own, other, mats, packed, sems)
    route = jnp.where(core == 0, own_route[core], other_route[...])
    gate = jnp.sum(router_zero[...] * chosen(z, route), axis=1, keepdims=True)
    token_out = get_slots(z, back, 0, slot_picks(z, route))
    layer_out = (middle_zero[...] + gate * token_out).astype(BF16)
    out_zero[...] = layer_out
    middle, normed_two, router = attend(
        z, layer_out.astype(F32), waits, mats, packed, small, lengths, core, qkv, probs, attended
    )
    middle_ref[...] = middle
    router_ref[...] = router
    route = jnp.where(core == 1, own_route[core], other_route[...])
    picks = slot_picks(z, route)
    put_slots(z, send, 0, picks, normed_two)
    gate = jnp.sum(router * chosen(z, route), axis=1, keepdims=True)
    grad = (gate * cotangent[core].astype(F32)).astype(BF16)
    put_slots(z, send, z.slot_width, picks, grad)


def third_kernel(
    z, section, cotangent, own_route, other_route, own, other, back, inputs, router_zero,
    qkv, probs, attended, middle, router,
    send, pair, slab,
    mats, packed, small, sems, held, held_sems, *kept,
):
    core = section[0]
    arrive = fetch_kept((qkv, probs, attended, middle), kept[:4], kept[4])
    waits = fetch_halves(
        z, core, own, other, mats, packed, sems, (4, 3, 0, 1, 2))
    route = jnp.where(core == 1, own_route[core], other_route[...])
    picks = slot_picks(z, route)
    token_out = get_slots(z, back, 0, picks)
    grad_token = get_slots(z, back, z.slot_width, picks)
    gate = jnp.sum(router[...] * chosen(z, route), axis=1, keepdims=True)
    arrive(3)
    pair[0] = (kept[3][...] + gate * token_out).astype(BF16)
    grad_in, copies = attend_back(
        z, cotangent[core].astype(F32), token_out, grad_token, inputs[...].astype(F32), route,
        waits, mats, packed, small, (kept[:4], router, arrive), slab, held, held_sems,
    )
    pair[1] = grad_in
    route = jnp.where(core == 0, own_route[core], other_route[...])
    gate = jnp.sum(router_zero[...] * chosen(z, route), axis=1, keepdims=True)
    grad = (gate * grad_in.astype(F32)).astype(BF16)
    put_slots(z, send, 0, slot_picks(z, route), grad)
    for copy in copies:
        copy.wait()


def fourth_kernel(
    z, section, place, out_zero, pair_one, tokens, own_route, other_route, o0, o1, o2, o3, r0, r1, r2, r3, back_out, back_grad,
    qkv, probs, attended, middle, router,
    pair, slab,
    mats, packed, small, sems, held, held_sems, *kept,
):
    core = section[0]
    arrive = fetch_kept((qkv, probs, attended, middle), kept[:4], kept[4])
    waits = fetch_weights(
        z, core == 0, place[0], (o0, o1, o2, o3), (r0, r1, r2, r3), mats, packed, sems, (4, 3, 0, 1, 2))
    route = jnp.where(core == 0, own_route[core], other_route[...])
    picks = slot_picks(z, route)
    token_out = get_slots(z, back_out, 0, picks)
    grad_token = get_slots(z, back_grad, 0, picks)
    pair[0] = out_zero[...]
    arrive(3)
    pair[1], copies = attend_back(
        z, pair_one[1].astype(F32), token_out, grad_token, tokens[core].astype(F32), route,
        waits, mats, packed, small, (kept[:4], router, arrive), slab, held, held_sems,
    )
    for copy in copies:
        copy.wait()


def fetch_experts(z, mine, own_in, own_out, other_in, other_out, w_in, w_out, sems):
    def copies(source_in, source_out, c):
        at = pl.ds(c * z.chunk, z.chunk)
        return (
            pltpu.make_async_copy(source_in.at[:, at], w_in.at[c], sems.at[2 * c]),
            pltpu.make_async_copy(source_out.at[at], w_out.at[c], sems.at[2 * c + 1]),
        )

    def start(source_in, source_out):
        for c in range(z.hidden // z.chunk):
            for copy in copies(source_in, source_out, c):
                copy.start()

    @pl.when(mine)
    def _():
        start(own_in, own_out)

    @pl.when(jnp.logical_not(mine))
    def _():
        start(other_in, other_out)

    def wait(c):
        for copy in copies(own_in, own_out, c):
            copy.wait()

    return wait


def expert_scratch(z, sums, stuff=None):
    chunks = z.hidden // z.chunk
    kept = [] if stuff is None else [
        pltpu.VMEM(stuff.shape, stuff.dtype), pltpu.SemaphoreType.DMA((2 * chunks + 1,)),
    ]
    return [
        pltpu.VMEM((chunks, z.width, z.chunk), BF16),
        pltpu.VMEM((chunks, z.chunk, z.width), BF16),
        pltpu.SemaphoreType.DMA((2 * chunks,)),
        *kept,
    ] + [pltpu.VMEM((z.expert_rows, z.width), F32)] * sums


def smooth(values):
    square = values * values
    bent = jnp.tanh(GELU_SCALE * values * (1.0 + GELU_CUBE * square))
    return (0.5 * values * (1.0 + bent), square, bent)


def smooth_slope(values, square, bent):
    inner = GELU_SCALE * (1.0 + 3.0 * GELU_CUBE * square)
    return 0.5 * (1.0 + bent) + 0.5 * values * (1.0 - bent * bent) * inner


def expert_forward_kernel(
    z, section, arrived, own_in, own_out, other_in, other_out, result, w_in, w_out, sems, produced
):
    wait = fetch_experts(
        z, section[0] == 0, own_in, own_out, other_in, other_out, w_in, w_out, sems
    )
    rows = rows_of_slots(z, arrived, 0)
    for c in range(z.hidden // z.chunk):
        wait(c)
        hidden = smooth(dot_nn(rows, w_in[c]))[0].astype(BF16)
        made = dot_nn(hidden, w_out[c])
        produced[...] = made if c == 0 else produced[...] + made
    slots_of_rows(z, result, 0, produced[...])


def expert_backward_kernel(
    z, layer, section, arrived, arrived_grad, own_in, own_out, other_in, other_out,
    result, stuff_out, w_in, w_out, sems, stuff, out_sems, grad_sum, *produced
):
    sent = []

    def send(first, wide):
        columns = pl.ds(first, wide)
        copy = pltpu.make_async_copy(
            stuff.at[:, columns], stuff_out.at[:, columns], out_sems.at[len(sent)]
        )
        copy.start()
        sent.append(copy)

    wait = fetch_experts(
        z, section[0] == layer, own_in, own_out, other_in, other_out, w_in, w_out, sems
    )
    rows = rows_of_slots(z, arrived, 0)
    grads = rows_of_slots(z, arrived_grad, z.slot_width if produced else 0)
    stuff[:, 2 * z.hidden : 2 * z.hidden + z.width] = rows
    stuff[:, 2 * z.hidden + z.width : 2 * z.hidden + 2 * z.width] = grads
    send(2 * z.hidden, 2 * z.width)
    for c in range(z.hidden // z.chunk):
        wait(c)
        before = dot_nn(rows, w_in[c])
        hidden, square, bent = smooth(before)
        hidden = hidden.astype(BF16)
        stuff[:, c * z.chunk : (c + 1) * z.chunk] = hidden
        if produced:
            made = dot_nn(hidden, w_out[c])
            produced[0][...] = made if c == 0 else produced[0][...] + made
        grad_pre = dot_nt(grads, w_out[c]) * smooth_slope(before, square, bent)
        grad_pre = grad_pre.astype(BF16)
        stuff[:, z.hidden + c * z.chunk : z.hidden + (c + 1) * z.chunk] = grad_pre
        send(c * z.chunk, z.chunk)
        send(z.hidden + c * z.chunk, z.chunk)
        made = dot_nt(grad_pre, w_in[c])
        grad_sum[...] = made if c == 0 else grad_sum[...] + made
    if produced:
        slots_of_rows(z, result, 0, produced[0][...])
    slots_of_rows(z, result, z.slot_width if produced else 0, grad_sum[...])
    for copy in sent:
        copy.wait()


def expert_weights_kernel(
    z, section, own_zero, other_zero, own_one, other_one, grad_in, grad_out, held, turned, sems
):
    step = pl.program_id(0)

    @pl.when(step == 0)
    def _():
        def copies(own, other):
            return [
                pltpu.make_async_copy(
                    source, held.at[pl.ds(i * z.expert_rows, z.expert_rows)], sems.at[i]
                )
                for i, source in enumerate((own, other))
            ]

        @pl.when(section[0] == 0)
        def _():
            for copy in copies(own_zero, other_zero):
                copy.start()

        @pl.when(section[0] != 0)
        def _():
            for copy in copies(own_one, other_one):
                copy.start()

        for copy in copies(own_zero, other_zero):
            copy.wait()
        rows = held[:, 2 * z.hidden : 2 * z.hidden + z.width]
        turned[...] = jnp.transpose(rows.astype(F32)).astype(BF16)

    start = pl.multiple_of(step * z.chunk, z.chunk)
    grad_pre = held[:, pl.ds(z.hidden + start, z.chunk)]
    hidden = held[:, pl.ds(start, z.chunk)]
    grads = held[:, 2 * z.hidden + z.width : 2 * z.hidden + 2 * z.width]
    grad_in[...] = dot_nn(turned[...], grad_pre).astype(BF16)
    grad_out[...] = dot_tn(hidden, grads).astype(BF16)


def attention_weights_kernel(z, layer, section, place, own, other, *refs):
    outs, made = (refs[: z.shards], refs[z.shards])
    second = section[0] ^ layer

    def both(column):
        at = pl.ds(pl.multiple_of(column * z.width, 128), z.width)
        return jnp.concatenate([own[:, at], other[:, at]], axis=0)

    for i, (left, right) in enumerate(
        ((0, 1 + 2 * second), (4 * second, 2 + 3 * second))
    ):
        made[...] = dot_tn(both(left), both(right))
        for k in range(z.shards):
            start = pl.multiple_of((place[0] ^ k) * z.part, 16)
            outs[k][i * z.part : (i + 1) * z.part] = made[pl.ds(start, z.part)].astype(BF16)
    for i in range(z.width // z.rows):
        columns = slice(6 * z.width + i * z.small, 6 * z.width + (i + 1) * z.small)
        total = own[:, columns].astype(F32) + other[:, columns].astype(F32)
        made[i * z.rows : (i + 1) * z.rows, : z.small] = total
    for k in range(z.shards):
        for g in range(z.small_groups):
            start = pl.multiple_of((place[0] ^ k) * z.part + g * z.small_rows, 16)
            outs[k][2 * z.part :, g * z.small : (g + 1) * z.small] = made[
                pl.ds(start, z.small_rows), : z.small
            ].astype(BF16)


def pieces_sum_kernel(*refs):
    out = refs[-1]
    rows = out.shape[1]
    total = sum(piece[...].astype(F32) for piece in refs[:-1])
    for i in range(out.shape[0]):
        out[i] = total[i * rows : (i + 1) * rows].astype(BF16)


def spread_sum_kernel(pieces, out):
    total = sum(pieces[i].astype(F32) for i in range(pieces.shape[0])).astype(BF16)
    for i in range(out.shape[0]):
        out[i] = total


def final_kernel(
    z, section, own_zero, got_zero, own_one, got_one, pair_zero, other_zero, pair_one, other_one,
    layer_out, input_grad, query, key, value, output, gain_one, gain_two, router, table, held, small,
):
    rows = own_zero.shape[1]

    def finish(own, other, micros):
        for source, targets in ((own, (query, key)), (other, (value, output))):
            for i in range(source.shape[0]):
                held[i * rows : (i + 1) * rows] = source[i].astype(F32)
            for i, target in enumerate(targets):
                target[0] = held[i * z.part : (i + 1) * z.part].astype(BF16)
            if source is own:
                for g in range(z.small_groups):
                    small[g * z.small_rows : (g + 1) * z.small_rows] = held[
                        2 * z.part :, g * z.small : (g + 1) * z.small
                    ]
        for i, pair in enumerate(micros):
            layer_out[0, i] = pair[0]
            input_grad[0, i] = pair[1]

    @pl.when(section[0] == 0)
    def _():
        finish(own_zero, got_zero, (pair_zero, other_zero))

    @pl.when(section[0] != 0)
    def _():
        finish(own_one, got_one, (other_one, pair_one))

    gains = gain_rows(z, small[...].astype(BF16))
    gain_one[...] = gains[0].astype(BF16)
    gain_two[...] = gains[1].astype(BF16)
    router[0] = dot_nt(identity(z.experts), small[:, : z.experts].astype(BF16)).astype(BF16)
    table[0] = small[: z.bucket_part, z.experts : z.gain_lane].astype(BF16)


def swap(value):
    return lax.ppermute(value, "section", [(0, 1), (1, 0)])


def cross(value, target):
    return lax.ppermute(value, "section", [(1 - target, target)])


def within(value, distance, layer):
    size = lax.axis_size("shard")
    pairs = [(layer * size + i, layer * size + (i ^ distance)) for i in range(size)]
    return lax.ppermute(value, ("section", "shard"), pairs)


def exchange(buffer, axes=("expert", "shard")):
    return lax.all_to_all(buffer, axes, split_axis=0, concat_axis=0, tiled=True)


def shards(
    tokens_in,
    cotangent,
    lengths,
    routes,
    w_query,
    w_key,
    w_value,
    w_output,
    gain_attn,
    gain_moe,
    w_router,
    bias_table,
    w_in,
    w_out,
):
    z = Sizes(tokens_in, w_query, w_router, bias_table, w_in, lax.axis_size("shard"))
    micro_count = tokens_in.shape[0]
    section = lax.axis_index("section").astype(I32)
    core = section.reshape(1)
    place = lax.axis_index("shard").astype(I32).reshape(1)

    def shape(*dims, kind=BF16):
        return jax.ShapeDtypeStruct(dims, kind)

    own_route = routes[0]
    sent_route = lax.dynamic_index_in_dim(own_route, 1 - section, 0, keepdims=False)
    piece = call(
        functools.partial(pack_kernel, z),
        shape(z.piece, z.width),
        (
            w_query, w_key, w_value, w_output, jnp.swapaxes(w_router, 1, 2), gain_attn, gain_moe,
            bias_table,
        ),
        [HBM] * 4 + [VMEM] * 4,
        [pltpu.VMEM((z.part, z.small), F32), pltpu.SemaphoreType.DMA((4,))],
        grant=8,
        cost=2,
    )

    def spread(piece, layer):
        return (piece, *[within(piece, distance, layer) for distance in range(1, z.shards)])

    def after(values, *first):
        values, unused = lax.optimization_barrier((values, first))
        return values

    half = cross(piece[: z.half_rows], 0)
    half = jnp.where(section == 0, half, piece[z.piece - z.half_rows :])
    half_one = lax.all_gather(half, "shard", axis=0, tiled=True)

    piece, sent_route = lax.optimization_barrier((piece, sent_route))
    route_pair = (own_route, swap(sent_route))
    pieces = spread(piece, 0)
    experts = (w_in[0, 0], w_out[0, 0])
    given = [cross(piece, 1)]
    given += [cross(after(member, half), 1) for member in pieces[1:]]
    given_zero = tuple(cross(member, 1) for member in experts)
    weights_zero = (*pieces, *given)

    buffer = shape(z.experts, 8, z.slot_width)
    wide_buffer = shape(z.experts, 8, 2 * z.slot_width)
    kept = (
        shape(z.rows, 3 * z.width),
        shape(z.heads // 2, z.rows, 2 * z.rows),
        shape(z.rows, z.width),
        shape(z.rows, z.width, kind=F32),
        shape(z.rows, z.small, kind=F32),
    )
    scratch = weight_scratch(z)
    rows_shape = shape(z.rows, z.width)
    slab_shape = shape(z.rows, z.slab)
    back_scratch = [
        *scratch,
        pltpu.VMEM(slab_shape.shape, slab_shape.dtype),
        pltpu.SemaphoreType.DMA((3,)),
        *[pltpu.VMEM(member.shape, member.dtype) for member in kept[:4]],
        pltpu.SemaphoreType.DMA((4,)),
    ]

    sent, *kept_zero = call(
        functools.partial(first_kernel, z),
        (buffer, *kept),
        (core, place, after(lengths, given_zero), tokens_in, *route_pair, *weights_zero),
        [SMEM, SMEM, SMEM, VMEM, VMEM, VMEM] + [ANY] * 8,
        scratch,
        cost=6,
        loose=(0,),
    )
    arrived_zero = exchange(sent)
    produced = call(
        functools.partial(expert_forward_kernel, z),
        buffer,
        (core, arrived_zero, *experts, *given_zero),
        [SMEM, LOOSE, HBM, HBM, HBM, HBM],
        expert_scratch(z, 1),
        cost=6,
        loose=(0,),
    )
    back_zero = exchange(produced)
    weights_one = (half_one, swap(after(half_one, produced)))
    given_one = tuple(cross(member, 0) for member in after(experts, produced))

    sent, out_zero, *kept_one = call(
        functools.partial(second_kernel, z),
        (wide_buffer, rows_shape, *kept),
        (core, lengths, cotangent, *route_pair, *weights_one, back_zero, *kept_zero[3:]),
        [SMEM, SMEM, VMEM, VMEM, VMEM] + [ANY] * 2 + [LOOSE] + [VMEM] * 2,
        scratch,
        cost=7,
        loose=(0,),
    )
    arrived_one = exchange(sent)
    stuff_shape = shape(z.expert_rows, 2 * z.hidden + 2 * z.width)
    result, stuff_one = call(
        lambda section, arrived, *rest: expert_backward_kernel(
            z, 1, section, arrived, arrived, *rest
        ),
        (wide_buffer, stuff_shape),
        (core, arrived_one, *experts, *given_one),
        [SMEM, LOOSE, HBM, HBM, HBM, HBM],
        expert_scratch(z, 2, stuff_shape),
        grant=28,
        cost=10,
        out_specs=(VMEM, HBM),
        loose=(0,),
    )
    back_one = exchange(result)

    pair_shape = shape(2, z.rows, z.width)
    sent, pair_one, slab_one = call(
        functools.partial(third_kernel, z),
        (buffer, pair_shape, slab_shape),
        (core, cotangent, *route_pair, *weights_one, back_one, out_zero, kept_zero[4], *kept_one),
        [SMEM, VMEM, VMEM, VMEM] + [ANY] * 2 + [LOOSE] + [VMEM] * 2 + [HBM] * 4 + [VMEM],
        back_scratch,
        cost=8,
        loose=(0,),
        out_specs=(VMEM, VMEM, HBM),
    )
    arrived_grad = exchange(sent)

    count = lax.axis_size("expert")

    def partial_sums(slab, layer):
        return call(
            functools.partial(attention_weights_kernel, z, layer),
            (shape(z.half_rows, z.width),) * z.shards,
            (core, place, slab, swap(slab)),
            [SMEM, SMEM, VMEM, LOOSE],
            [pltpu.VMEM((z.width, z.width), F32)],
            cost=4,
        )

    def send_pieces(pieces):
        size = lax.axis_size("shard")
        got = [pieces[0]]
        for distance in range(1, z.shards):
            pairs = [(i, i ^ distance) for i in range(size)]
            got.append(lax.ppermute(pieces[distance], "shard", pairs))
        return tuple(got)

    part = shape(count, z.half_rows // count, z.width)

    def pieces_sum(pieces, loose=()):
        return call(pieces_sum_kernel, part, pieces, [LOOSE] * z.shards, cost=2, loose=loose)

    sums_one = partial_sums(slab_one, 1)
    other_stuff_one = cross(stuff_one, 1)
    arrived_grad, *sums_one = lax.optimization_barrier((arrived_grad, *sums_one))
    arrived_grad = after(arrived_grad, other_stuff_one)
    got_one = send_pieces(sums_one)

    result, stuff_zero = call(
        functools.partial(expert_backward_kernel, z, 0),
        (buffer, stuff_shape),
        (core, arrived_zero, arrived_grad, *experts, *given_zero),
        [SMEM, VMEM, LOOSE, HBM, HBM, HBM, HBM],
        expert_scratch(z, 1, stuff_shape),
        grant=28,
        cost=8,
        out_specs=(VMEM, HBM),
        loose=(0,),
    )
    back_grad = after(exchange(result), got_one)
    whole_one = pieces_sum(after(got_one, back_grad)).reshape(z.half_rows, z.width)
    whole_one = lax.psum(whole_one, "expert").reshape(part.shape)
    pair_zero, slab_zero = call(
        functools.partial(fourth_kernel, z),
        (pair_shape, slab_shape),
        (
            core, place, out_zero, pair_one, tokens_in, *route_pair, *weights_zero,
            back_zero, back_grad, *kept_zero,
        ),
        [SMEM, SMEM, VMEM, VMEM, VMEM, VMEM, VMEM] + [ANY] * 8 + [VMEM] * 2 + [HBM] * 4 + [VMEM],
        back_scratch,
        cost=8,
        out_specs=(VMEM, HBM),
    )

    sums_zero = partial_sums(slab_zero, 0)
    got_zero = send_pieces(sums_zero)
    other_stuff_zero = cross(after(stuff_zero, sums_zero), 0)
    other_pairs = (cross(pair_zero, 0), cross(pair_one, 1))

    chunks = z.hidden // z.chunk
    grad_w_in, grad_w_out = call(
        functools.partial(expert_weights_kernel, z),
        (shape(z.width, z.hidden), shape(z.hidden, z.width)),
        (
            core, after(stuff_zero, sums_zero), other_stuff_zero, stuff_one, other_stuff_one,
        ),
        [SMEM, HBM, HBM, HBM, HBM],
        [
            pltpu.VMEM((2 * z.expert_rows, stuff_shape.shape[1]), BF16),
            pltpu.VMEM((z.width, 2 * z.expert_rows), BF16),
            pltpu.SemaphoreType.DMA((2,)),
        ],
        grant=28,
        cost=9,
        grid=(chunks,),
        out_specs=(
            pl.BlockSpec((z.width, z.chunk), lambda i: (0, i)),
            pl.BlockSpec((z.chunk, z.width), lambda i: (i, 0)),
        ),
    )

    got_zero = after(got_zero, whole_one, grad_w_in, other_pairs)
    summed_zero = call(
        spread_sum_kernel, part, (exchange(pieces_sum(got_zero, (0,)), "expert"),), [LOOSE],
        cost=1, loose=(0,),
    )
    whole_zero = exchange(summed_zero, "expert")

    matrix = shape(1, z.part, z.width)
    finals = call(
        functools.partial(final_kernel, z),
        (
            *[shape(1, micro_count, z.rows, z.width)] * 2,
            *[matrix] * 4,
            *[shape(1, z.part)] * 2,
            shape(1, z.experts, z.part),
            shape(1, z.bucket_part, z.heads),
        ),
        (
            core, whole_zero, swap(whole_zero), whole_one, swap(whole_one),
            pair_zero, other_pairs[0], pair_one, other_pairs[1],
        ),
        [SMEM] + [LOOSE] * 8,
        [pltpu.VMEM((z.half_rows, z.width), F32), pltpu.VMEM((z.part, z.small), F32)],
        cost=3,
    )
    finals = (*finals[:8], jnp.swapaxes(finals[8], 1, 2), finals[9])
    return (*finals, grad_w_in[None, None], grad_w_out[None, None])


def solution(mesh):
    both = ("expert", "shard")
    plain = P("section", "shard", None)
    gains = P("section", "shard")
    blocks = P("section", None, both, None)
    experts = P("section", both, None, None)
    tokens = P(None, both, None)
    attention = (plain, plain, plain, plain, gains, gains, plain, plain, experts, experts)
    return jax.shard_map(
        shards,
        mesh=mesh,
        in_specs=(tokens, tokens, tokens, blocks, *attention),
        out_specs=(blocks, blocks, *attention),
        check_vma=False,
    )
```

```python
import functools

import jax
import jax.numpy as jnp
from jax import lax
from jax.experimental import pallas as pl
from jax.experimental.pallas import tpu as pltpu
from jax.sharding import PartitionSpec as P

EPSILON = 1e-06
BOUNDS = (8, 12, 16, 23, 32, 46, 64, 91)
MASKED = -1e30
F32 = jnp.float32
BF16 = jnp.bfloat16
I32 = jnp.int32
GELU_SCALE = 0.7978845608028654
GELU_CUBE = 0.044715
SMEM = pl.BlockSpec(memory_space=pltpu.SMEM)
VMEM = pl.BlockSpec(memory_space=pltpu.VMEM)
LOOSE = pl.BlockSpec(memory_space=pltpu.VMEM)
HBM = pl.BlockSpec(memory_space=pltpu.HBM)
ANY = pl.BlockSpec(memory_space=pl.ANY)


def dot_nn(a, b):
    return jnp.dot(a, b, preferred_element_type=F32)


def dot_nt(a, b):
    return lax.dot_general(a, b, (((1,), (1,)), ((), ())), preferred_element_type=F32)


def dot_tn(a, b):
    return lax.dot_general(a, b, (((0,), (0,)), ((), ())), preferred_element_type=F32)


def iota(shape, dimension):
    return lax.broadcasted_iota(I32, shape, dimension)


def call(body, outs, ins, specs, scratch=(), grant=24, cost=5, loose=(), **more):
    ins = [
        value if spec is SMEM or spec is LOOSE else pltpu.with_memory_space_constraint(value, pltpu.HBM)
        for value, spec in zip(ins, specs)
    ]
    single = not isinstance(outs, tuple)
    outs = (outs,) if single else outs
    outs = tuple(
        out if i in loose else pltpu.HBM(out.shape, out.dtype) for i, out in enumerate(outs)
    )
    more.setdefault("out_specs", (VMEM,) * len(outs))
    made = pl.pallas_call(
        body,
        out_shape=outs,
        in_specs=specs,
        scratch_shapes=scratch,
        compiler_params=pltpu.CompilerParams(vmem_limit_bytes=grant * 1024 * 1024),
        cost_estimate=pl.CostEstimate(
            flops=int(cost * 1e8), bytes_accessed=int(cost * 4e5), transcendentals=0
        ),
        **more,
    )(*ins)
    return made[0] if single else made


def bucket_of(relative):
    distance = jnp.abs(relative)
    bucket = jnp.zeros_like(relative)
    for lowest in tuple(range(1, 8)) + BOUNDS:
        bucket = bucket + (distance >= lowest).astype(I32)
    return bucket + 16 * (relative > 0).astype(I32)


class Sizes:
    def __init__(self, tokens_in, w_query, w_router, bias_table, w_in, shards):
        self.rows, self.width = tokens_in.shape[1:]
        self.part = w_query.shape[1]
        self.shards = shards
        self.experts = w_router.shape[2]
        self.bucket_part, self.heads = bias_table.shape[1:]
        self.buckets = self.bucket_part * shards
        self.hidden = w_in.shape[3]
        self.chunk = self.hidden // 6
        self.capacity = max(
            2, (3 * self.rows + 2 * self.experts - 1) // (2 * self.experts)
        )
        self.full, rest = divmod(self.capacity, 8)
        self.rest = next((power for power in (0, 1, 2, 4) if power >= rest), None)
        if self.rest is None:
            self.full, self.rest = (self.full + 1, 0)
        self.cuts = 8 // self.rest if self.rest else 0
        self.cut = self.width // self.cuts if self.rest else 0
        self.slot_width = self.full * self.width + self.cut
        self.slot_rows = self.experts * 8
        self.expert_rows = self.slot_rows * self.full + self.experts * self.rest
        self.small = -(-(self.experts + self.heads + 2) // 128) * 128
        self.small_groups = self.width // self.small
        self.small_rows = self.part // self.small_groups
        self.gain_lane = self.experts + self.heads
        self.piece = 4 * self.part + self.small_rows
        self.half_rows = 2 * self.part + self.small_rows
        self.slab = 6 * self.width + self.small * self.width // self.rows


def slot_picks(z, route):
    onehot = (route == iota((z.rows, z.experts), 1)).astype(F32)
    lower = (iota((z.rows, z.rows), 0) >= iota((z.rows, z.rows), 1)).astype(F32).astype(BF16)
    running = dot_nn(lower, onehot.astype(BF16))
    place = jnp.sum(running * onehot, axis=1, keepdims=True).astype(I32) - 1
    slots = iota((z.rows, z.slot_rows), 1)

    def pick(first, wide, shift):
        inside = (place >= first) & (place < first + wide)
        target = jnp.where(inside, route * 8 + place - first + shift, -1)
        return (slots == target).astype(F32).astype(BF16)

    picks = [pick(8 * i, 8, 0) for i in range(z.full)]
    return picks + [pick(8 * z.full, z.rest, z.rest * i) for i in range(z.cuts)]


def cut_sum(z, picks, values):
    return sum(dot_tn(pick, values[:, i * z.cut : (i + 1) * z.cut]) for i, pick in enumerate(picks))


def put_slots(z, ref, offset, picks, values):
    for i in range(z.full):
        block = dot_tn(picks[i], values)
        ref[:, :, offset : offset + z.width] = block.reshape(z.experts, 8, z.width).astype(BF16)
        offset += z.width
    if z.rest:
        block = cut_sum(z, picks[z.full :], values)
        ref[:, :, offset : offset + z.cut] = block.reshape(z.experts, 8, z.cut).astype(BF16)


def read_slots(z, ref, offset, wide):
    block = ref[:, :, offset : offset + wide].astype(F32)
    return block.reshape(z.slot_rows, wide).astype(BF16)


def get_slots(z, ref, offset, picks):
    total = 0.0
    for i in range(z.full):
        total += dot_nn(picks[i], read_slots(z, ref, offset, z.width))
        offset += z.width
    if z.rest:
        block = read_slots(z, ref, offset, z.cut)
        total += jnp.concatenate([dot_nn(pick, block) for pick in picks[z.full :]], axis=1)
    return total


def extra_picks(z):
    shape = (z.experts * z.rest, z.slot_rows)
    rows, slots = (iota(shape, 0), iota(shape, 1))
    first = (rows // z.rest) * 8 + rows % z.rest
    return [(slots == first + z.rest * i).astype(F32).astype(BF16) for i in range(z.cuts)]


def rows_of_slots(z, ref, offset):
    parts = []
    for i in range(z.full):
        parts.append(read_slots(z, ref, offset, z.width))
        offset += z.width
    if z.rest:
        block = read_slots(z, ref, offset, z.cut)
        pieces = [dot_nn(pick, block) for pick in extra_picks(z)]
        parts.append(jnp.concatenate(pieces, axis=1).astype(BF16))
    return jnp.concatenate(parts, axis=0) if len(parts) > 1 else parts[0]


def slots_of_rows(z, ref, offset, rows):
    for i in range(z.full):
        block = rows[i * z.slot_rows : (i + 1) * z.slot_rows]
        ref[:, :, offset : offset + z.width] = block.reshape(z.experts, 8, z.width).astype(BF16)
        offset += z.width
    if z.rest:
        block = cut_sum(z, extra_picks(z), rows[z.full * z.slot_rows :].astype(BF16))
        ref[:, :, offset : offset + z.cut] = block.reshape(z.experts, 8, z.cut).astype(BF16)


def fetch_weights(z, mine, place, own, other, mats, packed, sems, order=(4, 0, 1, 2, 3)):
    def copy(pieces, i, k):
        shard = place ^ k
        count = z.small_rows if i == 4 else z.part
        start = i * z.part
        source = pieces[k]
        target = pl.ds(pl.multiple_of(shard * count, 16), count)
        held = packed.at[target] if i == 4 else mats.at[i, target]
        return pltpu.make_async_copy(source.at[pl.ds(start, count)], held, sems.at[i, k])

    def start(pieces):
        for i in order:
            for k in range(z.shards):
                copy(pieces, i, k).start()

    def wait(i):
        for k in range(z.shards):
            copy(own, i, k).wait()

    @pl.when(mine)
    def _():
        start(own)

    @pl.when(jnp.logical_not(mine))
    def _():
        start(other)

    return [functools.partial(wait, i) for i in range(5)]


def fetch_halves(z, core, own, other, mats, packed, sems, order=(4, 0, 1, 2, 3)):
    def copy(source, i, k):
        count = z.small_rows if i == 4 else z.part
        start = k * z.half_rows + (i if i < 2 else i - 2) * z.part
        target = pl.ds(k * count, count)
        held = packed.at[target] if i == 4 else mats.at[i, target]
        return pltpu.make_async_copy(source.at[pl.ds(start, count)], held, sems.at[i, k])

    def start(first, second):
        for i in order:
            for k in range(z.shards):
                copy(first if i < 2 else second, i, k).start()

    def wait(i):
        for k in range(z.shards):
            copy(own, i, k).wait()

    @pl.when(core == 0)
    def _():
        start(own, other)

    @pl.when(core != 0)
    def _():
        start(other, own)

    return [functools.partial(wait, i) for i in range(5)]


def weight_scratch(z):
    return [
        pltpu.VMEM((4, z.width, z.width), BF16),
        pltpu.VMEM((z.shards * z.small_rows, z.width), BF16),
        pltpu.VMEM((z.width, z.small), BF16),
        pltpu.SemaphoreType.DMA((5, z.shards)),
    ]


def unpack_small(z, packed, small):
    for j in range(z.shards):
        for g in range(z.small_groups):
            row = j * z.part + g * z.small_rows
            small[row : row + z.small_rows, :] = packed[
                j * z.small_rows : (j + 1) * z.small_rows, g * z.small : (g + 1) * z.small
            ]


def bucket_rows(z):
    rows, buckets = (iota((z.width, z.buckets), 0), iota((z.width, z.buckets), 1))
    held = (buckets // z.bucket_part) * z.part + buckets % z.bucket_part
    return (rows == held).astype(F32).astype(BF16)


def bucket_lanes(z):
    shape = (z.buckets, 2 * z.rows)
    return (bucket_of(iota(shape, 1) - z.rows) == iota(shape, 0)).astype(F32).astype(BF16)


def identity(size):
    return (iota((size, size), 0) == iota((size, size), 1)).astype(F32).astype(BF16)


def gain_rows(z, small):
    rows, lanes = (iota((8, z.small), 0), iota((8, z.small), 1))
    pick = ((lanes == z.gain_lane + rows) & (rows < 2)).astype(F32).astype(BF16)
    made = dot_nt(pick, small)
    return (made[0:1], made[1:2])


def unit_rows(values):
    inverse = lax.rsqrt(jnp.mean(values * values, axis=-1, keepdims=True) + EPSILON)
    return (values * inverse, inverse)


def pair_masks(z):
    lanes = iota((z.rows, 128), 1)
    first = (lanes < 64).astype(F32).astype(BF16)
    return (first, (lanes >= 64).astype(F32).astype(BF16))


def double(values, masks):
    return jnp.concatenate([values * masks[0], values * masks[1]], axis=0)


def attend(z, inputs, waits, mats, packed, small, lengths, section, qkv_ref, probs_ref, attended_ref):
    waits[4]()
    unpack_small(z, packed, small)
    small_full = small[...]
    gain_one, gain_two = gain_rows(z, small_full)
    normed_one = (unit_rows(inputs)[0] * gain_one).astype(BF16)
    for i in range(3):
        waits[i]()
        qkv_ref[:, i * z.width : (i + 1) * z.width] = dot_nn(normed_one, mats[i]).astype(BF16)

    table = dot_tn(bucket_rows(z), small_full).astype(BF16)
    bias = dot_tn(table, bucket_lanes(z))[z.experts : z.experts + z.heads]

    rows, lanes = (iota((z.rows, z.rows), 0), iota((z.rows, z.rows), 1))
    segment_q, segment_k = (jnp.zeros_like(rows), jnp.zeros_like(rows))
    end = jnp.int32(0)
    for i in range(lengths.shape[2]):
        end = end + lengths[section, 0, i]
        segment_q += (rows >= end).astype(I32)
        segment_k += (lanes >= end).astype(I32)
    visible = segment_q == segment_k

    masks = pair_masks(z)
    scale = 64 ** (-0.5)
    for p in range(z.heads // 2):
        at = slice(p * 128, (p + 1) * 128)
        query = qkv_ref[:, p * 128 : (p + 1) * 128]
        key = qkv_ref[:, z.width + p * 128 : z.width + (p + 1) * 128]
        value = qkv_ref[:, 2 * z.width + p * 128 : 2 * z.width + (p + 1) * 128]
        scores = dot_nt(query, double(key, masks)) * scale
        halves = []
        for i in range(2):
            spread = jnp.broadcast_to(bias[2 * p + i : 2 * p + i + 1], (z.rows, 2 * z.rows))
            spread = pltpu.roll(spread, z.rows, 1, stride=1, stride_axis=0)[:, : z.rows]
            part = scores[:, i * z.rows : (i + 1) * z.rows] + spread
            part = jnp.where(visible, part, MASKED)
            part = jnp.exp(part - jnp.max(part, axis=-1, keepdims=True))
            halves.append(part / jnp.sum(part, axis=-1, keepdims=True))
        probs = jnp.concatenate(halves, axis=1).astype(BF16)
        probs_ref[p] = probs
        attended_ref[:, at] = dot_nn(probs, double(value, masks)).astype(BF16)

    waits[3]()
    middle = inputs + dot_nn(attended_ref[...], mats[3])
    normed_two = (unit_rows(middle)[0] * gain_two).astype(BF16)
    logits = dot_nn(normed_two, small_full)
    logits = jnp.where(iota((z.rows, z.small), 1) < z.experts, logits, MASKED)
    logits = jnp.exp(logits - jnp.max(logits, axis=-1, keepdims=True))
    router = logits / jnp.sum(logits, axis=-1, keepdims=True)
    return (middle, normed_two, router)


def chosen(z, route):
    return (route == iota((z.rows, z.small), 1)).astype(F32)


def attend_back(
    z, grad_out, token_out, grad_token, inputs, route, waits, mats, packed, small, kept, slab_out,
    slab_ref, slab_sems,
):
    def send(i, first, last):
        columns = pl.ds(first, last - first)
        copy = pltpu.make_async_copy(
            slab_ref.at[:, columns], slab_out.at[:, columns], slab_sems.at[i]
        )
        copy.start()
        return copy

    qkv_ref, probs_ref, attended_ref, middle_ref, router_ref = kept
    waits[4]()
    unpack_small(z, packed, small)
    small_full = small[...]
    gain_one, gain_two = gain_rows(z, small_full)
    onehot = chosen(z, route)
    router = router_ref[...]
    gate = jnp.sum(router * onehot, axis=1, keepdims=True)
    grad_gate = jnp.sum(grad_out * token_out, axis=1, keepdims=True)
    grad_logits = (grad_gate * gate * (onehot - router)).astype(BF16)
    unit_two, inverse_two = unit_rows(middle_ref[...])
    grad_small = dot_tn((unit_two * gain_two).astype(BF16), grad_logits)
    grad_normed = grad_token + dot_nt(grad_logits, small_full)
    gain_two_grad = jnp.sum(grad_normed * unit_two, axis=0, keepdims=True)
    grad_unit = grad_normed * gain_two
    grad_unit -= unit_two * jnp.mean(grad_unit * unit_two, axis=1, keepdims=True)
    grad_middle = grad_out + inverse_two * grad_unit
    grad_branch = grad_middle.astype(BF16)
    slab_ref[:, 4 * z.width : 5 * z.width] = attended_ref[...]
    slab_ref[:, 5 * z.width : 6 * z.width] = grad_branch
    sent = [send(0, 4 * z.width, 6 * z.width)]
    waits[3]()
    grad_attended = dot_nt(grad_branch, mats[3]).astype(BF16)

    masks = pair_masks(z)
    scale = 64 ** (-0.5)
    relative = []
    turn = iota((z.rows, z.rows), 0) + iota((z.rows, z.rows), 1) == z.rows - 1
    turn = turn.astype(F32).astype(BF16)
    for p in range(z.heads // 2):
        at = slice(p * 128, (p + 1) * 128)
        query = qkv_ref[:, p * 128 : (p + 1) * 128]
        keys = double(qkv_ref[:, z.width + p * 128 : z.width + (p + 1) * 128], masks)
        values = double(qkv_ref[:, 2 * z.width + p * 128 : 2 * z.width + (p + 1) * 128], masks)
        grad_heads = grad_attended[:, at]
        probs_low = probs_ref[p]
        probs = probs_low.astype(F32)
        grad_probs = dot_nt(grad_heads, values)
        halves = []
        for i in range(2):
            part = slice(i * z.rows, (i + 1) * z.rows)
            product = grad_probs[:, part] * probs[:, part]
            dots = jnp.sum(product, axis=-1, keepdims=True)
            grads = (product - probs[:, part] * dots).astype(BF16)
            halves.append(grads)
        grad_scores = jnp.concatenate(halves, axis=1)
        turned = dot_nn(turn, grad_scores)
        for i in range(2):
            wide = [turned[:, i * z.rows : (i + 1) * z.rows], jnp.zeros((z.rows, z.rows), F32)]
            wide = pltpu.roll(jnp.concatenate(wide, axis=1), 1, 1, stride=1, stride_axis=0)
            relative.append(jnp.sum(wide, axis=0, keepdims=True))
        start = z.width + p * 128
        slab_ref[:, start : start + 128] = (dot_nn(grad_scores, keys) * scale).astype(BF16)
        made = dot_tn(grad_scores, query) * scale
        mask = masks[0].astype(F32)
        made = made[: z.rows] * mask + made[z.rows :] * (1.0 - mask)
        slab_ref[:, start + z.width : start + z.width + 128] = made.astype(BF16)
        made = dot_tn(probs_low, grad_heads)
        made = made[: z.rows] * mask + made[z.rows :] * (1.0 - mask)
        slab_ref[:, start + 2 * z.width : start + 2 * z.width + 128] = made.astype(BF16)

    unit_one, inverse_one = unit_rows(inputs)
    slab_ref[:, : z.width] = (unit_one * gain_one).astype(BF16)
    sent.append(send(1, 0, 4 * z.width))
    grad_normed = 0.0
    for i in range(3):
        waits[i]()
        grad_normed += dot_nt(slab_ref[:, (i + 1) * z.width : (i + 2) * z.width], mats[i])
    gain_one_grad = jnp.sum(grad_normed * unit_one, axis=0, keepdims=True)
    grad_unit = grad_normed * gain_one
    grad_unit -= unit_one * jnp.mean(grad_unit * unit_one, axis=1, keepdims=True)
    grad_in = (grad_middle + inverse_one * grad_unit).astype(BF16)

    relative += [jnp.zeros((1, 2 * z.rows), F32)] * (-z.heads % 8)
    relative = jnp.concatenate(relative, axis=0)
    lanes_of = bucket_lanes(z)
    high = relative.astype(BF16)
    table = dot_nt(lanes_of, high) + dot_nt(lanes_of, (relative - high.astype(F32)).astype(BF16))
    count = relative.shape[0]
    places = iota((count, z.small), 1) == iota((count, z.small), 0) + z.experts
    places = places & (iota((count, z.small), 0) < z.heads)
    table = dot_nn(table.astype(BF16), places.astype(F32).astype(BF16)).astype(BF16)
    grad_small += dot_nn(bucket_rows(z), table)
    gains = jnp.concatenate([gain_one_grad, gain_two_grad, jnp.zeros((6, z.width), F32)], axis=0)
    rows, lanes = (iota((8, z.small), 0), iota((8, z.small), 1))
    pick = ((lanes == z.gain_lane + rows) & (rows < 2)).astype(F32).astype(BF16)
    grad_small += dot_tn(gains.astype(BF16), pick)
    for i in range(z.width // z.rows):
        start = 6 * z.width + i * z.small
        slab_ref[:, start : start + z.small] = grad_small[i * z.rows : (i + 1) * z.rows].astype(BF16)
    sent.append(send(2, 6 * z.width, z.slab))
    return (grad_in, sent)


def pack_kernel(z, query, key, value, output, router, gain_one, gain_two, table, piece, small, sems):
    copies = [
        pltpu.make_async_copy(source.at[0], piece.at[pl.ds(i * z.part, z.part)], sems.at[i])
        for i, source in enumerate((query, key, value, output))
    ]
    for copy in copies:
        copy.start()
    gains = [gain_one[...].astype(F32), gain_two[...].astype(F32), jnp.zeros((6, z.part), F32)]
    rows, lanes = (iota((8, z.small), 0), iota((8, z.small), 1))
    pick = ((lanes == z.gain_lane + rows) & (rows < 2)).astype(F32).astype(BF16)
    small[...] = dot_tn(jnp.concatenate(gains, axis=0).astype(BF16), pick)
    small[:, : z.experts] = dot_tn(router[0], identity(z.experts))
    small[: z.bucket_part, z.experts : z.gain_lane] = table[0].astype(F32)
    for g in range(z.small_groups):
        piece[4 * z.part :, g * z.small : (g + 1) * z.small] = small[
            g * z.small_rows : (g + 1) * z.small_rows
        ].astype(BF16)
    for copy in copies:
        copy.wait()


def first_kernel(
    z, section, place, lengths, tokens, own_route, other_route, o0, o1, o2, o3, r0, r1, r2, r3,
    send, qkv, probs, attended, middle_ref, router_ref,
    mats, packed, small, sems,
):
    core = section[0]
    waits = fetch_weights(
        z, core == 0, place[0], (o0, o1, o2, o3), (r0, r1, r2, r3), mats, packed, sems)
    inputs = tokens[core].astype(F32)
    middle, normed_two, router = attend(
        z, inputs, waits, mats, packed, small, lengths, core, qkv, probs, attended
    )
    middle_ref[...] = middle
    router_ref[...] = router
    route = jnp.where(core == 0, own_route[core], other_route[...])
    put_slots(z, send, 0, slot_picks(z, route), normed_two)


def second_kernel(
    z, section, lengths, cotangent, own_route, other_route, own, other, back, middle_zero, router_zero,
    send, out_zero, qkv, probs, attended, middle_ref, router_ref,
    mats, packed, small, sems,
):
    core = section[0]
    waits = fetch_halves(
        z, core, own, other, mats, packed, sems)
    route = jnp.where(core == 0, own_route[core], other_route[...])
    gate = jnp.sum(router_zero[...] * chosen(z, route), axis=1, keepdims=True)
    token_out = get_slots(z, back, 0, slot_picks(z, route))
    layer_out = (middle_zero[...] + gate * token_out).astype(BF16)
    out_zero[...] = layer_out
    middle, normed_two, router = attend(
        z, layer_out.astype(F32), waits, mats, packed, small, lengths, core, qkv, probs, attended
    )
    middle_ref[...] = middle
    router_ref[...] = router
    route = jnp.where(core == 1, own_route[core], other_route[...])
    picks = slot_picks(z, route)
    put_slots(z, send, 0, picks, normed_two)
    gate = jnp.sum(router * chosen(z, route), axis=1, keepdims=True)
    grad = (gate * cotangent[core].astype(F32)).astype(BF16)
    put_slots(z, send, z.slot_width, picks, grad)


def third_kernel(
    z, section, cotangent, own_route, other_route, own, other, back, inputs, router_zero,
    qkv, probs, attended, middle, router,
    send, pair, slab,
    mats, packed, small, sems, held, held_sems,
):
    core = section[0]
    waits = fetch_halves(
        z, core, own, other, mats, packed, sems, (4, 3, 0, 1, 2))
    route = jnp.where(core == 1, own_route[core], other_route[...])
    picks = slot_picks(z, route)
    token_out = get_slots(z, back, 0, picks)
    grad_token = get_slots(z, back, z.slot_width, picks)
    gate = jnp.sum(router[...] * chosen(z, route), axis=1, keepdims=True)
    pair[0] = (middle[...] + gate * token_out).astype(BF16)
    grad_in, copies = attend_back(
        z, cotangent[core].astype(F32), token_out, grad_token, inputs[...].astype(F32), route,
        waits, mats, packed, small, (qkv, probs, attended, middle, router), slab, held, held_sems,
    )
    pair[1] = grad_in
    route = jnp.where(core == 0, own_route[core], other_route[...])
    gate = jnp.sum(router_zero[...] * chosen(z, route), axis=1, keepdims=True)
    grad = (gate * grad_in.astype(F32)).astype(BF16)
    put_slots(z, send, 0, slot_picks(z, route), grad)
    for copy in copies:
        copy.wait()


def fourth_kernel(
    z, section, place, out_zero, pair_one, tokens, own_route, other_route, o0, o1, o2, o3, r0, r1, r2, r3, back_out, back_grad,
    qkv, probs, attended, middle, router,
    pair, slab,
    mats, packed, small, sems, held, held_sems,
):
    core = section[0]
    waits = fetch_weights(
        z, core == 0, place[0], (o0, o1, o2, o3), (r0, r1, r2, r3), mats, packed, sems, (4, 3, 0, 1, 2))
    route = jnp.where(core == 0, own_route[core], other_route[...])
    picks = slot_picks(z, route)
    token_out = get_slots(z, back_out, 0, picks)
    grad_token = get_slots(z, back_grad, 0, picks)
    pair[0] = out_zero[...]
    pair[1], copies = attend_back(
        z, pair_one[1].astype(F32), token_out, grad_token, tokens[core].astype(F32), route,
        waits, mats, packed, small, (qkv, probs, attended, middle, router), slab, held, held_sems,
    )
    for copy in copies:
        copy.wait()


def fetch_experts(z, mine, own_in, own_out, other_in, other_out, w_in, w_out, sems):
    def copies(source_in, source_out, c):
        at = pl.ds(c * z.chunk, z.chunk)
        return (
            pltpu.make_async_copy(source_in.at[:, at], w_in.at[c], sems.at[2 * c]),
            pltpu.make_async_copy(source_out.at[at], w_out.at[c], sems.at[2 * c + 1]),
        )

    def start(source_in, source_out):
        for c in range(z.hidden // z.chunk):
            for copy in copies(source_in, source_out, c):
                copy.start()

    @pl.when(mine)
    def _():
        start(own_in, own_out)

    @pl.when(jnp.logical_not(mine))
    def _():
        start(other_in, other_out)

    def wait(c):
        for copy in copies(own_in, own_out, c):
            copy.wait()

    return wait


def expert_scratch(z, sums, stuff=None):
    chunks = z.hidden // z.chunk
    kept = [] if stuff is None else [
        pltpu.VMEM(stuff.shape, stuff.dtype), pltpu.SemaphoreType.DMA((2 * chunks + 1,)),
    ]
    return [
        pltpu.VMEM((chunks, z.width, z.chunk), BF16),
        pltpu.VMEM((chunks, z.chunk, z.width), BF16),
        pltpu.SemaphoreType.DMA((2 * chunks,)),
        *kept,
    ] + [pltpu.VMEM((z.expert_rows, z.width), F32)] * sums


def smooth(values):
    square = values * values
    bent = jnp.tanh(GELU_SCALE * values * (1.0 + GELU_CUBE * square))
    return (0.5 * values * (1.0 + bent), square, bent)


def smooth_slope(values, square, bent):
    inner = GELU_SCALE * (1.0 + 3.0 * GELU_CUBE * square)
    return 0.5 * (1.0 + bent) + 0.5 * values * (1.0 - bent * bent) * inner


def expert_forward_kernel(
    z, section, arrived, own_in, own_out, other_in, other_out, result, w_in, w_out, sems, produced
):
    wait = fetch_experts(
        z, section[0] == 0, own_in, own_out, other_in, other_out, w_in, w_out, sems
    )
    rows = rows_of_slots(z, arrived, 0)
    for c in range(z.hidden // z.chunk):
        wait(c)
        hidden = smooth(dot_nn(rows, w_in[c]))[0].astype(BF16)
        made = dot_nn(hidden, w_out[c])
        produced[...] = made if c == 0 else produced[...] + made
    slots_of_rows(z, result, 0, produced[...])


def expert_backward_kernel(
    z, layer, section, arrived, arrived_grad, own_in, own_out, other_in, other_out,
    result, stuff_out, w_in, w_out, sems, stuff, out_sems, grad_sum, *produced
):
    sent = []

    def send(first, wide):
        columns = pl.ds(first, wide)
        copy = pltpu.make_async_copy(
            stuff.at[:, columns], stuff_out.at[:, columns], out_sems.at[len(sent)]
        )
        copy.start()
        sent.append(copy)

    wait = fetch_experts(
        z, section[0] == layer, own_in, own_out, other_in, other_out, w_in, w_out, sems
    )
    rows = rows_of_slots(z, arrived, 0)
    grads = rows_of_slots(z, arrived_grad, z.slot_width if produced else 0)
    stuff[:, 2 * z.hidden : 2 * z.hidden + z.width] = rows
    stuff[:, 2 * z.hidden + z.width : 2 * z.hidden + 2 * z.width] = grads
    send(2 * z.hidden, 2 * z.width)
    for c in range(z.hidden // z.chunk):
        wait(c)
        before = dot_nn(rows, w_in[c])
        hidden, square, bent = smooth(before)
        hidden = hidden.astype(BF16)
        stuff[:, c * z.chunk : (c + 1) * z.chunk] = hidden
        if produced:
            made = dot_nn(hidden, w_out[c])
            produced[0][...] = made if c == 0 else produced[0][...] + made
        grad_pre = dot_nt(grads, w_out[c]) * smooth_slope(before, square, bent)
        grad_pre = grad_pre.astype(BF16)
        stuff[:, z.hidden + c * z.chunk : z.hidden + (c + 1) * z.chunk] = grad_pre
        send(c * z.chunk, z.chunk)
        send(z.hidden + c * z.chunk, z.chunk)
        made = dot_nt(grad_pre, w_in[c])
        grad_sum[...] = made if c == 0 else grad_sum[...] + made
    if produced:
        slots_of_rows(z, result, 0, produced[0][...])
    slots_of_rows(z, result, z.slot_width if produced else 0, grad_sum[...])
    for copy in sent:
        copy.wait()


def expert_weights_kernel(
    z, section, own_zero, other_zero, own_one, other_one, grad_in, grad_out, held, turned, sems
):
    step = pl.program_id(0)

    @pl.when(step == 0)
    def _():
        def copies(own, other):
            return [
                pltpu.make_async_copy(
                    source, held.at[pl.ds(i * z.expert_rows, z.expert_rows)], sems.at[i]
                )
                for i, source in enumerate((own, other))
            ]

        @pl.when(section[0] == 0)
        def _():
            for copy in copies(own_zero, other_zero):
                copy.start()

        @pl.when(section[0] != 0)
        def _():
            for copy in copies(own_one, other_one):
                copy.start()

        for copy in copies(own_zero, other_zero):
            copy.wait()
        rows = held[:, 2 * z.hidden : 2 * z.hidden + z.width]
        turned[...] = jnp.transpose(rows.astype(F32)).astype(BF16)

    start = pl.multiple_of(step * z.chunk, z.chunk)
    grad_pre = held[:, pl.ds(z.hidden + start, z.chunk)]
    hidden = held[:, pl.ds(start, z.chunk)]
    grads = held[:, 2 * z.hidden + z.width : 2 * z.hidden + 2 * z.width]
    grad_in[...] = dot_nn(turned[...], grad_pre).astype(BF16)
    grad_out[...] = dot_tn(hidden, grads).astype(BF16)


def attention_weights_kernel(z, layer, section, place, own, other, *refs):
    outs, made = (refs[: z.shards], refs[z.shards])
    second = section[0] ^ layer

    def both(column):
        at = pl.ds(pl.multiple_of(column * z.width, 128), z.width)
        return jnp.concatenate([own[:, at], other[:, at]], axis=0)

    for i, (left, right) in enumerate(
        ((0, 1 + 2 * second), (4 * second, 2 + 3 * second))
    ):
        made[...] = dot_tn(both(left), both(right))
        for k in range(z.shards):
            start = pl.multiple_of((place[0] ^ k) * z.part, 16)
            outs[k][i * z.part : (i + 1) * z.part] = made[pl.ds(start, z.part)].astype(BF16)
    for i in range(z.width // z.rows):
        columns = slice(6 * z.width + i * z.small, 6 * z.width + (i + 1) * z.small)
        total = own[:, columns].astype(F32) + other[:, columns].astype(F32)
        made[i * z.rows : (i + 1) * z.rows, : z.small] = total
    for k in range(z.shards):
        for g in range(z.small_groups):
            start = pl.multiple_of((place[0] ^ k) * z.part + g * z.small_rows, 16)
            outs[k][2 * z.part :, g * z.small : (g + 1) * z.small] = made[
                pl.ds(start, z.small_rows), : z.small
            ].astype(BF16)


def pieces_sum_kernel(*refs):
    out = refs[-1]
    rows = out.shape[1]
    total = sum(piece[...].astype(F32) for piece in refs[:-1])
    for i in range(out.shape[0]):
        out[i] = total[i * rows : (i + 1) * rows].astype(BF16)


def spread_sum_kernel(pieces, out):
    total = sum(pieces[i].astype(F32) for i in range(pieces.shape[0])).astype(BF16)
    for i in range(out.shape[0]):
        out[i] = total


def final_kernel(
    z, section, own_zero, got_zero, own_one, got_one, pair_zero, other_zero, pair_one, other_one,
    layer_out, input_grad, query, key, value, output, gain_one, gain_two, router, table, held, small,
):
    rows = own_zero.shape[1]

    def finish(own, other, micros):
        for source, targets in ((own, (query, key)), (other, (value, output))):
            for i in range(source.shape[0]):
                held[i * rows : (i + 1) * rows] = source[i].astype(F32)
            for i, target in enumerate(targets):
                target[0] = held[i * z.part : (i + 1) * z.part].astype(BF16)
            if source is own:
                for g in range(z.small_groups):
                    small[g * z.small_rows : (g + 1) * z.small_rows] = held[
                        2 * z.part :, g * z.small : (g + 1) * z.small
                    ]
        for i, pair in enumerate(micros):
            layer_out[0, i] = pair[0]
            input_grad[0, i] = pair[1]

    @pl.when(section[0] == 0)
    def _():
        finish(own_zero, got_zero, (pair_zero, other_zero))

    @pl.when(section[0] != 0)
    def _():
        finish(own_one, got_one, (other_one, pair_one))

    gains = gain_rows(z, small[...].astype(BF16))
    gain_one[...] = gains[0].astype(BF16)
    gain_two[...] = gains[1].astype(BF16)
    router[0] = dot_nt(identity(z.experts), small[:, : z.experts].astype(BF16)).astype(BF16)
    table[0] = small[: z.bucket_part, z.experts : z.gain_lane].astype(BF16)


def swap(value):
    return lax.ppermute(value, "section", [(0, 1), (1, 0)])


def cross(value, target):
    return lax.ppermute(value, "section", [(1 - target, target)])


def within(value, distance, layer):
    size = lax.axis_size("shard")
    pairs = [(layer * size + i, layer * size + (i ^ distance)) for i in range(size)]
    return lax.ppermute(value, ("section", "shard"), pairs)


def exchange(buffer, axes=("expert", "shard")):
    return lax.all_to_all(buffer, axes, split_axis=0, concat_axis=0, tiled=True)


def shards(
    tokens_in,
    cotangent,
    lengths,
    routes,
    w_query,
    w_key,
    w_value,
    w_output,
    gain_attn,
    gain_moe,
    w_router,
    bias_table,
    w_in,
    w_out,
):
    z = Sizes(tokens_in, w_query, w_router, bias_table, w_in, lax.axis_size("shard"))
    micro_count = tokens_in.shape[0]
    section = lax.axis_index("section").astype(I32)
    core = section.reshape(1)
    place = lax.axis_index("shard").astype(I32).reshape(1)

    def shape(*dims, kind=BF16):
        return jax.ShapeDtypeStruct(dims, kind)

    own_route = routes[0]
    sent_route = lax.dynamic_index_in_dim(own_route, 1 - section, 0, keepdims=False)
    piece = call(
        functools.partial(pack_kernel, z),
        shape(z.piece, z.width),
        (
            w_query, w_key, w_value, w_output, jnp.swapaxes(w_router, 1, 2), gain_attn, gain_moe,
            bias_table,
        ),
        [HBM] * 4 + [VMEM] * 4,
        [pltpu.VMEM((z.part, z.small), F32), pltpu.SemaphoreType.DMA((4,))],
        grant=8,
        cost=2,
    )

    def spread(piece, layer):
        return (piece, *[within(piece, distance, layer) for distance in range(1, z.shards)])

    def after(values, *first):
        values, unused = lax.optimization_barrier((values, first))
        return values

    half = cross(piece[: z.half_rows], 0)
    half = jnp.where(section == 0, half, piece[z.piece - z.half_rows :])
    half_one = lax.all_gather(half, "shard", axis=0, tiled=True)

    piece, sent_route = lax.optimization_barrier((piece, sent_route))
    route_pair = (own_route, swap(sent_route))
    pieces = spread(piece, 0)
    experts = (w_in[0, 0], w_out[0, 0])
    given = [cross(piece, 1)]
    early = (given[0], route_pair[1], half)
    given += [cross(after(member, early), 1) for member in pieces[1:]]
    given_zero = tuple(cross(member, 1) for member in after(experts, given))
    weights_zero = (*pieces, *given)

    buffer = shape(z.experts, 8, z.slot_width)
    wide_buffer = shape(z.experts, 8, 2 * z.slot_width)
    kept = (
        shape(z.rows, 3 * z.width),
        shape(z.heads // 2, z.rows, 2 * z.rows),
        shape(z.rows, z.width),
        shape(z.rows, z.width, kind=F32),
        shape(z.rows, z.small, kind=F32),
    )
    scratch = weight_scratch(z)
    rows_shape = shape(z.rows, z.width)
    slab_shape = shape(z.rows, z.slab)
    back_scratch = [
        *scratch,
        pltpu.VMEM(slab_shape.shape, slab_shape.dtype),
        pltpu.SemaphoreType.DMA((3,)),
    ]

    sent, *kept_zero = call(
        functools.partial(first_kernel, z),
        (buffer, *kept),
        (core, place, lengths, tokens_in, *route_pair, *weights_zero),
        [SMEM, SMEM, SMEM, VMEM, VMEM, VMEM] + [ANY] * 8,
        scratch,
        cost=6,
        loose=(0,),
    )
    arrived_zero = exchange(sent)
    produced = call(
        functools.partial(expert_forward_kernel, z),
        buffer,
        (core, arrived_zero, *experts, *given_zero),
        [SMEM, LOOSE, HBM, HBM, HBM, HBM],
        expert_scratch(z, 1),
        cost=6,
        loose=(0,),
    )
    back_zero = exchange(produced)
    weights_one = (half_one, swap(after(half_one, produced)))
    given_one = tuple(cross(member, 0) for member in after(experts, produced))

    sent, out_zero, *kept_one = call(
        functools.partial(second_kernel, z),
        (wide_buffer, rows_shape, *kept),
        (core, lengths, cotangent, *route_pair, *weights_one, back_zero, *kept_zero[3:]),
        [SMEM, SMEM, VMEM, VMEM, VMEM] + [ANY] * 2 + [LOOSE] + [VMEM] * 2,
        scratch,
        cost=7,
        loose=(0,),
    )
    arrived_one = exchange(sent)
    stuff_shape = shape(z.expert_rows, 2 * z.hidden + 2 * z.width)
    result, stuff_one = call(
        lambda section, arrived, *rest: expert_backward_kernel(
            z, 1, section, arrived, arrived, *rest
        ),
        (wide_buffer, stuff_shape),
        (core, arrived_one, *experts, *given_one),
        [SMEM, LOOSE, HBM, HBM, HBM, HBM],
        expert_scratch(z, 2, stuff_shape),
        grant=28,
        cost=10,
        out_specs=(VMEM, HBM),
        loose=(0,),
    )
    back_one = exchange(result)

    pair_shape = shape(2, z.rows, z.width)
    sent, pair_one, slab_one = call(
        functools.partial(third_kernel, z),
        (buffer, pair_shape, slab_shape),
        (core, cotangent, *route_pair, *weights_one, back_one, out_zero, kept_zero[4], *kept_one),
        [SMEM, VMEM, VMEM, VMEM] + [ANY] * 2 + [LOOSE] + [VMEM] * 7,
        back_scratch,
        cost=8,
        loose=(0,),
        out_specs=(VMEM, VMEM, HBM),
    )
    arrived_grad = exchange(sent)

    count = lax.axis_size("expert")

    def partial_sums(slab, other, layer):
        return call(
            functools.partial(attention_weights_kernel, z, layer),
            (shape(z.half_rows, z.width),) * z.shards,
            (core, place, slab, other),
            [SMEM, SMEM, VMEM, LOOSE],
            [pltpu.VMEM((z.width, z.width), F32)],
            cost=4,
        )

    def send_pieces(pieces):
        size = lax.axis_size("shard")
        got = [pieces[0]]
        for distance in range(1, z.shards):
            pairs = [(i, i ^ distance) for i in range(size)]
            got.append(lax.ppermute(pieces[distance], "shard", pairs))
        return tuple(got)

    part = shape(count, z.half_rows // count, z.width)

    def pieces_sum(pieces, loose=()):
        return call(pieces_sum_kernel, part, pieces, [LOOSE] * z.shards, cost=2, loose=loose)

    sums_one = partial_sums(slab_one, swap(slab_one), 1)
    other_stuff_one = cross(stuff_one, 1)
    arrived_grad, *sums_one = lax.optimization_barrier((arrived_grad, *sums_one))
    arrived_grad = after(arrived_grad, other_stuff_one)
    got_one = send_pieces(sums_one)

    result, stuff_zero = call(
        functools.partial(expert_backward_kernel, z, 0),
        (buffer, stuff_shape),
        (core, arrived_zero, arrived_grad, *experts, *given_zero),
        [SMEM, VMEM, LOOSE, HBM, HBM, HBM, HBM],
        expert_scratch(z, 1, stuff_shape),
        grant=28,
        cost=8,
        out_specs=(VMEM, HBM),
        loose=(0,),
    )
    back_grad = after(exchange(result), got_one)
    whole_one = pieces_sum(after(got_one, back_grad)).reshape(z.half_rows, z.width)
    whole_one = lax.psum(whole_one, "expert").reshape(part.shape)
    pair_zero, slab_zero = call(
        functools.partial(fourth_kernel, z),
        (pair_shape, slab_shape),
        (
            core, place, out_zero, pair_one, tokens_in, *route_pair, *weights_zero,
            back_zero, back_grad, *kept_zero,
        ),
        [SMEM, SMEM, VMEM, VMEM, VMEM, VMEM, VMEM] + [ANY] * 8 + [VMEM] * 7,
        back_scratch,
        cost=8,
        out_specs=(VMEM, HBM),
    )

    other_slab = swap(slab_zero)
    sums_zero = partial_sums(slab_zero, other_slab, 0)
    got_zero = send_pieces(sums_zero)
    other_stuff_zero = cross(after(stuff_zero, other_slab), 0)
    other_pairs = (cross(pair_zero, 0), cross(pair_one, 1))

    chunks = z.hidden // z.chunk
    grad_w_in, grad_w_out = call(
        functools.partial(expert_weights_kernel, z),
        (shape(z.width, z.hidden), shape(z.hidden, z.width)),
        (
            core, after(stuff_zero, sums_zero), other_stuff_zero, stuff_one, other_stuff_one,
        ),
        [SMEM, HBM, HBM, HBM, HBM],
        [
            pltpu.VMEM((2 * z.expert_rows, stuff_shape.shape[1]), BF16),
            pltpu.VMEM((z.width, 2 * z.expert_rows), BF16),
            pltpu.SemaphoreType.DMA((2,)),
        ],
        grant=28,
        cost=9,
        grid=(chunks,),
        out_specs=(
            pl.BlockSpec((z.width, z.chunk), lambda i: (0, i)),
            pl.BlockSpec((z.chunk, z.width), lambda i: (i, 0)),
        ),
    )

    got_zero = after(got_zero, whole_one, grad_w_in, other_pairs)
    summed_zero = call(
        spread_sum_kernel, part, (exchange(pieces_sum(got_zero, (0,)), "expert"),), [LOOSE],
        cost=1, loose=(0,),
    )
    whole_zero = exchange(summed_zero, "expert")

    matrix = shape(1, z.part, z.width)
    finals = call(
        functools.partial(final_kernel, z),
        (
            *[shape(1, micro_count, z.rows, z.width)] * 2,
            *[matrix] * 4,
            *[shape(1, z.part)] * 2,
            shape(1, z.experts, z.part),
            shape(1, z.bucket_part, z.heads),
        ),
        (
            core, whole_zero, swap(whole_zero), whole_one, swap(whole_one),
            pair_zero, other_pairs[0], pair_one, other_pairs[1],
        ),
        [SMEM] + [LOOSE] * 8,
        [pltpu.VMEM((z.half_rows, z.width), F32), pltpu.VMEM((z.part, z.small), F32)],
        cost=3,
    )
    finals = (*finals[:8], jnp.swapaxes(finals[8], 1, 2), finals[9])
    return (*finals, grad_w_in[None, None], grad_w_out[None, None])


def solution(mesh):
    both = ("expert", "shard")
    plain = P("section", "shard", None)
    gains = P("section", "shard")
    blocks = P("section", None, both, None)
    experts = P("section", both, None, None)
    tokens = P(None, both, None)
    attention = (plain, plain, plain, plain, gains, gains, plain, plain, experts, experts)
    return jax.shard_map(
        shards,
        mesh=mesh,
        in_specs=(tokens, tokens, tokens, blocks, *attention),
        out_specs=(blocks, blocks, *attention),
        check_vma=False,
    )
```
